32 devices in a mesh: clip: 8 (over z, y), win: 4 (over x, core).
Axes of the slice: x: 2, y: 2, z: 4, core: 2. Of those that a mesh axis runs over, the one named last changes fastest.
Arguments:
- tokens: bfloat16 [16, 8, 392, 512], P('clip', 'win'), may hold values from -6 to 6
- cotangent: bfloat16 [16, 8, 392, 512], P('clip', 'win'), may hold values from -6 to 6
- adapter_ids: int32 [16], P('clip'), may hold values from 0 to 7, as said below
- ln1_gain: bfloat16 [512], P('clip'), may hold values from 0.5 to 1.5
- qkv_weight: bfloat16 [512, 1536], P('clip', 'win'), may hold values from -0.25 to 0.25
- qkv_bias: bfloat16 [1536], P('clip'), may hold values from -1.5 to 1.5
- proj_weight: bfloat16 [512, 512], P('clip', 'win'), may hold values from -2 to 2
- proj_bias: bfloat16 [512], P('clip'), may hold values from -1.5 to 1.5
- ln2_gain: bfloat16 [512], P('clip'), may hold values from 0.5 to 1.5
- fc1_weight: bfloat16 [512, 2048], P('clip', 'win'), may hold values from -0.25 to 0.25
- fc1_bias: bfloat16 [2048], P('clip'), may hold values from -1.5 to 1.5
- fc2_weight: bfloat16 [2048, 512], P('clip', 'win'), may hold values from -0.125 to 0.125
- fc2_bias: bfloat16 [512], P('clip'), may hold values from -1.5 to 1.5
- bias_table: bfloat16 [16, 2535], replicated, may hold values from -4 to 4
- qkv_down: bfloat16 [8, 512, 16], P('win', 'clip'), may hold values from -0.25 to 0.25
- qkv_up: bfloat16 [8, 16, 1536], P('win', None, 'clip'), may hold values from -0.75 to 0.75
- proj_down: bfloat16 [8, 512, 16], P('win', 'clip'), may hold values from -2 to 2
- proj_up: bfloat16 [8, 16, 512], P('win', None, 'clip'), may hold values from -0.75 to 0.75
- fc1_down: bfloat16 [8, 512, 16], P('win', 'clip'), may hold values from -0.25 to 0.25
- fc1_up: bfloat16 [8, 16, 2048], P('win', None, 'clip'), may hold values from -0.75 to 0.75
- fc2_down: bfloat16 [8, 2048, 16], P('win', 'clip'), may hold values from -0.125 to 0.125
- fc2_up: bfloat16 [8, 16, 512], P('win', None, 'clip'), may hold values from -0.75 to 0.75
Outputs:
- activations: bfloat16 [16, 8, 392, 512], P('clip', 'win')
- input_grad: bfloat16 [16, 8, 392, 512], P('clip', 'win')
- grad_qkv_down: float32 [8, 512, 16], P('win', 'clip')
- grad_qkv_up: float32 [8, 16, 1536], P('win', None, 'clip')
- grad_proj_down: float32 [8, 512, 16], P('win', 'clip')
- grad_proj_up: float32 [8, 16, 512], P('win', None, 'clip')
- grad_fc1_down: float32 [8, 512, 16], P('win', 'clip')
- grad_fc1_up: float32 [8, 16, 2048], P('win', None, 'clip')
- grad_fc2_down: float32 [8, 2048, 16], P('win', 'clip')
- grad_fc2_up: float32 [8, 16, 512], P('win', None, 'clip')
The draws below stay inside these ranges and needn't reach their ends.
Inputs may be any that keep to these rules, and one draw needn't show every extreme that they name: `adapter_ids`: ids never fall from one clip to the next (clips are grouped by adapter); adapters 0 and 7 appear in every draw.
All inputs are finite; a program needn't handle non-finite values.
Results may differ from the reference program's by a relative error of at most 0.017.
Values may be sent and summed in bfloat16 or wider, within the bound.
A program may use at most 256 MiB of HBM per device.

```python
import jax
import jax.numpy as jnp
from jax import lax

D = 512
HEADS = 16
FF = 2048
RANK = 16
ADAPTERS = 8
WINDOWS = 8
WIN_TOK = 392
BIAS_ROWS = 2535
CLIPS = 16


def draw_adapter_ids(key, part):
    inner = jax.random.randint(key, (CLIPS - 2,), 0, ADAPTERS).astype(jnp.int32)
    ends = jnp.array([0, ADAPTERS - 1], jnp.int32)
    return jnp.sort(jnp.concatenate([ends, inner]))


def levels(key, shape, pieces, smallest, high):
    level, own = 1.0, jax.random.fold_in(key, 6)
    for axis_at, blocks in pieces:
        steps = jnp.exp(jax.random.uniform(jax.random.fold_in(own, axis_at), (blocks,), jnp.float32, smallest / len(pieces), high / len(pieces)))
        level = level * jnp.repeat(steps, shape[axis_at] // blocks).reshape([-1 if axis == axis_at else 1 for axis in range(len(shape))])
    return level


def gaussian(own_key, extent, spread, reach, split=(), held_as=jnp.bfloat16):
    values = spread * jax.random.normal(own_key, extent, jnp.float32)
    if split:
        values = values * levels(own_key, extent, split, -0.22, 0.18)
    return jnp.clip(values, -reach, reach).astype(held_as)


def setup_inputs(seed: int = 0) -> dict:
    keys = jax.random.split(jax.random.key(seed), 23)
    tokens = gaussian(keys[0], (CLIPS, WINDOWS, WIN_TOK, D), 1.0, 6.0, ((0, 8), (1, 4)))
    cotangent = gaussian(keys[1], (CLIPS, WINDOWS, WIN_TOK, D), 1.0, 6.0, ((0, 8), (1, 4)))
    adapter_ids = draw_adapter_ids(jax.random.fold_in(keys[22], 71), 0)
    ln1_gain = jnp.clip(1.0 + 0.1 * jax.random.normal(keys[3], (D,), jnp.float32), 0.5, 1.5).astype(jnp.bfloat16)
    qkv_weight = gaussian(keys[4], (D, 3 * D), D ** -0.5, 0.25, ((0, 8), (1, 4)))
    qkv_bias = gaussian(keys[5], (3 * D,), 0.3, 1.5, ((0, 8),))
    proj_weight = gaussian(keys[6], (D, D), (max(D // 64, 1)) ** -0.5, 2.0, ((0, 8), (1, 4)))
    proj_bias = gaussian(keys[7], (D,), 0.3, 1.5, ((0, 8),))
    ln2_gain = jnp.clip(1.0 + 0.1 * jax.random.normal(keys[8], (D,), jnp.float32), 0.5, 1.5).astype(jnp.bfloat16)
    fc1_weight = gaussian(keys[9], (D, FF), D ** -0.5, 0.25, ((0, 8), (1, 4)))
    fc1_bias = gaussian(keys[10], (FF,), 0.3, 1.5, ((0, 8),))
    fc2_weight = gaussian(keys[11], (FF, D), FF ** -0.5, 0.125, ((0, 8), (1, 4)))
    fc2_bias = gaussian(keys[12], (D,), 0.3, 1.5, ((0, 8),))
    bias_table = gaussian(keys[13], (HEADS, BIAS_ROWS), 1.0, 4.0)
    qkv_down = gaussian(keys[14], (ADAPTERS, D, RANK), D ** -0.5, 0.25, ((0, 4), (1, 8)))
    qkv_up = gaussian(keys[15], (ADAPTERS, RANK, 3 * D), (4 * RANK) ** -0.5, 0.75, ((0, 4), (2, 8)))
    proj_down = gaussian(keys[16], (ADAPTERS, D, RANK), (max(D // 64, 1)) ** -0.5, 2.0, ((0, 4), (1, 8)))
    proj_up = gaussian(keys[17], (ADAPTERS, RANK, D), (4 * RANK) ** -0.5, 0.75, ((0, 4), (2, 8)))
    fc1_down = gaussian(keys[18], (ADAPTERS, D, RANK), D ** -0.5, 0.25, ((0, 4), (1, 8)))
    fc1_up = gaussian(keys[19], (ADAPTERS, RANK, FF), (4 * RANK) ** -0.5, 0.75, ((0, 4), (2, 8)))
    fc2_down = gaussian(keys[20], (ADAPTERS, FF, RANK), FF ** -0.5, 0.125, ((0, 4), (1, 8)))
    fc2_up = gaussian(keys[21], (ADAPTERS, RANK, D), (4 * RANK) ** -0.5, 0.75, ((0, 4), (2, 8)))
    return {"tokens": tokens, "cotangent": cotangent, "adapter_ids": adapter_ids, "ln1_gain": ln1_gain, "qkv_weight": qkv_weight, "qkv_bias": qkv_bias, "proj_weight": proj_weight, "proj_bias": proj_bias, "ln2_gain": ln2_gain, "fc1_weight": fc1_weight, "fc1_bias": fc1_bias, "fc2_weight": fc2_weight, "fc2_bias": fc2_bias, "bias_table": bias_table, "qkv_down": qkv_down, "qkv_up": qkv_up, "proj_down": proj_down, "proj_up": proj_up, "fc1_down": fc1_down, "fc1_up": fc1_up, "fc2_down": fc2_down, "fc2_up": fc2_up}


@jax.custom_vjp
def low(v):
    return lax.optimization_barrier(v.astype(jnp.bfloat16)).astype(jnp.float32)

@jax.custom_vjp
def low_back(v):
    return v

def low_keep(v):
    return (low(v), None)

def low_pass(kept, grad):
    return (grad,)

def back_keep(v):
    return (v, None)

def back_low(kept, grad):
    return (low(grad),)
low.defvjp(low_keep, low_pass)
low_back.defvjp(back_keep, back_low)
highest = lax.Precision.HIGHEST
masked_score = -1000000000.0

def matmul(left, right):
    return jnp.dot(left, right, precision=highest)

def norm_rows(values, gain):
    average = lax.optimization_barrier(jnp.mean(values, axis=-1, keepdims=True))
    centred = values - average
    variance = lax.optimization_barrier(jnp.mean(centred * centred, axis=-1, keepdims=True))
    return centred * lax.rsqrt(variance + 1e-05) * gain

def gelu_exact(values):
    return 0.5 * values * (1.0 + lax.erf(values * 0.7071067811865476))

def to_grid(windows):
    features = windows.shape[-1]
    return windows.reshape(2, 2, 2, 8, 7, 7, features).transpose(0, 3, 1, 4, 2, 5, 6).reshape(16, 14, 14, features)

def to_windows(grid):
    features = grid.shape[-1]
    return grid.reshape(2, 8, 2, 7, 2, 7, features).transpose(0, 2, 4, 1, 3, 5, 6).reshape(8, 392, features)

def region(length, window_size, amount):
    cells = jnp.arange(length)
    return jnp.where(cells < length - window_size, 0, jnp.where(cells < length - amount, 1, 2)).astype(jnp.int32)

def window_tables():
    token_ids = jnp.arange(WIN_TOK)
    depth_pos = token_ids // 49
    height_pos = token_ids // 7 % 7
    width_pos = token_ids % 7
    relative = (depth_pos[:, None] - depth_pos[None, :] + 7) * 169 + (height_pos[:, None] - height_pos[None, :] + 6) * 13 + (width_pos[:, None] - width_pos[None, :] + 6)
    labels = region(16, 8, 4)[:, None, None] * 9 + region(14, 7, 3)[None, :, None] * 3 + region(14, 7, 3)[None, None, :]
    window_labels = to_windows(labels[..., None])[..., 0]
    allowed = window_labels[:, :, None] == window_labels[:, None, :]
    return (relative.astype(jnp.int32), allowed)

def clip_forward(clip_tokens, hot, adapters, frozen, pos_bias, allowed):
    selected = [jnp.tensordot(hot, table, axes=1, precision=highest) for table in adapters]
    triple_down_matrix, triple_up_matrix, projection_down_matrix, projection_up_matrix, hidden_down_matrix, hidden_up_matrix, outer_down_matrix, outer_up_matrix = selected
    gain_first, triple_input_weight, triple_input_bias, projection_weight_matrix, projection_bias_vector, gain_second, hidden_dense_weight, hidden_dense_bias, outer_dense_weight, outer_dense_bias = frozen
    features = clip_tokens.shape[-1]
    head_count = pos_bias.shape[0]
    head_size = features // head_count
    scale = head_size ** (-0.5)
    rows_in = clip_tokens.reshape(-1, features)
    first_norm = low(norm_rows(rows_in, gain_first))
    rolled_tokens = low_back(to_windows(jnp.roll(to_grid(first_norm.reshape(WINDOWS, WIN_TOK, features)), (-4, -3, -3), axis=(0, 1, 2))).reshape(-1, features))
    triple_reduced = low_back(low(matmul(rolled_tokens, triple_down_matrix)))
    triple_rows = matmul(rolled_tokens, triple_input_weight) + triple_input_bias + matmul(triple_reduced, triple_up_matrix)

    def split_heads(columns):
        return low_back(low(columns)).reshape(WINDOWS, WIN_TOK, head_count, head_size)
    query = split_heads(triple_rows[:, :features])
    keys_all = split_heads(triple_rows[:, features:2 * features])
    values_all = split_heads(triple_rows[:, 2 * features:])

    def window(operands):
        query_rows, key_rows, value_rows, allowed_pairs = operands
        raw_scores = low_back(jnp.einsum('qhd,khd->hqk', query_rows, key_rows, precision=highest))
        scores = jnp.where(allowed_pairs[None], raw_scores * scale + pos_bias, masked_score)
        largest = lax.optimization_barrier(jnp.max(scores, axis=-1, keepdims=True))
        log_total = largest + jnp.log(lax.optimization_barrier(jnp.sum(jnp.exp(scores - largest), axis=-1, keepdims=True)))
        probs = low(jnp.exp(scores - log_total))
        return low(jnp.einsum('hqk,khd->qhd', probs, value_rows, precision=highest))
    attended = lax.map(jax.checkpoint(window), (query, keys_all, values_all, allowed))
    unshifted_tokens = low_back(to_windows(jnp.roll(to_grid(attended.reshape(WINDOWS, WIN_TOK, features)), (4, 3, 3), axis=(0, 1, 2))).reshape(-1, features))
    projection_reduced = low_back(low(matmul(unshifted_tokens, projection_down_matrix)))
    branch_attn = low_back(matmul(unshifted_tokens, projection_weight_matrix) + projection_bias_vector + matmul(projection_reduced, projection_up_matrix))
    middle_state = rows_in + branch_attn
    second_norm = low(norm_rows(middle_state, gain_second))
    hidden_rank_reduced = low_back(low(matmul(second_norm, hidden_down_matrix)))
    preactivation = low_back(matmul(second_norm, hidden_dense_weight) + hidden_dense_bias + matmul(hidden_rank_reduced, hidden_up_matrix))
    gelu_activated = low(gelu_exact(preactivation))
    outer_rank_reduced = low_back(low(matmul(gelu_activated, outer_down_matrix)))
    branch_mlp = low_back(matmul(gelu_activated, outer_dense_weight) + outer_dense_bias + matmul(outer_rank_reduced, outer_up_matrix))
    return (middle_state + branch_mlp).reshape(WINDOWS, WIN_TOK, features)

def reference(tokens, cotangent, adapter_ids, ln1_gain, qkv_weight, qkv_bias, proj_weight, proj_bias, ln2_gain, fc1_weight, fc1_bias, fc2_weight, fc2_bias, bias_table, qkv_down, qkv_up, proj_down, proj_up, fc1_down, fc1_up, fc2_down, fc2_up):
    frozen = tuple((value.astype(jnp.float32) for value in (ln1_gain, qkv_weight, qkv_bias, proj_weight, proj_bias, ln2_gain, fc1_weight, fc1_bias, fc2_weight, fc2_bias)))
    adapters = tuple((value.astype(jnp.float32) for value in (qkv_down, qkv_up, proj_down, proj_up, fc1_down, fc1_up, fc2_down, fc2_up)))
    relative, allowed = window_tables()
    pos_bias = jnp.take(bias_table.astype(jnp.float32), relative, axis=1)
    hots = (adapter_ids[:, None] == jnp.arange(ADAPTERS, dtype=jnp.int32)[None, :]).astype(jnp.float32)

    def step(totals, operands):
        clip_tokens, clip_cotangent, hot = operands

        def forward(tokens_in, adapters_in):
            return clip_forward(tokens_in, hot, adapters_in, frozen, pos_bias, allowed)
        result, pull = jax.vjp(forward, clip_tokens.astype(jnp.float32), adapters)
        grad_tokens, grad_adapters = pull(clip_cotangent.astype(jnp.float32))
        totals = jax.tree.map(lambda left, right: left + right, totals, grad_adapters)
        return (totals, (result.astype(jnp.bfloat16), grad_tokens.astype(jnp.bfloat16)))
    zeros = tuple((jnp.zeros_like(value) for value in adapters))
    totals, (activations, input_grad) = lax.scan(step, zeros, (tokens, cotangent, hots))
    return (activations, input_grad, totals[0], totals[1], totals[2], totals[3], totals[4], totals[5], totals[6], totals[7])
```

```python
import functools
import jax
import jax.numpy as jnp
from jax import lax
from jax.experimental import pallas as pl
from jax.experimental.pallas import tpu as pltpu
from jax.sharding import PartitionSpec as P

BF = jnp.bfloat16
F32 = jnp.float32
NN = (((1,), (0,)), ((), ()))
NT = (((1,), (1,)), ((), ()))
TN = (((0,), (0,)), ((), ()))
LOG2E = 1.4426950408889634
LN2 = 0.6931471805599453
FAR = 1e9
VMEM_LIMIT = 60 * 2**20
TOK = 392


def dot(left, right, dims):
    return lax.dot_general(left, right, dims, preferred_element_type=F32)


def lane_ids(shape):
    return lax.broadcasted_iota(jnp.int32, shape, len(shape) - 1)


def norm_stats(values):
    average = jnp.mean(values, axis=-1, keepdims=True)
    centred = values - average
    variance = jnp.mean(centred * centred, axis=-1, keepdims=True)
    inverse = lax.rsqrt(variance + 1e-05)
    return centred * inverse, inverse


def norm_back(gradient, gain, normed, inverse):
    scaled = gradient * gain
    centre = jnp.mean(scaled, axis=-1, keepdims=True)
    slope = jnp.mean(scaled * normed, axis=-1, keepdims=True)
    return inverse * (scaled - centre - normed * slope)


def add_rows(ref, at, value, first):
    @pl.when(first)
    def _():
        ref[0, :, at] = value

    @pl.when(jnp.logical_not(first))
    def _():
        ref[0, :, at] += value


def attend_kernel(
    ids_ref,
    x_ref,
    gain_ref,
    weight_ref,
    bias_ref,
    down_ref,
    up_ref,
    key_mask_ref,
    query_mask_ref,
    table_ref,
    probs_ref,
    out_ref,
    qkv_ref,
    reduced_ref,
    keys,
    queries,
    values_t,
    out_t,
    scores,
    *,
    scale,
    per_group,
    width,
):
    group = pl.program_id(1)
    groups = pl.num_programs(1)
    feats = x_ref.shape[-1]

    @pl.when(group == 0)
    def _():
        normed, _ = norm_stats(x_ref[0].astype(F32))
        low = (normed * gain_ref[...]).astype(BF)
        reduced = dot(low, down_ref[0], NT).astype(BF)
        reduced_ref[0] = reduced

        def columns(part):
            at = pl.ds(part * feats, feats)
            return (
                dot(low, weight_ref[:, at], NN)
                + bias_ref[:, at]
                + dot(reduced, up_ref[0, :, at], NN)
            )

        query = (columns(0) * (scale * LOG2E)).astype(BF)
        queries[...] = query
        qkv_ref[0, :, :feats] = query
        key = columns(1).astype(BF)
        qkv_ref[0, :, feats : 2 * feats] = key
        for g in range(feats // 128):
            keys[:, 256 * g : 256 * g + 128] = key[:, 128 * g : 128 * g + 128]
            keys[:, 256 * g + 128 : 256 * g + 256] = key_mask_ref[0]
        value = columns(2)
        qkv_ref[0, :, 2 * feats :] = value.astype(BF)
        values_t[...] = value.T.astype(BF)

    keys_now = keys[:, pl.ds(pl.multiple_of(group * 256, 256), 256)]
    query_now = queries[:, pl.ds(pl.multiple_of(group * 128, 128), 128)]
    head_of_lane = lane_ids(query_now.shape) // width

    def raw(h):
        own = jnp.where(head_of_lane == h, query_now, jnp.zeros_like(query_now))
        own = jnp.concatenate([own, query_mask_ref[0]], axis=1)
        return dot(keys_now, own, NT) + table_ref[group * per_group + h]

    def finish(h):
        score = scores[h % 2]
        largest = jnp.max(score, axis=0, keepdims=True)
        probs = jnp.exp2(score - largest)
        total = jnp.sum(probs, axis=0, keepdims=True)
        probs = (probs * (1.0 / total)).astype(BF)
        probs_ref[0, h] = probs
        at = pl.ds(pl.multiple_of((group * per_group + h) * width, width), width)
        out_t[at, :] = dot(values_t[at, :], probs, NN)

    scores[0] = raw(0)
    for h in range(per_group):
        if h + 1 < per_group:
            scores[(h + 1) % 2] = raw(h + 1)
        finish(h)

    @pl.when(group == groups - 1)
    def _():
        out_ref[0] = out_t[...].T.astype(BF)


def dense_kernel(
    ids_ref,
    x_ref,
    attn_ref,
    dy_ref,
    gain_ref,
    proj_ref,
    proj_bias_ref,
    fc1_ref,
    fc1_bias_ref,
    fc2_ref,
    fc2_bias_ref,
    proj_down_ref,
    proj_up_ref,
    fc1_down_ref,
    fc1_up_ref,
    fc2_down_ref,
    fc2_up_ref,
    act_ref,
    dx1_ref,
    dattn_ref,
    grad_ref,
    *,
    per_clip,
    chunk,
):
    first = pl.program_id(0) % per_clip == 0
    feats = x_ref.shape[-1]
    hidden = fc1_ref.shape[-1]
    attn = attn_ref[0]
    reduced_proj = dot(attn, proj_down_ref[0], NT).astype(BF)
    middle = (
        x_ref[0].astype(F32)
        + dot(attn, proj_ref[...], NN)
        + proj_bias_ref[...]
        + dot(reduced_proj, proj_up_ref[0], NN)
    )
    normed, inverse = norm_stats(middle)
    low = (normed * gain_ref[...]).astype(BF)
    reduced_fc1 = dot(low, fc1_down_ref[0], NT).astype(BF)
    dy = dy_ref[0]
    grad_reduced_fc2 = dot(dy, fc2_up_ref[0], NT).astype(BF)
    fc1_up_at = 3 * feats
    fc2_down_at = fc1_up_at + hidden
    fc2_up_at = fc2_down_at + hidden
    total = middle + fc2_bias_ref[...]
    reduced_fc2 = None
    grad_low = None
    grad_reduced_fc1 = None
    for j in range(hidden // chunk):
        at = slice(j * chunk, (j + 1) * chunk)
        pre = (
            dot(low, fc1_ref[:, at], NN)
            + fc1_bias_ref[:, at]
            + dot(reduced_fc1, fc1_up_ref[0, :, at], NN)
        )
        size = jnp.abs(pre)
        bell = jnp.exp2((pre * pre) * (-0.5 * LOG2E))
        t = 1.0 / (1.0 + size * (0.3275911 * 0.7071067811865476))
        poly = ((((0.5 * 1.061405429) * t - 0.5 * 1.453152027) * t + 0.5 * 1.421413741) * t - 0.5 * 0.284496736) * t + 0.5 * 0.254829592
        tail = poly * t * bell
        below = jnp.where(pre >= 0.0, 1.0 - tail, tail)
        act = (pre * below).astype(BF)
        slope = below + pre * bell * 0.3989422804014327
        partial = dot(act, fc2_ref[at, :], NN)
        total = total + partial
        partial = dot(act, fc2_down_ref[0, :, at], NT)
        reduced_fc2 = partial if reduced_fc2 is None else reduced_fc2 + partial
        dact = dot(dy, fc2_ref[at, :], NT) + dot(grad_reduced_fc2, fc2_down_ref[0, :, at], NN)
        dpre = (dact * slope).astype(BF)
        partial = dot(dpre, fc1_ref[:, at], NT)
        grad_low = partial if grad_low is None else grad_low + partial
        partial = dot(dpre, fc1_up_ref[0, :, at], NT)
        grad_reduced_fc1 = partial if grad_reduced_fc1 is None else grad_reduced_fc1 + partial
        add_rows(grad_ref, slice(fc1_up_at + j * chunk, fc1_up_at + (j + 1) * chunk), dot(reduced_fc1, dpre, TN), first)
        add_rows(grad_ref, slice(fc2_down_at + j * chunk, fc2_down_at + (j + 1) * chunk), dot(grad_reduced_fc2, act, TN), first)
    reduced_fc2 = reduced_fc2.astype(BF)
    act_ref[0] = (total + dot(reduced_fc2, fc2_up_ref[0], NN)).astype(BF)
    add_rows(grad_ref, slice(fc2_up_at, fc2_up_at + feats), dot(reduced_fc2, dy, TN), first)
    grad_reduced_fc1 = grad_reduced_fc1.astype(BF)
    grad_low = grad_low + dot(grad_reduced_fc1, fc1_down_ref[0], NN)
    add_rows(grad_ref, slice(2 * feats, 3 * feats), dot(grad_reduced_fc1, low, TN), first)
    dx1 = dy.astype(F32) + norm_back(grad_low, gain_ref[...], normed, inverse)
    dx1_ref[0] = dx1
    branch = dx1.astype(BF)
    grad_reduced_proj = dot(branch, proj_up_ref[0], NT).astype(BF)
    add_rows(grad_ref, slice(feats, 2 * feats), dot(reduced_proj, branch, TN), first)
    add_rows(grad_ref, slice(0, feats), dot(grad_reduced_proj, attn, TN), first)
    dattn_ref[0] = (
        dot(branch, proj_ref[...], NT) + dot(grad_reduced_proj, proj_down_ref[0], NN)
    ).astype(BF)


def attend_back_kernel(
    ids_ref,
    x_ref,
    gain_ref,
    weight_ref,
    down_ref,
    up_ref,
    probs_ref,
    attn_ref,
    qkv_ref,
    reduced_ref,
    dattn_ref,
    dx1_ref,
    dx_ref,
    grad_ref,
    values,
    keys_t,
    inner,
    dqkv,
    dquery_t,
    *,
    scale,
    per_group,
    width,
    per_clip,
):
    group = pl.program_id(1)
    groups = pl.num_programs(1)
    feats = x_ref.shape[-1]
    rows = x_ref.shape[1]

    @pl.when(group == 0)
    def _():
        keys_t[...] = qkv_ref[0, :, feats : 2 * feats].astype(F32).T.astype(BF)
        lane = lane_ids((rows, 128))
        ones = jnp.where(lane % width < 2, 1.0, 0.0).astype(BF)
        source = lax.broadcasted_iota(jnp.int32, (128, 128), 0)
        target = lane_ids((128, 128))
        pick = jnp.where(
            (source // width == target // width) & (target % width < 2), 1.0, 0.0
        ).astype(BF)
        pick = jnp.concatenate([pick, pick], axis=0)
        for g in range(feats // 128):
            at = slice(128 * g, 128 * g + 128)
            values[:, 256 * g : 256 * g + 128] = qkv_ref[0, :, 2 * feats + 128 * g : 2 * feats + 128 * g + 128]
            values[:, 256 * g + 128 : 256 * g + 256] = ones
            product = dattn_ref[0, :, at].astype(F32) * attn_ref[0, :, at].astype(F32)
            high = product.astype(BF)
            rest = (product - high.astype(F32)).astype(BF)
            sums = dot(jnp.concatenate([high, rest], axis=1), pick, NN)
            coarse = sums.astype(BF)
            fine = (sums - coarse.astype(F32)).astype(BF)
            inner[:, at] = -jnp.where(lane % width == 0, coarse, fine)

    blocks = pl.ds(pl.multiple_of(group * 128, 128), 128)
    values_now = values[:, pl.ds(pl.multiple_of(group * 256, 256), 256)]
    dattn_now = dattn_ref[0, :, blocks]
    inner_now = inner[:, blocks]
    query_now = qkv_ref[0, :, blocks]
    head_of_lane = lane_ids((rows, 128)) // width
    zero = jnp.zeros((rows, 128), BF)
    dvalue = None
    dkey = None
    for h in range(per_group):
        mine = head_of_lane == h
        dattn_own = jnp.where(mine, dattn_now, zero)
        query_own = jnp.where(mine, query_now, zero)
        right = jnp.concatenate([dattn_own, jnp.where(mine, inner_now, zero)], axis=1)
        probs = probs_ref[0, h]
        dscore = probs * dot(values_now, right, NT).astype(BF)
        partial = dot(probs, dattn_own, NN)
        dvalue = partial if dvalue is None else dvalue + partial
        partial = dot(dscore, query_own, NN)
        dkey = partial if dkey is None else dkey + partial
        at = pl.ds(pl.multiple_of((group * per_group + h) * width, width), width)
        dquery_t[at, :] = dot(keys_t[at, :], dscore, NN)
    dqkv[:, pl.ds(pl.multiple_of(2 * feats + group * 128, 128), 128)] = dvalue.astype(BF)
    dqkv[:, pl.ds(pl.multiple_of(feats + group * 128, 128), 128)] = (dkey * LN2).astype(BF)

    @pl.when(group == groups - 1)
    def _():
        first = pl.program_id(0) % per_clip == 0
        dqkv[:, :feats] = (dquery_t[...].T * scale).astype(BF)
        dall = dqkv[...]
        normed, inverse = norm_stats(x_ref[0].astype(F32))
        low = (normed * gain_ref[...]).astype(BF)
        grad_reduced = dot(dall, up_ref[0], NT).astype(BF)
        add_rows(grad_ref, slice(feats, 4 * feats), dot(reduced_ref[0], dall, TN), first)
        add_rows(grad_ref, slice(0, feats), dot(grad_reduced, low, TN), first)
        dlow = (dot(dall, weight_ref[...], NT) + dot(grad_reduced, down_ref[0], NN)).astype(BF)
        dx_ref[0] = (
            dx1_ref[0] + norm_back(dlow.astype(F32), gain_ref[...], normed, inverse)
        ).astype(BF)


def whole(shape):
    return pl.BlockSpec(shape, lambda *at: (0,) * len(shape), pipeline_mode=pl.Buffered(1))


def compute(
    x,
    dy,
    item_ids,
    vectors,
    weights,
    adapters,
    masks,
    table,
    per_clip,
):
    items, rows, feats = x.shape
    heads = table.shape[0]
    width = feats // heads
    per_group = 128 // width
    groups = heads // per_group
    scale = width**-0.5
    gain1, qkv_bias, proj_bias, gain2, fc1_bias, fc2_bias = vectors
    qkv_w, proj_w, fc1_w, fc2_w = weights
    qkv_down, qkv_up, proj_down, proj_up, fc1_down, fc1_up, fc2_down, fc2_up = adapters
    key_mask, query_mask = masks
    rank = qkv_down.shape[1]
    hidden = fc1_w.shape[1]
    clips = items // per_clip

    def item(shape):
        return pl.BlockSpec((1, *shape), lambda i, *rest: (i,) + (0,) * len(shape))

    def adapter(array):
        return pl.BlockSpec((1, *array.shape[1:]), lambda i, *rest: (rest[-1][i], 0, 0))

    probs, attn, qkv, reduced = pl.pallas_call(
        functools.partial(attend_kernel, scale=scale, per_group=per_group, width=width),
        grid_spec=pltpu.PrefetchScalarGridSpec(
            num_scalar_prefetch=1,
            grid=(items, groups),
            in_specs=[
                item((rows, feats)),
                whole(gain1.shape),
                whole(qkv_w.shape),
                whole(qkv_bias.shape),
                adapter(qkv_down),
                adapter(qkv_up),
                pl.BlockSpec((1, rows, 128), lambda i, g, ids: (i % per_clip, 0, 0)),
                pl.BlockSpec((1, rows, 128), lambda i, g, ids: (i % per_clip, 0, 0)),
                whole(table.shape),
            ],
            out_specs=[
                pl.BlockSpec((1, per_group, rows, rows), lambda i, g, ids: (i, g, 0, 0)),
                item((rows, feats)),
                item((rows, 3 * feats)),
                item((rows, rank)),
            ],
            scratch_shapes=[
                pltpu.VMEM((rows, 2 * feats), BF),
                pltpu.VMEM((rows, feats), BF),
                pltpu.VMEM((feats, rows), BF),
                pltpu.VMEM((feats, rows), F32),
                pltpu.VMEM((2, rows, rows), F32),
            ],
        ),
        out_shape=[
            jax.ShapeDtypeStruct((items, heads, rows, rows), BF),
            jax.ShapeDtypeStruct((items, rows, feats), BF),
            jax.ShapeDtypeStruct((items, rows, 3 * feats), BF),
            jax.ShapeDtypeStruct((items, rows, rank), BF),
        ],
        compiler_params=pltpu.CompilerParams(
            vmem_limit_bytes=VMEM_LIMIT, dimension_semantics=("arbitrary", "arbitrary")
        ),
        name="attend",
    )(item_ids, x, gain1, qkv_w, qkv_bias, qkv_down, qkv_up, key_mask, query_mask, table)

    span = 4 * feats + 2 * hidden
    act, dx1, dattn, grad_dense = pl.pallas_call(
        functools.partial(dense_kernel, per_clip=per_clip, chunk=512),
        grid_spec=pltpu.PrefetchScalarGridSpec(
            num_scalar_prefetch=1,
            grid=(items,),
            in_specs=[
                item((rows, feats)),
                item((rows, feats)),
                item((rows, feats)),
                whole(gain2.shape),
                whole(proj_w.shape),
                whole(proj_bias.shape),
                whole(fc1_w.shape),
                whole(fc1_bias.shape),
                whole(fc2_w.shape),
                whole(fc2_bias.shape),
                adapter(proj_down),
                adapter(proj_up),
                adapter(fc1_down),
                adapter(fc1_up),
                adapter(fc2_down),
                adapter(fc2_up),
            ],
            out_specs=[
                item((rows, feats)),
                item((rows, feats)),
                item((rows, feats)),
                pl.BlockSpec((1, rank, span), lambda i, ids: (i // per_clip, 0, 0)),
            ],
        ),
        out_shape=[
            jax.ShapeDtypeStruct((items, rows, feats), BF),
            jax.ShapeDtypeStruct((items, rows, feats), F32),
            jax.ShapeDtypeStruct((items, rows, feats), BF),
            jax.ShapeDtypeStruct((clips, rank, span), F32),
        ],
        compiler_params=pltpu.CompilerParams(
            vmem_limit_bytes=VMEM_LIMIT, dimension_semantics=("arbitrary",)
        ),
        name="dense",
    )(
        item_ids, x, attn, dy, gain2, proj_w, proj_bias, fc1_w, fc1_bias, fc2_w, fc2_bias,
        proj_down, proj_up, fc1_down, fc1_up, fc2_down, fc2_up,
    )

    dx, grad_qkv = pl.pallas_call(
        functools.partial(
            attend_back_kernel, scale=scale, per_group=per_group, width=width, per_clip=per_clip
        ),
        grid_spec=pltpu.PrefetchScalarGridSpec(
            num_scalar_prefetch=1,
            grid=(items, groups),
            in_specs=[
                item((rows, feats)),
                whole(gain1.shape),
                whole(qkv_w.shape),
                adapter(qkv_down),
                adapter(qkv_up),
                pl.BlockSpec((1, per_group, rows, rows), lambda i, g, ids: (i, g, 0, 0)),
                item((rows, feats)),
                item((rows, 3 * feats)),
                item((rows, rank)),
                item((rows, feats)),
                item((rows, feats)),
            ],
            out_specs=[
                item((rows, feats)),
                pl.BlockSpec((1, rank, 4 * feats), lambda i, g, ids: (i // per_clip, 0, 0)),
            ],
            scratch_shapes=[
                pltpu.VMEM((rows, 2 * feats), BF),
                pltpu.VMEM((feats, rows), BF),
                pltpu.VMEM((rows, feats), BF),
                pltpu.VMEM((rows, 3 * feats), BF),
                pltpu.VMEM((feats, rows), F32),
            ],
        ),
        out_shape=[
            jax.ShapeDtypeStruct((items, rows, feats), BF),
            jax.ShapeDtypeStruct((clips, rank, 4 * feats), F32),
        ],
        compiler_params=pltpu.CompilerParams(
            vmem_limit_bytes=VMEM_LIMIT, dimension_semantics=("arbitrary", "arbitrary")
        ),
        name="attend_back",
    )(item_ids, x, gain1, qkv_w, qkv_down, qkv_up, probs, attn, qkv, reduced, dattn, dx1)
    return act, dx, grad_qkv, grad_dense


def exchange(x, win_size):
    local = x.shape[1]
    bits = local.bit_length() - 1
    at = jnp.arange(TOK)
    taken = (at // 49 < 4, at // 7 % 7 < 3, at % 7 < 3)
    for bit, rows in zip((2, 1, 0), taken):
        if bit < bits:
            split = x.reshape(x.shape[0], local >> (bit + 1), 2, 1 << bit, TOK, -1)
            other = jnp.flip(split, axis=2).reshape(x.shape)
        elif bit == 2:
            half = lax.ppermute(
                x[:, :, : TOK // 2], "win", [(i, i ^ 1 << bit - bits) for i in range(win_size)]
            )
            x = jnp.concatenate((half, x[:, :, TOK // 2 :]), axis=2)
            continue
        else:
            other = lax.ppermute(x, "win", [(i, i ^ 1 << bit - bits) for i in range(win_size)])
        x = jnp.where(rows[None, None, :, None], other, x)
    return x


def place():
    at = jnp.arange(TOK)
    return at // 49, at // 7 % 7, at % 7


def window_masks(win_index, local):
    depth, height, across = place()
    number = win_index * local + jnp.arange(local)
    label = (
        number[:, None] // 4 % 2 * (depth < 4) * 4
        + number[:, None] // 2 % 2 * (height < 3) * 2
        + number[:, None] % 2 * (across < 3)
    )
    lane = jnp.arange(128)
    same = label[:, :, None] == lane
    return (
        same.astype(BF),
        jnp.where(same | (lane >= 8), 0.0, -FAR).astype(BF),
    )


def bias_by_pair(table):
    heads = table.shape[0]
    side = jnp.arange(49)
    high, wide = (side // 7 + 4) % 7, (side % 7 + 4) % 7
    offset = (high[None, :] - high[:, None] + 6) * 13 + wide[None, :] - wide[:, None] + 6
    pick = (jnp.arange(169)[:, None, None] == offset[None]).astype(BF)
    found = jnp.einsum(
        "mad,dkq->mkaq", table.reshape(heads, 15, 169), pick, preferred_element_type=F32
    )
    found = (found * LOG2E).reshape(heads, 49, 15 * 49)
    blocks = []
    for key_block in range(8):
        t = (key_block + 4) % 8
        blocks.append(
            jnp.concatenate(
                (found[..., (11 - t) * 49 : (15 - t) * 49], found[..., (7 - t) * 49 : (11 - t) * 49]),
                axis=-1,
            )
        )
    return jnp.stack(blocks, axis=1).reshape(heads, TOK, TOK)


def per_device(
    tokens, cotangent, adapter_ids, ln1_gain, qkv_weight, qkv_bias, proj_weight, proj_bias, ln2_gain,
    fc1_weight, fc1_bias, fc2_weight, fc2_bias, bias_table, qkv_down, qkv_up, proj_down, proj_up,
    fc1_down, fc1_up, fc2_down, fc2_up, *, clip_size, win_size,
):
    clips, local, rows, feats = tokens.shape
    items = clips * local
    matrices = (qkv_weight, proj_weight, fc1_weight, fc2_weight)
    downs = (qkv_down, proj_down, fc1_down, fc2_down)
    ups = (qkv_up, proj_up, fc1_up, fc2_up)
    vecs = (ln1_gain, qkv_bias, proj_bias, ln2_gain, fc1_bias, fc2_bias)
    pieces = [*matrices, *downs, *ups]
    flat = jnp.concatenate([p.reshape(-1) for p in pieces])
    got = lax.all_gather(flat, ("clip", "win"))
    got = got.reshape(clip_size, win_size, -1)
    full, at = [], 0
    for n, p in enumerate(pieces):
        part = got[:, :, at : at + p.size].reshape(clip_size, win_size, *p.shape)
        at += p.size
        if n < 4:
            full.append(part.transpose(0, 2, 1, 3).reshape(clip_size * p.shape[0], -1))
        elif n < 8:
            full.append(part.transpose(1, 2, 4, 0, 3).reshape(win_size * p.shape[0], p.shape[2], -1))
        else:
            full.append(part.transpose(1, 2, 3, 0, 4).reshape(win_size * p.shape[0], p.shape[1], -1))
    weights = full[:4]
    adapters = [a for pair in zip(full[4:8], full[8:]) for a in pair]
    flat = lax.all_gather(jnp.concatenate(vecs), "clip")
    vectors, at = [], 0
    for p in vecs:
        vectors.append(flat[:, at : at + p.size].reshape(1, -1).astype(F32))
        at += p.size
    x = exchange(tokens, win_size).reshape(items, rows, feats)
    dy = exchange(cotangent, win_size).reshape(items, rows, feats)
    act, dx, grad_qkv, grad_dense = compute(
        x,
        dy,
        jnp.repeat(adapter_ids, local),
        vectors,
        weights,
        adapters,
        window_masks(lax.axis_index("win"), local),
        bias_by_pair(bias_table),
        local,
    )
    activations = exchange(act.reshape(tokens.shape), win_size)
    input_grad = exchange(dx.reshape(tokens.shape), win_size)
    adapter_count = win_size * qkv_down.shape[0]
    hot = (adapter_ids[:, None] == jnp.arange(adapter_count)[None]).astype(F32)
    hidden = fc1_weight.shape[1] * win_size
    spans = (feats, 3 * feats, feats, feats, feats, hidden, hidden, feats)
    grads = jnp.concatenate((grad_qkv, grad_dense), axis=-1)
    rank = grads.shape[1]
    parts, at = [], 0
    for span in spans:
        part = grads[..., at : at + span].reshape(clips, rank, clip_size, span // clip_size)
        at += span
        parts.append(part)
    mine = jnp.concatenate(parts, axis=-1)
    spread = jnp.sum(hot[:, :, None, None, None] * mine[:, None], axis=0)
    spread = spread.transpose(2, 0, 1, 3).astype(BF)
    total = lax.psum_scatter(spread, "clip", scatter_dimension=0, tiled=True)[0]
    total = lax.psum_scatter(total, "win", scatter_dimension=0, tiled=True).astype(F32)
    outs, at = [], 0
    for n, span in enumerate(spans):
        width = span // clip_size
        part = total[..., at : at + width]
        at += width
        outs.append(part.transpose(0, 2, 1) if n % 2 == 0 else part)
    return (activations, input_grad, *outs)


def solution(mesh):
    split = P("clip", "win", None, None)
    grid2 = P("clip", "win")
    down = P("win", "clip", None)
    up = P("win", None, "clip")
    one = P("clip")
    return jax.shard_map(
        functools.partial(
            per_device, clip_size=mesh.shape["clip"], win_size=mesh.shape["win"]
        ),
        mesh=mesh,
        in_specs=(
            split, split, one, one, grid2, one, grid2, one, one, grid2, one, grid2, one, P(),
            down, up, down, up, down, up, down, up,
        ),
        out_specs=(split, split, down, up, down, up, down, up, down, up),
        check_vma=False,
    )
```

```python
import functools
import jax
import jax.numpy as jnp
from jax import lax
from jax.experimental import pallas as pl
from jax.experimental.pallas import tpu as pltpu
from jax.sharding import PartitionSpec as P

BF = jnp.bfloat16
F32 = jnp.float32
NN = (((1,), (0,)), ((), ()))
NT = (((1,), (1,)), ((), ()))
TN = (((0,), (0,)), ((), ()))
LOG2E = 1.4426950408889634
LN2 = 0.6931471805599453
FAR = 1e9
VMEM_LIMIT = 60 * 2**20
TOK = 392
TOP = 208


def dot(left, right, dims):
    return lax.dot_general(left, right, dims, preferred_element_type=F32)


def lane_ids(shape):
    return lax.broadcasted_iota(jnp.int32, shape, len(shape) - 1)


def norm_stats(values):
    average = jnp.mean(values, axis=-1, keepdims=True)
    centred = values - average
    variance = jnp.mean(centred * centred, axis=-1, keepdims=True)
    inverse = lax.rsqrt(variance + 1e-05)
    return centred * inverse, inverse


def norm_back(gradient, gain, normed, inverse):
    scaled = gradient * gain
    centre = jnp.mean(scaled, axis=-1, keepdims=True)
    slope = jnp.mean(scaled * normed, axis=-1, keepdims=True)
    return inverse * (scaled - centre - normed * slope)


def add_rows(ref, at, value, first):
    @pl.when(first)
    def _():
        ref[0, :, at] = value

    @pl.when(jnp.logical_not(first))
    def _():
        ref[0, :, at] += value


def attend_kernel(
    ids_ref,
    x_ref,
    gain_ref,
    weight_ref,
    bias_ref,
    down_ref,
    up_ref,
    key_mask_ref,
    query_mask_ref,
    table_ref,
    probs_ref,
    out_ref,
    qkv_ref,
    reduced_ref,
    keys,
    queries,
    values_t,
    out_t,
    scores,
    *,
    scale,
    per_group,
    width,
):
    group = pl.program_id(1)
    groups = pl.num_programs(1)
    feats = x_ref.shape[-1]

    @pl.when(group == 0)
    def _():
        normed, _ = norm_stats(x_ref[0].astype(F32))
        low = (normed * gain_ref[...]).astype(BF)
        reduced = dot(low, down_ref[0], NT).astype(BF)
        reduced_ref[0] = reduced

        def columns(part):
            at = pl.ds(part * feats, feats)
            return (
                dot(low, weight_ref[:, at], NN)
                + bias_ref[:, at]
                + dot(reduced, up_ref[0, :, at], NN)
            )

        query = (columns(0) * (scale * LOG2E)).astype(BF)
        queries[...] = query
        qkv_ref[0, :, :feats] = query
        key = columns(1).astype(BF)
        qkv_ref[0, :, feats : 2 * feats] = key
        for g in range(feats // 128):
            keys[:, 256 * g : 256 * g + 128] = key[:, 128 * g : 128 * g + 128]
            keys[:, 256 * g + 128 : 256 * g + 256] = key_mask_ref[0]
        value = columns(2)
        qkv_ref[0, :, 2 * feats :] = value.astype(BF)
        values_t[...] = value.T.astype(BF)

    keys_now = keys[:, pl.ds(pl.multiple_of(group * 256, 256), 256)]
    query_now = queries[:, pl.ds(pl.multiple_of(group * 128, 128), 128)]
    head_of_lane = lane_ids(query_now.shape) // width

    def raw(h):
        own = jnp.where(head_of_lane == h, query_now, jnp.zeros_like(query_now))
        own = jnp.concatenate([own, query_mask_ref[0]], axis=1)
        return dot(keys_now, own, NT) + table_ref[group * per_group + h]

    def finish(h):
        score = scores[h % 2]
        largest = jnp.max(score, axis=0, keepdims=True)
        probs = jnp.exp2(score - largest)
        total = jnp.sum(probs, axis=0, keepdims=True)
        probs = (probs * (1.0 / total)).astype(BF)
        probs_ref[0, h] = probs
        at = pl.ds(pl.multiple_of((group * per_group + h) * width, width), width)
        out_t[at, :] = dot(values_t[at, :], probs, NN)

    scores[0] = raw(0)
    for h in range(per_group):
        if h + 1 < per_group:
            scores[(h + 1) % 2] = raw(h + 1)
        finish(h)

    @pl.when(group == groups - 1)
    def _():
        out_ref[0] = out_t[...].T.astype(BF)


def row_masks(rows, columns):
    row = lax.broadcasted_iota(jnp.int32, (rows, columns), 0)
    return row < TOK // 2, row % 49 < 21, row % 7 < 3


def with_top(part, top, early):
    return jnp.concatenate([jnp.where(early[:TOP], top, part[:TOP]), part[TOP:]], axis=0)


def join_pieces(refs, e):
    own, beside, across, far = refs
    early, low_h, low_w = row_masks(own.shape[1], own.shape[2])

    def window(n):
        part = jnp.where(low_h, beside[n], own[n])
        return with_top(part, jnp.where(low_h[:TOP], far[n], across[n]), early)

    return jnp.where(low_w, window(1 - e), window(e))


def dense_kernel(
    ids_ref,
    x_ref,
    attn_ref,
    gain_ref,
    proj_bias_ref,
    fc1_bias_ref,
    fc2_bias_ref,
    staged_ref,
    *refs,
    per_clip,
    chunk,
    pieces,
):
    tiles, refs = refs[:6], refs[6:]
    dy_refs, refs = refs[:pieces], refs[pieces:]
    act_ref, dx1_ref, dattn_ref, grad_ref, *refs = refs
    proj_ref, fc1_ref, fc2_ref, proj_down, proj_up, fc1_down, fc1_up, fc2_down, fc2_up, sem = refs

    @pl.when(pl.program_id(0) == 0)
    def _():
        copies = []
        for n in range(4):
            moves = [(0, 64, proj_ref, 128 * n), (320, 256, fc2_ref, 128 * n)]
            moves += [(64 + 64 * t, 64, fc1_ref, 512 * n + 128 * t) for t in range(4)]
            for start, size, target, lane in moves:
                copies.append(
                    pltpu.make_async_copy(
                        staged_ref.at[:, n, pl.ds(start, size), :],
                        target.at[:, :, pl.ds(lane, 128)],
                        sem.at[len(copies)],
                    )
                )
        for copy in copies:
            copy.start()
        for copy in copies:
            copy.wait()

    @pl.when(pl.program_id(0) % per_clip == 0)
    def _():
        for n in range(8):
            short = slice(64 * n, 64 * n + 64)
            proj_down[:, short] = tiles[0][n, 0, :, 0:64]
            proj_up[:, short] = tiles[0][n, 0, :, 64:128]
            fc1_down[:, short] = tiles[1][n, 0, :, 0:64]
            fc2_up[:, short] = tiles[1][n, 0, :, 64:128]
            for half in range(2):
                long = slice(256 * n + 128 * half, 256 * n + 128 * half + 128)
                fc1_up[:, long] = tiles[2 + half][n, 0]
                fc2_down[:, long] = tiles[4 + half][n, 0]

    if pieces == 1:
        dy = dy_refs[0][0]
    else:
        dy = join_pieces(dy_refs, pl.program_id(0) % 2)
    proj_w = proj_ref[...].reshape(proj_ref.shape[0] * proj_ref.shape[1], -1)
    per_chunk = chunk // fc2_ref.shape[1]
    first = pl.program_id(0) % per_clip == 0
    feats = x_ref.shape[-1]
    hidden = fc1_ref.shape[-1]
    attn = attn_ref[0]
    reduced_proj = dot(attn, proj_down[...], NT).astype(BF)
    middle = (
        x_ref[0].astype(F32)
        + dot(attn, proj_w, NN)
        + proj_bias_ref[...]
        + dot(reduced_proj, proj_up[...], NN)
    )
    normed, inverse = norm_stats(middle)
    low = (normed * gain_ref[...]).astype(BF)
    reduced_fc1 = dot(low, fc1_down[...], NT).astype(BF)
    grad_reduced_fc2 = dot(dy, fc2_up[...], NT).astype(BF)
    fc1_up_at = 3 * feats
    fc2_down_at = fc1_up_at + hidden
    fc2_up_at = fc2_down_at + hidden
    total = middle + fc2_bias_ref[...]
    reduced_fc2 = None
    grad_low = None
    grad_reduced_fc1 = None
    for j in range(hidden // chunk):
        at = slice(j * chunk, (j + 1) * chunk)
        fc1_w = fc1_ref[:, :, at].reshape(feats, chunk)
        fc2_w = fc2_ref[j * per_chunk : (j + 1) * per_chunk].reshape(chunk, feats)
        pre = (
            dot(low, fc1_w, NN)
            + fc1_bias_ref[:, at]
            + dot(reduced_fc1, fc1_up[:, at], NN)
        )
        size = jnp.abs(pre)
        bell = jnp.exp2((pre * pre) * (-0.5 * LOG2E))
        t = 1.0 / (1.0 + size * (0.3275911 * 0.7071067811865476))
        poly = ((((0.5 * 1.061405429) * t - 0.5 * 1.453152027) * t + 0.5 * 1.421413741) * t - 0.5 * 0.284496736) * t + 0.5 * 0.254829592
        tail = poly * t * bell
        below = jnp.where(pre >= 0.0, 1.0 - tail, tail)
        act = (pre * below).astype(BF)
        slope = below + pre * bell * 0.3989422804014327
        partial = dot(act, fc2_w, NN)
        total = total + partial
        partial = dot(act, fc2_down[:, at], NT)
        reduced_fc2 = partial if reduced_fc2 is None else reduced_fc2 + partial
        dact = dot(dy, fc2_w, NT) + dot(grad_reduced_fc2, fc2_down[:, at], NN)
        dpre = (dact * slope).astype(BF)
        partial = dot(dpre, fc1_w, NT)
        grad_low = partial if grad_low is None else grad_low + partial
        partial = dot(dpre, fc1_up[:, at], NT)
        grad_reduced_fc1 = partial if grad_reduced_fc1 is None else grad_reduced_fc1 + partial
        add_rows(grad_ref, slice(fc1_up_at + j * chunk, fc1_up_at + (j + 1) * chunk), dot(reduced_fc1, dpre, TN), first)
        add_rows(grad_ref, slice(fc2_down_at + j * chunk, fc2_down_at + (j + 1) * chunk), dot(grad_reduced_fc2, act, TN), first)
    reduced_fc2 = reduced_fc2.astype(BF)
    act_ref[0] = (total + dot(reduced_fc2, fc2_up[...], NN)).astype(BF)
    add_rows(grad_ref, slice(fc2_up_at, fc2_up_at + feats), dot(reduced_fc2, dy, TN), first)
    grad_reduced_fc1 = grad_reduced_fc1.astype(BF)
    grad_low = grad_low + dot(grad_reduced_fc1, fc1_down[...], NN)
    add_rows(grad_ref, slice(2 * feats, 3 * feats), dot(grad_reduced_fc1, low, TN), first)
    dx1 = dy.astype(F32) + norm_back(grad_low, gain_ref[...], normed, inverse)
    dx1_ref[0] = dx1
    branch = dx1.astype(BF)
    grad_reduced_proj = dot(branch, proj_up[...], NT).astype(BF)
    add_rows(grad_ref, slice(feats, 2 * feats), dot(reduced_proj, branch, TN), first)
    add_rows(grad_ref, slice(0, feats), dot(grad_reduced_proj, attn, TN), first)
    dattn_ref[0] = (
        dot(branch, proj_w, NT) + dot(grad_reduced_proj, proj_down[...], NN)
    ).astype(BF)


def attend_back_kernel(
    ids_ref,
    x_ref,
    gain_ref,
    weight_ref,
    down_ref,
    up_ref,
    probs_ref,
    attn_ref,
    qkv_ref,
    reduced_ref,
    dattn_ref,
    dx1_ref,
    dx_ref,
    grad_ref,
    values,
    keys_t,
    inner,
    dqkv,
    dquery_t,
    *,
    scale,
    per_group,
    width,
    per_clip,
):
    group = pl.program_id(1)
    groups = pl.num_programs(1)
    feats = x_ref.shape[-1]
    rows = x_ref.shape[1]

    @pl.when(group == 0)
    def _():
        keys_t[...] = qkv_ref[0, :, feats : 2 * feats].astype(F32).T.astype(BF)
        lane = lane_ids((rows, 128))
        ones = jnp.where(lane % width < 2, 1.0, 0.0).astype(BF)
        source = lax.broadcasted_iota(jnp.int32, (128, 128), 0)
        target = lane_ids((128, 128))
        pick = jnp.where(
            (source // width == target // width) & (target % width < 2), 1.0, 0.0
        ).astype(BF)
        pick = jnp.concatenate([pick, pick], axis=0)
        for g in range(feats // 128):
            at = slice(128 * g, 128 * g + 128)
            values[:, 256 * g : 256 * g + 128] = qkv_ref[0, :, 2 * feats + 128 * g : 2 * feats + 128 * g + 128]
            values[:, 256 * g + 128 : 256 * g + 256] = ones
            product = dattn_ref[0, :, at].astype(F32) * attn_ref[0, :, at].astype(F32)
            high = product.astype(BF)
            rest = (product - high.astype(F32)).astype(BF)
            sums = dot(jnp.concatenate([high, rest], axis=1), pick, NN)
            coarse = sums.astype(BF)
            fine = (sums - coarse.astype(F32)).astype(BF)
            inner[:, at] = -jnp.where(lane % width == 0, coarse, fine)

    blocks = pl.ds(pl.multiple_of(group * 128, 128), 128)
    values_now = values[:, pl.ds(pl.multiple_of(group * 256, 256), 256)]
    dattn_now = dattn_ref[0, :, blocks]
    inner_now = inner[:, blocks]
    query_now = qkv_ref[0, :, blocks]
    head_of_lane = lane_ids((rows, 128)) // width
    zero = jnp.zeros((rows, 128), BF)
    dvalue = None
    dkey = None
    for h in range(per_group):
        mine = head_of_lane == h
        dattn_own = jnp.where(mine, dattn_now, zero)
        query_own = jnp.where(mine, query_now, zero)
        right = jnp.concatenate([dattn_own, jnp.where(mine, inner_now, zero)], axis=1)
        probs = probs_ref[0, h]
        dscore = probs * dot(values_now, right, NT).astype(BF)
        partial = dot(probs, dattn_own, NN)
        dvalue = partial if dvalue is None else dvalue + partial
        partial = dot(dscore, query_own, NN)
        dkey = partial if dkey is None else dkey + partial
        at = pl.ds(pl.multiple_of((group * per_group + h) * width, width), width)
        dquery_t[at, :] = dot(keys_t[at, :], dscore, NN)
    dqkv[:, pl.ds(pl.multiple_of(2 * feats + group * 128, 128), 128)] = dvalue.astype(BF)
    dqkv[:, pl.ds(pl.multiple_of(feats + group * 128, 128), 128)] = (dkey * LN2).astype(BF)

    @pl.when(group == groups - 1)
    def _():
        first = pl.program_id(0) % per_clip == 0
        dqkv[:, :feats] = (dquery_t[...].T * scale).astype(BF)
        dall = dqkv[...]
        normed, inverse = norm_stats(x_ref[0].astype(F32))
        low = (normed * gain_ref[...]).astype(BF)
        grad_reduced = dot(dall, up_ref[0], NT).astype(BF)
        add_rows(grad_ref, slice(feats, 4 * feats), dot(reduced_ref[0], dall, TN), first)
        add_rows(grad_ref, slice(0, feats), dot(grad_reduced, low, TN), first)
        dlow = (dot(dall, weight_ref[...], NT) + dot(grad_reduced, down_ref[0], NN)).astype(BF)
        dx_ref[0] = (
            dx1_ref[0] + norm_back(dlow.astype(F32), gain_ref[...], normed, inverse)
        ).astype(BF)


def whole(shape):
    return pl.BlockSpec(shape, lambda *at: (0,) * len(shape), pipeline_mode=pl.Buffered(1))


def compute(x, dy, item_ids, vectors, qkv_parts, staged, masks, table, per_clip):
    items, rows, feats = x.shape
    heads = table.shape[0]
    width = feats // heads
    per_group = 128 // width
    groups = heads // per_group
    scale = width**-0.5
    gain1, qkv_bias, proj_bias, gain2, fc1_bias, fc2_bias = vectors
    qkv_w, qkv_down, qkv_up = qkv_parts
    key_mask, query_mask = masks
    rank = qkv_down.shape[1]
    hidden = fc1_bias.shape[1]
    clips = items // per_clip

    def item(shape):
        return pl.BlockSpec((1, *shape), lambda i, *rest: (i,) + (0,) * len(shape))

    def adapter(array):
        return pl.BlockSpec((1, *array.shape[1:]), lambda i, *rest: (rest[-1][i], 0, 0))

    probs, attn, qkv, reduced = pl.pallas_call(
        functools.partial(attend_kernel, scale=scale, per_group=per_group, width=width),
        grid_spec=pltpu.PrefetchScalarGridSpec(
            num_scalar_prefetch=1,
            grid=(items, groups),
            in_specs=[
                item((rows, feats)),
                whole(gain1.shape),
                whole(qkv_w.shape),
                whole(qkv_bias.shape),
                adapter(qkv_down),
                adapter(qkv_up),
                pl.BlockSpec((1, rows, 128), lambda i, g, ids: (i % per_clip, 0, 0)),
                pl.BlockSpec((1, rows, 128), lambda i, g, ids: (i % per_clip, 0, 0)),
                whole(table.shape),
            ],
            out_specs=[
                pl.BlockSpec((1, per_group, rows, rows), lambda i, g, ids: (i, g, 0, 0)),
                item((rows, feats)),
                item((rows, 3 * feats)),
                item((rows, rank)),
            ],
            scratch_shapes=[
                pltpu.VMEM((rows, 2 * feats), BF),
                pltpu.VMEM((rows, feats), BF),
                pltpu.VMEM((feats, rows), BF),
                pltpu.VMEM((feats, rows), F32),
                pltpu.VMEM((2, rows, rows), F32),
            ],
        ),
        out_shape=[
            jax.ShapeDtypeStruct((items, heads, rows, rows), BF),
            jax.ShapeDtypeStruct((items, rows, feats), BF),
            jax.ShapeDtypeStruct((items, rows, 3 * feats), BF),
            jax.ShapeDtypeStruct((items, rows, rank), BF),
        ],
        compiler_params=pltpu.CompilerParams(
            vmem_limit_bytes=VMEM_LIMIT, dimension_semantics=("arbitrary", "arbitrary")
        ),
        cost_estimate=pl.CostEstimate(flops=4 * 10**10, bytes_accessed=10**7, transcendentals=0),
        name="attend",
    )(item_ids, x, gain1, qkv_w, qkv_bias, qkv_down, qkv_up, key_mask, query_mask, table)

    span = 4 * feats + 2 * hidden
    def tile(n):
        return pl.BlockSpec(
            (8, 1, rank, 128), lambda i, ids: (0, ids[i] // 2, 36 + 2 * n + ids[i] % 2, 0)
        )

    def piece(array):
        if len(dy) == 1:
            return item(array.shape[1:])
        return pl.BlockSpec((per_clip, *array.shape[1:]), lambda i, ids: (i // per_clip, 0, 0))

    act, dx1, dattn, grad_dense = pl.pallas_call(
        functools.partial(dense_kernel, per_clip=per_clip, chunk=512, pieces=len(dy)),
        grid_spec=pltpu.PrefetchScalarGridSpec(
            num_scalar_prefetch=1,
            grid=(items,),
            in_specs=[
                item((rows, feats)),
                item((rows, feats)),
                whole(gain2.shape),
                whole(proj_bias.shape),
                whole(fc1_bias.shape),
                whole(fc2_bias.shape),
                pl.BlockSpec(memory_space=pl.ANY),
                *[tile(n) for n in range(6)],
                *[piece(a) for a in dy],
            ],
            out_specs=[
                item((rows, feats)),
                item((rows, feats)),
                item((rows, feats)),
                pl.BlockSpec((1, rank, span), lambda i, ids: (i // per_clip, 0, 0)),
            ],
            scratch_shapes=[
                pltpu.VMEM((8, feats // 8, feats), BF),
                pltpu.VMEM((8, feats // 8, hidden), BF),
                pltpu.VMEM((8, hidden // 8, feats), BF),
                *[pltpu.VMEM((rank, n), BF) for n in (feats, feats, feats, hidden, hidden, feats)],
                pltpu.SemaphoreType.DMA((24,)),
            ],
        ),
        out_shape=[
            jax.ShapeDtypeStruct((items, rows, feats), BF),
            jax.ShapeDtypeStruct((items, rows, feats), F32),
            jax.ShapeDtypeStruct((items, rows, feats), BF),
            jax.ShapeDtypeStruct((clips, rank, span), F32),
        ],
        compiler_params=pltpu.CompilerParams(
            vmem_limit_bytes=VMEM_LIMIT, dimension_semantics=("arbitrary",)
        ),
        cost_estimate=pl.CostEstimate(flops=5 * 10**10, bytes_accessed=10**7, transcendentals=0),
        name="dense",
    )(
        item_ids, x, attn, gain2, proj_bias, fc1_bias, fc2_bias, staged, *([staged] * 6), *dy
    )

    dx, grad_qkv = pl.pallas_call(
        functools.partial(
            attend_back_kernel, scale=scale, per_group=per_group, width=width, per_clip=per_clip
        ),
        grid_spec=pltpu.PrefetchScalarGridSpec(
            num_scalar_prefetch=1,
            grid=(items, groups),
            in_specs=[
                item((rows, feats)),
                whole(gain1.shape),
                whole(qkv_w.shape),
                adapter(qkv_down),
                adapter(qkv_up),
                pl.BlockSpec((1, per_group, rows, rows), lambda i, g, ids: (i, g, 0, 0)),
                item((rows, feats)),
                item((rows, 3 * feats)),
                item((rows, rank)),
                item((rows, feats)),
                item((rows, feats)),
            ],
            out_specs=[
                item((rows, feats)),
                pl.BlockSpec((1, rank, 4 * feats), lambda i, g, ids: (i // per_clip, 0, 0)),
            ],
            scratch_shapes=[
                pltpu.VMEM((rows, 2 * feats), BF),
                pltpu.VMEM((feats, rows), BF),
                pltpu.VMEM((rows, feats), BF),
                pltpu.VMEM((rows, 3 * feats), BF),
                pltpu.VMEM((feats, rows), F32),
            ],
        ),
        out_shape=[
            jax.ShapeDtypeStruct((items, rows, feats), BF),
            jax.ShapeDtypeStruct((clips, rank, 4 * feats), F32),
        ],
        compiler_params=pltpu.CompilerParams(
            vmem_limit_bytes=VMEM_LIMIT, dimension_semantics=("arbitrary", "arbitrary")
        ),
        cost_estimate=pl.CostEstimate(flops=5 * 10**10, bytes_accessed=10**7, transcendentals=0),
        name="attend_back",
    )(item_ids, x, gain1, qkv_w, qkv_down, qkv_up, probs, attn, qkv, reduced, dattn, dx1)
    return act, dx, grad_qkv, grad_dense


MESH = pl.DeviceIdType.MESH


def enter(peers):
    barrier = pltpu.get_barrier_semaphore()
    for peer in peers:
        pl.semaphore_signal(barrier, inc=1, device_id=peer, device_id_type=MESH)
    pl.semaphore_wait(barrier, len(peers))


class Sender:
    def __init__(self, send_sem, recv_sem):
        self.send_sem, self.recv_sem, self.count = send_sem, recv_sem, 0

    def copy(self, src, dst, peer):
        n = self.count
        self.count += 1
        made = pltpu.make_async_remote_copy(
            src_ref=src,
            dst_ref=dst,
            send_sem=self.send_sem.at[n],
            recv_sem=self.recv_sem.at[n],
            device_id=peer,
            device_id_type=MESH,
        )
        made.start()
        return made


def pack_vectors(vecs, ids):
    flat = jnp.concatenate([v.astype(F32) for v in vecs] + [ids.astype(F32)])
    return jnp.pad(flat, (0, 1024 - flat.shape[0])).reshape(8, 128)


def spread_kernel(
    tok_ref, unit_ref, vec_ref, pairs_ref,
    x_ref, weight_ref, down_ref, up_ref, gain1_ref, qkv_bias_ref, proj_bias_ref, gain2_ref, fc1_bias_ref,
    fc2_bias_ref, ids_ref, table_ref,
    units, vecs, beside, mixed, tops, found, wide, select, bias, send_sem, recv_sem, out_sem,
    *, clip_size,
):
    c, w = lax.axis_index("clip"), lax.axis_index("win")
    z, y = c // 2, c % 2
    x, k = w // 2, w % 2
    sibling = (c, x * 2 + 1 - k)
    across = (c, (1 - x) * 2 + k)
    zs = clip_size // 2

    def at(z_step, other_y):
        return (z + z_step + zs) % zs * 2 + (1 - y if other_y else y)

    items, rows, feats = tok_ref.shape
    enter([sibling, across] + [((c + d) % clip_size, w) for d in range(1, clip_size)])
    send = Sender(send_sem, recv_sem)
    waits = []
    units[k, c, x] = unit_ref[...]
    vecs[c] = vec_ref[...]
    to_across = send.copy(unit_ref, units.at[k, c, x], across)
    tokens_beside = [send.copy(tok_ref.at[i], beside.at[i], sibling) for i in range(items)]
    from_sibling = [send.copy(unit_ref, units.at[k, c, x], sibling)]
    vec_copies = [
        send.copy(vec_ref, vecs.at[c], ((c + d) % clip_size, w)) for d in range(1, clip_size)
    ]
    to_across.wait_recv()
    along_z = [send.copy(units.at[k, c], units.at[k, c], (at(j, False), w)) for j in range(1, zs)]
    along_y = [send.copy(units.at[k, c], units.at[k, c], (at(0, True), w))]
    from_sibling.append(send.copy(units.at[k, c, 1 - x], units.at[k, c, 1 - x], sibling))
    early, low_h, low_w = row_masks(rows, feats)
    token_tops = []
    for i in range(items):
        tokens_beside[i].wait_recv()
        mixed[i] = jnp.where(low_h, beside[i], tok_ref[i])
        token_tops.append(send.copy(mixed.at[i, pl.ds(0, TOP)], tops.at[i], across))

    heads = pairs_ref.shape[0] // 15
    off_lane = lane_ids((pairs_ref.shape[1], 128))
    off_row = lax.broadcasted_iota(jnp.int32, (pairs_ref.shape[1], 128), 0)
    query_at = (off_lane // 7 + 4) % 7 * 13 + (off_lane % 7 + 4) % 7
    wanted = off_row - query_at - 84
    valid = off_lane < 49

    def one_key(key, carry):
        key_at = (key // 7 + 4) % 7 * 13 + (key % 7 + 4) % 7
        pick = jnp.where(valid & (wanted + key_at == 0), 1.0, 0.0).astype(BF)
        value = dot(pairs_ref[...], pick, NN)
        for a in range(15):
            found[a, pl.ds(key, heads, stride=56), :] = value[a * heads : (a + 1) * heads]
        return carry

    lax.fori_loop(0, 49, one_key, 0)

    from_z = []
    for j in range(1, zs):
        along_z[j - 1].wait_recv()
        slot = at(-j, False)
        along_y.append(send.copy(units.at[k, slot], units.at[k, slot], (at(0, True), w)))
        from_sibling.append(send.copy(units.at[k, slot], units.at[k, slot], sibling))

    for a in range(15):
        wide[:, 128 * a : 128 * a + 128] = found[a].astype(BF)
    sel_row = lax.broadcasted_iota(jnp.int32, (128, rows), 0)
    sel_lane = lane_ids((128, rows))
    for t in range(8):
        select[128 * t : 128 * t + 128, :] = jnp.where(
            (sel_lane == sel_row + (t + 4) % 8 * 49) & (sel_row < 49), 1.0, 0.0
        ).astype(BF)

    for j in range(zs):
        along_y[j].wait_recv()
        slot = at(-j, True)
        from_sibling.append(send.copy(units.at[k, slot], units.at[k, slot], sibling))

    for block in range(8):
        t = (block + 4) % 8
        value = dot(wide[:, (7 - t) * 128 : (15 - t) * 128], select[...], NN) * LOG2E
        for m in range(heads):
            bias[m, 49 * block : 49 * block + 49, :] = value[56 * m : 56 * m + 49]
    out = pltpu.make_async_copy(bias, table_ref, out_sem)
    out.start()

    for copy in vec_copies:
        copy.wait_recv()
    for c2 in range(clip_size):
        v = vecs[c2]
        gain1_ref[:, 64 * c2 : 64 * c2 + 64] = v[0:1, 0:64]
        qkv_bias_ref[:, 192 * c2 : 192 * c2 + 64] = v[0:1, 64:128]
        qkv_bias_ref[:, 192 * c2 + 64 : 192 * c2 + 192] = v[1:2, :]
        proj_bias_ref[:, 64 * c2 : 64 * c2 + 64] = v[2:3, 0:64]
        gain2_ref[:, 64 * c2 : 64 * c2 + 64] = v[2:3, 64:128]
        fc1_bias_ref[:, 256 * c2 : 256 * c2 + 128] = v[3:4, :]
        fc1_bias_ref[:, 256 * c2 + 128 : 256 * c2 + 256] = v[4:5, :]
        fc2_bias_ref[:, 64 * c2 : 64 * c2 + 64] = v[5:6, 0:64]
        for n in range(2):
            ids_ref[2 * c2 + n : 2 * c2 + n + 1, :] = jnp.broadcast_to(
                v[5:6, 64 + n : 65 + n], (1, ids_ref.shape[1])
            )

    for copy in from_sibling:
        copy.wait_recv()
    for c2 in range(clip_size):
        for x2 in range(2):
            for k2 in range(2):
                n = 2 * x2 + k2
                weight_ref[64 * c2 : 64 * c2 + 64, 384 * n : 384 * n + 384] = units[k2, c2, x2, :, 0:384]
                for a in range(2):
                    low = units[k2, c2, x2, 16 * a : 16 * a + 16, 384:512]
                    high = units[k2, c2, x2, 32 + 16 * a : 48 + 16 * a, 384:512]
                    down_ref[2 * n + a, :, 64 * c2 : 64 * c2 + 64] = low[:, 0:64]
                    up_ref[2 * n + a, :, 192 * c2 : 192 * c2 + 64] = low[:, 64:128]
                    up_ref[2 * n + a, :, 192 * c2 + 64 : 192 * c2 + 192] = high

    for i in range(0, items, 2):
        both = []
        for e in range(2):
            token_tops[i + e].wait_recv()
            both.append(with_top(mixed[i + e], tops[i + e], early))
        for e in range(2):
            x_ref[i + e] = jnp.where(low_w, both[1 - e], both[e])

    for copy in [to_across, *tokens_beside, *from_sibling, *vec_copies, *along_z, *along_y, *token_tops]:
        copy.wait_send()
    out.wait()


def spread(tokens, unit, vec, pairs, clip_size):
    items, rows, feats = tokens.shape
    heads = pairs.shape[0] // 15
    f = functools.partial(jax.ShapeDtypeStruct)
    vm = pl.BlockSpec(memory_space=pltpu.VMEM)
    return pl.pallas_call(
        functools.partial(spread_kernel, clip_size=clip_size),
        in_specs=[vm] * 4,
        out_specs=[vm] * 11 + [pl.BlockSpec(memory_space=pl.ANY)],
        out_shape=[
            f((items, rows, feats), BF),
            f((512, 1536), BF),
            f((8, 16, 512), BF),
            f((8, 16, 1536), BF),
            f((1, 512), F32),
            f((1, 1536), F32),
            f((1, 512), F32),
            f((1, 512), F32),
            f((1, 2048), F32),
            f((1, 512), F32),
            f((16, 512), F32),
            f((heads, rows, rows), F32),
        ],
        scratch_shapes=[
            pltpu.VMEM((2, clip_size, 2, 64, 512), BF),
            pltpu.VMEM((clip_size, 8, 128), F32),
            pltpu.VMEM((items, rows, feats), BF),
            pltpu.VMEM((items, rows, feats), BF),
            pltpu.VMEM((items, TOP, feats), BF),
            pltpu.VMEM((15, 56 * heads, 128), F32),
            pltpu.VMEM((56 * heads, 15 * 128), BF),
            pltpu.VMEM((8 * 128, rows), BF),
            pltpu.VMEM((heads, rows, rows), F32),
            pltpu.SemaphoreType.DMA((32,)),
            pltpu.SemaphoreType.DMA((32,)),
            pltpu.SemaphoreType.DMA,
        ],
        compiler_params=pltpu.CompilerParams(
            collective_id=0, has_side_effects=True, vmem_limit_bytes=VMEM_LIMIT
        ),
        cost_estimate=pl.CostEstimate(flops=3 * 10**10, bytes_accessed=2 * 10**7, transcendentals=0),
        name="spread",
    )(tokens, unit, vec, pairs)


PIECES = (("q", 0, 64), ("q", 512, 192), ("d", 0, 64), ("d", 512, 64), ("d", 1024, 64), ("d", 5632, 64), ("d", 1536, 256), ("d", 3584, 256))


def finish_kernel(
    act_ref, act_beside_ref, act_across_ref, act_far_ref, dx_ref, grad_qkv_ref, grad_dense_ref, ids_ref,
    act_out_ref, dx_out_ref, qd_ref, qu_ref, pd_ref, pu_ref, f1d_ref, f1u_ref, f2d_ref, f2u_ref,
    beside, mixed, tops, own, other, from_core, half, from_x, shares, from_clips, adapters, from_win, whole_out,
    send_sem, recv_sem,
    *, clip_size,
):
    c, w = lax.axis_index("clip"), lax.axis_index("win")
    x, k = w // 2, w % 2
    sibling = (c, x * 2 + 1 - k)
    across = (c, (1 - x) * 2 + k)
    items, rows, feats = dx_ref.shape
    enter(
        [(c, (w + d) % 4) for d in range(1, 4)]
        + [((c + d) % clip_size, w) for d in range(1, clip_size)]
    )
    send = Sender(send_sem, recv_sem)
    dx_beside = [send.copy(dx_ref.at[i], beside.at[i], sibling) for i in range(items)]

    def rows_of(part, j):
        halves = []
        for n in range(2):
            cells = []
            for name, start, width in PIECES:
                ref = grad_qkv_ref if name == "q" else grad_dense_ref
                cells.append(
                    ref[n, pl.ds(pl.multiple_of(part * 8, 8), 8), start + j * width : start + (j + 1) * width]
                )
            halves.append(jnp.concatenate(cells, axis=1))
        return jnp.concatenate(halves, axis=0)

    for j in range(clip_size):
        other[j] = rows_of(1 - k, j).astype(BF)
    core_copy = send.copy(other, from_core, sibling)

    early, low_h, low_w = row_masks(rows, feats)
    dx_tops = []
    for i in range(items):
        dx_beside[i].wait_recv()
        mixed[i] = jnp.where(low_h, beside[i], dx_ref[i])
        dx_tops.append(send.copy(mixed.at[i, pl.ds(0, TOP)], tops.at[i], across))

    for j in range(clip_size):
        own[j] = rows_of(k, j)
    core_copy.wait_recv()
    own[...] += from_core[...].astype(F32)
    half[...] = own[:, :, pl.ds(pl.multiple_of((1 - x) * 512, 512), 512)].astype(BF)
    x_copy = send.copy(half, from_x, across)

    for i in range(0, items, 2):
        both = []
        for e in range(2):
            part = jnp.where(low_h, act_beside_ref[i + e], act_ref[i + e])
            top = jnp.where(low_h[:TOP], act_far_ref[i + e], act_across_ref[i + e])
            both.append(with_top(part, top, early))
        for e in range(2):
            act_out_ref[i + e] = jnp.where(low_w, both[1 - e], both[e])

    x_copy.wait_recv()
    shares[...] = (
        own[:, :, pl.ds(pl.multiple_of(x * 512, 512), 512)] + from_x[...].astype(F32)
    ).astype(BF)
    from_clips[c] = shares[c]
    clip_copies = []
    for d in range(1, clip_size):
        to = (c + d) % clip_size
        clip_copies.append(send.copy(shares.at[to], from_clips.at[c], (to, w)))
    for copy in clip_copies:
        copy.wait_recv()
    for a in range(8):
        total = None
        for n in range(2 * clip_size):
            value = from_clips[n // 2].astype(F32)[8 * (n % 2) : 8 * (n % 2) + 8]
            value = jnp.where(ids_ref[n : n + 1, :] == float(a), value, 0.0)
            total = value if total is None else total + value
        adapters[a // 2, 8 * (a % 2) : 8 * (a % 2) + 8, :] = total
    from_win[w] = adapters[w]
    win_copies = []
    for d in range(1, 4):
        to = (w + d) % 4
        win_copies.append(send.copy(adapters.at[to], from_win.at[w], (c, to)))

    for i in range(0, items, 2):
        both = []
        for e in range(2):
            dx_tops[i + e].wait_recv()
            both.append(with_top(mixed[i + e], tops[i + e], early))
        for e in range(2):
            dx_out_ref[i + e] = jnp.where(low_w, both[1 - e], both[e])

    for copy in win_copies:
        copy.wait_recv()
    for x2 in range(2):
        for k2 in range(2):
            for a in range(2):
                whole_out[a, 8 * k2 : 8 * k2 + 8, 512 * x2 : 512 * x2 + 512] = from_win[
                    2 * x2 + k2, 8 * a : 8 * a + 8, :
                ]
    for a in range(2):
        qd_ref[a] = whole_out[a, :, 0:64]
        qu_ref[a] = whole_out[a, :, 64:256]
        pd_ref[a] = whole_out[a, :, 256:320]
        pu_ref[a] = whole_out[a, :, 320:384]
        f1d_ref[a] = whole_out[a, :, 384:448]
        f2u_ref[a] = whole_out[a, :, 448:512]
        f1u_ref[a] = whole_out[a, :, 512:768]
        f2d_ref[a] = whole_out[a, :, 768:1024]
    for copy in [*dx_beside, core_copy, *dx_tops, x_copy, *clip_copies, *win_copies]:
        copy.wait_send()


def finish(act, act_pieces, dx, grad_qkv, grad_dense, ids, clip_size):
    items, rows, feats = dx.shape
    f = jax.ShapeDtypeStruct
    vm = pl.BlockSpec(memory_space=pltpu.VMEM)
    widths = (64, 192, 64, 64, 64, 256, 256, 64)
    return pl.pallas_call(
        functools.partial(finish_kernel, clip_size=clip_size),
        in_specs=[vm] * 8,
        out_specs=[vm] * 10,
        out_shape=[f(dx.shape, BF), f(dx.shape, BF)] + [f((2, 16, n), F32) for n in widths],
        scratch_shapes=[
            pltpu.VMEM((items, rows, feats), BF),
            pltpu.VMEM((items, rows, feats), BF),
            pltpu.VMEM((items, TOP, feats), BF),
            pltpu.VMEM((clip_size, 16, 1024), F32),
            pltpu.VMEM((clip_size, 16, 1024), BF),
            pltpu.VMEM((clip_size, 16, 1024), BF),
            pltpu.VMEM((clip_size, 16, 512), BF),
            pltpu.VMEM((clip_size, 16, 512), BF),
            pltpu.VMEM((clip_size, 16, 512), BF),
            pltpu.VMEM((clip_size, 16, 512), BF),
            pltpu.VMEM((4, 16, 512), F32),
            pltpu.VMEM((4, 16, 512), F32),
            pltpu.VMEM((2, 16, 1024), F32),
            pltpu.SemaphoreType.DMA((20,)),
            pltpu.SemaphoreType.DMA((20,)),
        ],
        compiler_params=pltpu.CompilerParams(
            collective_id=1, has_side_effects=True, vmem_limit_bytes=VMEM_LIMIT
        ),
        cost_estimate=pl.CostEstimate(flops=2 * 10**10, bytes_accessed=2 * 10**7, transcendentals=0),
        name="finish",
    )(act, *act_pieces, dx, grad_qkv, grad_dense, ids)


def exchange(x, win_size):
    local = x.shape[1]
    bits = local.bit_length() - 1
    at = jnp.arange(TOK)
    taken = (at // 49 < 4, at // 7 % 7 < 3, at % 7 < 3)
    for bit, rows in zip((2, 1, 0), taken):
        if bit < bits:
            split = x.reshape(x.shape[0], local >> (bit + 1), 2, 1 << bit, TOK, -1)
            other = jnp.flip(split, axis=2).reshape(x.shape)
        else:
            other = lax.ppermute(x, "win", [(i, i ^ 1 << bit - bits) for i in range(win_size)])
        x = jnp.where(rows[None, None, :, None], other, x)
    return x


def pieces_of(x):
    top = x[:, :TOP]
    return (
        x,
        lax.ppermute(x, "win", [(i, i ^ 1) for i in range(4)]),
        lax.ppermute(top, "win", [(i, i ^ 2) for i in range(4)]),
        lax.ppermute(top, "win", [(i, i ^ 3) for i in range(4)]),
    )


def place():
    at = jnp.arange(TOK)
    return at // 49, at // 7 % 7, at % 7


def window_masks(win_index, local):
    depth, height, across = place()
    number = win_index * local + jnp.arange(local)
    label = (
        number[:, None] // 4 % 2 * (depth < 4) * 4
        + number[:, None] // 2 % 2 * (height < 3) * 2
        + number[:, None] % 2 * (across < 3)
    )
    lane = jnp.arange(128)
    same = label[:, :, None] == lane
    return (
        same.astype(BF),
        jnp.where(same | (lane >= 8), 0.0, -FAR).astype(BF),
    )


def bias_by_pair(table):
    heads = table.shape[0]
    side = jnp.arange(49)
    high, wide = (side // 7 + 4) % 7, (side % 7 + 4) % 7
    offset = (high[None, :] - high[:, None] + 6) * 13 + wide[None, :] - wide[:, None] + 6
    pick = (jnp.arange(169)[:, None, None] == offset[None]).astype(BF)
    found = jnp.einsum(
        "mad,dkq->mkaq", table.reshape(heads, 15, 169), pick, preferred_element_type=F32
    )
    found = (found * LOG2E).reshape(heads, 49, 15 * 49)
    blocks = []
    for key_block in range(8):
        t = (key_block + 4) % 8
        blocks.append(
            jnp.concatenate(
                (found[..., (11 - t) * 49 : (15 - t) * 49], found[..., (7 - t) * 49 : (11 - t) * 49]),
                axis=-1,
            )
        )
    return jnp.stack(blocks, axis=1).reshape(heads, TOK, TOK)


def gather(array, spec):
    for axis, name in enumerate(spec):
        if name is not None:
            array = lax.all_gather(array, name, axis=axis, tiled=True)
    return array


def stage_whole(proj_w, fc1_w, fc2_w, maps):
    proj_down, proj_up, fc1_down, fc1_up, fc2_down, fc2_up = maps
    count = proj_down.shape[0]

    def short(a):
        return a.reshape(4, count // 4 * 16, 8, 64).transpose(2, 0, 1, 3)

    def long(a):
        return a.reshape(4, count // 4 * 16, 8, 2, 128).transpose(2, 0, 3, 1, 4).reshape(8, 4, -1, 128)

    return jnp.concatenate(
        (
            proj_w.reshape(8, 64, 4, 128).transpose(0, 2, 1, 3),
            fc1_w.reshape(8, 64, 4, 4, 128).transpose(0, 2, 3, 1, 4).reshape(8, 4, 256, 128),
            fc2_w.reshape(8, 256, 4, 128).transpose(0, 2, 1, 3),
            jnp.concatenate((short(proj_down), short(proj_up)), axis=-1),
            jnp.concatenate((short(fc1_down), short(fc2_up)), axis=-1),
            long(fc1_up),
            long(fc2_down),
        ),
        axis=2,
    )


def per_device(
    tokens, cotangent, adapter_ids, ln1_gain, qkv_weight, qkv_bias, proj_weight, proj_bias, ln2_gain,
    fc1_weight, fc1_bias, fc2_weight, fc2_bias, bias_table, qkv_down, qkv_up, proj_down, proj_up,
    fc1_down, fc1_up, fc2_down, fc2_up, *, clip_size, win_size,
):
    clips, local, rows, feats = tokens.shape
    items = clips * local
    heads = bias_table.shape[0]
    vecs = (ln1_gain, qkv_bias, proj_bias, ln2_gain, fc1_bias, fc2_bias)
    item_ids = jnp.repeat(adapter_ids, local)
    masks = window_masks(lax.axis_index("win"), local)
    flat = (items, rows, feats)
    downs = [a.transpose(0, 2, 1) for a in (qkv_down, proj_down, fc1_down, fc2_down)]
    own_kernels = (clip_size, win_size, clips, local) == (8, 4, 2, 2)
    if own_kernels:
        maps = [a.reshape(32, -1) for a in (downs[1], proj_up, downs[2], fc1_up, downs[3], fc2_up)]
        later = jnp.concatenate(
            (
                proj_weight,
                fc1_weight.reshape(64, 4, 128).transpose(1, 0, 2).reshape(256, 128),
                fc2_weight,
                jnp.concatenate((maps[0], maps[1]), axis=1),
                jnp.concatenate((maps[2], maps[5]), axis=1),
                maps[3][:, :128],
                maps[3][:, 128:],
                maps[4][:, :128],
                maps[4][:, 128:],
            ),
            axis=0,
        )
        staged = lax.all_gather(later, ("clip", "win")).reshape(8, 4, 768, 128)
        early = jnp.concatenate((downs[0].reshape(32, 64), qkv_up.reshape(32, 192)), axis=1)
        unit = jnp.concatenate(
            (qkv_weight, jnp.concatenate((early[:, :128], early[:, 128:]), axis=0)), axis=1
        )
        pairs = bias_table.reshape(heads, 15, 169).transpose(1, 0, 2).reshape(15 * heads, 169)
        pairs = jnp.pad(pairs, ((0, 0), (0, 7)))
        x, qkv_w, down, up, *vectors, ids, table = spread(
            tokens.reshape(flat), unit, pack_vectors(vecs, adapter_ids), pairs, clip_size
        )
        dy = pieces_of(cotangent.reshape(flat))
        qkv_parts = (qkv_w, down, up)
    else:
        grid2, by_down, by_up = ("clip", "win"), ("win", None, "clip"), ("win", None, "clip")
        qkv_parts = (gather(qkv_weight, grid2), gather(downs[0], by_down), gather(qkv_up, by_up))
        maps = (downs[1], proj_up, downs[2], fc1_up, downs[3], fc2_up)
        staged = stage_whole(
            *[gather(a, grid2) for a in (proj_weight, fc1_weight, fc2_weight)],
            [gather(a, by_up) for a in maps],
        )
        vectors = [gather(v, ("clip",)).reshape(1, -1).astype(F32) for v in vecs]
        table = bias_by_pair(bias_table)
        x = exchange(tokens, win_size).reshape(flat)
        dy = (exchange(cotangent, win_size).reshape(flat),)
    act, dx, grad_qkv, grad_dense = compute(
        x, dy, item_ids, vectors, qkv_parts, staged, masks, table, local
    )
    if own_kernels:
        act_out, dx_out, qd, qu, pd, pu, f1d, f1u, f2d, f2u = finish(
            act, pieces_of(act)[1:], dx, grad_qkv, grad_dense, ids, clip_size
        )
        turned = [a.transpose(0, 2, 1) for a in (qd, pd, f1d, f2d)]
        return (
            act_out.reshape(tokens.shape), dx_out.reshape(tokens.shape),
            turned[0], qu, turned[1], pu, turned[2], f1u, turned[3], f2u,
        )
    activations = exchange(act.reshape(tokens.shape), win_size)
    input_grad = exchange(dx.reshape(tokens.shape), win_size)
    adapter_count = win_size * qkv_down.shape[0]
    hot = (adapter_ids[:, None] == jnp.arange(adapter_count)[None]).astype(F32)
    hidden = fc1_weight.shape[1] * win_size
    spans = (feats, 3 * feats, feats, feats, feats, hidden, hidden, feats)
    grads = jnp.concatenate((grad_qkv, grad_dense), axis=-1)
    rank = grads.shape[1]
    parts, at = [], 0
    for span in spans:
        parts.append(
            grads[..., at : at + span].reshape(clips, rank, clip_size, span // clip_size)
        )
        at += span
    mine = jnp.concatenate(parts, axis=-1)
    grown = jnp.sum(hot[:, :, None, None, None] * mine[:, None], axis=0)
    grown = grown.transpose(2, 0, 1, 3).astype(BF)
    total = lax.psum_scatter(grown, "clip", scatter_dimension=0, tiled=True)[0]
    total = lax.psum_scatter(total, "win", scatter_dimension=0, tiled=True).astype(F32)
    outs, at = [], 0
    for n, span in enumerate(spans):
        width = span // clip_size
        part = total[..., at : at + width]
        at += width
        outs.append(part.transpose(0, 2, 1) if n % 2 == 0 else part)
    return (activations, input_grad, *outs)


def solution(mesh):
    split = P("clip", "win", None, None)
    grid2 = P("clip", "win")
    down = P("win", "clip", None)
    up = P("win", None, "clip")
    one = P("clip")
    return jax.shard_map(
        functools.partial(
            per_device, clip_size=mesh.shape["clip"], win_size=mesh.shape["win"]
        ),
        mesh=mesh,
        in_specs=(
            split, split, one, one, grid2, one, grid2, one, one, grid2, one, grid2, one, P(),
            down, up, down, up, down, up, down, up,
        ),
        out_specs=(split, split, down, up, down, up, down, up, down, up),
        check_vma=False,
    )
```

```python
import functools
import jax
import jax.numpy as jnp
from jax import lax
from jax.experimental import pallas as pl
from jax.experimental.pallas import tpu as pltpu
from jax.sharding import PartitionSpec as P

BF = jnp.bfloat16
F32 = jnp.float32
NN = (((1,), (0,)), ((), ()))
NT = (((1,), (1,)), ((), ()))
TN = (((0,), (0,)), ((), ()))
LOG2E = 1.4426950408889634
LN2 = 0.6931471805599453
FAR = 1e9
VMEM_LIMIT = 60 * 2**20
TOK = 392
TOP = 208


def dot(left, right, dims):
    return lax.dot_general(left, right, dims, preferred_element_type=F32)


def lane_ids(shape):
    return lax.broadcasted_iota(jnp.int32, shape, len(shape) - 1)


def norm_stats(values):
    average = jnp.mean(values, axis=-1, keepdims=True)
    centred = values - average
    variance = jnp.mean(centred * centred, axis=-1, keepdims=True)
    inverse = lax.rsqrt(variance + 1e-05)
    return centred * inverse, inverse


def norm_back(gradient, gain, normed, inverse):
    scaled = gradient * gain
    centre = jnp.mean(scaled, axis=-1, keepdims=True)
    slope = jnp.mean(scaled * normed, axis=-1, keepdims=True)
    return inverse * (scaled - centre - normed * slope)


def add_rows(ref, at, value, first):
    @pl.when(first)
    def _():
        ref[0, :, at] = value

    @pl.when(jnp.logical_not(first))
    def _():
        ref[0, :, at] += value


def attend_kernel(
    ids_ref,
    x_ref,
    gain_ref,
    weight_ref,
    bias_ref,
    down_ref,
    up_ref,
    key_mask_ref,
    query_mask_ref,
    table_ref,
    probs_ref,
    out_ref,
    qkv_ref,
    reduced_ref,
    keys,
    queries,
    values_t,
    out_t,
    scores,
    table,
    table_sem,
    *,
    scale,
    per_group,
    width,
):
    group = pl.program_id(1)
    groups = pl.num_programs(1)
    feats = x_ref.shape[-1]
    starting = pl.program_id(0) == 0

    def table_copy(g):
        at = pl.ds(g * per_group, per_group)
        return pltpu.make_async_copy(table_ref.at[at], table.at[at], table_sem.at[g])

    @pl.when(starting & (group == 0))
    def _():
        for g in range(table.shape[0] // per_group):
            table_copy(g).start()

    @pl.when(group == 0)
    def _():
        normed, _ = norm_stats(x_ref[0].astype(F32))
        low = (normed * gain_ref[...]).astype(BF)
        reduced = dot(down_ref[0], low, NT).astype(BF)
        reduced_ref[0] = reduced

        def columns(part):
            at = pl.ds(part * feats, feats)
            return (
                dot(low, weight_ref[:, at], NN)
                + bias_ref[:, at]
                + dot(reduced, up_ref[0, :, at], TN)
            )

        query = (columns(0) * (scale * LOG2E)).astype(BF)
        queries[...] = query
        qkv_ref[0, :, :feats] = query
        key = columns(1).astype(BF)
        qkv_ref[0, :, feats : 2 * feats] = key
        for g in range(feats // 128):
            keys[:, 256 * g : 256 * g + 128] = key[:, 128 * g : 128 * g + 128]
            keys[:, 256 * g + 128 : 256 * g + 256] = key_mask_ref[0]
        value = columns(2)
        value = value.astype(BF)
        qkv_ref[0, :, 2 * feats :] = value
        values_t[...] = value.T

    @pl.when(starting)
    def _():
        table_copy(group).wait()

    keys_now = keys[:, pl.ds(pl.multiple_of(group * 256, 256), 256)]
    query_now = queries[:, pl.ds(pl.multiple_of(group * 128, 128), 128)]
    head_of_lane = lane_ids(query_now.shape) // width

    def raw(h):
        own = jnp.where(head_of_lane == h, query_now, jnp.zeros_like(query_now))
        own = jnp.concatenate([own, query_mask_ref[0]], axis=1)
        return dot(keys_now, own, NT) + table[group * per_group + h]

    def finish(h):
        score = scores[h % 2]
        largest = jnp.max(score, axis=0, keepdims=True)
        probs = jnp.exp2(score - largest)
        total = jnp.sum(probs, axis=0, keepdims=True)
        probs = (probs * (1.0 / total)).astype(BF)
        probs_ref[0, h] = probs
        at = pl.ds(pl.multiple_of((group * per_group + h) * width, width), width)
        out_t[at, :] = dot(values_t[at, :], probs, NN).astype(BF)

    scores[0] = raw(0)
    for h in range(per_group):
        if h + 1 < per_group:
            scores[(h + 1) % 2] = raw(h + 1)
        finish(h)

    @pl.when(group == groups - 1)
    def _():
        out_ref[0] = out_t[...].T


def row_masks(rows, columns):
    row = lax.broadcasted_iota(jnp.int32, (rows, columns), 0)
    return row < TOK // 2, row % 49 < 21, row % 7 < 3


def with_top(part, top, early):
    return jnp.concatenate([jnp.where(early[:TOP], top, part[:TOP]), part[TOP:]], axis=0)


def join_pieces(refs, e):
    own, beside, across, far = refs
    early, low_h, low_w = row_masks(own.shape[1], own.shape[2])

    def window(n):
        part = jnp.where(low_h, beside[n], own[n])
        return with_top(part, jnp.where(low_h[:TOP], far[n], across[n]), early)

    return jnp.where(low_w, window(1 - e), window(e))


def dense_kernel(
    ids_ref,
    x_ref,
    attn_ref,
    gain_ref,
    proj_bias_ref,
    fc1_bias_ref,
    fc2_bias_ref,
    staged_ref,
    *refs,
    per_clip,
    chunk,
    pieces,
):
    tiles, refs = refs[:6], refs[6:]
    dy_refs, refs = refs[:pieces], refs[pieces:]
    act_ref, dx1_ref, dattn_ref, grad_ref, *refs = refs
    proj_ref, fc1_ref, fc2_ref, proj_down, proj_up, fc1_down, fc1_up, fc2_down, fc2_up, *refs = refs
    pres, acts, dpres, sem = refs
    starting = pl.program_id(0) == 0
    count = x_ref.shape[1]
    feats = x_ref.shape[-1]
    hidden = fc1_ref.shape[-1]

    def moves(first=0, last=24):
        found = [(0, 64, proj_ref, 128 * n, n) for n in range(4)]
        found += [(64 + 64 * t, 64, fc1_ref, 512 * n + 128 * t, n) for n in range(4) for t in range(4)]
        found += [(320, 256, fc2_ref, 128 * n, n) for n in range(4)]
        return [
            pltpu.make_async_copy(
                staged_ref.at[:, n, pl.ds(start, size), :],
                target.at[:, :, pl.ds(lane, 128)],
                sem.at[at],
            )
            for at, (start, size, target, lane, n) in enumerate(found)
            if first <= at < last
        ]

    def arrive(first, last):
        @pl.when(starting)
        def _():
            for copy in moves(first, last):
                copy.wait()

    @pl.when(starting)
    def _():
        for copy in moves():
            copy.start()

    for n in range(8):
        short = slice(64 * n, 64 * n + 64)
        proj_down[:, short] = tiles[0][n, 0, :, 0:64]
        proj_up[:, short] = tiles[0][n, 0, :, 64:128]
        fc1_down[:, short] = tiles[1][n, 0, :, 0:64]
        fc2_up[:, short] = tiles[1][n, 0, :, 64:128]
        for half in range(2):
            long = slice(256 * n + 128 * half, 256 * n + 128 * half + 128)
            fc1_up[:, long] = tiles[2 + half][n, 0]
            fc2_down[:, long] = tiles[4 + half][n, 0]

    def join(parts):
        return jnp.concatenate(parts, axis=0) if per_clip > 1 else parts[0]

    if pieces == 1:
        dy = join([dy_refs[0][e] for e in range(per_clip)])
    else:
        dy = join([join_pieces(dy_refs, e) for e in range(per_clip)])
    attn = join([attn_ref[e] for e in range(per_clip)])
    reduced_proj = dot(proj_down[...], attn, NT).astype(BF)
    arrive(0, 4)
    proj_w = proj_ref[...].reshape(feats, feats)
    middle = (
        join([x_ref[e].astype(F32) for e in range(per_clip)])
        + dot(attn, proj_w, NN)
        + proj_bias_ref[...]
        + dot(reduced_proj, proj_up[...], TN)
    )
    normed, inverse = norm_stats(middle)
    low = (normed * gain_ref[...]).astype(BF)
    reduced_fc1 = dot(fc1_down[...], low, NT).astype(BF)
    grad_reduced_fc2 = dot(fc2_up[...], dy, NT).astype(BF)
    per_chunk = chunk // fc2_ref.shape[1]
    steps = hidden // chunk

    def pre_of(j):
        at = slice(j * chunk, (j + 1) * chunk)
        pres[j % 2] = (
            dot(low, fc1_ref[:, :, at].reshape(feats, chunk), NN)
            + fc1_bias_ref[:, at]
            + dot(reduced_fc1, fc1_up[:, at], TN)
        )

    arrive(4, 20)
    pre_of(0)
    arrive(20, 24)
    for j in range(steps):
        at = slice(j * chunk, (j + 1) * chunk)
        if j + 1 < steps:
            pre_of(j + 1)
        fc2_w = fc2_ref[j * per_chunk : (j + 1) * per_chunk].reshape(chunk, feats)
        dact = dot(dy, fc2_w, NT) + dot(grad_reduced_fc2, fc2_down[:, at], TN)
        pre = pres[j % 2]
        bell = jnp.exp2((pre * pre) * (-0.5 * LOG2E))
        t = 1.0 / (1.0 + jnp.abs(pre) * (0.3275911 * 0.7071067811865476))
        poly = (
            (((0.5 * 1.061405429) * t - 0.5 * 1.453152027) * t + 0.5 * 1.421413741) * t
            - 0.5 * 0.284496736
        ) * t + 0.5 * 0.254829592
        tail = poly * t * bell
        below = jnp.where(pre >= 0.0, 1.0 - tail, tail)
        acts[:, at] = (pre * below).astype(BF)
        dpres[:, at] = (dact * (below + pre * bell * 0.3989422804014327)).astype(BF)
    act = acts[...]
    dpre = dpres[...]
    fc1_up_at = 3 * feats
    fc2_down_at = fc1_up_at + hidden
    fc2_up_at = fc2_down_at + hidden
    fc1_w = fc1_ref[...].reshape(feats, hidden)
    fc2_w = fc2_ref[...].reshape(hidden, feats)
    grad_reduced_fc1 = dot(fc1_up[...], dpre, NT).astype(BF)
    dlow = dot(dpre, fc1_w, NT) + dot(grad_reduced_fc1, fc1_down[...], TN)
    dx1 = dy.astype(F32) + norm_back(dlow, gain_ref[...], normed, inverse)
    branch = dx1.astype(BF)
    reduced_fc2 = dot(fc2_down[...], act, NT).astype(BF)
    total = (
        middle + fc2_bias_ref[...] + dot(act, fc2_w, NN) + dot(reduced_fc2, fc2_up[...], TN)
    ).astype(BF)
    grad_reduced_proj = dot(proj_up[...], branch, NT).astype(BF)
    dattn = (
        dot(branch, proj_w, NT) + dot(grad_reduced_proj, proj_down[...], TN)
    ).astype(BF)
    for e in range(per_clip):
        rows = slice(e * count, (e + 1) * count)
        act_ref[e] = total[rows]
        dx1_ref[e] = dx1[rows]
        dattn_ref[e] = dattn[rows]
    grad_ref[0, :, :feats] = dot(grad_reduced_proj, attn, NN)
    grad_ref[0, :, feats : 2 * feats] = dot(reduced_proj, branch, NN)
    grad_ref[0, :, 2 * feats : fc1_up_at] = dot(grad_reduced_fc1, low, NN)
    grad_ref[0, :, fc1_up_at:fc2_down_at] = dot(reduced_fc1, dpre, NN)
    grad_ref[0, :, fc2_down_at:fc2_up_at] = dot(grad_reduced_fc2, act, NN)
    grad_ref[0, :, fc2_up_at:] = dot(reduced_fc2, dy, NN)


def attend_back_kernel(
    ids_ref,
    x_ref,
    gain_ref,
    weight_ref,
    down_ref,
    up_ref,
    probs_ref,
    attn_ref,
    qkv_ref,
    reduced_ref,
    dattn_ref,
    dx1_ref,
    dx_ref,
    grad_ref,
    values,
    keys_t,
    inner,
    dqkv,
    dquery_t,
    *,
    scale,
    per_group,
    width,
    per_clip,
):
    group = pl.program_id(1)
    groups = pl.num_programs(1)
    feats = x_ref.shape[-1]
    rows = x_ref.shape[1]

    @pl.when(group == 0)
    def _():
        keys_t[...] = qkv_ref[0, :, feats : 2 * feats].T
        lane = lane_ids((rows, 128))
        ones = jnp.where(lane % width < 2, 1.0, 0.0).astype(BF)
        source = lax.broadcasted_iota(jnp.int32, (128, 128), 0)
        target = lane_ids((128, 128))
        pick = jnp.where(
            (source // width == target // width) & (target % width < 2), 1.0, 0.0
        ).astype(BF)
        pick = jnp.concatenate([pick, pick], axis=0)
        for g in range(feats // 128):
            at = slice(128 * g, 128 * g + 128)
            values[:, 256 * g : 256 * g + 128] = qkv_ref[0, :, 2 * feats + 128 * g : 2 * feats + 128 * g + 128]
            values[:, 256 * g + 128 : 256 * g + 256] = ones
            product = dattn_ref[0, :, at].astype(F32) * attn_ref[0, :, at].astype(F32)
            high = product.astype(BF)
            rest = (product - high.astype(F32)).astype(BF)
            sums = dot(jnp.concatenate([high, rest], axis=1), pick, NN)
            coarse = sums.astype(BF)
            fine = (sums - coarse.astype(F32)).astype(BF)
            inner[:, at] = -jnp.where(lane % width == 0, coarse, fine)

    blocks = pl.ds(pl.multiple_of(group * 128, 128), 128)
    values_now = values[:, pl.ds(pl.multiple_of(group * 256, 256), 256)]
    dattn_now = dattn_ref[0, :, blocks]
    inner_now = inner[:, blocks]
    query_now = qkv_ref[0, :, blocks]
    head_of_lane = lane_ids((rows, 128)) // width
    zero = jnp.zeros((rows, 128), BF)
    dvalue = None
    dkey = None
    for h in range(per_group):
        mine = head_of_lane == h
        dattn_own = jnp.where(mine, dattn_now, zero)
        query_own = jnp.where(mine, query_now, zero)
        right = jnp.concatenate([dattn_own, jnp.where(mine, inner_now, zero)], axis=1)
        probs = probs_ref[0, h]
        dscore = probs * dot(values_now, right, NT).astype(BF)
        partial = dot(probs, dattn_own, NN)
        dvalue = partial if dvalue is None else dvalue + partial
        partial = dot(dscore, query_own, NN)
        dkey = partial if dkey is None else dkey + partial
        at = pl.ds(pl.multiple_of((group * per_group + h) * width, width), width)
        dquery_t[at, :] = (dot(keys_t[at, :], dscore, NN) * scale).astype(BF)
    dqkv[:, pl.ds(pl.multiple_of(2 * feats + group * 128, 128), 128)] = dvalue.astype(BF)
    dqkv[:, pl.ds(pl.multiple_of(feats + group * 128, 128), 128)] = (dkey * LN2).astype(BF)

    @pl.when(group == groups - 1)
    def _():
        first = pl.program_id(0) % per_clip == 0
        dqkv[:, :feats] = dquery_t[...].T
        dall = dqkv[...]
        normed, inverse = norm_stats(x_ref[0].astype(F32))
        low = (normed * gain_ref[...]).astype(BF)
        grad_reduced = dot(up_ref[0], dall, NT).astype(BF)
        add_rows(grad_ref, slice(feats, 4 * feats), dot(reduced_ref[0], dall, NN), first)
        add_rows(grad_ref, slice(0, feats), dot(grad_reduced, low, NN), first)
        dlow = (dot(dall, weight_ref[...], NT) + dot(grad_reduced, down_ref[0], TN)).astype(BF)
        dx_ref[0] = (
            dx1_ref[0] + norm_back(dlow.astype(F32), gain_ref[...], normed, inverse)
        ).astype(BF)


def whole(shape):
    return pl.BlockSpec(shape, lambda *at: (0,) * len(shape), pipeline_mode=pl.Buffered(1))


def compute(x, dy, item_ids, vectors, qkv_parts, staged, masks, table, per_clip):
    items, rows, feats = x.shape
    heads = table.shape[0]
    width = feats // heads
    per_group = 128 // width
    groups = heads // per_group
    scale = width**-0.5
    gain1, qkv_bias, proj_bias, gain2, fc1_bias, fc2_bias = vectors
    qkv_w, qkv_down, qkv_up = qkv_parts
    key_mask, query_mask = masks
    rank = qkv_down.shape[1]
    hidden = fc1_bias.shape[1]
    clips = items // per_clip

    def item(shape):
        return pl.BlockSpec((1, *shape), lambda i, *rest: (i,) + (0,) * len(shape))

    def adapter(array):
        return pl.BlockSpec((1, *array.shape[1:]), lambda i, *rest: (rest[-1][i], 0, 0))

    probs, attn, qkv, reduced = pl.pallas_call(
        functools.partial(attend_kernel, scale=scale, per_group=per_group, width=width),
        grid_spec=pltpu.PrefetchScalarGridSpec(
            num_scalar_prefetch=1,
            grid=(items, groups),
            in_specs=[
                item((rows, feats)),
                whole(gain1.shape),
                whole(qkv_w.shape),
                whole(qkv_bias.shape),
                adapter(qkv_down),
                adapter(qkv_up),
                pl.BlockSpec((1, rows, 128), lambda i, g, ids: (i % per_clip, 0, 0)),
                pl.BlockSpec((1, rows, 128), lambda i, g, ids: (i % per_clip, 0, 0)),
                pl.BlockSpec(memory_space=pl.ANY),
            ],
            out_specs=[
                pl.BlockSpec((1, per_group, rows, rows), lambda i, g, ids: (i, g, 0, 0)),
                item((rows, feats)),
                item((rows, 3 * feats)),
                item((rank, rows)),
            ],
            scratch_shapes=[
                pltpu.VMEM((rows, 2 * feats), BF),
                pltpu.VMEM((rows, feats), BF),
                pltpu.VMEM((feats, rows), BF),
                pltpu.VMEM((feats, rows), BF),
                pltpu.VMEM((2, rows, rows), F32),
                pltpu.VMEM(table.shape, F32),
                pltpu.SemaphoreType.DMA((groups,)),
            ],
        ),
        out_shape=[
            jax.ShapeDtypeStruct((items, heads, rows, rows), BF),
            jax.ShapeDtypeStruct((items, rows, feats), BF),
            jax.ShapeDtypeStruct((items, rows, 3 * feats), BF),
            jax.ShapeDtypeStruct((items, rank, rows), BF),
        ],
        compiler_params=pltpu.CompilerParams(
            vmem_limit_bytes=VMEM_LIMIT, dimension_semantics=("arbitrary", "arbitrary")
        ),
        cost_estimate=pl.CostEstimate(flops=4 * 10**10, bytes_accessed=10**7, transcendentals=0),
        name="attend",
    )(item_ids, x, gain1, qkv_w, qkv_bias, qkv_down, qkv_up, key_mask, query_mask, table)

    span = 4 * feats + 2 * hidden
    def tile(n):
        return pl.BlockSpec(
            (8, 1, rank, 128),
            lambda c, ids: (0, ids[c * per_clip] // 2, 36 + 2 * n + ids[c * per_clip] % 2, 0),
        )

    def clip(array_shape):
        return pl.BlockSpec((per_clip, *array_shape[1:]), lambda c, ids: (c, 0, 0))

    chunk = 512
    act, dx1, dattn, grad_dense = pl.pallas_call(
        functools.partial(dense_kernel, per_clip=per_clip, chunk=chunk, pieces=len(dy)),
        grid_spec=pltpu.PrefetchScalarGridSpec(
            num_scalar_prefetch=1,
            grid=(clips,),
            in_specs=[
                clip(x.shape),
                clip(x.shape),
                whole(gain2.shape),
                whole(proj_bias.shape),
                whole(fc1_bias.shape),
                whole(fc2_bias.shape),
                pl.BlockSpec(memory_space=pl.ANY),
                *[tile(n) for n in range(6)],
                *[clip(a.shape) for a in dy],
            ],
            out_specs=[
                clip(x.shape),
                clip(x.shape),
                clip(x.shape),
                pl.BlockSpec((1, rank, span), lambda c, ids: (c, 0, 0)),
            ],
            scratch_shapes=[
                pltpu.VMEM((8, feats // 8, feats), BF),
                pltpu.VMEM((8, feats // 8, hidden), BF),
                pltpu.VMEM((8, hidden // 8, feats), BF),
                *[pltpu.VMEM((rank, n), BF) for n in (feats, feats, feats, hidden, hidden, feats)],
                pltpu.VMEM((2, per_clip * rows, chunk), F32),
                pltpu.VMEM((per_clip * rows, hidden), BF),
                pltpu.VMEM((per_clip * rows, hidden), BF),
                pltpu.SemaphoreType.DMA((24,)),
            ],
        ),
        out_shape=[
            jax.ShapeDtypeStruct((items, rows, feats), BF),
            jax.ShapeDtypeStruct((items, rows, feats), F32),
            jax.ShapeDtypeStruct((items, rows, feats), BF),
            jax.ShapeDtypeStruct((clips, rank, span), F32),
        ],
        compiler_params=pltpu.CompilerParams(
            vmem_limit_bytes=VMEM_LIMIT, dimension_semantics=("arbitrary",)
        ),
        cost_estimate=pl.CostEstimate(flops=5 * 10**10, bytes_accessed=10**7, transcendentals=0),
        name="dense",
    )(
        item_ids, x, attn, gain2, proj_bias, fc1_bias, fc2_bias, staged, *([staged] * 6), *dy
    )

    dx, grad_qkv = pl.pallas_call(
        functools.partial(
            attend_back_kernel, scale=scale, per_group=per_group, width=width, per_clip=per_clip
        ),
        grid_spec=pltpu.PrefetchScalarGridSpec(
            num_scalar_prefetch=1,
            grid=(items, groups),
            in_specs=[
                item((rows, feats)),
                whole(gain1.shape),
                whole(qkv_w.shape),
                adapter(qkv_down),
                adapter(qkv_up),
                pl.BlockSpec((1, per_group, rows, rows), lambda i, g, ids: (i, g, 0, 0)),
                item((rows, feats)),
                item((rows, 3 * feats)),
                item((rank, rows)),
                item((rows, feats)),
                item((rows, feats)),
            ],
            out_specs=[
                item((rows, feats)),
                pl.BlockSpec((1, rank, 4 * feats), lambda i, g, ids: (i // per_clip, 0, 0)),
            ],
            scratch_shapes=[
                pltpu.VMEM((rows, 2 * feats), BF),
                pltpu.VMEM((feats, rows), BF),
                pltpu.VMEM((rows, feats), BF),
                pltpu.VMEM((rows, 3 * feats), BF),
                pltpu.VMEM((feats, rows), BF),
            ],
        ),
        out_shape=[
            jax.ShapeDtypeStruct((items, rows, feats), BF),
            jax.ShapeDtypeStruct((clips, rank, 4 * feats), F32),
        ],
        compiler_params=pltpu.CompilerParams(
            vmem_limit_bytes=VMEM_LIMIT, dimension_semantics=("arbitrary", "arbitrary")
        ),
        cost_estimate=pl.CostEstimate(flops=5 * 10**10, bytes_accessed=10**7, transcendentals=0),
        name="attend_back",
    )(item_ids, x, gain1, qkv_w, qkv_down, qkv_up, probs, attn, qkv, reduced, dattn, dx1)
    return act, dx, grad_qkv, grad_dense


MESH = pl.DeviceIdType.MESH


def enter(peers):
    barrier = pltpu.get_barrier_semaphore()
    for peer in peers:
        pl.semaphore_signal(barrier, inc=1, device_id=peer, device_id_type=MESH)
    pl.semaphore_wait(barrier, len(peers))


class Sender:
    def __init__(self, send_sem, recv_sem):
        self.send_sem, self.recv_sem, self.count = send_sem, recv_sem, 0

    def copy(self, src, dst, peer):
        n = self.count
        self.count += 1
        made = pltpu.make_async_remote_copy(
            src_ref=src,
            dst_ref=dst,
            send_sem=self.send_sem.at[n],
            recv_sem=self.recv_sem.at[n],
            device_id=peer,
            device_id_type=MESH,
        )
        made.start()
        return made


def pack_vectors(vecs, ids):
    flat = jnp.concatenate([v.astype(F32) for v in vecs] + [ids.astype(F32)])
    return jnp.pad(flat, (0, 1024 - flat.shape[0])).reshape(8, 128)


def spread_kernel(
    tok_ref, unit_ref, vec_ref, pairs_ref,
    x_ref, weight_ref, down_ref, up_ref, gain1_ref, qkv_bias_ref, proj_bias_ref, gain2_ref, fc1_bias_ref,
    fc2_bias_ref, ids_ref, table_ref,
    units, vecs, beside, mixed, tops, found, wide, select, bias, send_sem, recv_sem, out_sem,
    *, clip_size,
):
    c, w = lax.axis_index("clip"), lax.axis_index("win")
    z, y = c // 2, c % 2
    x, k = w // 2, w % 2
    sibling = (c, x * 2 + 1 - k)
    across = (c, (1 - x) * 2 + k)
    zs = clip_size // 2

    def at(z_step, other_y):
        return (z + z_step + zs) % zs * 2 + (1 - y if other_y else y)

    items, rows, feats = tok_ref.shape
    enter([sibling, across] + [((c + d) % clip_size, w) for d in range(1, clip_size)])
    send = Sender(send_sem, recv_sem)
    waits = []
    units[k, c, x] = unit_ref[...]
    vecs[c] = vec_ref[...]
    to_across = send.copy(unit_ref, units.at[k, c, x], across)
    tokens_beside = [send.copy(tok_ref.at[i], beside.at[i], sibling) for i in range(items)]
    from_sibling = [send.copy(unit_ref, units.at[k, c, x], sibling)]
    vec_copies = [
        send.copy(vec_ref, vecs.at[c], ((c + d) % clip_size, w)) for d in range(1, clip_size)
    ]
    to_across.wait_recv()
    along_z = [send.copy(units.at[k, c], units.at[k, c], (at(j, False), w)) for j in range(1, zs)]
    along_y = [send.copy(units.at[k, c], units.at[k, c], (at(0, True), w))]
    from_sibling.append(send.copy(units.at[k, c, 1 - x], units.at[k, c, 1 - x], sibling))
    early, low_h, low_w = row_masks(rows, feats)
    token_tops = []
    for i in range(items):
        tokens_beside[i].wait_recv()
        mixed[i] = jnp.where(low_h, beside[i], tok_ref[i])
        token_tops.append(send.copy(mixed.at[i, pl.ds(0, TOP)], tops.at[i], across))

    heads = pairs_ref.shape[0] // 15
    off_lane = lane_ids((pairs_ref.shape[1], 128))
    off_row = lax.broadcasted_iota(jnp.int32, (pairs_ref.shape[1], 128), 0)
    query_at = (off_lane // 7 + 4) % 7 * 13 + (off_lane % 7 + 4) % 7
    wanted = off_row - query_at - 84
    valid = off_lane < 49

    def one_key(key, carry):
        key_at = (key // 7 + 4) % 7 * 13 + (key % 7 + 4) % 7
        pick = jnp.where(valid & (wanted + key_at == 0), 1.0, 0.0).astype(BF)
        value = dot(pairs_ref[...], pick, NN)
        for a in range(15):
            found[a, pl.ds(key, heads, stride=56), :] = value[a * heads : (a + 1) * heads]
        return carry

    lax.fori_loop(0, 49, one_key, 0)

    from_z = []
    for j in range(1, zs):
        along_z[j - 1].wait_recv()
        slot = at(-j, False)
        along_y.append(send.copy(units.at[k, slot], units.at[k, slot], (at(0, True), w)))
        from_sibling.append(send.copy(units.at[k, slot], units.at[k, slot], sibling))

    for a in range(15):
        wide[:, 128 * a : 128 * a + 128] = found[a].astype(BF)
    sel_row = lax.broadcasted_iota(jnp.int32, (128, rows), 0)
    sel_lane = lane_ids((128, rows))
    for t in range(8):
        select[128 * t : 128 * t + 128, :] = jnp.where(
            (sel_lane == sel_row + (t + 4) % 8 * 49) & (sel_row < 49), 1.0, 0.0
        ).astype(BF)

    for j in range(zs):
        along_y[j].wait_recv()
        slot = at(-j, True)
        from_sibling.append(send.copy(units.at[k, slot], units.at[k, slot], sibling))

    for block in range(8):
        t = (block + 4) % 8
        value = dot(wide[:, (7 - t) * 128 : (15 - t) * 128], select[...], NN) * LOG2E
        for m in range(heads):
            bias[m, 49 * block : 49 * block + 49, :] = value[56 * m : 56 * m + 49]
    out = pltpu.make_async_copy(bias, table_ref, out_sem)
    out.start()

    for copy in vec_copies:
        copy.wait_recv()
    for c2 in range(clip_size):
        v = vecs[c2]
        gain1_ref[:, 64 * c2 : 64 * c2 + 64] = v[0:1, 0:64]
        qkv_bias_ref[:, 192 * c2 : 192 * c2 + 64] = v[0:1, 64:128]
        qkv_bias_ref[:, 192 * c2 + 64 : 192 * c2 + 192] = v[1:2, :]
        proj_bias_ref[:, 64 * c2 : 64 * c2 + 64] = v[2:3, 0:64]
        gain2_ref[:, 64 * c2 : 64 * c2 + 64] = v[2:3, 64:128]
        fc1_bias_ref[:, 256 * c2 : 256 * c2 + 128] = v[3:4, :]
        fc1_bias_ref[:, 256 * c2 + 128 : 256 * c2 + 256] = v[4:5, :]
        fc2_bias_ref[:, 64 * c2 : 64 * c2 + 64] = v[5:6, 0:64]
        for n in range(2):
            ids_ref[2 * c2 + n : 2 * c2 + n + 1, :] = jnp.broadcast_to(
                v[5:6, 64 + n : 65 + n], (1, ids_ref.shape[1])
            )

    for copy in from_sibling:
        copy.wait_recv()
    for c2 in range(clip_size):
        for x2 in range(2):
            for k2 in range(2):
                n = 2 * x2 + k2
                weight_ref[64 * c2 : 64 * c2 + 64, 384 * n : 384 * n + 384] = units[k2, c2, x2, :, 0:384]
                for a in range(2):
                    low = units[k2, c2, x2, 16 * a : 16 * a + 16, 384:512]
                    high = units[k2, c2, x2, 32 + 16 * a : 48 + 16 * a, 384:512]
                    down_ref[2 * n + a, :, 64 * c2 : 64 * c2 + 64] = low[:, 0:64]
                    up_ref[2 * n + a, :, 192 * c2 : 192 * c2 + 64] = low[:, 64:128]
                    up_ref[2 * n + a, :, 192 * c2 + 64 : 192 * c2 + 192] = high

    for i in range(0, items, 2):
        both = []
        for e in range(2):
            token_tops[i + e].wait_recv()
            both.append(with_top(mixed[i + e], tops[i + e], early))
        for e in range(2):
            x_ref[i + e] = jnp.where(low_w, both[1 - e], both[e])

    for copy in [to_across, *tokens_beside, *from_sibling, *vec_copies, *along_z, *along_y, *token_tops]:
        copy.wait_send()
    out.wait()


def spread(tokens, unit, vec, pairs, clip_size):
    items, rows, feats = tokens.shape
    heads = pairs.shape[0] // 15
    f = functools.partial(jax.ShapeDtypeStruct)
    vm = pl.BlockSpec(memory_space=pltpu.VMEM)
    return pl.pallas_call(
        functools.partial(spread_kernel, clip_size=clip_size),
        in_specs=[vm] * 4,
        out_specs=[vm] * 11 + [pl.BlockSpec(memory_space=pl.ANY)],
        out_shape=[
            f((items, rows, feats), BF),
            f((512, 1536), BF),
            f((8, 16, 512), BF),
            f((8, 16, 1536), BF),
            f((1, 512), F32),
            f((1, 1536), F32),
            f((1, 512), F32),
            f((1, 512), F32),
            f((1, 2048), F32),
            f((1, 512), F32),
            f((16, 512), F32),
            f((heads, rows, rows), F32),
        ],
        scratch_shapes=[
            pltpu.VMEM((2, clip_size, 2, 64, 512), BF),
            pltpu.VMEM((clip_size, 8, 128), F32),
            pltpu.VMEM((items, rows, feats), BF),
            pltpu.VMEM((items, rows, feats), BF),
            pltpu.VMEM((items, TOP, feats), BF),
            pltpu.VMEM((15, 56 * heads, 128), F32),
            pltpu.VMEM((56 * heads, 15 * 128), BF),
            pltpu.VMEM((8 * 128, rows), BF),
            pltpu.VMEM((heads, rows, rows), F32),
            pltpu.SemaphoreType.DMA((32,)),
            pltpu.SemaphoreType.DMA((32,)),
            pltpu.SemaphoreType.DMA,
        ],
        compiler_params=pltpu.CompilerParams(
            collective_id=0, has_side_effects=True, vmem_limit_bytes=VMEM_LIMIT
        ),
        cost_estimate=pl.CostEstimate(flops=3 * 10**10, bytes_accessed=2 * 10**7, transcendentals=0),
        name="spread",
    )(tokens, unit, vec, pairs)


PIECES = (("q", 0, 64), ("q", 512, 192), ("d", 0, 64), ("d", 512, 64), ("d", 1024, 64), ("d", 5632, 64), ("d", 1536, 256), ("d", 3584, 256))


def finish_kernel(
    act_ref, act_beside_ref, act_across_ref, act_far_ref, dx_ref, grad_qkv_ref, grad_dense_ref, ids_ref,
    act_out_ref, dx_out_ref, qd_ref, qu_ref, pd_ref, pu_ref, f1d_ref, f1u_ref, f2d_ref, f2u_ref,
    beside, mixed, tops, own, other, from_core, half, from_x, shares, from_clips, adapters, from_win, whole_out,
    send_sem, recv_sem,
    *, clip_size,
):
    c, w = lax.axis_index("clip"), lax.axis_index("win")
    x, k = w // 2, w % 2
    sibling = (c, x * 2 + 1 - k)
    across = (c, (1 - x) * 2 + k)
    items, rows, feats = dx_ref.shape
    enter(
        [(c, (w + d) % 4) for d in range(1, 4)]
        + [((c + d) % clip_size, w) for d in range(1, clip_size)]
    )
    send = Sender(send_sem, recv_sem)
    dx_beside = [send.copy(dx_ref.at[i], beside.at[i], sibling) for i in range(items)]

    def rows_of(part, j):
        halves = []
        for n in range(2):
            cells = []
            for name, start, width in PIECES:
                ref = grad_qkv_ref if name == "q" else grad_dense_ref
                cells.append(
                    ref[n, pl.ds(pl.multiple_of(part * 8, 8), 8), start + j * width : start + (j + 1) * width]
                )
            halves.append(jnp.concatenate(cells, axis=1))
        return jnp.concatenate(halves, axis=0)

    for j in range(clip_size):
        other[j] = rows_of(1 - k, j).astype(BF)
    core_copy = send.copy(other, from_core, sibling)

    early, low_h, low_w = row_masks(rows, feats)
    dx_tops = []
    for i in range(items):
        dx_beside[i].wait_recv()
        mixed[i] = jnp.where(low_h, beside[i], dx_ref[i])
        dx_tops.append(send.copy(mixed.at[i, pl.ds(0, TOP)], tops.at[i], across))

    for j in range(clip_size):
        own[j] = rows_of(k, j)
    core_copy.wait_recv()
    own[...] += from_core[...].astype(F32)
    half[...] = own[:, :, pl.ds(pl.multiple_of((1 - x) * 512, 512), 512)].astype(BF)
    x_copy = send.copy(half, from_x, across)

    for i in range(0, items, 2):
        both = []
        for e in range(2):
            part = jnp.where(low_h, act_beside_ref[i + e], act_ref[i + e])
            top = jnp.where(low_h[:TOP], act_far_ref[i + e], act_across_ref[i + e])
            both.append(with_top(part, top, early))
        for e in range(2):
            act_out_ref[i + e] = jnp.where(low_w, both[1 - e], both[e])

    x_copy.wait_recv()
    shares[...] = (
        own[:, :, pl.ds(pl.multiple_of(x * 512, 512), 512)] + from_x[...].astype(F32)
    ).astype(BF)
    from_clips[c] = shares[c]
    clip_copies = []
    for d in range(1, clip_size):
        to = (c + d) % clip_size
        clip_copies.append(send.copy(shares.at[to], from_clips.at[c], (to, w)))
    for copy in clip_copies:
        copy.wait_recv()
    for a in range(8):
        total = None
        for n in range(2 * clip_size):
            value = from_clips[n // 2].astype(F32)[8 * (n % 2) : 8 * (n % 2) + 8]
            value = jnp.where(ids_ref[n : n + 1, :] == float(a), value, 0.0)
            total = value if total is None else total + value
        adapters[a // 2, 8 * (a % 2) : 8 * (a % 2) + 8, :] = total
    from_win[w] = adapters[w]
    win_copies = []
    for d in range(1, 4):
        to = (w + d) % 4
        win_copies.append(send.copy(adapters.at[to], from_win.at[w], (c, to)))

    for i in range(0, items, 2):
        both = []
        for e in range(2):
            dx_tops[i + e].wait_recv()
            both.append(with_top(mixed[i + e], tops[i + e], early))
        for e in range(2):
            dx_out_ref[i + e] = jnp.where(low_w, both[1 - e], both[e])

    for copy in win_copies:
        copy.wait_recv()
    for x2 in range(2):
        for k2 in range(2):
            for a in range(2):
                whole_out[a, 8 * k2 : 8 * k2 + 8, 512 * x2 : 512 * x2 + 512] = from_win[
                    2 * x2 + k2, 8 * a : 8 * a + 8, :
                ]
    for a in range(2):
        qd_ref[a] = whole_out[a, :, 0:64]
        qu_ref[a] = whole_out[a, :, 64:256]
        pd_ref[a] = whole_out[a, :, 256:320]
        pu_ref[a] = whole_out[a, :, 320:384]
        f1d_ref[a] = whole_out[a, :, 384:448]
        f2u_ref[a] = whole_out[a, :, 448:512]
        f1u_ref[a] = whole_out[a, :, 512:768]
        f2d_ref[a] = whole_out[a, :, 768:1024]
    for copy in [*dx_beside, core_copy, *dx_tops, x_copy, *clip_copies, *win_copies]:
        copy.wait_send()


def finish(act, act_pieces, dx, grad_qkv, grad_dense, ids, clip_size):
    items, rows, feats = dx.shape
    f = jax.ShapeDtypeStruct
    vm = pl.BlockSpec(memory_space=pltpu.VMEM)
    widths = (64, 192, 64, 64, 64, 256, 256, 64)
    return pl.pallas_call(
        functools.partial(finish_kernel, clip_size=clip_size),
        in_specs=[vm] * 8,
        out_specs=[vm] * 10,
        out_shape=[f(dx.shape, BF), f(dx.shape, BF)] + [f((2, 16, n), F32) for n in widths],
        scratch_shapes=[
            pltpu.VMEM((items, rows, feats), BF),
            pltpu.VMEM((items, rows, feats), BF),
            pltpu.VMEM((items, TOP, feats), BF),
            pltpu.VMEM((clip_size, 16, 1024), F32),
            pltpu.VMEM((clip_size, 16, 1024), BF),
            pltpu.VMEM((clip_size, 16, 1024), BF),
            pltpu.VMEM((clip_size, 16, 512), BF),
            pltpu.VMEM((clip_size, 16, 512), BF),
            pltpu.VMEM((clip_size, 16, 512), BF),
            pltpu.VMEM((clip_size, 16, 512), BF),
            pltpu.VMEM((4, 16, 512), F32),
            pltpu.VMEM((4, 16, 512), F32),
            pltpu.VMEM((2, 16, 1024), F32),
            pltpu.SemaphoreType.DMA((20,)),
            pltpu.SemaphoreType.DMA((20,)),
        ],
        compiler_params=pltpu.CompilerParams(
            collective_id=1, has_side_effects=True, vmem_limit_bytes=VMEM_LIMIT
        ),
        cost_estimate=pl.CostEstimate(flops=2 * 10**10, bytes_accessed=2 * 10**7, transcendentals=0),
        name="finish",
    )(act, *act_pieces, dx, grad_qkv, grad_dense, ids)


def exchange(x, win_size):
    local = x.shape[1]
    bits = local.bit_length() - 1
    at = jnp.arange(TOK)
    taken = (at // 49 < 4, at // 7 % 7 < 3, at % 7 < 3)
    for bit, rows in zip((2, 1, 0), taken):
        if bit < bits:
            split = x.reshape(x.shape[0], local >> (bit + 1), 2, 1 << bit, TOK, -1)
            other = jnp.flip(split, axis=2).reshape(x.shape)
        else:
            other = lax.ppermute(x, "win", [(i, i ^ 1 << bit - bits) for i in range(win_size)])
        x = jnp.where(rows[None, None, :, None], other, x)
    return x


def pieces_of(x):
    top = x[:, :TOP]
    return (
        x,
        lax.ppermute(x, "win", [(i, i ^ 1) for i in range(4)]),
        lax.ppermute(top, "win", [(i, i ^ 2) for i in range(4)]),
        lax.ppermute(top, "win", [(i, i ^ 3) for i in range(4)]),
    )


def place():
    at = jnp.arange(TOK)
    return at // 49, at // 7 % 7, at % 7


def window_masks(win_index, local):
    depth, height, across = place()
    number = win_index * local + jnp.arange(local)
    label = (
        number[:, None] // 4 % 2 * (depth < 4) * 4
        + number[:, None] // 2 % 2 * (height < 3) * 2
        + number[:, None] % 2 * (across < 3)
    )
    lane = jnp.arange(128)
    same = label[:, :, None] == lane
    return (
        same.astype(BF),
        jnp.where(same | (lane >= 8), 0.0, -FAR).astype(BF),
    )


def bias_by_pair(table):
    heads = table.shape[0]
    side = jnp.arange(49)
    high, wide = (side // 7 + 4) % 7, (side % 7 + 4) % 7
    offset = (high[None, :] - high[:, None] + 6) * 13 + wide[None, :] - wide[:, None] + 6
    pick = (jnp.arange(169)[:, None, None] == offset[None]).astype(BF)
    found = jnp.einsum(
        "mad,dkq->mkaq", table.reshape(heads, 15, 169), pick, preferred_element_type=F32
    )
    found = (found * LOG2E).reshape(heads, 49, 15 * 49)
    blocks = []
    for key_block in range(8):
        t = (key_block + 4) % 8
        blocks.append(
            jnp.concatenate(
                (found[..., (11 - t) * 49 : (15 - t) * 49], found[..., (7 - t) * 49 : (11 - t) * 49]),
                axis=-1,
            )
        )
    return jnp.stack(blocks, axis=1).reshape(heads, TOK, TOK)


def gather(array, spec):
    for axis, name in enumerate(spec):
        if name is not None:
            array = lax.all_gather(array, name, axis=axis, tiled=True)
    return array


def stage_whole(proj_w, fc1_w, fc2_w, maps):
    proj_down, proj_up, fc1_down, fc1_up, fc2_down, fc2_up = maps
    count = proj_down.shape[0]

    def short(a):
        return a.reshape(4, count // 4 * 16, 8, 64).transpose(2, 0, 1, 3)

    def long(a):
        return a.reshape(4, count // 4 * 16, 8, 2, 128).transpose(2, 0, 3, 1, 4).reshape(8, 4, -1, 128)

    return jnp.concatenate(
        (
            proj_w.reshape(8, 64, 4, 128).transpose(0, 2, 1, 3),
            fc1_w.reshape(8, 64, 4, 4, 128).transpose(0, 2, 3, 1, 4).reshape(8, 4, 256, 128),
            fc2_w.reshape(8, 256, 4, 128).transpose(0, 2, 1, 3),
            jnp.concatenate((short(proj_down), short(proj_up)), axis=-1),
            jnp.concatenate((short(fc1_down), short(fc2_up)), axis=-1),
            long(fc1_up),
            long(fc2_down),
        ),
        axis=2,
    )


def per_device(
    tokens, cotangent, adapter_ids, ln1_gain, qkv_weight, qkv_bias, proj_weight, proj_bias, ln2_gain,
    fc1_weight, fc1_bias, fc2_weight, fc2_bias, bias_table, qkv_down, qkv_up, proj_down, proj_up,
    fc1_down, fc1_up, fc2_down, fc2_up, *, clip_size, win_size,
):
    clips, local, rows, feats = tokens.shape
    items = clips * local
    heads = bias_table.shape[0]
    vecs = (ln1_gain, qkv_bias, proj_bias, ln2_gain, fc1_bias, fc2_bias)
    item_ids = jnp.repeat(adapter_ids, local)
    masks = window_masks(lax.axis_index("win"), local)
    flat = (items, rows, feats)
    downs = [a.transpose(0, 2, 1) for a in (qkv_down, proj_down, fc1_down, fc2_down)]
    own_kernels = (clip_size, win_size, clips, local) == (8, 4, 2, 2)
    if own_kernels:
        maps = [a.reshape(32, -1) for a in (downs[1], proj_up, downs[2], fc1_up, downs[3], fc2_up)]
        later = jnp.concatenate(
            (
                proj_weight,
                fc1_weight.reshape(64, 4, 128).transpose(1, 0, 2).reshape(256, 128),
                fc2_weight,
                jnp.concatenate((maps[0], maps[1]), axis=1),
                jnp.concatenate((maps[2], maps[5]), axis=1),
                maps[3][:, :128],
                maps[3][:, 128:],
                maps[4][:, :128],
                maps[4][:, 128:],
            ),
            axis=0,
        )
        staged = lax.all_gather(later, ("clip", "win")).reshape(8, 4, 768, 128)
        early = jnp.concatenate((downs[0].reshape(32, 64), qkv_up.reshape(32, 192)), axis=1)
        unit = jnp.concatenate(
            (qkv_weight, jnp.concatenate((early[:, :128], early[:, 128:]), axis=0)), axis=1
        )
        pairs = bias_table.reshape(heads, 15, 169).transpose(1, 0, 2).reshape(15 * heads, 169)
        pairs = jnp.pad(pairs, ((0, 0), (0, 7)))
        x, qkv_w, down, up, *vectors, ids, table = spread(
            tokens.reshape(flat), unit, pack_vectors(vecs, adapter_ids), pairs, clip_size
        )
        later_dy, table = lax.optimization_barrier((cotangent, table))
        dy = pieces_of(later_dy.reshape(flat))
        qkv_parts = (qkv_w, down, up)
    else:
        grid2, by_down, by_up = ("clip", "win"), ("win", None, "clip"), ("win", None, "clip")
        qkv_parts = (gather(qkv_weight, grid2), gather(downs[0], by_down), gather(qkv_up, by_up))
        maps = (downs[1], proj_up, downs[2], fc1_up, downs[3], fc2_up)
        staged = stage_whole(
            *[gather(a, grid2) for a in (proj_weight, fc1_weight, fc2_weight)],
            [gather(a, by_up) for a in maps],
        )
        vectors = [gather(v, ("clip",)).reshape(1, -1).astype(F32) for v in vecs]
        table = bias_by_pair(bias_table)
        x = exchange(tokens, win_size).reshape(flat)
        dy = (exchange(cotangent, win_size).reshape(flat),)
    act, dx, grad_qkv, grad_dense = compute(
        x, dy, item_ids, vectors, qkv_parts, staged, masks, table, local
    )
    if own_kernels:
        act_out, dx_out, qd, qu, pd, pu, f1d, f1u, f2d, f2u = finish(
            act, pieces_of(act)[1:], dx, grad_qkv, grad_dense, ids, clip_size
        )
        turned = [a.transpose(0, 2, 1) for a in (qd, pd, f1d, f2d)]
        return (
            act_out.reshape(tokens.shape), dx_out.reshape(tokens.shape),
            turned[0], qu, turned[1], pu, turned[2], f1u, turned[3], f2u,
        )
    activations = exchange(act.reshape(tokens.shape), win_size)
    input_grad = exchange(dx.reshape(tokens.shape), win_size)
    adapter_count = win_size * qkv_down.shape[0]
    hot = (adapter_ids[:, None] == jnp.arange(adapter_count)[None]).astype(F32)
    hidden = fc1_weight.shape[1] * win_size
    spans = (feats, 3 * feats, feats, feats, feats, hidden, hidden, feats)
    grads = jnp.concatenate((grad_qkv, grad_dense), axis=-1)
    rank = grads.shape[1]
    parts, at = [], 0
    for span in spans:
        parts.append(
            grads[..., at : at + span].reshape(clips, rank, clip_size, span // clip_size)
        )
        at += span
    mine = jnp.concatenate(parts, axis=-1)
    grown = jnp.sum(hot[:, :, None, None, None] * mine[:, None], axis=0)
    grown = grown.transpose(2, 0, 1, 3).astype(BF)
    total = lax.psum_scatter(grown, "clip", scatter_dimension=0, tiled=True)[0]
    total = lax.psum_scatter(total, "win", scatter_dimension=0, tiled=True).astype(F32)
    outs, at = [], 0
    for n, span in enumerate(spans):
        width = span // clip_size
        part = total[..., at : at + width]
        at += width
        outs.append(part.transpose(0, 2, 1) if n % 2 == 0 else part)
    return (activations, input_grad, *outs)


def solution(mesh):
    split = P("clip", "win", None, None)
    grid2 = P("clip", "win")
    down = P("win", "clip", None)
    up = P("win", None, "clip")
    one = P("clip")
    return jax.shard_map(
        functools.partial(
            per_device, clip_size=mesh.shape["clip"], win_size=mesh.shape["win"]
        ),
        mesh=mesh,
        in_specs=(
            split, split, one, one, grid2, one, grid2, one, one, grid2, one, grid2, one, P(),
            down, up, down, up, down, up, down, up,
        ),
        out_specs=(split, split, down, up, down, up, down, up, down, up),
        check_vma=False,
    )
```

```python
import functools
import jax
import jax.numpy as jnp
from jax import lax
from jax.experimental import pallas as pl
from jax.experimental.pallas import tpu as pltpu
from jax.sharding import PartitionSpec as P

BF = jnp.bfloat16
F32 = jnp.float32
NN = (((1,), (0,)), ((), ()))
NT = (((1,), (1,)), ((), ()))
TN = (((0,), (0,)), ((), ()))
LOG2E = 1.4426950408889634
LN2 = 0.6931471805599453
FAR = 1e9
VMEM_LIMIT = 60 * 2**20
TOK = 392
TOP = 208


def dot(left, right, dims):
    return lax.dot_general(left, right, dims, preferred_element_type=F32)


def lane_ids(shape):
    return lax.broadcasted_iota(jnp.int32, shape, len(shape) - 1)


def norm_stats(values):
    average = jnp.mean(values, axis=-1, keepdims=True)
    centred = values - average
    variance = jnp.mean(centred * centred, axis=-1, keepdims=True)
    inverse = lax.rsqrt(variance + 1e-05)
    return centred * inverse, inverse


def norm_back(gradient, gain, normed, inverse):
    scaled = gradient * gain
    centre = jnp.mean(scaled, axis=-1, keepdims=True)
    slope = jnp.mean(scaled * normed, axis=-1, keepdims=True)
    return inverse * (scaled - centre - normed * slope)


def add_rows(ref, at, value, first):
    @pl.when(first)
    def _():
        ref[0, :, at] = value

    @pl.when(jnp.logical_not(first))
    def _():
        ref[0, :, at] += value


MESH = pl.DeviceIdType.MESH


def enter(peers):
    barrier = pltpu.get_barrier_semaphore()
    for peer in peers:
        pl.semaphore_signal(barrier, inc=1, device_id=peer, device_id_type=MESH)
    pl.semaphore_wait(barrier, len(peers))


def remote(src, dst, send_sem, recv_sem, peer):
    return pltpu.make_async_remote_copy(
        src_ref=src,
        dst_ref=dst,
        send_sem=send_sem,
        recv_sem=recv_sem,
        device_id=peer,
        device_id_type=MESH,
    )


class Sender:
    def __init__(self, send_sem, recv_sem):
        self.send_sem, self.recv_sem, self.count = send_sem, recv_sem, 0

    def copy(self, src, dst, peer):
        n = self.count
        self.count += 1
        made = remote(src, dst, self.send_sem.at[n], self.recv_sem.at[n], peer)
        made.start()
        return made


def row_masks(rows, columns):
    row = lax.broadcasted_iota(jnp.int32, (rows, columns), 0)
    return row < TOK // 2, row % 49 < 21, row % 7 < 3


def with_top(part, top, early):
    return jnp.concatenate([jnp.where(early[:TOP], top, part[:TOP]), part[TOP:]], axis=0)


class Place:
    def __init__(self, clip_size):
        self.c, self.w = lax.axis_index("clip"), lax.axis_index("win")
        self.z, self.y = self.c // 2, self.c % 2
        self.x, self.k = self.w // 2, self.w % 2
        self.zs = clip_size // 2
        self.sibling = (self.c, self.x * 2 + 1 - self.k)
        self.across = (self.c, (1 - self.x) * 2 + self.k)

    def clip_at(self, z_step, other_y):
        return (self.z + z_step + self.zs) % self.zs * 2 + (1 - self.y if other_y else self.y)

    def along_z(self, step):
        return (self.clip_at(step, False), self.w)

    def along_y(self):
        return (self.clip_at(0, True), self.w)


class Gather:
    COPIES = 29

    def __init__(self, place, unit, units, send_sem, recv_sem):
        self.place, self.unit, self.units = place, unit, units
        self.send_sem, self.recv_sem = send_sem, recv_sem
        self.hops = range(place.zs - 1)

    def make(self, kind, t=0):
        p, units = self.place, self.units
        kinds = ("up", "down", "y_up", "y_down", "s_up", "s_down", "sy_up", "sy_down")
        single = ("across", "own", "theirs", "y", "s_y")
        n = single.index(kind) if kind in single else 5 + 8 * t + kinds.index(kind)
        sems = self.send_sem.at[n], self.recv_sem.at[n]
        mine = units.at[p.k, p.c, p.x]
        if kind == "across":
            return remote(self.unit, mine, *sems, p.across)
        if kind == "own":
            return remote(self.unit, mine, *sems, p.sibling)
        if kind == "theirs":
            part = units.at[p.k, p.c, 1 - p.x]
        elif kind == "y":
            part = units.at[p.k, p.c]
        elif kind == "s_y":
            part = units.at[p.k, p.z * 2 + 1 - p.y]
        else:
            sign = -1 if kind.endswith("up") else 1
            far = p.z + sign * (t if kind in ("up", "down") else t + 1)
            part = units.at[p.k, far * 2 + (1 - p.y if kind.startswith("sy") else p.y)]
        if kind in ("up", "down"):
            peer = (p.c - 2 * sign, p.w)
        else:
            peer = p.along_y() if kind.startswith("y") else p.sibling
        return remote(part, part, *sems, peer)

    def when(self, kind, t, sending, act):
        p, last = self.place, self.place.zs - 1
        if kind.endswith("up"):
            holds = (p.z >= t) & (p.z < last) if sending and kind == "up" else p.z >= t + 1
        elif kind.endswith("down"):
            holds = (p.z <= last - t) & (p.z > 0) if sending and kind == "down" else p.z <= last - 1 - t
        else:
            act()
            return
        pl.when(holds)(act)

    def start(self, kind, t=0):
        self.when(kind, t, True, lambda: self.make(kind, t).start())

    def wait_recv(self, kind, t=0):
        self.when(kind, t, False, lambda: self.make(kind, t).wait_recv())

    def wait_send(self, kind, t=0):
        self.when(kind, t, True, lambda: self.make(kind, t).wait_send())

    def begin(self):
        self.start("across")
        self.start("own")

    def second(self):
        self.wait_recv("across")
        for kind in ("up", "down", "y", "theirs"):
            self.start(kind)

    def from_z(self, t):
        for way in ("up", "down"):
            self.wait_recv(way, t)
            if t + 1 in self.hops:
                self.start(way, t + 1)
            self.start("y_" + way, t)
            self.start("s_" + way, t)

    def from_y(self, t):
        if t < 0:
            self.wait_recv("y")
            self.start("s_y")
        else:
            for way in ("up", "down"):
                self.wait_recv("y_" + way, t)
                self.start("sy_" + way, t)

    def finish(self):
        for kind in ("own", "theirs", "s_y"):
            self.wait_recv(kind)
        for t in self.hops:
            for kind in ("s_up", "s_down", "sy_up", "sy_down"):
                self.wait_recv(kind, t)
        for kind in ("across", "own", "theirs", "y", "s_y"):
            self.wait_send(kind)
        for t in self.hops:
            for kind in ("up", "down", "y_up", "y_down", "s_up", "s_down", "sy_up", "sy_down"):
                self.wait_send(kind, t)


def attend_kernel(
    x_ref,
    gain_ref,
    weight_ref,
    bias_ref,
    ids_ref,
    down_ref,
    up_ref,
    table_ref,
    *refs,
    scale,
    per_group,
    width,
    per_clip,
    remote_size,
):
    if remote_size:
        (dy_ref, proj_ref, fc1_ref, fc2_ref, pd_ref, pu_ref, f1d_ref, f1u_ref, f2d_ref, f2u_ref, *refs) = refs
    probs_ref, out_ref, qkv_ref, reduced_ref, down_own, up_own, *refs = refs
    if remote_size:
        dy_out_ref, units_ref, *refs = refs
    keys, queries, values_t, out_t, scores, table, table_sem, query_mask, *refs = refs
    group = pl.program_id(1)
    groups = pl.num_programs(1)
    item = pl.program_id(0)
    step = item * groups + group
    feats = x_ref.shape[-1]
    rows = x_ref.shape[1]
    starting = item == 0

    def table_copy(g):
        at = pl.ds(g * per_group, per_group)
        return pltpu.make_async_copy(table_ref.at[at], table.at[at], table_sem.at[g])

    @pl.when(step == 0)
    def _():
        for g in range(table.shape[0] // per_group):
            table_copy(g).start()

    if remote_size:
        unit, beside, mixed, tops, send_sem, recv_sem, dy_send, dy_recv, own_sem = refs
        place = Place(remote_size)
        gather_units = Gather(place, unit, units_ref, send_sem, recv_sem)
        items = dy_ref.shape[0]

        def dy_copy(kind, i):
            n = kind * items + i
            sems = dy_send.at[n], dy_recv.at[n]
            if kind == 0:
                return remote(dy_ref.at[i], beside.at[i], *sems, place.sibling)
            return remote(mixed.at[i, pl.ds(0, TOP)], tops.at[i], *sems, place.across)

        @pl.when(step == 0)
        def _():
            unit[0:64] = proj_ref[...]
            for t in range(4):
                unit[64 + 64 * t : 128 + 64 * t] = fc1_ref[:, 128 * t : 128 * t + 128]
            unit[320:576] = fc2_ref[...]
            for a in range(2):
                at = 576 + 16 * a
                unit[at : at + 16, 0:64] = pd_ref[a]
                unit[at : at + 16, 64:128] = pu_ref[a]
                unit[at + 32 : at + 48, 0:64] = f1d_ref[a]
                unit[at + 32 : at + 48, 64:128] = f2u_ref[a]
                for half in range(2):
                    lanes = slice(128 * half, 128 * half + 128)
                    unit[at + 64 + 32 * half : at + 80 + 32 * half] = f1u_ref[a, :, lanes]
                    unit[at + 128 + 32 * half : at + 144 + 32 * half] = f2d_ref[a, :, lanes]
            own = pltpu.make_async_copy(unit, units_ref.at[place.k, place.c, place.x], own_sem)
            own.start()
            enter(
                [place.sibling, place.across, place.along_y()]
                + [place.along_z(j) for j in range(1, place.zs)]
            )
            gather_units.begin()
            for i in range(items):
                dy_copy(0, i).start()
            own.wait()

        @pl.when(step == 1)
        def _():
            gather_units.second()

        @pl.when(step == 2)
        def _():
            low_h = row_masks(rows, feats)[1]
            for i in range(items):
                dy_copy(0, i).wait_recv()
                mixed[i] = jnp.where(low_h, beside[i], dy_ref[i])
                dy_copy(1, i).start()

        for t, at in enumerate((4, 8, 11)):

            @pl.when(step == at)
            def _():
                gather_units.from_z(t)

        for t, at in ((-1, 5), (0, 9), (1, 12), (2, 15)):

            @pl.when(step == at)
            def _():
                gather_units.from_y(t)

        @pl.when(step == 4 * items - 1)
        def _():
            early, _, low_w = row_masks(rows, feats)
            for i in range(0, items, 2):
                both = []
                for e in range(2):
                    dy_copy(1, i + e).wait_recv()
                    both.append(with_top(mixed[i + e], tops[i + e], early))
                for e in range(2):
                    dy_out_ref[i + e] = jnp.where(low_w, both[1 - e], both[e])
            gather_units.finish()
            for i in range(items):
                dy_copy(0, i).wait_send()
                dy_copy(1, i).wait_send()

    @pl.when((group == 0) & (item % per_clip == 0))
    def _():
        clip = item // per_clip
        for ref, target in ((down_ref, down_own), (up_ref, up_own)):
            total = jnp.zeros(ref.shape[1:], F32)
            for a in range(ref.shape[0]):
                total = total + jnp.where(
                    ids_ref[pl.ds(clip, 1), 0:1] == float(a), ref[a].astype(F32), 0.0
                )
            target[0] = total.astype(BF)

    @pl.when(group == 0)
    def _():
        number = lax.axis_index("win") * per_clip + item % per_clip
        early, low_h, low_w = row_masks(rows, 128)
        label = (
            jnp.where(early, number // 4 % 2 * 4, 0)
            + jnp.where(low_h, number // 2 % 2 * 2, 0)
            + jnp.where(low_w, number % 2, 0)
        )
        lane = lane_ids((rows, 128))
        same = label == lane
        key_mask = jnp.where(same, 1.0, 0.0).astype(BF)
        query_mask[...] = jnp.where(same | (lane >= 8), 0.0, -FAR).astype(BF)
        normed, _ = norm_stats(x_ref[0].astype(F32))
        low = (normed * gain_ref[...]).astype(BF)
        reduced = dot(down_own[0], low, NT).astype(BF)
        reduced_ref[0] = reduced

        def columns(part):
            at = pl.ds(part * feats, feats)
            return (
                dot(low, weight_ref[:, at], NN)
                + bias_ref[:, at]
                + dot(reduced, up_own[0, :, at], TN)
            )

        query = (columns(0) * (scale * LOG2E)).astype(BF)
        queries[...] = query
        qkv_ref[0, :, :feats] = query
        key = columns(1).astype(BF)
        qkv_ref[0, :, feats : 2 * feats] = key
        for g in range(feats // 128):
            keys[:, 256 * g : 256 * g + 128] = key[:, 128 * g : 128 * g + 128]
            keys[:, 256 * g + 128 : 256 * g + 256] = key_mask
        value = columns(2).astype(BF)
        qkv_ref[0, :, 2 * feats :] = value
        values_t[...] = value.T

    @pl.when(starting)
    def _():
        table_copy(group).wait()

    keys_now = keys[:, pl.ds(pl.multiple_of(group * 256, 256), 256)]
    query_now = queries[:, pl.ds(pl.multiple_of(group * 128, 128), 128)]
    head_of_lane = lane_ids(query_now.shape) // width

    def raw(h):
        own = jnp.where(head_of_lane == h, query_now, jnp.zeros_like(query_now))
        own = jnp.concatenate([own, query_mask[...]], axis=1)
        return dot(keys_now, own, NT) + table[group * per_group + h]

    def finish(h):
        score = scores[h % 2]
        largest = jnp.max(score, axis=0, keepdims=True)
        probs = jnp.exp2(score - largest)
        total = jnp.sum(probs, axis=0, keepdims=True)
        probs = (probs * (1.0 / total)).astype(BF)
        probs_ref[0, h] = probs
        at = pl.ds(pl.multiple_of((group * per_group + h) * width, width), width)
        out_t[at, :] = dot(values_t[at, :], probs, NN).astype(BF)

    scores[0] = raw(0)
    for h in range(per_group):
        if h + 1 < per_group:
            scores[(h + 1) % 2] = raw(h + 1)
        finish(h)

    @pl.when(group == groups - 1)
    def _():
        out_ref[0] = out_t[...].T


def dense_kernel(
    ids_ref,
    x_ref,
    attn_ref,
    gain_ref,
    proj_bias_ref,
    fc1_bias_ref,
    fc2_bias_ref,
    dy_ref,
    staged_ref,
    *refs,
    per_clip,
    chunk,
):
    tiles, refs = refs[:6], refs[6:]
    act_ref, dx1_ref, dattn_ref, grad_ref, *refs = refs
    proj_ref, fc1_ref, fc2_ref, proj_down, proj_up, fc1_down, fc1_up, fc2_down, fc2_up, *refs = refs
    pres, acts, dpres, sem = refs
    starting = pl.program_id(0) == 0
    count = x_ref.shape[1]
    feats = x_ref.shape[-1]
    hidden = fc1_ref.shape[-1]

    def moves(first=0, last=24):
        found = [(0, 64, proj_ref, 128 * n, n) for n in range(4)]
        found += [(64 + 64 * t, 64, fc1_ref, 512 * n + 128 * t, n) for n in range(4) for t in range(4)]
        found += [(320, 256, fc2_ref, 128 * n, n) for n in range(4)]
        return [
            pltpu.make_async_copy(
                staged_ref.at[n % 2, :, n // 2, pl.ds(start, size), :],
                target.at[:, :, pl.ds(lane, 128)],
                sem.at[at],
            )
            for at, (start, size, target, lane, n) in enumerate(found)
            if first <= at < last
        ]

    def arrive(first, last):
        @pl.when(starting)
        def _():
            for copy in moves(first, last):
                copy.wait()

    @pl.when(starting)
    def _():
        for copy in moves():
            copy.start()

    for n in range(8):
        short = slice(64 * n, 64 * n + 64)
        proj_down[:, short] = tiles[0][0, n, 0, :, 0:64]
        proj_up[:, short] = tiles[0][0, n, 0, :, 64:128]
        fc1_down[:, short] = tiles[1][0, n, 0, :, 0:64]
        fc2_up[:, short] = tiles[1][0, n, 0, :, 64:128]
        for half in range(2):
            long = slice(256 * n + 128 * half, 256 * n + 128 * half + 128)
            fc1_up[:, long] = tiles[2 + half][0, n, 0]
            fc2_down[:, long] = tiles[4 + half][0, n, 0]

    def join(parts):
        return jnp.concatenate(parts, axis=0) if per_clip > 1 else parts[0]

    dy = join([dy_ref[e] for e in range(per_clip)])
    attn = join([attn_ref[e] for e in range(per_clip)])
    reduced_proj = dot(proj_down[...], attn, NT).astype(BF)
    arrive(0, 4)
    proj_w = proj_ref[...].reshape(feats, feats)
    middle = (
        join([x_ref[e].astype(F32) for e in range(per_clip)])
        + dot(attn, proj_w, NN)
        + proj_bias_ref[...]
        + dot(reduced_proj, proj_up[...], TN)
    )
    normed, inverse = norm_stats(middle)
    low = (normed * gain_ref[...]).astype(BF)
    reduced_fc1 = dot(fc1_down[...], low, NT).astype(BF)
    grad_reduced_fc2 = dot(fc2_up[...], dy, NT).astype(BF)
    per_chunk = chunk // fc2_ref.shape[1]
    steps = hidden // chunk

    def pre_of(j):
        at = slice(j * chunk, (j + 1) * chunk)
        pres[j % 2] = (
            dot(low, fc1_ref[:, :, at].reshape(feats, chunk), NN)
            + fc1_bias_ref[:, at]
            + dot(reduced_fc1, fc1_up[:, at], TN)
        )

    arrive(4, 20)
    pre_of(0)
    arrive(20, 24)
    for j in range(steps):
        at = slice(j * chunk, (j + 1) * chunk)
        if j + 1 < steps:
            pre_of(j + 1)
        fc2_w = fc2_ref[j * per_chunk : (j + 1) * per_chunk].reshape(chunk, feats)
        dact = dot(dy, fc2_w, NT) + dot(grad_reduced_fc2, fc2_down[:, at], TN)
        pre = pres[j % 2]
        bell = jnp.exp2((pre * pre) * (-0.5 * LOG2E))
        t = 1.0 / (1.0 + jnp.abs(pre) * (0.3275911 * 0.7071067811865476))
        poly = (
            (((0.5 * 1.061405429) * t - 0.5 * 1.453152027) * t + 0.5 * 1.421413741) * t
            - 0.5 * 0.284496736
        ) * t + 0.5 * 0.254829592
        tail = poly * t * bell
        below = jnp.where(pre >= 0.0, 1.0 - tail, tail)
        acts[:, at] = (pre * below).astype(BF)
        dpres[:, at] = (dact * (below + pre * bell * 0.3989422804014327)).astype(BF)
    act = acts[...]
    dpre = dpres[...]
    fc1_up_at = 3 * feats
    fc2_down_at = fc1_up_at + hidden
    fc2_up_at = fc2_down_at + hidden
    fc2_w = fc2_ref[...].reshape(hidden, feats)
    grad_reduced_fc1 = dot(fc1_up[...], dpre, NT).astype(BF)
    dlow = dot(dpre, fc1_ref[...].reshape(feats, hidden), NT) + dot(grad_reduced_fc1, fc1_down[...], TN)
    dx1 = dy.astype(F32) + norm_back(dlow, gain_ref[...], normed, inverse)
    branch = dx1.astype(BF)
    reduced_fc2 = dot(fc2_down[...], act, NT).astype(BF)
    total = (
        middle + fc2_bias_ref[...] + dot(act, fc2_w, NN) + dot(reduced_fc2, fc2_up[...], TN)
    ).astype(BF)
    grad_reduced_proj = dot(proj_up[...], branch, NT).astype(BF)
    dattn = (
        dot(branch, proj_w, NT) + dot(grad_reduced_proj, proj_down[...], TN)
    ).astype(BF)
    for e in range(per_clip):
        rows = slice(e * count, (e + 1) * count)
        act_ref[e] = total[rows]
        dx1_ref[e] = dx1[rows]
        dattn_ref[e] = dattn[rows]
    grad_ref[0, :, :feats] = dot(grad_reduced_proj, attn, NN)
    grad_ref[0, :, feats : 2 * feats] = dot(reduced_proj, branch, NN)
    grad_ref[0, :, 2 * feats : fc1_up_at] = dot(grad_reduced_fc1, low, NN)
    grad_ref[0, :, fc1_up_at:fc2_down_at] = dot(reduced_fc1, dpre, NN)
    grad_ref[0, :, fc2_down_at:fc2_up_at] = dot(grad_reduced_fc2, act, NN)
    grad_ref[0, :, fc2_up_at:] = dot(reduced_fc2, dy, NN)


def attend_back_kernel(
    x_ref,
    gain_ref,
    weight_ref,
    down_ref,
    up_ref,
    probs_ref,
    attn_ref,
    qkv_ref,
    reduced_ref,
    dattn_ref,
    dx1_ref,
    dx_ref,
    grad_ref,
    values,
    keys_t,
    inner,
    dqkv,
    dquery_t,
    *,
    scale,
    per_group,
    width,
    per_clip,
):
    group = pl.program_id(1)
    groups = pl.num_programs(1)
    feats = x_ref.shape[-1]
    rows = x_ref.shape[1]

    @pl.when(group == 0)
    def _():
        keys_t[...] = qkv_ref[0, :, feats : 2 * feats].T
        lane = lane_ids((rows, 128))
        ones = jnp.where(lane % width < 2, 1.0, 0.0).astype(BF)
        source = lax.broadcasted_iota(jnp.int32, (128, 128), 0)
        target = lane_ids((128, 128))
        pick = jnp.where(
            (source // width == target // width) & (target % width < 2), 1.0, 0.0
        ).astype(BF)
        pick = jnp.concatenate([pick, pick], axis=0)
        for g in range(feats // 128):
            at = slice(128 * g, 128 * g + 128)
            values[:, 256 * g : 256 * g + 128] = qkv_ref[0, :, 2 * feats + 128 * g : 2 * feats + 128 * g + 128]
            values[:, 256 * g + 128 : 256 * g + 256] = ones
            product = dattn_ref[0, :, at].astype(F32) * attn_ref[0, :, at].astype(F32)
            high = product.astype(BF)
            rest = (product - high.astype(F32)).astype(BF)
            sums = dot(jnp.concatenate([high, rest], axis=1), pick, NN)
            coarse = sums.astype(BF)
            fine = (sums - coarse.astype(F32)).astype(BF)
            inner[:, at] = -jnp.where(lane % width == 0, coarse, fine)

    blocks = pl.ds(pl.multiple_of(group * 128, 128), 128)
    values_now = values[:, pl.ds(pl.multiple_of(group * 256, 256), 256)]
    dattn_now = dattn_ref[0, :, blocks]
    inner_now = inner[:, blocks]
    query_now = qkv_ref[0, :, blocks]
    head_of_lane = lane_ids((rows, 128)) // width
    zero = jnp.zeros((rows, 128), BF)
    dvalue = None
    dkey = None
    for h in range(per_group):
        mine = head_of_lane == h
        dattn_own = jnp.where(mine, dattn_now, zero)
        query_own = jnp.where(mine, query_now, zero)
        right = jnp.concatenate([dattn_own, jnp.where(mine, inner_now, zero)], axis=1)
        probs = probs_ref[0, h]
        dscore = probs * dot(values_now, right, NT).astype(BF)
        partial = dot(probs, dattn_own, NN)
        dvalue = partial if dvalue is None else dvalue + partial
        partial = dot(dscore, query_own, NN)
        dkey = partial if dkey is None else dkey + partial
        at = pl.ds(pl.multiple_of((group * per_group + h) * width, width), width)
        dquery_t[at, :] = (dot(keys_t[at, :], dscore, NN) * scale).astype(BF)
    dqkv[:, pl.ds(pl.multiple_of(2 * feats + group * 128, 128), 128)] = dvalue.astype(BF)
    dqkv[:, pl.ds(pl.multiple_of(feats + group * 128, 128), 128)] = (dkey * LN2).astype(BF)

    @pl.when(group == groups - 1)
    def _():
        first = pl.program_id(0) % per_clip == 0
        dqkv[:, :feats] = dquery_t[...].T
        dall = dqkv[...]
        normed, inverse = norm_stats(x_ref[0].astype(F32))
        low = (normed * gain_ref[...]).astype(BF)
        grad_reduced = dot(up_ref[0], dall, NT).astype(BF)
        add_rows(grad_ref, slice(feats, 4 * feats), dot(reduced_ref[0], dall, NN), first)
        add_rows(grad_ref, slice(0, feats), dot(grad_reduced, low, NN), first)
        dlow = (dot(dall, weight_ref[...], NT) + dot(grad_reduced, down_ref[0], TN)).astype(BF)
        dx_ref[0] = (
            dx1_ref[0] + norm_back(dlow.astype(F32), gain_ref[...], normed, inverse)
        ).astype(BF)


def whole(shape):
    return pl.BlockSpec(shape, lambda *at: (0,) * len(shape), pipeline_mode=pl.Buffered(1))


def compute(x, dy, adapter_ids, vectors, qkv_parts, later, table, per_clip, remote_size):
    items, rows, feats = x.shape
    heads = table.shape[0]
    width = feats // heads
    per_group = 128 // width
    groups = heads // per_group
    scale = width**-0.5
    gain1, qkv_bias, proj_bias, gain2, fc1_bias, fc2_bias = vectors
    qkv_w, qkv_down, qkv_up = qkv_parts
    rank = qkv_down.shape[1]
    hidden = fc1_bias.shape[1]
    clips = items // per_clip

    def item(shape):
        return pl.BlockSpec((1, *shape), lambda i, *rest: (i,) + (0,) * len(shape))

    clip_ids = jnp.broadcast_to(adapter_ids.astype(F32)[:, None], (clips, 128))
    item_ids = adapter_ids
    any_space = pl.BlockSpec(memory_space=pl.ANY)

    def of_clip(shape):
        return pl.BlockSpec((1, *shape), lambda i, *rest: (i // per_clip, 0, 0))

    if remote_size:
        unit_shape = (768, 128)
        sent = (dy, *later)
        sent_out = [
            jax.ShapeDtypeStruct(dy.shape, BF),
            jax.ShapeDtypeStruct((2, remote_size, 2, *unit_shape), BF),
        ]
        sent_scratch = [
            pltpu.VMEM(unit_shape, BF),
            pltpu.VMEM(dy.shape, BF),
            pltpu.VMEM(dy.shape, BF),
            pltpu.VMEM((items, TOP, feats), BF),
            pltpu.SemaphoreType.DMA((Gather.COPIES,)),
            pltpu.SemaphoreType.DMA((Gather.COPIES,)),
            pltpu.SemaphoreType.DMA((2 * items,)),
            pltpu.SemaphoreType.DMA((2 * items,)),
            pltpu.SemaphoreType.DMA,
        ]
    else:
        sent, sent_out, sent_scratch = (), [], []
    probs, attn, qkv, reduced, down_own, up_own, *arrived = pl.pallas_call(
        functools.partial(
            attend_kernel,
            scale=scale,
            per_group=per_group,
            width=width,
            per_clip=per_clip,
            remote_size=remote_size,
        ),
        grid=(items, groups),
        in_specs=[
            item((rows, feats)),
            whole(gain1.shape),
            whole(qkv_w.shape),
            whole(qkv_bias.shape),
            whole(clip_ids.shape),
            whole(qkv_down.shape),
            whole(qkv_up.shape),
            any_space,
            *[whole(a.shape) for a in sent],
        ],
        out_specs=[
            pl.BlockSpec((1, per_group, rows, rows), lambda i, g: (i, g, 0, 0)),
            item((rows, feats)),
            item((rows, 3 * feats)),
            item((rank, rows)),
            of_clip((rank, feats)),
            of_clip((rank, 3 * feats)),
            *([whole(dy.shape), any_space] if remote_size else []),
        ],
        scratch_shapes=[
            pltpu.VMEM((rows, 2 * feats), BF),
            pltpu.VMEM((rows, feats), BF),
            pltpu.VMEM((feats, rows), BF),
            pltpu.VMEM((feats, rows), BF),
            pltpu.VMEM((2, rows, rows), F32),
            pltpu.VMEM(table.shape, F32),
            pltpu.SemaphoreType.DMA((groups,)),
            pltpu.VMEM((rows, 128), BF),
            *sent_scratch,
        ],
        out_shape=[
            jax.ShapeDtypeStruct((items, heads, rows, rows), BF),
            jax.ShapeDtypeStruct((items, rows, feats), BF),
            jax.ShapeDtypeStruct((items, rows, 3 * feats), BF),
            jax.ShapeDtypeStruct((items, rank, rows), BF),
            jax.ShapeDtypeStruct((clips, rank, feats), BF),
            jax.ShapeDtypeStruct((clips, rank, 3 * feats), BF),
            *sent_out,
        ],
        compiler_params=pltpu.CompilerParams(
            vmem_limit_bytes=VMEM_LIMIT,
            dimension_semantics=("arbitrary", "arbitrary"),
            **({"collective_id": 2, "has_side_effects": True} if remote_size else {}),
        ),
        cost_estimate=pl.CostEstimate(flops=4 * 10**10, bytes_accessed=10**7, transcendentals=0),
        name="attend",
    )(x, gain1, qkv_w, qkv_bias, clip_ids, qkv_down, qkv_up, table, *sent)
    if remote_size:
        dy, staged = arrived
    else:
        (staged,) = later

    span = 4 * feats + 2 * hidden
    def tile(n):
        def index(c, ids):
            return ids[c] // 2 % 2, 0, ids[c] // 4, 36 + 2 * n + ids[c] % 2, 0

        return pl.BlockSpec((1, 8, 1, rank, 128), index)

    def clip(array_shape):
        return pl.BlockSpec((per_clip, *array_shape[1:]), lambda c, ids: (c, 0, 0))

    chunk = 512
    act, dx1, dattn, grad_dense = pl.pallas_call(
        functools.partial(dense_kernel, per_clip=per_clip, chunk=chunk),
        grid_spec=pltpu.PrefetchScalarGridSpec(
            num_scalar_prefetch=1,
            grid=(clips,),
            in_specs=[
                clip(x.shape),
                clip(x.shape),
                whole(gain2.shape),
                whole(proj_bias.shape),
                whole(fc1_bias.shape),
                whole(fc2_bias.shape),
                clip(x.shape),
                any_space,
                *[tile(n) for n in range(6)],
            ],
            out_specs=[
                clip(x.shape),
                clip(x.shape),
                clip(x.shape),
                pl.BlockSpec((1, rank, span), lambda c, ids: (c, 0, 0)),
            ],
            scratch_shapes=[
                pltpu.VMEM((8, feats // 8, feats), BF),
                pltpu.VMEM((8, feats // 8, hidden), BF),
                pltpu.VMEM((8, hidden // 8, feats), BF),
                *[pltpu.VMEM((rank, n), BF) for n in (feats, feats, feats, hidden, hidden, feats)],
                pltpu.VMEM((2, per_clip * rows, chunk), F32),
                pltpu.VMEM((per_clip * rows, hidden), BF),
                pltpu.VMEM((per_clip * rows, hidden), BF),
                pltpu.SemaphoreType.DMA((24,)),
            ],
        ),
        out_shape=[
            jax.ShapeDtypeStruct((items, rows, feats), BF),
            jax.ShapeDtypeStruct((items, rows, feats), F32),
            jax.ShapeDtypeStruct((items, rows, feats), BF),
            jax.ShapeDtypeStruct((clips, rank, span), F32),
        ],
        compiler_params=pltpu.CompilerParams(
            vmem_limit_bytes=VMEM_LIMIT, dimension_semantics=("arbitrary",)
        ),
        cost_estimate=pl.CostEstimate(flops=5 * 10**10, bytes_accessed=10**7, transcendentals=0),
        name="dense",
    )(
        item_ids, x, attn, gain2, proj_bias, fc1_bias, fc2_bias, dy, staged, *([staged] * 6)
    )

    dx, grad_qkv = pl.pallas_call(
        functools.partial(
            attend_back_kernel, scale=scale, per_group=per_group, width=width, per_clip=per_clip
        ),
        grid=(items, groups),
        in_specs=[
            item((rows, feats)),
            whole(gain1.shape),
            whole(qkv_w.shape),
            of_clip((rank, feats)),
            of_clip((rank, 3 * feats)),
            pl.BlockSpec((1, per_group, rows, rows), lambda i, g: (i, g, 0, 0)),
            item((rows, feats)),
            item((rows, 3 * feats)),
            item((rank, rows)),
            item((rows, feats)),
            item((rows, feats)),
        ],
        out_specs=[
            item((rows, feats)),
            pl.BlockSpec((1, rank, 4 * feats), lambda i, g: (i // per_clip, 0, 0)),
        ],
        scratch_shapes=[
            pltpu.VMEM((rows, 2 * feats), BF),
            pltpu.VMEM((feats, rows), BF),
            pltpu.VMEM((rows, feats), BF),
            pltpu.VMEM((rows, 3 * feats), BF),
            pltpu.VMEM((feats, rows), BF),
        ],
        out_shape=[
            jax.ShapeDtypeStruct((items, rows, feats), BF),
            jax.ShapeDtypeStruct((clips, rank, 4 * feats), F32),
        ],
        compiler_params=pltpu.CompilerParams(
            vmem_limit_bytes=VMEM_LIMIT, dimension_semantics=("arbitrary", "arbitrary")
        ),
        cost_estimate=pl.CostEstimate(flops=5 * 10**10, bytes_accessed=10**7, transcendentals=0),
        name="attend_back",
    )(x, gain1, qkv_w, down_own, up_own, probs, attn, qkv, reduced, dattn, dx1)
    return act, dx, grad_qkv, grad_dense


def spread_kernel(
    tok_ref, table_in_ref, qkv_ref, qd_ref, qu_ref, ids_in_ref,
    g1_ref, qb_ref, pb_ref, g2_ref, f1b_ref, f2b_ref,
    x_ref, weight_ref, down_ref, up_ref, gain1_ref, qkv_bias_ref, proj_bias_ref, gain2_ref, fc1_bias_ref,
    fc2_bias_ref, ids_ref, table_ref,
    unit_ref, vec_ref, pairs_ref,
    units, vecs, beside, mixed, tops, found, wide, select, bias,
    send_sem, recv_sem, unit_send, unit_recv, out_sem,
    *, clip_size,
):
    place = Place(clip_size)
    c, w, x, k = place.c, place.w, place.x, place.k
    sibling, across = place.sibling, place.across
    gather_units = Gather(place, unit_ref, units, unit_send, unit_recv)
    items, rows, feats = tok_ref.shape
    unit_ref[:, 0:384] = qkv_ref[...]
    for a in range(2):
        unit_ref[16 * a : 16 * a + 16, 384:448] = qd_ref[a]
        unit_ref[16 * a : 16 * a + 16, 448:512] = qu_ref[a, :, 0:64]
        unit_ref[32 + 16 * a : 48 + 16 * a, 384:512] = qu_ref[a, :, 64:192]
    vec_ref[0:1, 0:64] = g1_ref[...].astype(F32)
    vec_ref[0:1, 64:128] = qb_ref[:, 0:64].astype(F32)
    vec_ref[1:2, :] = qb_ref[:, 64:192].astype(F32)
    vec_ref[2:3, 0:64] = pb_ref[...].astype(F32)
    vec_ref[2:3, 64:128] = g2_ref[...].astype(F32)
    vec_ref[3:4, :] = f1b_ref[:, 0:128].astype(F32)
    vec_ref[4:5, :] = f1b_ref[:, 128:256].astype(F32)
    vec_ref[5:6, 0:64] = f2b_ref[...].astype(F32)
    vec_ref[5:6, 64:128] = ids_in_ref[:, 0:64]
    vec_ref[6:8, :] = jnp.zeros((2, 128), F32)
    enter([sibling, across] + [((c + d) % clip_size, w) for d in range(1, clip_size)])
    send = Sender(send_sem, recv_sem)
    units[k, c, x] = unit_ref[...]
    vecs[c] = vec_ref[...]
    gather_units.begin()
    tokens_beside = [send.copy(tok_ref.at[i], beside.at[i], sibling) for i in range(items)]
    vec_copies = [
        send.copy(vec_ref, vecs.at[c], ((c + d) % clip_size, w)) for d in range(1, clip_size)
    ]
    gather_units.second()
    early, low_h, low_w = row_masks(rows, feats)
    token_tops = []
    for i in range(items):
        tokens_beside[i].wait_recv()
        mixed[i] = jnp.where(low_h, beside[i], tok_ref[i])
        token_tops.append(send.copy(mixed.at[i, pl.ds(0, TOP)], tops.at[i], across))

    heads = pairs_ref.shape[0] // 15
    pairs_ref[...] = jnp.zeros(pairs_ref.shape, BF)
    for a in range(15):
        pairs_ref[a * heads : (a + 1) * heads, 0:169] = table_in_ref[:, 169 * a : 169 * a + 169]
    off_lane = lane_ids((pairs_ref.shape[1], 128))
    off_row = lax.broadcasted_iota(jnp.int32, (pairs_ref.shape[1], 128), 0)
    query_at = (off_lane // 7 + 4) % 7 * 13 + (off_lane % 7 + 4) % 7
    wanted = off_row - query_at - 84
    valid = off_lane < 49

    def one_key(key, carry):
        key_at = (key // 7 + 4) % 7 * 13 + (key % 7 + 4) % 7
        pick = jnp.where(valid & (wanted + key_at == 0), 1.0, 0.0).astype(BF)
        value = dot(pairs_ref[...], pick, NN)
        for a in range(15):
            found[a, pl.ds(key, heads, stride=56), :] = value[a * heads : (a + 1) * heads]
        return carry

    lax.fori_loop(0, 49, one_key, 0)

    gather_units.from_z(0)

    for a in range(15):
        wide[:, 128 * a : 128 * a + 128] = found[a].astype(BF)
    sel_row = lax.broadcasted_iota(jnp.int32, (128, rows), 0)
    sel_lane = lane_ids((128, rows))
    for t in range(8):
        select[128 * t : 128 * t + 128, :] = jnp.where(
            (sel_lane == sel_row + (t + 4) % 8 * 49) & (sel_row < 49), 1.0, 0.0
        ).astype(BF)

    gather_units.from_y(-1)
    gather_units.from_z(1)
    gather_units.from_y(0)
    for block in range(8):
        t = (block + 4) % 8
        value = dot(wide[:, (7 - t) * 128 : (15 - t) * 128], select[...], NN) * LOG2E
        for m in range(heads):
            bias[m, 49 * block : 49 * block + 49, :] = value[56 * m : 56 * m + 49]
    out = pltpu.make_async_copy(bias, table_ref, out_sem)
    out.start()
    gather_units.from_z(2)
    gather_units.from_y(1)

    for copy in vec_copies:
        copy.wait_recv()
    for c2 in range(clip_size):
        v = vecs[c2]
        gain1_ref[:, 64 * c2 : 64 * c2 + 64] = v[0:1, 0:64]
        qkv_bias_ref[:, 192 * c2 : 192 * c2 + 64] = v[0:1, 64:128]
        qkv_bias_ref[:, 192 * c2 + 64 : 192 * c2 + 192] = v[1:2, :]
        proj_bias_ref[:, 64 * c2 : 64 * c2 + 64] = v[2:3, 0:64]
        gain2_ref[:, 64 * c2 : 64 * c2 + 64] = v[2:3, 64:128]
        fc1_bias_ref[:, 256 * c2 : 256 * c2 + 128] = v[3:4, :]
        fc1_bias_ref[:, 256 * c2 + 128 : 256 * c2 + 256] = v[4:5, :]
        fc2_bias_ref[:, 64 * c2 : 64 * c2 + 64] = v[5:6, 0:64]
        for n in range(2):
            ids_ref[2 * c2 + n : 2 * c2 + n + 1, :] = jnp.broadcast_to(
                v[5:6, 64 + n : 65 + n], (1, ids_ref.shape[1])
            )

    gather_units.from_y(2)
    gather_units.finish()
    for c2 in range(clip_size):
        for x2 in range(2):
            for k2 in range(2):
                n = 2 * x2 + k2
                weight_ref[64 * c2 : 64 * c2 + 64, 384 * n : 384 * n + 384] = units[k2, c2, x2, :, 0:384]
                for a in range(2):
                    low = units[k2, c2, x2, 16 * a : 16 * a + 16, 384:512]
                    high = units[k2, c2, x2, 32 + 16 * a : 48 + 16 * a, 384:512]
                    down_ref[2 * n + a, :, 64 * c2 : 64 * c2 + 64] = low[:, 0:64]
                    up_ref[2 * n + a, :, 192 * c2 : 192 * c2 + 64] = low[:, 64:128]
                    up_ref[2 * n + a, :, 192 * c2 + 64 : 192 * c2 + 192] = high

    for i in range(0, items, 2):
        both = []
        for e in range(2):
            token_tops[i + e].wait_recv()
            both.append(with_top(mixed[i + e], tops[i + e], early))
        for e in range(2):
            x_ref[i + e] = jnp.where(low_w, both[1 - e], both[e])

    for copy in [*tokens_beside, *vec_copies, *token_tops]:
        copy.wait_send()
    out.wait()


def spread(tokens, table, qkv_w, qkv_down, qkv_up, ids, vecs, clip_size):
    items, rows, feats = tokens.shape
    heads = table.shape[0]
    f = functools.partial(jax.ShapeDtypeStruct)
    vm = pl.BlockSpec(memory_space=pltpu.VMEM)
    return pl.pallas_call(
        functools.partial(spread_kernel, clip_size=clip_size),
        in_specs=[vm] * 12,
        out_specs=[vm] * 11 + [pl.BlockSpec(memory_space=pl.ANY)],
        out_shape=[
            f((items, rows, feats), BF),
            f((512, 1536), BF),
            f((8, 16, 512), BF),
            f((8, 16, 1536), BF),
            f((1, 512), F32),
            f((1, 1536), F32),
            f((1, 512), F32),
            f((1, 512), F32),
            f((1, 2048), F32),
            f((1, 512), F32),
            f((16, 512), F32),
            f((heads, rows, rows), F32),
        ],
        scratch_shapes=[
            pltpu.VMEM((64, 512), BF),
            pltpu.VMEM((8, 128), F32),
            pltpu.VMEM((15 * heads, 176), BF),
            pltpu.VMEM((2, clip_size, 2, 64, 512), BF),
            pltpu.VMEM((clip_size, 8, 128), F32),
            pltpu.VMEM((items, rows, feats), BF),
            pltpu.VMEM((items, rows, feats), BF),
            pltpu.VMEM((items, TOP, feats), BF),
            pltpu.VMEM((15, 56 * heads, 128), F32),
            pltpu.VMEM((56 * heads, 15 * 128), BF),
            pltpu.VMEM((8 * 128, rows), BF),
            pltpu.VMEM((heads, rows, rows), F32),
            pltpu.SemaphoreType.DMA((16,)),
            pltpu.SemaphoreType.DMA((16,)),
            pltpu.SemaphoreType.DMA((Gather.COPIES,)),
            pltpu.SemaphoreType.DMA((Gather.COPIES,)),
            pltpu.SemaphoreType.DMA,
        ],
        compiler_params=pltpu.CompilerParams(
            collective_id=0, has_side_effects=True, vmem_limit_bytes=VMEM_LIMIT
        ),
        cost_estimate=pl.CostEstimate(flops=3 * 10**10, bytes_accessed=2 * 10**7, transcendentals=0),
        name="spread",
    )(tokens, table, qkv_w, qkv_down, qkv_up, ids, *vecs)


PIECES = (("q", 0, 64), ("q", 512, 192), ("d", 0, 64), ("d", 512, 64), ("d", 1024, 64), ("d", 5632, 64), ("d", 1536, 256), ("d", 3584, 256))


def finish_kernel(
    act_ref, act_beside_ref, act_across_ref, act_far_ref, dx_ref, grad_qkv_ref, grad_dense_ref, ids_ref,
    act_out_ref, dx_out_ref, qd_ref, qu_ref, pd_ref, pu_ref, f1d_ref, f1u_ref, f2d_ref, f2u_ref,
    beside, mixed, tops, own, other, from_core, half, from_x, shares, from_clips, adapters, from_win, whole_out,
    send_sem, recv_sem,
    *, clip_size,
):
    c, w = lax.axis_index("clip"), lax.axis_index("win")
    x, k = w // 2, w % 2
    sibling = (c, x * 2 + 1 - k)
    across = (c, (1 - x) * 2 + k)
    items, rows, feats = dx_ref.shape
    enter(
        [(c, (w + d) % 4) for d in range(1, 4)]
        + [((c + d) % clip_size, w) for d in range(1, clip_size)]
    )
    send = Sender(send_sem, recv_sem)
    dx_beside = [send.copy(dx_ref.at[i], beside.at[i], sibling) for i in range(items)]

    def rows_of(part, j):
        halves = []
        for n in range(2):
            cells = []
            for name, start, width in PIECES:
                ref = grad_qkv_ref if name == "q" else grad_dense_ref
                cells.append(
                    ref[n, pl.ds(pl.multiple_of(part * 8, 8), 8), start + j * width : start + (j + 1) * width]
                )
            halves.append(jnp.concatenate(cells, axis=1))
        return jnp.concatenate(halves, axis=0)

    for j in range(clip_size):
        other[j] = rows_of(1 - k, j).astype(BF)
    core_copy = send.copy(other, from_core, sibling)

    early, low_h, low_w = row_masks(rows, feats)
    dx_tops = []
    for i in range(items):
        dx_beside[i].wait_recv()
        mixed[i] = jnp.where(low_h, beside[i], dx_ref[i])
        dx_tops.append(send.copy(mixed.at[i, pl.ds(0, TOP)], tops.at[i], across))

    for j in range(clip_size):
        own[j] = rows_of(k, j)
    core_copy.wait_recv()
    own[...] += from_core[...].astype(F32)
    half[...] = own[:, :, pl.ds(pl.multiple_of((1 - x) * 512, 512), 512)].astype(BF)
    x_copy = send.copy(half, from_x, across)

    for i in range(0, items, 2):
        both = []
        for e in range(2):
            part = jnp.where(low_h, act_beside_ref[i + e], act_ref[i + e])
            top = jnp.where(low_h[:TOP], act_far_ref[i + e], act_across_ref[i + e])
            both.append(with_top(part, top, early))
        for e in range(2):
            act_out_ref[i + e] = jnp.where(low_w, both[1 - e], both[e])

    x_copy.wait_recv()
    shares[...] = (
        own[:, :, pl.ds(pl.multiple_of(x * 512, 512), 512)] + from_x[...].astype(F32)
    ).astype(BF)
    from_clips[c] = shares[c]
    clip_copies = []
    for d in range(1, clip_size):
        to = (c + d) % clip_size
        clip_copies.append(send.copy(shares.at[to], from_clips.at[c], (to, w)))
    for copy in clip_copies:
        copy.wait_recv()
    for a in range(8):
        total = None
        for n in range(2 * clip_size):
            value = from_clips[n // 2].astype(F32)[8 * (n % 2) : 8 * (n % 2) + 8]
            value = jnp.where(ids_ref[n : n + 1, :] == float(a), value, 0.0)
            total = value if total is None else total + value
        adapters[a // 2, 8 * (a % 2) : 8 * (a % 2) + 8, :] = total
    from_win[w] = adapters[w]
    win_copies = []
    for d in range(1, 4):
        to = (w + d) % 4
        win_copies.append(send.copy(adapters.at[to], from_win.at[w], (c, to)))

    for i in range(0, items, 2):
        both = []
        for e in range(2):
            dx_tops[i + e].wait_recv()
            both.append(with_top(mixed[i + e], tops[i + e], early))
        for e in range(2):
            dx_out_ref[i + e] = jnp.where(low_w, both[1 - e], both[e])

    for copy in win_copies:
        copy.wait_recv()
    for x2 in range(2):
        for k2 in range(2):
            for a in range(2):
                whole_out[a, 8 * k2 : 8 * k2 + 8, 512 * x2 : 512 * x2 + 512] = from_win[
                    2 * x2 + k2, 8 * a : 8 * a + 8, :
                ]
    for a in range(2):
        qd_ref[a] = whole_out[a, :, 0:64]
        qu_ref[a] = whole_out[a, :, 64:256]
        pd_ref[a] = whole_out[a, :, 256:320]
        pu_ref[a] = whole_out[a, :, 320:384]
        f1d_ref[a] = whole_out[a, :, 384:448]
        f2u_ref[a] = whole_out[a, :, 448:512]
        f1u_ref[a] = whole_out[a, :, 512:768]
        f2d_ref[a] = whole_out[a, :, 768:1024]
    for copy in [*dx_beside, core_copy, *dx_tops, x_copy, *clip_copies, *win_copies]:
        copy.wait_send()


def finish(act, act_pieces, dx, grad_qkv, grad_dense, ids, clip_size):
    items, rows, feats = dx.shape
    f = jax.ShapeDtypeStruct
    vm = pl.BlockSpec(memory_space=pltpu.VMEM)
    widths = (64, 192, 64, 64, 64, 256, 256, 64)
    return pl.pallas_call(
        functools.partial(finish_kernel, clip_size=clip_size),
        in_specs=[vm] * 8,
        out_specs=[vm] * 10,
        out_shape=[f(dx.shape, BF), f(dx.shape, BF)] + [f((2, 16, n), F32) for n in widths],
        scratch_shapes=[
            pltpu.VMEM((items, rows, feats), BF),
            pltpu.VMEM((items, rows, feats), BF),
            pltpu.VMEM((items, TOP, feats), BF),
            pltpu.VMEM((clip_size, 16, 1024), F32),
            pltpu.VMEM((clip_size, 16, 1024), BF),
            pltpu.VMEM((clip_size, 16, 1024), BF),
            pltpu.VMEM((clip_size, 16, 512), BF),
            pltpu.VMEM((clip_size, 16, 512), BF),
            pltpu.VMEM((clip_size, 16, 512), BF),
            pltpu.VMEM((clip_size, 16, 512), BF),
            pltpu.VMEM((4, 16, 512), F32),
            pltpu.VMEM((4, 16, 512), F32),
            pltpu.VMEM((2, 16, 1024), F32),
            pltpu.SemaphoreType.DMA((20,)),
            pltpu.SemaphoreType.DMA((20,)),
        ],
        compiler_params=pltpu.CompilerParams(
            collective_id=1, has_side_effects=True, vmem_limit_bytes=VMEM_LIMIT
        ),
        cost_estimate=pl.CostEstimate(flops=2 * 10**10, bytes_accessed=2 * 10**7, transcendentals=0),
        name="finish",
    )(act, *act_pieces, dx, grad_qkv, grad_dense, ids)


def exchange(x, win_size):
    local = x.shape[1]
    bits = local.bit_length() - 1
    at = jnp.arange(TOK)
    taken = (at // 49 < 4, at // 7 % 7 < 3, at % 7 < 3)
    for bit, rows in zip((2, 1, 0), taken):
        if bit < bits:
            split = x.reshape(x.shape[0], local >> (bit + 1), 2, 1 << bit, TOK, -1)
            other = jnp.flip(split, axis=2).reshape(x.shape)
        else:
            other = lax.ppermute(x, "win", [(i, i ^ 1 << bit - bits) for i in range(win_size)])
        x = jnp.where(rows[None, None, :, None], other, x)
    return x


def pieces_of(x):
    top = x[:, :TOP]
    return (
        x,
        lax.ppermute(x, "win", [(i, i ^ 1) for i in range(4)]),
        lax.ppermute(top, "win", [(i, i ^ 2) for i in range(4)]),
        lax.ppermute(top, "win", [(i, i ^ 3) for i in range(4)]),
    )


def bias_by_pair(table):
    heads = table.shape[0]
    side = jnp.arange(49)
    high, wide = (side // 7 + 4) % 7, (side % 7 + 4) % 7
    offset = (high[None, :] - high[:, None] + 6) * 13 + wide[None, :] - wide[:, None] + 6
    pick = (jnp.arange(169)[:, None, None] == offset[None]).astype(BF)
    found = jnp.einsum(
        "mad,dkq->mkaq", table.reshape(heads, 15, 169), pick, preferred_element_type=F32
    )
    found = (found * LOG2E).reshape(heads, 49, 15 * 49)
    blocks = []
    for key_block in range(8):
        t = (key_block + 4) % 8
        blocks.append(
            jnp.concatenate(
                (found[..., (11 - t) * 49 : (15 - t) * 49], found[..., (7 - t) * 49 : (11 - t) * 49]),
                axis=-1,
            )
        )
    return jnp.stack(blocks, axis=1).reshape(heads, TOK, TOK)


def gather(array, spec):
    for axis, name in enumerate(spec):
        if name is not None:
            array = lax.all_gather(array, name, axis=axis, tiled=True)
    return array


def stage_whole(proj_w, fc1_w, fc2_w, maps):
    proj_down, proj_up, fc1_down, fc1_up, fc2_down, fc2_up = maps
    count = proj_down.shape[0]

    def short(a):
        return a.reshape(4, count // 4 * 16, 8, 64).transpose(2, 0, 1, 3)

    def long(a):
        return a.reshape(4, count // 4 * 16, 8, 2, 128).transpose(2, 0, 3, 1, 4).reshape(8, 4, -1, 128)

    return jnp.concatenate(
        (
            proj_w.reshape(8, 64, 4, 128).transpose(0, 2, 1, 3),
            fc1_w.reshape(8, 64, 4, 4, 128).transpose(0, 2, 3, 1, 4).reshape(8, 4, 256, 128),
            fc2_w.reshape(8, 256, 4, 128).transpose(0, 2, 1, 3),
            jnp.concatenate((short(proj_down), short(proj_up)), axis=-1),
            jnp.concatenate((short(fc1_down), short(fc2_up)), axis=-1),
            long(fc1_up),
            long(fc2_down),
        ),
        axis=2,
    )


def by_core(staged):
    return staged.reshape(8, 2, 2, *staged.shape[2:]).transpose(2, 0, 1, 3, 4)


def per_device(
    tokens, cotangent, adapter_ids, ln1_gain, qkv_weight, qkv_bias, proj_weight, proj_bias, ln2_gain,
    fc1_weight, fc1_bias, fc2_weight, fc2_bias, bias_table, qkv_down, qkv_up, proj_down, proj_up,
    fc1_down, fc1_up, fc2_down, fc2_up, *, clip_size, win_size,
):
    clips, local, rows, feats = tokens.shape
    items = clips * local
    heads = bias_table.shape[0]
    vecs = (ln1_gain, qkv_bias, proj_bias, ln2_gain, fc1_bias, fc2_bias)
    flat = (items, rows, feats)
    downs = [a.transpose(0, 2, 1) for a in (qkv_down, proj_down, fc1_down, fc2_down)]
    own_kernels = (clip_size, win_size, clips, local) == (8, 4, 2, 2)
    if own_kernels:
        rows_of_ids = jnp.pad(adapter_ids.astype(F32)[None], ((0, 0), (0, 126)))
        x, qkv_w, down, up, *vectors, ids, table = spread(
            tokens.reshape(flat), bias_table, qkv_weight, downs[0], qkv_up, rows_of_ids,
            [v.reshape(1, -1) for v in vecs], clip_size,
        )
        dy = cotangent.reshape(flat)
        qkv_parts = (qkv_w, down, up)
        later = (proj_weight, fc1_weight, fc2_weight, downs[1], proj_up, downs[2], fc1_up, downs[3], fc2_up)
    else:
        grid2, by_down, by_up = ("clip", "win"), ("win", None, "clip"), ("win", None, "clip")
        qkv_parts = (gather(qkv_weight, grid2), gather(downs[0], by_down), gather(qkv_up, by_up))
        maps = (downs[1], proj_up, downs[2], fc1_up, downs[3], fc2_up)
        staged = stage_whole(
            *[gather(a, grid2) for a in (proj_weight, fc1_weight, fc2_weight)],
            [gather(a, by_up) for a in maps],
        )
        later = (by_core(staged),)
        vectors = [gather(v, ("clip",)).reshape(1, -1).astype(F32) for v in vecs]
        table = bias_by_pair(bias_table)
        x = exchange(tokens, win_size).reshape(flat)
        dy = exchange(cotangent, win_size).reshape(flat)
    act, dx, grad_qkv, grad_dense = compute(
        x, dy, adapter_ids, vectors, qkv_parts, later, table, local, clip_size if own_kernels else 0
    )
    if own_kernels:
        act_out, dx_out, qd, qu, pd, pu, f1d, f1u, f2d, f2u = finish(
            act, pieces_of(act)[1:], dx, grad_qkv, grad_dense, ids, clip_size
        )
        turned = [a.transpose(0, 2, 1) for a in (qd, pd, f1d, f2d)]
        return (
            act_out.reshape(tokens.shape), dx_out.reshape(tokens.shape),
            turned[0], qu, turned[1], pu, turned[2], f1u, turned[3], f2u,
        )
    activations = exchange(act.reshape(tokens.shape), win_size)
    input_grad = exchange(dx.reshape(tokens.shape), win_size)
    adapter_count = win_size * qkv_down.shape[0]
    hot = (adapter_ids[:, None] == jnp.arange(adapter_count)[None]).astype(F32)
    hidden = fc1_weight.shape[1] * win_size
    spans = (feats, 3 * feats, feats, feats, feats, hidden, hidden, feats)
    grads = jnp.concatenate((grad_qkv, grad_dense), axis=-1)
    rank = grads.shape[1]
    parts, at = [], 0
    for span in spans:
        parts.append(
            grads[..., at : at + span].reshape(clips, rank, clip_size, span // clip_size)
        )
        at += span
    mine = jnp.concatenate(parts, axis=-1)
    grown = jnp.sum(hot[:, :, None, None, None] * mine[:, None], axis=0)
    grown = grown.transpose(2, 0, 1, 3).astype(BF)
    total = lax.psum_scatter(grown, "clip", scatter_dimension=0, tiled=True)[0]
    total = lax.psum_scatter(total, "win", scatter_dimension=0, tiled=True).astype(F32)
    outs, at = [], 0
    for n, span in enumerate(spans):
        width = span // clip_size
        part = total[..., at : at + width]
        at += width
        outs.append(part.transpose(0, 2, 1) if n % 2 == 0 else part)
    return (activations, input_grad, *outs)


def solution(mesh):
    split = P("clip", "win", None, None)
    grid2 = P("clip", "win")
    down = P("win", "clip", None)
    up = P("win", None, "clip")
    one = P("clip")
    return jax.shard_map(
        functools.partial(
            per_device, clip_size=mesh.shape["clip"], win_size=mesh.shape["win"]
        ),
        mesh=mesh,
        in_specs=(
            split, split, one, one, grid2, one, grid2, one, one, grid2, one, grid2, one, P(),
            down, up, down, up, down, up, down, up,
        ),
        out_specs=(split, split, down, up, down, up, down, up, down, up),
        check_vma=False,
    )
```

```python
import functools
import jax
import jax.numpy as jnp
from jax import lax
from jax.experimental import pallas as pl
from jax.experimental.pallas import tpu as pltpu
from jax.sharding import PartitionSpec as P

BF = jnp.bfloat16
F32 = jnp.float32
NN = (((1,), (0,)), ((), ()))
NT = (((1,), (1,)), ((), ()))
TN = (((0,), (0,)), ((), ()))
LOG2E = 1.4426950408889634
LN2 = 0.6931471805599453
FAR = 1e9
VMEM_LIMIT = 60 * 2**20
TOK = 392
TOP = 208


def dot(left, right, dims):
    return lax.dot_general(left, right, dims, preferred_element_type=F32)


def lane_ids(shape):
    return lax.broadcasted_iota(jnp.int32, shape, len(shape) - 1)


def norm_stats(values):
    average = jnp.mean(values, axis=-1, keepdims=True)
    centred = values - average
    variance = jnp.mean(centred * centred, axis=-1, keepdims=True)
    inverse = lax.rsqrt(variance + 1e-05)
    return centred * inverse, inverse


def norm_back(gradient, gain, normed, inverse):
    scaled = gradient * gain
    centre = jnp.mean(scaled, axis=-1, keepdims=True)
    slope = jnp.mean(scaled * normed, axis=-1, keepdims=True)
    return inverse * (scaled - centre - normed * slope)


def add_rows(ref, n, at, value, first):
    @pl.when(first)
    def _():
        ref[n, :, at] = value

    @pl.when(jnp.logical_not(first))
    def _():
        ref[n, :, at] += value


MESH = pl.DeviceIdType.MESH


def enter(peers):
    barrier = pltpu.get_barrier_semaphore()
    for peer in peers:
        pl.semaphore_signal(barrier, inc=1, device_id=peer, device_id_type=MESH)
    pl.semaphore_wait(barrier, len(peers))


def remote(src, dst, send_sem, recv_sem, peer):
    return pltpu.make_async_remote_copy(
        src_ref=src,
        dst_ref=dst,
        send_sem=send_sem,
        recv_sem=recv_sem,
        device_id=peer,
        device_id_type=MESH,
    )


class Sender:
    def __init__(self, send_sem, recv_sem):
        self.send_sem, self.recv_sem, self.count = send_sem, recv_sem, 0

    def copy(self, src, dst, peer):
        n = self.count
        self.count += 1
        made = remote(src, dst, self.send_sem.at[n], self.recv_sem.at[n], peer)
        made.start()
        return made


def row_masks(rows, columns):
    row = lax.broadcasted_iota(jnp.int32, (rows, columns), 0)
    return row < TOK // 2, row % 49 < 21, row % 7 < 3


def with_top(part, top, early):
    return jnp.concatenate([jnp.where(early[:TOP], top, part[:TOP]), part[TOP:]], axis=0)


class Place:
    def __init__(self, clip_size):
        self.c, self.w = lax.axis_index("clip"), lax.axis_index("win")
        self.z, self.y = self.c // 2, self.c % 2
        self.x, self.k = self.w // 2, self.w % 2
        self.zs = clip_size // 2
        self.sibling = (self.c, self.x * 2 + 1 - self.k)
        self.across = (self.c, (1 - self.x) * 2 + self.k)

    def clip_at(self, z_step, other_y):
        return (self.z + z_step + self.zs) % self.zs * 2 + (1 - self.y if other_y else self.y)

    def along_z(self, step):
        return (self.clip_at(step, False), self.w)

    def along_y(self):
        return (self.clip_at(0, True), self.w)


class Gather:
    COPIES = 29

    def __init__(self, place, unit, units, send_sem, recv_sem):
        self.place, self.unit, self.units = place, unit, units
        self.send_sem, self.recv_sem = send_sem, recv_sem
        self.hops = range(place.zs - 1)

    def make(self, kind, t=0):
        p, units = self.place, self.units
        kinds = ("up", "down", "y_up", "y_down", "s_up", "s_down", "sy_up", "sy_down")
        single = ("across", "own", "theirs", "y", "s_y")
        n = single.index(kind) if kind in single else 5 + 8 * t + kinds.index(kind)
        sems = self.send_sem.at[n], self.recv_sem.at[n]
        mine = units.at[p.k, p.c, p.x]
        if kind == "across":
            return remote(self.unit, mine, *sems, p.across)
        if kind == "own":
            return remote(self.unit, mine, *sems, p.sibling)
        if kind == "theirs":
            part = units.at[p.k, p.c, 1 - p.x]
        elif kind == "y":
            part = units.at[p.k, p.c]
        elif kind == "s_y":
            part = units.at[p.k, p.z * 2 + 1 - p.y]
        else:
            sign = -1 if kind.endswith("up") else 1
            far = p.z + sign * (t if kind in ("up", "down") else t + 1)
            part = units.at[p.k, far * 2 + (1 - p.y if kind.startswith("sy") else p.y)]
        if kind in ("up", "down"):
            peer = (p.c - 2 * sign, p.w)
        else:
            peer = p.along_y() if kind.startswith("y") else p.sibling
        return remote(part, part, *sems, peer)

    def when(self, kind, t, sending, act):
        p, last = self.place, self.place.zs - 1
        if kind.endswith("up"):
            holds = (p.z >= t) & (p.z < last) if sending and kind == "up" else p.z >= t + 1
        elif kind.endswith("down"):
            holds = (p.z <= last - t) & (p.z > 0) if sending and kind == "down" else p.z <= last - 1 - t
        else:
            act()
            return
        pl.when(holds)(act)

    def start(self, kind, t=0):
        self.when(kind, t, True, lambda: self.make(kind, t).start())

    def wait_recv(self, kind, t=0):
        self.when(kind, t, False, lambda: self.make(kind, t).wait_recv())

    def wait_send(self, kind, t=0):
        self.when(kind, t, True, lambda: self.make(kind, t).wait_send())

    def begin(self):
        self.start("across")
        self.start("own")

    def second(self):
        self.wait_recv("across")
        for kind in ("up", "down", "y", "theirs"):
            self.start(kind)

    def from_z(self, t):
        for way in ("up", "down"):
            self.wait_recv(way, t)
            if t + 1 in self.hops:
                self.start(way, t + 1)
            self.start("y_" + way, t)
            self.start("s_" + way, t)

    def from_y(self, t):
        if t < 0:
            self.wait_recv("y")
            self.start("s_y")
        else:
            for way in ("up", "down"):
                self.wait_recv("y_" + way, t)
                self.start("sy_" + way, t)

    def finish(self):
        for kind in ("own", "theirs", "s_y"):
            self.wait_recv(kind)
        for t in self.hops:
            for kind in ("s_up", "s_down", "sy_up", "sy_down"):
                self.wait_recv(kind, t)
        for kind in ("across", "own", "theirs", "y", "s_y"):
            self.wait_send(kind)
        for t in self.hops:
            for kind in ("up", "down", "y_up", "y_down", "s_up", "s_down", "sy_up", "sy_down"):
                self.wait_send(kind, t)


def attend_kernel(
    x_ref,
    gain_ref,
    weight_ref,
    bias_ref,
    ids_ref,
    down_ref,
    up_ref,
    table_ref,
    *refs,
    scale,
    per_group,
    width,
    per_clip,
    remote_size,
):
    if remote_size:
        (dy_ref, proj_ref, fc1_ref, fc2_ref, pd_ref, pu_ref, f1d_ref, f1u_ref, f2d_ref, f2u_ref, *refs) = refs
    probs_ref, out_ref, qkv_ref, reduced_ref, down_own, up_own, *refs = refs
    if remote_size:
        dy_out_ref, units_ref, *refs = refs
    keys, queries, values_t, out_t, scores, table, table_sem, query_mask, *refs = refs
    group = pl.program_id(1)
    groups = pl.num_programs(1)
    item = pl.program_id(0)
    step = item * groups + group
    feats = x_ref.shape[-1]
    rows = x_ref.shape[1]
    starting = item == 0

    def table_copy(g):
        at = pl.ds(g * per_group, per_group)
        return pltpu.make_async_copy(table_ref.at[at], table.at[at], table_sem.at[g])

    @pl.when(step == 0)
    def _():
        for g in range(table.shape[0] // per_group):
            table_copy(g).start()

    if remote_size:
        unit, beside, mixed, tops, send_sem, recv_sem, dy_send, dy_recv, own_sem = refs
        place = Place(remote_size)
        gather_units = Gather(place, unit, units_ref, send_sem, recv_sem)
        items = dy_ref.shape[0]

        def dy_copy(kind, i):
            n = kind * items + i
            sems = dy_send.at[n], dy_recv.at[n]
            if kind == 0:
                return remote(dy_ref.at[i], beside.at[i], *sems, place.sibling)
            return remote(mixed.at[i, pl.ds(0, TOP)], tops.at[i], *sems, place.across)

        @pl.when(step == 0)
        def _():
            unit[0:64] = proj_ref[...]
            for t in range(4):
                unit[64 + 64 * t : 128 + 64 * t] = fc1_ref[:, 128 * t : 128 * t + 128]
            unit[320:576] = fc2_ref[...]
            for a in range(2):
                at = 576 + 16 * a
                unit[at : at + 16, 0:64] = pd_ref[a]
                unit[at : at + 16, 64:128] = pu_ref[a]
                unit[at + 32 : at + 48, 0:64] = f1d_ref[a]
                unit[at + 32 : at + 48, 64:128] = f2u_ref[a]
                for half in range(2):
                    lanes = slice(128 * half, 128 * half + 128)
                    unit[at + 64 + 32 * half : at + 80 + 32 * half] = f1u_ref[a, :, lanes]
                    unit[at + 128 + 32 * half : at + 144 + 32 * half] = f2d_ref[a, :, lanes]
            own = pltpu.make_async_copy(unit, units_ref.at[place.k, place.c, place.x], own_sem)
            own.start()
            enter(
                [place.sibling, place.across, place.along_y()]
                + [place.along_z(j) for j in range(1, place.zs)]
            )
            gather_units.begin()
            for i in range(items):
                dy_copy(0, i).start()
            own.wait()

        @pl.when(step == 1)
        def _():
            gather_units.second()

        @pl.when(step == 2)
        def _():
            low_h = row_masks(rows, feats)[1]
            for i in range(items):
                dy_copy(0, i).wait_recv()
                mixed[i] = jnp.where(low_h, beside[i], dy_ref[i])
                dy_copy(1, i).start()

        for t, at in enumerate((4, 8, 11)):

            @pl.when(step == at)
            def _():
                gather_units.from_z(t)

        for t, at in ((-1, 5), (0, 9), (1, 12), (2, 15)):

            @pl.when(step == at)
            def _():
                gather_units.from_y(t)

        @pl.when(step == 4 * items - 1)
        def _():
            early, _, low_w = row_masks(rows, feats)
            for i in range(0, items, 2):
                both = []
                for e in range(2):
                    dy_copy(1, i + e).wait_recv()
                    both.append(with_top(mixed[i + e], tops[i + e], early))
                for e in range(2):
                    dy_out_ref[i + e] = jnp.where(low_w, both[1 - e], both[e])
            gather_units.finish()
            for i in range(items):
                dy_copy(0, i).wait_send()
                dy_copy(1, i).wait_send()

    @pl.when((group == 0) & (item % per_clip == 0))
    def _():
        clip = item // per_clip
        for ref, target in ((down_ref, down_own), (up_ref, up_own)):
            total = jnp.zeros(ref.shape[1:], F32)
            for a in range(ref.shape[0]):
                total = total + jnp.where(
                    ids_ref[pl.ds(clip, 1), 0:1] == float(a), ref[a].astype(F32), 0.0
                )
            target[0] = total.astype(BF)

    @pl.when(group == 0)
    def _():
        number = lax.axis_index("win") * per_clip + item % per_clip
        early, low_h, low_w = row_masks(rows, 128)
        label = (
            jnp.where(early, number // 4 % 2 * 4, 0)
            + jnp.where(low_h, number // 2 % 2 * 2, 0)
            + jnp.where(low_w, number % 2, 0)
        )
        lane = lane_ids((rows, 128))
        same = label == lane
        key_mask = jnp.where(same, 1.0, 0.0).astype(BF)
        query_mask[...] = jnp.where(same | (lane >= 8), 0.0, -FAR).astype(BF)
        normed, _ = norm_stats(x_ref[0].astype(F32))
        low = (normed * gain_ref[...]).astype(BF)
        reduced = dot(down_own[0], low, NT).astype(BF)
        reduced_ref[0] = reduced

        def columns(part):
            at = pl.ds(part * feats, feats)
            return (
                dot(low, weight_ref[:, at], NN)
                + bias_ref[:, at]
                + dot(reduced, up_own[0, :, at], TN)
            )

        query = (columns(0) * (scale * LOG2E)).astype(BF)
        queries[...] = query
        qkv_ref[0, :, :feats] = query
        key = columns(1).astype(BF)
        qkv_ref[0, :, feats : 2 * feats] = key
        for g in range(feats // 128):
            keys[:, 256 * g : 256 * g + 128] = key[:, 128 * g : 128 * g + 128]
            keys[:, 256 * g + 128 : 256 * g + 256] = key_mask
        value = columns(2).astype(BF)
        qkv_ref[0, :, 2 * feats :] = value
        values_t[...] = value.T

    @pl.when(starting)
    def _():
        table_copy(group).wait()

    keys_now = keys[:, pl.ds(pl.multiple_of(group * 256, 256), 256)]
    query_now = queries[:, pl.ds(pl.multiple_of(group * 128, 128), 128)]
    head_of_lane = lane_ids(query_now.shape) // width

    def raw(h):
        own = jnp.where(head_of_lane == h, query_now, jnp.zeros_like(query_now))
        own = jnp.concatenate([own, query_mask[...]], axis=1)
        return dot(keys_now, own, NT) + table[group * per_group + h]

    def finish(h):
        score = scores[h % 2]
        largest = jnp.max(score, axis=0, keepdims=True)
        probs = jnp.exp2(score - largest)
        total = jnp.sum(probs, axis=0, keepdims=True)
        probs = (probs * (1.0 / total)).astype(BF)
        probs_ref[0, h] = probs
        at = pl.ds(pl.multiple_of((group * per_group + h) * width, width), width)
        out_t[at, :] = dot(values_t[at, :], probs, NN).astype(BF)

    scores[0] = raw(0)
    for h in range(per_group):
        if h + 1 < per_group:
            scores[(h + 1) % 2] = raw(h + 1)
        finish(h)

    @pl.when(group == groups - 1)
    def _():
        out_ref[0] = out_t[...].T


def dense_kernel(
    ids_ref,
    x_ref,
    attn_ref,
    gain_ref,
    proj_bias_ref,
    fc1_bias_ref,
    fc2_bias_ref,
    dy_ref,
    staged_ref,
    *refs,
    per_clip,
    chunk,
):
    tiles, refs = refs[:6], refs[6:]
    act_ref, dx1_ref, dattn_ref, grad_ref, *refs = refs
    proj_ref, fc1_ref, fc2_ref, proj_down, proj_up, fc1_down, fc1_up, fc2_down, fc2_up, *refs = refs
    pres, acts, dpres, sem = refs
    starting = pl.program_id(0) == 0
    count = x_ref.shape[1]
    feats = x_ref.shape[-1]
    hidden = fc1_ref.shape[-1]

    def moves(first=0, last=24):
        found = [(0, 64, proj_ref, 128 * n, n) for n in range(4)]
        found += [(64 + 64 * t, 64, fc1_ref, 512 * n + 128 * t, n) for n in range(4) for t in range(4)]
        found += [(320, 256, fc2_ref, 128 * n, n) for n in range(4)]
        return [
            pltpu.make_async_copy(
                staged_ref.at[n % 2, :, n // 2, pl.ds(start, size), :],
                target.at[:, :, pl.ds(lane, 128)],
                sem.at[at],
            )
            for at, (start, size, target, lane, n) in enumerate(found)
            if first <= at < last
        ]

    def arrive(first, last):
        @pl.when(starting)
        def _():
            for copy in moves(first, last):
                copy.wait()

    @pl.when(starting)
    def _():
        for copy in moves():
            copy.start()

    for n in range(8):
        short = slice(64 * n, 64 * n + 64)
        proj_down[:, short] = tiles[0][0, n, 0, :, 0:64]
        proj_up[:, short] = tiles[0][0, n, 0, :, 64:128]
        fc1_down[:, short] = tiles[1][0, n, 0, :, 0:64]
        fc2_up[:, short] = tiles[1][0, n, 0, :, 64:128]
        for half in range(2):
            long = slice(256 * n + 128 * half, 256 * n + 128 * half + 128)
            fc1_up[:, long] = tiles[2 + half][0, n, 0]
            fc2_down[:, long] = tiles[4 + half][0, n, 0]

    def join(parts):
        return jnp.concatenate(parts, axis=0) if per_clip > 1 else parts[0]

    dy = join([dy_ref[e] for e in range(per_clip)])
    attn = join([attn_ref[e] for e in range(per_clip)])
    reduced_proj = dot(proj_down[...], attn, NT).astype(BF)
    arrive(0, 4)
    proj_w = proj_ref[...].reshape(feats, feats)
    middle = (
        join([x_ref[e].astype(F32) for e in range(per_clip)])
        + dot(attn, proj_w, NN)
        + proj_bias_ref[...]
        + dot(reduced_proj, proj_up[...], TN)
    )
    normed, inverse = norm_stats(middle)
    low = (normed * gain_ref[...]).astype(BF)
    reduced_fc1 = dot(fc1_down[...], low, NT).astype(BF)
    grad_reduced_fc2 = dot(fc2_up[...], dy, NT).astype(BF)
    per_chunk = chunk // fc2_ref.shape[1]
    steps = hidden // chunk

    def pre_of(j):
        at = slice(j * chunk, (j + 1) * chunk)
        pres[j % 2] = (
            dot(low, fc1_ref[:, :, at].reshape(feats, chunk), NN)
            + fc1_bias_ref[:, at]
            + dot(reduced_fc1, fc1_up[:, at], TN)
        )

    arrive(4, 20)
    pre_of(0)
    arrive(20, 24)
    for j in range(steps):
        at = slice(j * chunk, (j + 1) * chunk)
        if j + 1 < steps:
            pre_of(j + 1)
        fc2_w = fc2_ref[j * per_chunk : (j + 1) * per_chunk].reshape(chunk, feats)
        dact = dot(dy, fc2_w, NT) + dot(grad_reduced_fc2, fc2_down[:, at], TN)
        pre = pres[j % 2]
        bell = jnp.exp2((pre * pre) * (-0.5 * LOG2E))
        t = 1.0 / (1.0 + jnp.abs(pre) * (0.3275911 * 0.7071067811865476))
        poly = (
            (((0.5 * 1.061405429) * t - 0.5 * 1.453152027) * t + 0.5 * 1.421413741) * t
            - 0.5 * 0.284496736
        ) * t + 0.5 * 0.254829592
        tail = poly * t * bell
        below = jnp.where(pre >= 0.0, 1.0 - tail, tail)
        acts[:, at] = (pre * below).astype(BF)
        dpres[:, at] = (dact * (below + pre * bell * 0.3989422804014327)).astype(BF)
    act = acts[...]
    dpre = dpres[...]
    fc1_up_at = 3 * feats
    fc2_down_at = fc1_up_at + hidden
    fc2_up_at = fc2_down_at + hidden
    fc2_w = fc2_ref[...].reshape(hidden, feats)
    grad_reduced_fc1 = dot(fc1_up[...], dpre, NT).astype(BF)
    dlow = dot(dpre, fc1_ref[...].reshape(feats, hidden), NT) + dot(grad_reduced_fc1, fc1_down[...], TN)
    dx1 = dy.astype(F32) + norm_back(dlow, gain_ref[...], normed, inverse)
    branch = dx1.astype(BF)
    reduced_fc2 = dot(fc2_down[...], act, NT).astype(BF)
    total = (
        middle + fc2_bias_ref[...] + dot(act, fc2_w, NN) + dot(reduced_fc2, fc2_up[...], TN)
    ).astype(BF)
    grad_reduced_proj = dot(proj_up[...], branch, NT).astype(BF)
    dattn = (
        dot(branch, proj_w, NT) + dot(grad_reduced_proj, proj_down[...], TN)
    ).astype(BF)
    for e in range(per_clip):
        rows = slice(e * count, (e + 1) * count)
        act_ref[e] = total[rows]
        dx1_ref[e] = dx1[rows]
        dattn_ref[e] = dattn[rows]
    grad_ref[0, :, :feats] = dot(grad_reduced_proj, attn, NN)
    grad_ref[0, :, feats : 2 * feats] = dot(reduced_proj, branch, NN)
    grad_ref[0, :, 2 * feats : fc1_up_at] = dot(grad_reduced_fc1, low, NN)
    grad_ref[0, :, fc1_up_at:fc2_down_at] = dot(reduced_fc1, dpre, NN)
    grad_ref[0, :, fc2_down_at:fc2_up_at] = dot(grad_reduced_fc2, act, NN)
    grad_ref[0, :, fc2_up_at:] = dot(reduced_fc2, dy, NN)


PIECES = (
    (0, 0, 64),
    (0, 512, 192),
    (1, 0, 64),
    (1, 512, 64),
    (1, 1024, 64),
    (1, 5632, 64),
    (1, 1536, 256),
    (1, 3584, 256),
)


class Rows:
    def __init__(self, place, own, beside, mixed, tops, send_sem, recv_sem):
        self.place, self.own, self.beside, self.mixed, self.tops = place, own, beside, mixed, tops
        self.send_sem, self.recv_sem = send_sem, recv_sem
        self.items, self.rows, self.feats = own.shape

    def copy(self, kind, i):
        n = kind * self.items + i
        sems = self.send_sem.at[n], self.recv_sem.at[n]
        if kind == 0:
            return remote(self.own.at[i], self.beside.at[i], *sems, self.place.sibling)
        top = self.mixed.at[i, pl.ds(0, TOP)]
        return remote(top, self.tops.at[i], *sems, self.place.across)

    def begin(self, i):
        self.copy(0, i).start()

    def mix(self, i):
        self.copy(0, i).wait_recv()
        low_h = row_masks(self.rows, self.feats)[1]
        self.mixed[i] = jnp.where(low_h, self.beside[i], self.own[i])
        self.copy(1, i).start()

    def end(self, out):
        early, _, low_w = row_masks(self.rows, self.feats)
        for i in range(0, self.items, 2):
            both = []
            for e in range(2):
                self.copy(1, i + e).wait_recv()
                both.append(with_top(self.mixed[i + e], self.tops[i + e], early))
            for e in range(2):
                out[i + e] = jnp.where(low_w, both[1 - e], both[e])
        for i in range(self.items):
            self.copy(0, i).wait_send()
            self.copy(1, i).wait_send()


def gradient_rows(sources, part, j):
    halves = []
    for n in range(2):
        cells = []
        for array, start, width in PIECES:
            at = slice(start + j * width, start + (j + 1) * width)
            cells.append(sources[array][n, pl.ds(pl.multiple_of(part * 8, 8), 8), at])
        halves.append(jnp.concatenate(cells, axis=1))
    return jnp.concatenate(halves, axis=0)


def share_gradients(place, sources, ids_ref, refs, send, between):
    own, other, from_core, half, from_x, shares, from_clips, adapters, from_win, out = refs
    c, w, x, k = place.c, place.w, place.x, place.k
    clip_size = own.shape[0]
    for j in range(clip_size):
        other[j] = gradient_rows(sources, 1 - k, j).astype(BF)
    core_copy = send.copy(other, from_core, place.sibling)
    between[0]()
    for j in range(clip_size):
        own[j] = gradient_rows(sources, k, j)
    core_copy.wait_recv()
    own[...] += from_core[...].astype(F32)
    half[...] = own[:, :, pl.ds(pl.multiple_of((1 - x) * 512, 512), 512)].astype(BF)
    x_copy = send.copy(half, from_x, place.across)
    between[1]()
    x_copy.wait_recv()
    shares[...] = (
        own[:, :, pl.ds(pl.multiple_of(x * 512, 512), 512)] + from_x[...].astype(F32)
    ).astype(BF)
    from_clips[c] = shares[c]
    clip_copies = []
    for d in range(1, clip_size):
        to = (c + d) % clip_size
        clip_copies.append(send.copy(shares.at[to], from_clips.at[c], (to, w)))
    for copy in clip_copies:
        copy.wait_recv()
    for a in range(8):
        total = None
        for n in range(2 * clip_size):
            value = from_clips[n // 2].astype(F32)[8 * (n % 2) : 8 * (n % 2) + 8]
            value = jnp.where(ids_ref[n : n + 1, :] == float(a), value, 0.0)
            total = value if total is None else total + value
        adapters[a // 2, 8 * (a % 2) : 8 * (a % 2) + 8, :] = total
    from_win[w] = adapters[w]
    win_copies = []
    for d in range(1, 4):
        to = (w + d) % 4
        win_copies.append(send.copy(adapters.at[to], from_win.at[w], (c, to)))
    between[2]()
    for copy in win_copies:
        copy.wait_recv()
    for x2 in range(2):
        for k2 in range(2):
            for a in range(2):
                out[a, 8 * k2 : 8 * k2 + 8, 512 * x2 : 512 * x2 + 512] = from_win[
                    2 * x2 + k2, 8 * a : 8 * a + 8, :
                ]
    for copy in [core_copy, x_copy, *clip_copies, *win_copies]:
        copy.wait_send()


def attend_back_kernel(
    x_ref,
    gain_ref,
    weight_ref,
    down_ref,
    up_ref,
    probs_ref,
    attn_ref,
    qkv_ref,
    reduced_ref,
    dattn_ref,
    dx1_ref,
    *refs,
    scale,
    per_group,
    width,
    per_clip,
    remote_size,
):
    if remote_size:
        act_ref, grad_dense_ref, ids_ref, act_out_ref, dx_out_ref, sums_ref, *refs = refs
    else:
        dx_ref, grad_ref, *refs = refs
    values, keys_t, inner, dqkv, dquery_t, *refs = refs
    group = pl.program_id(1)
    groups = pl.num_programs(1)
    item = pl.program_id(0)
    step = item * groups + group
    if remote_size:
        items = act_ref.shape[0]
        place = Place(remote_size)
        act_rows = Rows(place, act_ref, *refs[:5])
        dx_own = refs[5]
        dx_rows = Rows(place, *refs[5:11])
        grad_ref = refs[11]
        share_refs, sems = refs[12:21], refs[21:]

        @pl.when(step == 0)
        def _():
            enter(
                [(place.c, (place.w + d) % 4) for d in range(1, 4)]
                + [((place.c + d) % remote_size, place.w) for d in range(1, remote_size)]
            )
            for i in range(items):
                act_rows.begin(i)

        for i in range(items):

            @pl.when(step == i + 1)
            def _():
                act_rows.mix(i)

            if i < items - 1:

                @pl.when(step == (i + 1) * 4 + 1)
                def _():
                    dx_rows.mix(i)

        @pl.when(step == 4 * items - 3)
        def _():
            act_rows.end(act_out_ref)

    feats = x_ref.shape[-1]
    rows = x_ref.shape[1]

    @pl.when(group == 0)
    def _():
        keys_t[...] = qkv_ref[0, :, feats : 2 * feats].T
        lane = lane_ids((rows, 128))
        ones = jnp.where(lane % width < 2, 1.0, 0.0).astype(BF)
        source = lax.broadcasted_iota(jnp.int32, (128, 128), 0)
        target = lane_ids((128, 128))
        pick = jnp.where(
            (source // width == target // width) & (target % width < 2), 1.0, 0.0
        ).astype(BF)
        pick = jnp.concatenate([pick, pick], axis=0)
        for g in range(feats // 128):
            at = slice(128 * g, 128 * g + 128)
            values[:, 256 * g : 256 * g + 128] = qkv_ref[0, :, 2 * feats + 128 * g : 2 * feats + 128 * g + 128]
            values[:, 256 * g + 128 : 256 * g + 256] = ones
            product = dattn_ref[0, :, at].astype(F32) * attn_ref[0, :, at].astype(F32)
            high = product.astype(BF)
            rest = (product - high.astype(F32)).astype(BF)
            sums = dot(jnp.concatenate([high, rest], axis=1), pick, NN)
            coarse = sums.astype(BF)
            fine = (sums - coarse.astype(F32)).astype(BF)
            inner[:, at] = -jnp.where(lane % width == 0, coarse, fine)

    blocks = pl.ds(pl.multiple_of(group * 128, 128), 128)
    values_now = values[:, pl.ds(pl.multiple_of(group * 256, 256), 256)]
    dattn_now = dattn_ref[0, :, blocks]
    inner_now = inner[:, blocks]
    query_now = qkv_ref[0, :, blocks]
    head_of_lane = lane_ids((rows, 128)) // width
    zero = jnp.zeros((rows, 128), BF)
    dvalue = None
    dkey = None
    for h in range(per_group):
        mine = head_of_lane == h
        dattn_own = jnp.where(mine, dattn_now, zero)
        query_own = jnp.where(mine, query_now, zero)
        right = jnp.concatenate([dattn_own, jnp.where(mine, inner_now, zero)], axis=1)
        probs = probs_ref[0, h]
        dscore = probs * dot(values_now, right, NT).astype(BF)
        partial = dot(probs, dattn_own, NN)
        dvalue = partial if dvalue is None else dvalue + partial
        partial = dot(dscore, query_own, NN)
        dkey = partial if dkey is None else dkey + partial
        at = pl.ds(pl.multiple_of((group * per_group + h) * width, width), width)
        dquery_t[at, :] = (dot(keys_t[at, :], dscore, NN) * scale).astype(BF)
    dqkv[:, pl.ds(pl.multiple_of(2 * feats + group * 128, 128), 128)] = dvalue.astype(BF)
    dqkv[:, pl.ds(pl.multiple_of(feats + group * 128, 128), 128)] = (dkey * LN2).astype(BF)

    @pl.when(group == groups - 1)
    def _():
        first = pl.program_id(0) % per_clip == 0
        dqkv[:, :feats] = dquery_t[...].T
        dall = dqkv[...]
        normed, inverse = norm_stats(x_ref[0].astype(F32))
        low = (normed * gain_ref[...]).astype(BF)
        grad_reduced = dot(up_ref[0], dall, NT).astype(BF)
        slot = item // per_clip if remote_size else 0
        add_rows(grad_ref, slot, slice(feats, 4 * feats), dot(reduced_ref[0], dall, NN), first)
        add_rows(grad_ref, slot, slice(0, feats), dot(grad_reduced, low, NN), first)
        dlow = (dot(dall, weight_ref[...], NT) + dot(grad_reduced, down_ref[0], TN)).astype(BF)
        dx = (dx1_ref[0] + norm_back(dlow.astype(F32), gain_ref[...], normed, inverse)).astype(BF)
        if not remote_size:
            dx_ref[0] = dx
            return
        dx_own[item] = dx
        for i in range(items):

            @pl.when(item == i)
            def _():
                dx_rows.begin(i)

    if remote_size:

        @pl.when(step == 4 * items - 1)
        def _():
            share_gradients(
                place,
                (grad_ref, grad_dense_ref),
                ids_ref,
                (*share_refs, sums_ref),
                Sender(*sems),
                (
                    lambda: dx_rows.mix(items - 1),
                    lambda: None,
                    lambda: dx_rows.end(dx_out_ref),
                ),
            )


def whole(shape):
    return pl.BlockSpec(shape, lambda *at: (0,) * len(shape), pipeline_mode=pl.Buffered(1))


def compute(x, dy, adapter_ids, all_ids, vectors, qkv_parts, later, table, per_clip, remote_size):
    items, rows, feats = x.shape
    heads = table.shape[0]
    width = feats // heads
    per_group = 128 // width
    groups = heads // per_group
    scale = width**-0.5
    gain1, qkv_bias, proj_bias, gain2, fc1_bias, fc2_bias = vectors
    qkv_w, qkv_down, qkv_up = qkv_parts
    rank = qkv_down.shape[1]
    hidden = fc1_bias.shape[1]
    clips = items // per_clip

    def item(shape):
        return pl.BlockSpec((1, *shape), lambda i, *rest: (i,) + (0,) * len(shape))

    clip_ids = jnp.broadcast_to(adapter_ids.astype(F32)[:, None], (clips, 128))
    item_ids = adapter_ids
    any_space = pl.BlockSpec(memory_space=pl.ANY)

    def of_clip(shape):
        return pl.BlockSpec((1, *shape), lambda i, *rest: (i // per_clip, 0, 0))

    if remote_size:
        unit_shape = (768, 128)
        sent = (dy, *later)
        sent_out = [
            jax.ShapeDtypeStruct(dy.shape, BF),
            jax.ShapeDtypeStruct((2, remote_size, 2, *unit_shape), BF),
        ]
        sent_scratch = [
            pltpu.VMEM(unit_shape, BF),
            pltpu.VMEM(dy.shape, BF),
            pltpu.VMEM(dy.shape, BF),
            pltpu.VMEM((items, TOP, feats), BF),
            pltpu.SemaphoreType.DMA((Gather.COPIES,)),
            pltpu.SemaphoreType.DMA((Gather.COPIES,)),
            pltpu.SemaphoreType.DMA((2 * items,)),
            pltpu.SemaphoreType.DMA((2 * items,)),
            pltpu.SemaphoreType.DMA,
        ]
    else:
        sent, sent_out, sent_scratch = (), [], []
    probs, attn, qkv, reduced, down_own, up_own, *arrived = pl.pallas_call(
        functools.partial(
            attend_kernel,
            scale=scale,
            per_group=per_group,
            width=width,
            per_clip=per_clip,
            remote_size=remote_size,
        ),
        grid=(items, groups),
        in_specs=[
            item((rows, feats)),
            whole(gain1.shape),
            whole(qkv_w.shape),
            whole(qkv_bias.shape),
            whole(clip_ids.shape),
            whole(qkv_down.shape),
            whole(qkv_up.shape),
            any_space,
            *[whole(a.shape) for a in sent],
        ],
        out_specs=[
            pl.BlockSpec((1, per_group, rows, rows), lambda i, g: (i, g, 0, 0)),
            item((rows, feats)),
            item((rows, 3 * feats)),
            item((rank, rows)),
            of_clip((rank, feats)),
            of_clip((rank, 3 * feats)),
            *([whole(dy.shape), any_space] if remote_size else []),
        ],
        scratch_shapes=[
            pltpu.VMEM((rows, 2 * feats), BF),
            pltpu.VMEM((rows, feats), BF),
            pltpu.VMEM((feats, rows), BF),
            pltpu.VMEM((feats, rows), BF),
            pltpu.VMEM((2, rows, rows), F32),
            pltpu.VMEM(table.shape, F32),
            pltpu.SemaphoreType.DMA((groups,)),
            pltpu.VMEM((rows, 128), BF),
            *sent_scratch,
        ],
        out_shape=[
            jax.ShapeDtypeStruct((items, heads, rows, rows), BF),
            jax.ShapeDtypeStruct((items, rows, feats), BF),
            jax.ShapeDtypeStruct((items, rows, 3 * feats), BF),
            jax.ShapeDtypeStruct((items, rank, rows), BF),
            jax.ShapeDtypeStruct((clips, rank, feats), BF),
            jax.ShapeDtypeStruct((clips, rank, 3 * feats), BF),
            *sent_out,
        ],
        compiler_params=pltpu.CompilerParams(
            vmem_limit_bytes=VMEM_LIMIT,
            dimension_semantics=("arbitrary", "arbitrary"),
            **({"collective_id": 2, "has_side_effects": True} if remote_size else {}),
        ),
        cost_estimate=pl.CostEstimate(flops=4 * 10**10, bytes_accessed=10**7, transcendentals=0),
        name="attend",
    )(x, gain1, qkv_w, qkv_bias, clip_ids, qkv_down, qkv_up, table, *sent)
    if remote_size:
        dy, staged = arrived
    else:
        (staged,) = later

    span = 4 * feats + 2 * hidden
    def tile(n):
        def index(c, ids):
            return ids[c] // 2 % 2, 0, ids[c] // 4, 36 + 2 * n + ids[c] % 2, 0

        return pl.BlockSpec((1, 8, 1, rank, 128), index)

    def clip(array_shape):
        return pl.BlockSpec((per_clip, *array_shape[1:]), lambda c, ids: (c, 0, 0))

    chunk = 512
    act, dx1, dattn, grad_dense = pl.pallas_call(
        functools.partial(dense_kernel, per_clip=per_clip, chunk=chunk),
        grid_spec=pltpu.PrefetchScalarGridSpec(
            num_scalar_prefetch=1,
            grid=(clips,),
            in_specs=[
                clip(x.shape),
                clip(x.shape),
                whole(gain2.shape),
                whole(proj_bias.shape),
                whole(fc1_bias.shape),
                whole(fc2_bias.shape),
                clip(x.shape),
                any_space,
                *[tile(n) for n in range(6)],
            ],
            out_specs=[
                clip(x.shape),
                clip(x.shape),
                clip(x.shape),
                pl.BlockSpec((1, rank, span), lambda c, ids: (c, 0, 0)),
            ],
            scratch_shapes=[
                pltpu.VMEM((8, feats // 8, feats), BF),
                pltpu.VMEM((8, feats // 8, hidden), BF),
                pltpu.VMEM((8, hidden // 8, feats), BF),
                *[pltpu.VMEM((rank, n), BF) for n in (feats, feats, feats, hidden, hidden, feats)],
                pltpu.VMEM((2, per_clip * rows, chunk), F32),
                pltpu.VMEM((per_clip * rows, hidden), BF),
                pltpu.VMEM((per_clip * rows, hidden), BF),
                pltpu.SemaphoreType.DMA((24,)),
            ],
        ),
        out_shape=[
            jax.ShapeDtypeStruct((items, rows, feats), BF),
            jax.ShapeDtypeStruct((items, rows, feats), F32),
            jax.ShapeDtypeStruct((items, rows, feats), BF),
            jax.ShapeDtypeStruct((clips, rank, span), F32),
        ],
        compiler_params=pltpu.CompilerParams(
            vmem_limit_bytes=VMEM_LIMIT, dimension_semantics=("arbitrary",)
        ),
        cost_estimate=pl.CostEstimate(flops=5 * 10**10, bytes_accessed=10**7, transcendentals=0),
        name="dense",
    )(
        item_ids, x, attn, gain2, proj_bias, fc1_bias, fc2_bias, dy, staged, *([staged] * 6)
    )

    if remote_size:
        assert (clips, per_clip) == (2, 2)
        count = remote_size
        back_in = (act, grad_dense, all_ids)
        back_out = [whole(x.shape), whole(x.shape), whole((2, rank, 1024))]
        back_shape = [
            jax.ShapeDtypeStruct(x.shape, BF),
            jax.ShapeDtypeStruct(x.shape, BF),
            jax.ShapeDtypeStruct((2, rank, 1024), F32),
        ]
        sems = pltpu.SemaphoreType.DMA
        tops = pltpu.VMEM((items, TOP, feats), BF)
        row_scratch = [
            pltpu.VMEM(x.shape, BF),
            pltpu.VMEM(x.shape, BF),
            tops,
            sems((2 * items,)),
            sems((2 * items,)),
        ]
        back_scratch = [
            *row_scratch,
            pltpu.VMEM(x.shape, BF),
            *row_scratch,
            pltpu.VMEM((clips, rank, 4 * feats), F32),
            pltpu.VMEM((count, 16, 1024), F32),
            pltpu.VMEM((count, 16, 1024), BF),
            pltpu.VMEM((count, 16, 1024), BF),
            pltpu.VMEM((count, 16, 512), BF),
            pltpu.VMEM((count, 16, 512), BF),
            pltpu.VMEM((count, 16, 512), BF),
            pltpu.VMEM((count, 16, 512), BF),
            pltpu.VMEM((4, 16, 512), F32),
            pltpu.VMEM((4, 16, 512), F32),
            sems((16,)),
            sems((16,)),
        ]
    else:
        back_in, back_scratch = (), []
        back_out = [
            item((rows, feats)),
            pl.BlockSpec((1, rank, 4 * feats), lambda i, g: (i // per_clip, 0, 0)),
        ]
        back_shape = [
            jax.ShapeDtypeStruct((items, rows, feats), BF),
            jax.ShapeDtypeStruct((clips, rank, 4 * feats), F32),
        ]
    results = pl.pallas_call(
        functools.partial(
            attend_back_kernel,
            scale=scale,
            per_group=per_group,
            width=width,
            per_clip=per_clip,
            remote_size=remote_size,
        ),
        grid=(items, groups),
        in_specs=[
            item((rows, feats)),
            whole(gain1.shape),
            whole(qkv_w.shape),
            of_clip((rank, feats)),
            of_clip((rank, 3 * feats)),
            pl.BlockSpec((1, per_group, rows, rows), lambda i, g: (i, g, 0, 0)),
            item((rows, feats)),
            item((rows, 3 * feats)),
            item((rank, rows)),
            item((rows, feats)),
            item((rows, feats)),
            *[whole(a.shape) for a in back_in],
        ],
        out_specs=back_out,
        scratch_shapes=[
            pltpu.VMEM((rows, 2 * feats), BF),
            pltpu.VMEM((feats, rows), BF),
            pltpu.VMEM((rows, feats), BF),
            pltpu.VMEM((rows, 3 * feats), BF),
            pltpu.VMEM((feats, rows), BF),
            *back_scratch,
        ],
        out_shape=back_shape,
        compiler_params=pltpu.CompilerParams(
            vmem_limit_bytes=VMEM_LIMIT, dimension_semantics=("arbitrary", "arbitrary"),
            **({"collective_id": 1, "has_side_effects": True} if remote_size else {}),
        ),
        cost_estimate=pl.CostEstimate(flops=5 * 10**10, bytes_accessed=10**7, transcendentals=0),
        name="attend_back",
    )(x, gain1, qkv_w, down_own, up_own, probs, attn, qkv, reduced, dattn, dx1, *back_in)
    if remote_size:
        return results
    return (act, *results, grad_dense)


def spread_kernel(
    tok_ref, table_in_ref, qkv_ref, qd_ref, qu_ref, ids_in_ref,
    g1_ref, qb_ref, pb_ref, g2_ref, f1b_ref, f2b_ref,
    x_ref, weight_ref, down_ref, up_ref, gain1_ref, qkv_bias_ref, proj_bias_ref, gain2_ref, fc1_bias_ref,
    fc2_bias_ref, ids_ref, table_ref,
    unit_ref, vec_ref, pairs_ref,
    units, vecs, beside, mixed, tops, found, wide, select, bias,
    send_sem, recv_sem, unit_send, unit_recv, out_sem,
    *, clip_size,
):
    place = Place(clip_size)
    c, w, x, k = place.c, place.w, place.x, place.k
    sibling, across = place.sibling, place.across
    gather_units = Gather(place, unit_ref, units, unit_send, unit_recv)
    items, rows, feats = tok_ref.shape
    unit_ref[:, 0:384] = qkv_ref[...]
    for a in range(2):
        unit_ref[16 * a : 16 * a + 16, 384:448] = qd_ref[a]
        unit_ref[16 * a : 16 * a + 16, 448:512] = qu_ref[a, :, 0:64]
        unit_ref[32 + 16 * a : 48 + 16 * a, 384:512] = qu_ref[a, :, 64:192]
    vec_ref[0:1, 0:64] = g1_ref[...].astype(F32)
    vec_ref[0:1, 64:128] = qb_ref[:, 0:64].astype(F32)
    vec_ref[1:2, :] = qb_ref[:, 64:192].astype(F32)
    vec_ref[2:3, 0:64] = pb_ref[...].astype(F32)
    vec_ref[2:3, 64:128] = g2_ref[...].astype(F32)
    vec_ref[3:4, :] = f1b_ref[:, 0:128].astype(F32)
    vec_ref[4:5, :] = f1b_ref[:, 128:256].astype(F32)
    vec_ref[5:6, 0:64] = f2b_ref[...].astype(F32)
    vec_ref[5:6, 64:128] = ids_in_ref[:, 0:64]
    vec_ref[6:8, :] = jnp.zeros((2, 128), F32)
    enter([sibling, across] + [((c + d) % clip_size, w) for d in range(1, clip_size)])
    send = Sender(send_sem, recv_sem)
    units[k, c, x] = unit_ref[...]
    vecs[c] = vec_ref[...]
    gather_units.begin()
    tokens_beside = [send.copy(tok_ref.at[i], beside.at[i], sibling) for i in range(items)]
    vec_copies = [
        send.copy(vec_ref, vecs.at[c], ((c + d) % clip_size, w)) for d in range(1, clip_size)
    ]
    gather_units.second()
    early, low_h, low_w = row_masks(rows, feats)
    token_tops = []
    for i in range(items):
        tokens_beside[i].wait_recv()
        mixed[i] = jnp.where(low_h, beside[i], tok_ref[i])
        token_tops.append(send.copy(mixed.at[i, pl.ds(0, TOP)], tops.at[i], across))

    heads = pairs_ref.shape[0] // 15
    pairs_ref[...] = jnp.zeros(pairs_ref.shape, BF)
    for a in range(15):
        pairs_ref[a * heads : (a + 1) * heads, 0:169] = table_in_ref[:, 169 * a : 169 * a + 169]
    off_lane = lane_ids((pairs_ref.shape[1], 128))
    off_row = lax.broadcasted_iota(jnp.int32, (pairs_ref.shape[1], 128), 0)
    query_at = (off_lane // 7 + 4) % 7 * 13 + (off_lane % 7 + 4) % 7
    wanted = off_row - query_at - 84
    valid = off_lane < 49

    def one_key(key, carry):
        key_at = (key // 7 + 4) % 7 * 13 + (key % 7 + 4) % 7
        pick = jnp.where(valid & (wanted + key_at == 0), 1.0, 0.0).astype(BF)
        value = dot(pairs_ref[...], pick, NN)
        for a in range(15):
            found[a, pl.ds(key, heads, stride=56), :] = value[a * heads : (a + 1) * heads]
        return carry

    lax.fori_loop(0, 49, one_key, 0)

    gather_units.from_z(0)

    for a in range(15):
        wide[:, 128 * a : 128 * a + 128] = found[a].astype(BF)
    sel_row = lax.broadcasted_iota(jnp.int32, (128, rows), 0)
    sel_lane = lane_ids((128, rows))
    for t in range(8):
        select[128 * t : 128 * t + 128, :] = jnp.where(
            (sel_lane == sel_row + (t + 4) % 8 * 49) & (sel_row < 49), 1.0, 0.0
        ).astype(BF)

    gather_units.from_y(-1)
    gather_units.from_z(1)
    gather_units.from_y(0)
    for block in range(8):
        t = (block + 4) % 8
        value = dot(wide[:, (7 - t) * 128 : (15 - t) * 128], select[...], NN) * LOG2E
        for m in range(heads):
            bias[m, 49 * block : 49 * block + 49, :] = value[56 * m : 56 * m + 49]
    out = pltpu.make_async_copy(bias, table_ref, out_sem)
    out.start()
    gather_units.from_z(2)
    gather_units.from_y(1)

    for copy in vec_copies:
        copy.wait_recv()
    for c2 in range(clip_size):
        v = vecs[c2]
        gain1_ref[:, 64 * c2 : 64 * c2 + 64] = v[0:1, 0:64]
        qkv_bias_ref[:, 192 * c2 : 192 * c2 + 64] = v[0:1, 64:128]
        qkv_bias_ref[:, 192 * c2 + 64 : 192 * c2 + 192] = v[1:2, :]
        proj_bias_ref[:, 64 * c2 : 64 * c2 + 64] = v[2:3, 0:64]
        gain2_ref[:, 64 * c2 : 64 * c2 + 64] = v[2:3, 64:128]
        fc1_bias_ref[:, 256 * c2 : 256 * c2 + 128] = v[3:4, :]
        fc1_bias_ref[:, 256 * c2 + 128 : 256 * c2 + 256] = v[4:5, :]
        fc2_bias_ref[:, 64 * c2 : 64 * c2 + 64] = v[5:6, 0:64]
        for n in range(2):
            ids_ref[2 * c2 + n : 2 * c2 + n + 1, :] = jnp.broadcast_to(
                v[5:6, 64 + n : 65 + n], (1, ids_ref.shape[1])
            )

    gather_units.from_y(2)
    gather_units.finish()
    for c2 in range(clip_size):
        for x2 in range(2):
            for k2 in range(2):
                n = 2 * x2 + k2
                weight_ref[64 * c2 : 64 * c2 + 64, 384 * n : 384 * n + 384] = units[k2, c2, x2, :, 0:384]
                for a in range(2):
                    low = units[k2, c2, x2, 16 * a : 16 * a + 16, 384:512]
                    high = units[k2, c2, x2, 32 + 16 * a : 48 + 16 * a, 384:512]
                    down_ref[2 * n + a, :, 64 * c2 : 64 * c2 + 64] = low[:, 0:64]
                    up_ref[2 * n + a, :, 192 * c2 : 192 * c2 + 64] = low[:, 64:128]
                    up_ref[2 * n + a, :, 192 * c2 + 64 : 192 * c2 + 192] = high

    for i in range(0, items, 2):
        both = []
        for e in range(2):
            token_tops[i + e].wait_recv()
            both.append(with_top(mixed[i + e], tops[i + e], early))
        for e in range(2):
            x_ref[i + e] = jnp.where(low_w, both[1 - e], both[e])

    for copy in [*tokens_beside, *vec_copies, *token_tops]:
        copy.wait_send()
    out.wait()


def spread(tokens, table, qkv_w, qkv_down, qkv_up, ids, vecs, clip_size):
    items, rows, feats = tokens.shape
    heads = table.shape[0]
    f = functools.partial(jax.ShapeDtypeStruct)
    vm = pl.BlockSpec(memory_space=pltpu.VMEM)
    return pl.pallas_call(
        functools.partial(spread_kernel, clip_size=clip_size),
        in_specs=[vm] * 12,
        out_specs=[vm] * 11 + [pl.BlockSpec(memory_space=pl.ANY)],
        out_shape=[
            f((items, rows, feats), BF),
            f((512, 1536), BF),
            f((8, 16, 512), BF),
            f((8, 16, 1536), BF),
            f((1, 512), F32),
            f((1, 1536), F32),
            f((1, 512), F32),
            f((1, 512), F32),
            f((1, 2048), F32),
            f((1, 512), F32),
            f((16, 512), F32),
            f((heads, rows, rows), F32),
        ],
        scratch_shapes=[
            pltpu.VMEM((64, 512), BF),
            pltpu.VMEM((8, 128), F32),
            pltpu.VMEM((15 * heads, 176), BF),
            pltpu.VMEM((2, clip_size, 2, 64, 512), BF),
            pltpu.VMEM((clip_size, 8, 128), F32),
            pltpu.VMEM((items, rows, feats), BF),
            pltpu.VMEM((items, rows, feats), BF),
            pltpu.VMEM((items, TOP, feats), BF),
            pltpu.VMEM((15, 56 * heads, 128), F32),
            pltpu.VMEM((56 * heads, 15 * 128), BF),
            pltpu.VMEM((8 * 128, rows), BF),
            pltpu.VMEM((heads, rows, rows), F32),
            pltpu.SemaphoreType.DMA((16,)),
            pltpu.SemaphoreType.DMA((16,)),
            pltpu.SemaphoreType.DMA((Gather.COPIES,)),
            pltpu.SemaphoreType.DMA((Gather.COPIES,)),
            pltpu.SemaphoreType.DMA,
        ],
        compiler_params=pltpu.CompilerParams(
            collective_id=0, has_side_effects=True, vmem_limit_bytes=VMEM_LIMIT
        ),
        cost_estimate=pl.CostEstimate(flops=3 * 10**10, bytes_accessed=2 * 10**7, transcendentals=0),
        name="spread",
    )(tokens, table, qkv_w, qkv_down, qkv_up, ids, *vecs)


def exchange(x, win_size):
    local = x.shape[1]
    bits = local.bit_length() - 1
    at = jnp.arange(TOK)
    taken = (at // 49 < 4, at // 7 % 7 < 3, at % 7 < 3)
    for bit, rows in zip((2, 1, 0), taken):
        if bit < bits:
            split = x.reshape(x.shape[0], local >> (bit + 1), 2, 1 << bit, TOK, -1)
            other = jnp.flip(split, axis=2).reshape(x.shape)
        else:
            other = lax.ppermute(x, "win", [(i, i ^ 1 << bit - bits) for i in range(win_size)])
        x = jnp.where(rows[None, None, :, None], other, x)
    return x


def bias_by_pair(table):
    heads = table.shape[0]
    side = jnp.arange(49)
    high, wide = (side // 7 + 4) % 7, (side % 7 + 4) % 7
    offset = (high[None, :] - high[:, None] + 6) * 13 + wide[None, :] - wide[:, None] + 6
    pick = (jnp.arange(169)[:, None, None] == offset[None]).astype(BF)
    found = jnp.einsum(
        "mad,dkq->mkaq", table.reshape(heads, 15, 169), pick, preferred_element_type=F32
    )
    found = (found * LOG2E).reshape(heads, 49, 15 * 49)
    blocks = []
    for key_block in range(8):
        t = (key_block + 4) % 8
        blocks.append(
            jnp.concatenate(
                (found[..., (11 - t) * 49 : (15 - t) * 49], found[..., (7 - t) * 49 : (11 - t) * 49]),
                axis=-1,
            )
        )
    return jnp.stack(blocks, axis=1).reshape(heads, TOK, TOK)


def gather(array, spec):
    for axis, name in enumerate(spec):
        if name is not None:
            array = lax.all_gather(array, name, axis=axis, tiled=True)
    return array


def stage_whole(proj_w, fc1_w, fc2_w, maps):
    proj_down, proj_up, fc1_down, fc1_up, fc2_down, fc2_up = maps
    count = proj_down.shape[0]

    def short(a):
        return a.reshape(4, count // 4 * 16, 8, 64).transpose(2, 0, 1, 3)

    def long(a):
        return a.reshape(4, count // 4 * 16, 8, 2, 128).transpose(2, 0, 3, 1, 4).reshape(8, 4, -1, 128)

    return jnp.concatenate(
        (
            proj_w.reshape(8, 64, 4, 128).transpose(0, 2, 1, 3),
            fc1_w.reshape(8, 64, 4, 4, 128).transpose(0, 2, 3, 1, 4).reshape(8, 4, 256, 128),
            fc2_w.reshape(8, 256, 4, 128).transpose(0, 2, 1, 3),
            jnp.concatenate((short(proj_down), short(proj_up)), axis=-1),
            jnp.concatenate((short(fc1_down), short(fc2_up)), axis=-1),
            long(fc1_up),
            long(fc2_down),
        ),
        axis=2,
    )


def by_core(staged):
    return staged.reshape(8, 2, 2, *staged.shape[2:]).transpose(2, 0, 1, 3, 4)


def per_device(
    tokens, cotangent, adapter_ids, ln1_gain, qkv_weight, qkv_bias, proj_weight, proj_bias, ln2_gain,
    fc1_weight, fc1_bias, fc2_weight, fc2_bias, bias_table, qkv_down, qkv_up, proj_down, proj_up,
    fc1_down, fc1_up, fc2_down, fc2_up, *, clip_size, win_size,
):
    clips, local, rows, feats = tokens.shape
    items = clips * local
    heads = bias_table.shape[0]
    vecs = (ln1_gain, qkv_bias, proj_bias, ln2_gain, fc1_bias, fc2_bias)
    flat = (items, rows, feats)
    downs = [a.transpose(0, 2, 1) for a in (qkv_down, proj_down, fc1_down, fc2_down)]
    own_kernels = (clip_size, win_size, clips, local) == (8, 4, 2, 2)
    if own_kernels:
        rows_of_ids = jnp.pad(adapter_ids.astype(F32)[None], ((0, 0), (0, 126)))
        x, qkv_w, down, up, *vectors, ids, table = spread(
            tokens.reshape(flat), bias_table, qkv_weight, downs[0], qkv_up, rows_of_ids,
            [v.reshape(1, -1) for v in vecs], clip_size,
        )
        dy = cotangent.reshape(flat)
        qkv_parts = (qkv_w, down, up)
        later = (proj_weight, fc1_weight, fc2_weight, downs[1], proj_up, downs[2], fc1_up, downs[3], fc2_up)
    else:
        grid2, by_down, by_up = ("clip", "win"), ("win", None, "clip"), ("win", None, "clip")
        qkv_parts = (gather(qkv_weight, grid2), gather(downs[0], by_down), gather(qkv_up, by_up))
        maps = (downs[1], proj_up, downs[2], fc1_up, downs[3], fc2_up)
        staged = stage_whole(
            *[gather(a, grid2) for a in (proj_weight, fc1_weight, fc2_weight)],
            [gather(a, by_up) for a in maps],
        )
        later = (by_core(staged),)
        vectors = [gather(v, ("clip",)).reshape(1, -1).astype(F32) for v in vecs]
        table, ids = bias_by_pair(bias_table), None
        x = exchange(tokens, win_size).reshape(flat)
        dy = exchange(cotangent, win_size).reshape(flat)
    results = compute(
        x, dy, adapter_ids, ids, vectors, qkv_parts, later, table, local,
        clip_size if own_kernels else 0,
    )
    if own_kernels:
        act_out, dx_out, sums = results
        qd, qu, pd, pu, f1d, f2u, f1u, f2d = [
            sums[..., first:last]
            for first, last in zip(
                (0, 64, 256, 320, 384, 448, 512, 768), (64, 256, 320, 384, 448, 512, 768, 1024)
            )
        ]
        turned = [a.transpose(0, 2, 1) for a in (qd, pd, f1d, f2d)]
        return (
            act_out.reshape(tokens.shape), dx_out.reshape(tokens.shape),
            turned[0], qu, turned[1], pu, turned[2], f1u, turned[3], f2u,
        )
    act, dx, grad_qkv, grad_dense = results
    activations = exchange(act.reshape(tokens.shape), win_size)
    input_grad = exchange(dx.reshape(tokens.shape), win_size)
    adapter_count = win_size * qkv_down.shape[0]
    hot = (adapter_ids[:, None] == jnp.arange(adapter_count)[None]).astype(F32)
    hidden = fc1_weight.shape[1] * win_size
    spans = (feats, 3 * feats, feats, feats, feats, hidden, hidden, feats)
    grads = jnp.concatenate((grad_qkv, grad_dense), axis=-1)
    rank = grads.shape[1]
    parts, at = [], 0
    for span in spans:
        parts.append(
            grads[..., at : at + span].reshape(clips, rank, clip_size, span // clip_size)
        )
        at += span
    mine = jnp.concatenate(parts, axis=-1)
    grown = jnp.sum(hot[:, :, None, None, None] * mine[:, None], axis=0)
    grown = grown.transpose(2, 0, 1, 3).astype(BF)
    total = lax.psum_scatter(grown, "clip", scatter_dimension=0, tiled=True)[0]
    total = lax.psum_scatter(total, "win", scatter_dimension=0, tiled=True).astype(F32)
    outs, at = [], 0
    for n, span in enumerate(spans):
        width = span // clip_size
        part = total[..., at : at + width]
        at += width
        outs.append(part.transpose(0, 2, 1) if n % 2 == 0 else part)
    return (activations, input_grad, *outs)


def solution(mesh):
    split = P("clip", "win", None, None)
    grid2 = P("clip", "win")
    down = P("win", "clip", None)
    up = P("win", None, "clip")
    one = P("clip")
    return jax.shard_map(
        functools.partial(
            per_device, clip_size=mesh.shape["clip"], win_size=mesh.shape["win"]
        ),
        mesh=mesh,
        in_specs=(
            split, split, one, one, grid2, one, grid2, one, one, grid2, one, grid2, one, P(),
            down, up, down, up, down, up, down, up,
        ),
        out_specs=(split, split, down, up, down, up, down, up, down, up),
        check_vma=False,
    )
```

```python
import functools
import jax
import jax.numpy as jnp
from jax import lax
from jax.experimental import pallas as pl
from jax.experimental.pallas import tpu as pltpu
from jax.sharding import PartitionSpec as P

BF = jnp.bfloat16
F32 = jnp.float32
NN = (((1,), (0,)), ((), ()))
NT = (((1,), (1,)), ((), ()))
TN = (((0,), (0,)), ((), ()))
LOG2E = 1.4426950408889634
LN2 = 0.6931471805599453
FAR = 1e9
VMEM_LIMIT = 60 * 2**20
TOK = 392
TOP = 208


def dot(left, right, dims):
    return lax.dot_general(left, right, dims, preferred_element_type=F32)


def lane_ids(shape):
    return lax.broadcasted_iota(jnp.int32, shape, len(shape) - 1)


def norm_stats(values):
    average = jnp.mean(values, axis=-1, keepdims=True)
    centred = values - average
    variance = jnp.mean(centred * centred, axis=-1, keepdims=True)
    inverse = lax.rsqrt(variance + 1e-05)
    return centred * inverse, inverse


def norm_back(gradient, gain, normed, inverse):
    scaled = gradient * gain
    centre = jnp.mean(scaled, axis=-1, keepdims=True)
    slope = jnp.mean(scaled * normed, axis=-1, keepdims=True)
    return inverse * (scaled - centre - normed * slope)


def add_rows(ref, n, at, value, first):
    @pl.when(first)
    def _():
        ref[n, :, at] = value

    @pl.when(jnp.logical_not(first))
    def _():
        ref[n, :, at] += value


MESH = pl.DeviceIdType.MESH


def enter(peers):
    barrier = pltpu.get_barrier_semaphore()
    for peer in peers:
        pl.semaphore_signal(barrier, inc=1, device_id=peer, device_id_type=MESH)
    pl.semaphore_wait(barrier, len(peers))


def remote(src, dst, send_sem, recv_sem, peer):
    return pltpu.make_async_remote_copy(
        src_ref=src,
        dst_ref=dst,
        send_sem=send_sem,
        recv_sem=recv_sem,
        device_id=peer,
        device_id_type=MESH,
    )


class Sender:
    def __init__(self, send_sem, recv_sem):
        self.send_sem, self.recv_sem, self.count = send_sem, recv_sem, 0

    def copy(self, src, dst, peer):
        n = self.count
        self.count += 1
        made = remote(src, dst, self.send_sem.at[n], self.recv_sem.at[n], peer)
        made.start()
        return made


def row_masks(rows):
    row = lax.broadcasted_iota(jnp.int32, (rows, 128), 0)
    return row < TOK // 2, row % 49 < 21, row % 7 < 3


def choose(mask, first, second):
    return jnp.concatenate(
        [
            jnp.where(mask, first[:, at : at + 128], second[:, at : at + 128])
            for at in range(0, first.shape[1], 128)
        ],
        axis=1,
    )


class Rows:
    def __init__(self, place, own, beside, mixed, tops, send_sem, recv_sem):
        self.place, self.own, self.beside, self.mixed, self.tops = place, own, beside, mixed, tops
        self.send_sem, self.recv_sem = send_sem, recv_sem
        self.items, self.rows, self.feats = own.shape

    def copy(self, kind, i):
        n = kind * self.items + i
        sems = self.send_sem.at[n], self.recv_sem.at[n]
        if kind == 0:
            return remote(self.own.at[i], self.beside.at[i], *sems, self.place.sibling)
        top = self.mixed.at[i, pl.ds(0, TOP)]
        return remote(top, self.tops.at[i], *sems, self.place.across)

    def begin(self, i):
        self.copy(0, i).start()

    def mix(self, i):
        self.copy(0, i).wait_recv()
        self.mixed[i] = choose(row_masks(self.rows)[1], self.beside[i], self.own[i])
        self.copy(1, i).start()

    def end(self, out, i):
        early, _, low_w = row_masks(self.rows)
        both = []
        for e in range(2):
            self.copy(1, i + e).wait_recv()
            top = choose(early[:TOP], self.tops[i + e], self.mixed[i + e, :TOP])
            both.append(jnp.concatenate([top, self.mixed[i + e, TOP:]], axis=0))
        for e in range(2):
            out[i + e] = choose(low_w, both[1 - e], both[e])

    def drain(self):
        for i in range(self.items):
            self.copy(0, i).wait_send()
            self.copy(1, i).wait_send()


class Place:
    def __init__(self, clip_size):
        self.c, self.w = lax.axis_index("clip"), lax.axis_index("win")
        self.z, self.y = self.c // 2, self.c % 2
        self.x, self.k = self.w // 2, self.w % 2
        self.zs = clip_size // 2
        self.sibling = (self.c, self.x * 2 + 1 - self.k)
        self.across = (self.c, (1 - self.x) * 2 + self.k)

    def clip_at(self, z_step, other_y):
        return (self.z + z_step + self.zs) % self.zs * 2 + (1 - self.y if other_y else self.y)

    def along_z(self, step):
        return (self.clip_at(step, False), self.w)

    def along_y(self):
        return (self.clip_at(0, True), self.w)


class Gather:
    COPIES = 29

    def __init__(self, place, unit, units, send_sem, recv_sem):
        self.place, self.unit, self.units = place, unit, units
        self.send_sem, self.recv_sem = send_sem, recv_sem
        self.hops = range(place.zs - 1)

    def make(self, kind, t=0):
        p, units = self.place, self.units
        kinds = ("up", "down", "y_up", "y_down", "s_up", "s_down", "sy_up", "sy_down")
        single = ("across", "own", "theirs", "y", "s_y")
        n = single.index(kind) if kind in single else 5 + 8 * t + kinds.index(kind)
        sems = self.send_sem.at[n], self.recv_sem.at[n]
        mine = units.at[p.k, p.c, p.x]
        if kind == "across":
            return remote(self.unit, mine, *sems, p.across)
        if kind == "own":
            return remote(self.unit, mine, *sems, p.sibling)
        if kind == "theirs":
            part = units.at[p.k, p.c, 1 - p.x]
        elif kind == "y":
            part = units.at[p.k, p.c]
        elif kind == "s_y":
            part = units.at[p.k, p.z * 2 + 1 - p.y]
        else:
            sign = -1 if kind.endswith("up") else 1
            far = p.z + sign * (t if kind in ("up", "down") else t + 1)
            part = units.at[p.k, far * 2 + (1 - p.y if kind.startswith("sy") else p.y)]
        if kind in ("up", "down"):
            peer = (p.c - 2 * sign, p.w)
        else:
            peer = p.along_y() if kind.startswith("y") else p.sibling
        return remote(part, part, *sems, peer)

    def when(self, kind, t, sending, act):
        p, last = self.place, self.place.zs - 1
        if kind.endswith("up"):
            holds = (p.z >= t) & (p.z < last) if sending and kind == "up" else p.z >= t + 1
        elif kind.endswith("down"):
            holds = (p.z <= last - t) & (p.z > 0) if sending and kind == "down" else p.z <= last - 1 - t
        else:
            act()
            return
        pl.when(holds)(act)

    def start(self, kind, t=0):
        self.when(kind, t, True, lambda: self.make(kind, t).start())

    def wait_recv(self, kind, t=0):
        self.when(kind, t, False, lambda: self.make(kind, t).wait_recv())

    def wait_send(self, kind, t=0):
        self.when(kind, t, True, lambda: self.make(kind, t).wait_send())

    def begin(self):
        self.start("across")
        self.start("own")

    def second(self):
        self.wait_recv("across")
        for kind in ("up", "down", "y", "theirs"):
            self.start(kind)

    def from_z(self, t):
        for way in ("up", "down"):
            self.wait_recv(way, t)
            if t + 1 in self.hops:
                self.start(way, t + 1)
            self.start("y_" + way, t)
            self.start("s_" + way, t)

    def from_y(self, t):
        if t < 0:
            self.wait_recv("y")
            self.start("s_y")
        else:
            for way in ("up", "down"):
                self.wait_recv("y_" + way, t)
                self.start("sy_" + way, t)

    def finish(self):
        for kind in ("own", "theirs", "s_y"):
            self.wait_recv(kind)
        for t in self.hops:
            for kind in ("s_up", "s_down", "sy_up", "sy_down"):
                self.wait_recv(kind, t)
        for kind in ("across", "own", "theirs", "y", "s_y"):
            self.wait_send(kind)
        for t in self.hops:
            for kind in ("up", "down", "y_up", "y_down", "s_up", "s_down", "sy_up", "sy_down"):
                self.wait_send(kind, t)


def pack_first(unit, vec, qkv_ref, qd_ref, qu_ref, ids_ref, vec_refs):
    unit[:, 0:384] = qkv_ref[...]
    for a in range(2):
        unit[16 * a : 16 * a + 16, 384:448] = qd_ref[a]
        unit[16 * a : 16 * a + 16, 448:512] = qu_ref[a, :, 0:64]
        unit[32 + 16 * a : 48 + 16 * a, 384:512] = qu_ref[a, :, 64:192]
    g1_ref, qb_ref, pb_ref, g2_ref, f1b_ref, f2b_ref = vec_refs
    vec[0:1, 0:64] = g1_ref[...].astype(F32)
    vec[0:1, 64:128] = qb_ref[:, 0:64].astype(F32)
    vec[1:2, :] = qb_ref[:, 64:192].astype(F32)
    vec[2:3, 0:64] = pb_ref[...].astype(F32)
    vec[2:3, 64:128] = g2_ref[...].astype(F32)
    vec[3:4, :] = f1b_ref[:, 0:128].astype(F32)
    vec[4:5, :] = f1b_ref[:, 128:256].astype(F32)
    vec[5:6, 0:64] = f2b_ref[...].astype(F32)
    vec[5:6, 64:128] = ids_ref[:, 0:64]
    vec[6:8, :] = jnp.zeros((2, 128), F32)


def unpack_vectors(vecs, outs):
    gain1, qkv_bias, proj_bias, gain2, fc1_bias, fc2_bias, ids = outs
    for c in range(vecs.shape[0]):
        v = vecs[c]
        short = slice(64 * c, 64 * c + 64)
        gain1[:, short] = v[0:1, 0:64]
        qkv_bias[:, 192 * c : 192 * c + 64] = v[0:1, 64:128]
        qkv_bias[:, 192 * c + 64 : 192 * c + 192] = v[1:2, :]
        proj_bias[:, short] = v[2:3, 0:64]
        gain2[:, short] = v[2:3, 64:128]
        fc1_bias[:, 256 * c : 256 * c + 128] = v[3:4, :]
        fc1_bias[:, 256 * c + 128 : 256 * c + 256] = v[4:5, :]
        fc2_bias[:, short] = v[5:6, 0:64]
        for n in range(2):
            ids[2 * c + n : 2 * c + n + 1, :] = jnp.broadcast_to(
                v[5:6, 64 + n : 65 + n], (1, ids.shape[1])
            )


def unpack_first(units, weight, down, up):
    for c in range(units.shape[1]):
        for n in range(4):
            unit = units.at[n % 2, c, n // 2]
            weight[64 * c : 64 * c + 64, 384 * n : 384 * n + 384] = unit[:, 0:384]
            for a in range(2):
                low = unit[16 * a : 16 * a + 16, 384:512]
                high = unit[32 + 16 * a : 48 + 16 * a, 384:512]
                down[2 * n + a, :, 64 * c : 64 * c + 64] = low[:, 0:64]
                up[2 * n + a, :, 192 * c : 192 * c + 64] = low[:, 64:128]
                up[2 * n + a, :, 192 * c + 64 : 192 * c + 192] = high


def pack_second(unit, refs):
    proj_ref, fc1_ref, fc2_ref, pd_ref, pu_ref, f1d_ref, f1u_ref, f2d_ref, f2u_ref = refs
    unit[0:64] = proj_ref[...]
    for t in range(4):
        unit[64 + 64 * t : 128 + 64 * t] = fc1_ref[:, 128 * t : 128 * t + 128]
    unit[320:576] = fc2_ref[...]
    for a in range(2):
        at = 576 + 16 * a
        unit[at : at + 16, 0:64] = pd_ref[a]
        unit[at : at + 16, 64:128] = pu_ref[a]
        unit[at + 32 : at + 48, 0:64] = f1d_ref[a]
        unit[at + 32 : at + 48, 64:128] = f2u_ref[a]
        for half in range(2):
            lanes = slice(128 * half, 128 * half + 128)
            unit[at + 64 + 32 * half : at + 80 + 32 * half] = f1u_ref[a, :, lanes]
            unit[at + 128 + 32 * half : at + 144 + 32 * half] = f2d_ref[a, :, lanes]


class Bias:
    def __init__(self, source, table, pairs, found, wide, select):
        self.source, self.table, self.pairs, self.found = source, table, pairs, found
        self.wide, self.select = wide, select
        self.heads = source.shape[0]

    def prepare(self):
        heads, pairs = self.heads, self.pairs
        pairs[...] = jnp.zeros(pairs.shape, BF)
        for a in range(15):
            pairs[a * heads : (a + 1) * heads, 0:169] = self.source[:, 169 * a : 169 * a + 169]

    def first(self, start, end):
        heads, pairs, found = self.heads, self.pairs, self.found
        lane = lane_ids((pairs.shape[1], 128))
        row = lax.broadcasted_iota(jnp.int32, (pairs.shape[1], 128), 0)
        query_at = (lane // 7 + 4) % 7 * 13 + (lane % 7 + 4) % 7
        wanted = jnp.where(lane < 49, row - query_at - 84, 10000)

        def one_key(key, carry):
            key_at = (key // 7 + 4) % 7 * 13 + (key % 7 + 4) % 7
            pick = jnp.where(wanted + key_at == 0, 1.0, 0.0).astype(BF)
            value = dot(pairs[...], pick, NN)
            for a in range(15):
                found[a, pl.ds(key, heads, stride=56), :] = value[a * heads : (a + 1) * heads]
            return carry

        lax.fori_loop(start, end, one_key, 0, unroll=7)

    def middle(self):
        for a in range(15):
            self.wide[:, 128 * a : 128 * a + 128] = self.found[a].astype(BF)
        row = lax.broadcasted_iota(jnp.int32, (128, TOK), 0)
        gap = lane_ids((128, TOK)) - row
        for t in range(8):
            self.select[128 * t : 128 * t + 128, :] = jnp.where(
                (gap == (t + 4) % 8 * 49) & (row < 49), 1.0, 0.0
            ).astype(BF)

    def last(self, blocks):
        for block in blocks:
            t = (block + 4) % 8
            value = dot(self.wide[:, (7 - t) * 128 : (15 - t) * 128], self.select[...], NN) * LOG2E
            for m in range(self.heads):
                self.table[m, 49 * block : 49 * block + 49, :] = value[56 * m : 56 * m + 49]


def attend_kernel(*refs, scale, per_group, width, per_clip, remote_size):
    if remote_size:
        tok_ref, source_ref, *refs = refs
        first_refs, vec_refs, refs = refs[:4], refs[4:10], refs[10:]
        dy_ref, second_refs, refs = refs[0], refs[1:10], refs[10:]
    else:
        x_ref, gain_ref, weight_ref, bias_ref, ids_ref, down_ref, up_ref, table_ref, *refs = refs
    probs_ref, out_ref, qkv_ref, reduced_ref, down_own, up_own, *refs = refs
    if remote_size:
        dy_out_ref, units_ref, x_ref, weight_ref, gain_ref, *vec_outs, ids_ref = refs[:10]
        refs = refs[10:]
    keys, queries, values_t, out_t, scores, table, table_sem, query_mask, *refs = refs
    group = pl.program_id(1)
    groups = pl.num_programs(1)
    item = pl.program_id(0)
    step = item * groups + group
    feats = x_ref.shape[-1]
    rows = x_ref.shape[1]

    if remote_size:
        bias_ref, down_ref, up_ref, unit1, vec, unit2, units1, vecs, *refs = refs
        bias = Bias(source_ref, table, *refs[:4])
        place = Place(remote_size)
        x_rows = Rows(place, tok_ref, *refs[4:9])
        dy_rows = Rows(place, dy_ref, *refs[9:14])
        gather1 = Gather(place, unit1, units1, *refs[14:16])
        gather2 = Gather(place, unit2, units_ref, *refs[16:18])
        vec_send, vec_recv, own_sem = refs[18:]
        items = dy_ref.shape[0]

        def vec_copy(d):
            to = ((place.c + d) % remote_size, place.w)
            return remote(vec, vecs.at[place.c], vec_send.at[d], vec_recv.at[d], to)

        @pl.when(step == 0)
        def _():
            pack_first(unit1, vec, *first_refs, vec_refs)
            pack_second(unit2, second_refs)
            mine = place.k, place.c, place.x
            units1[mine] = unit1[...]
            vecs[place.c] = vec[...]
            own = pltpu.make_async_copy(unit2, units_ref.at[mine], own_sem)
            own.start()
            enter(
                [place.sibling, place.across]
                + [((place.c + d) % remote_size, place.w) for d in range(1, remote_size)]
            )
            gather1.begin()
            for i in range(items):
                x_rows.begin(i)
            for d in range(1, remote_size):
                vec_copy(d).start()
            bias.prepare()
            gather1.second()
            for i in range(items):
                x_rows.mix(i)
            bias.first(0, 14)
            gather1.from_z(0)
            bias.first(14, 28)
            gather1.from_y(-1)
            gather1.from_z(1)
            bias.first(28, 49)
            gather1.from_y(0)
            gather1.from_z(2)
            bias.middle()
            gather1.from_y(1)
            bias.last(range(0, 4))
            gather1.from_y(2)
            own.wait()
            gather2.begin()
            bias.last(range(4, 8))
            for d in range(1, remote_size):
                vec_copy(d).wait_recv()
            unpack_vectors(vecs, (gain_ref, bias_ref, *vec_outs, ids_ref))
            gather1.finish()
            unpack_first(units1, weight_ref, down_ref, up_ref)
            x_rows.end(x_ref, 0)
            gather2.second()
            for d in range(1, remote_size):
                vec_copy(d).wait_send()

        @pl.when(step == 1)
        def _():
            for i in range(items):
                dy_rows.begin(i)

        @pl.when(step == 3)
        def _():
            for i in range(items):
                dy_rows.mix(i)

        for n in range(2, items, 2):

            @pl.when(step == 4 * n)
            def _():
                x_rows.end(x_ref, n)

        for t, at in enumerate((4, 8, 11)):

            @pl.when(step == at)
            def _():
                gather2.from_z(t)

        for t, at in ((-1, 5), (0, 9), (1, 12), (2, 15)):

            @pl.when(step == at)
            def _():
                gather2.from_y(t)

        @pl.when(step == 4 * items - 1)
        def _():
            for i in range(0, items, 2):
                dy_rows.end(dy_out_ref, i)
            gather2.finish()
            x_rows.drain()
            dy_rows.drain()

    else:

        def table_copy(g):
            at = pl.ds(g * per_group, per_group)
            return pltpu.make_async_copy(table_ref.at[at], table.at[at], table_sem.at[g])

        @pl.when(step == 0)
        def _():
            for g in range(table.shape[0] // per_group):
                table_copy(g).start()

    @pl.when((group == 0) & (item % per_clip == 0))
    def _():
        clip = item // per_clip
        if remote_size:
            clip = clip + place.c * 2
        ids = ids_ref[...]
        row = lax.broadcasted_iota(jnp.int32, ids.shape, 0)
        mine = jnp.sum(jnp.where(row == clip, ids, 0.0), axis=0, keepdims=True)[:, 0:1]
        for ref, target in ((down_ref, down_own), (up_ref, up_own)):
            total = jnp.zeros(ref.shape[1:], F32)
            for a in range(ref.shape[0]):
                total = total + jnp.where(
                    mine == float(a), ref[a].astype(F32), 0.0
                )
            target[0] = total.astype(BF)

    @pl.when(group == 0)
    def _():
        number = lax.axis_index("win") * per_clip + item % per_clip
        early, low_h, low_w = row_masks(rows)
        label = (
            jnp.where(early, number // 4 % 2 * 4, 0)
            + jnp.where(low_h, number // 2 % 2 * 2, 0)
            + jnp.where(low_w, number % 2, 0)
        )
        lane = lane_ids((rows, 128))
        same = label == lane
        key_mask = jnp.where(same, 1.0, 0.0).astype(BF)
        query_mask[...] = jnp.where(same | (lane >= 8), 0.0, -FAR).astype(BF)
        normed, _ = norm_stats(x_ref[item if remote_size else 0].astype(F32))
        low = (normed * gain_ref[...]).astype(BF)
        reduced = dot(down_own[0], low, NT).astype(BF)
        reduced_ref[0] = reduced

        def columns(part):
            at = pl.ds(part * feats, feats)
            return (
                dot(low, weight_ref[:, at], NN)
                + bias_ref[:, at]
                + dot(reduced, up_own[0, :, at], TN)
            )

        query = (columns(0) * (scale * LOG2E)).astype(BF)
        queries[...] = query
        qkv_ref[0, :, :feats] = query
        key = columns(1).astype(BF)
        qkv_ref[0, :, feats : 2 * feats] = key
        for g in range(feats // 128):
            keys[:, 256 * g : 256 * g + 128] = key[:, 128 * g : 128 * g + 128]
            keys[:, 256 * g + 128 : 256 * g + 256] = key_mask
        value = columns(2).astype(BF)
        qkv_ref[0, :, 2 * feats :] = value
        values_t[...] = value.T

    if not remote_size:

        @pl.when(item == 0)
        def _():
            table_copy(group).wait()

    keys_now = keys[:, pl.ds(pl.multiple_of(group * 256, 256), 256)]
    query_now = queries[:, pl.ds(pl.multiple_of(group * 128, 128), 128)]
    head_of_lane = lane_ids(query_now.shape) // width

    def raw(h):
        own = jnp.where(head_of_lane == h, query_now, jnp.zeros_like(query_now))
        own = jnp.concatenate([own, query_mask[...]], axis=1)
        return dot(keys_now, own, NT) + table[group * per_group + h]

    def finish(h):
        score = scores[h % 2]
        largest = jnp.max(score, axis=0, keepdims=True)
        probs = jnp.exp2(score - largest)
        total = jnp.sum(probs, axis=0, keepdims=True)
        probs = (probs * (1.0 / total)).astype(BF)
        probs_ref[0, h] = probs
        at = pl.ds(pl.multiple_of((group * per_group + h) * width, width), width)
        out_t[at, :] = dot(values_t[at, :], probs, NN).astype(BF)

    scores[0] = raw(0)
    for h in range(per_group):
        if h + 1 < per_group:
            scores[(h + 1) % 2] = raw(h + 1)
        finish(h)

    @pl.when(group == groups - 1)
    def _():
        out_ref[0] = out_t[...].T


def dense_kernel(
    ids_ref,
    x_ref,
    attn_ref,
    gain_ref,
    proj_bias_ref,
    fc1_bias_ref,
    fc2_bias_ref,
    dy_ref,
    staged_ref,
    *refs,
    per_clip,
    chunk,
):
    tiles, refs = refs[:6], refs[6:]
    act_ref, dx1_ref, dattn_ref, grad_ref, *refs = refs
    proj_ref, fc1_ref, fc2_ref, proj_down, proj_up, fc1_down, fc1_up, fc2_down, fc2_up, *refs = refs
    pres, acts, dpres, sem = refs
    starting = pl.program_id(0) == 0
    count = x_ref.shape[1]
    feats = x_ref.shape[-1]
    hidden = fc1_ref.shape[-1]

    def moves(first=0, last=24):
        found = [(0, 64, proj_ref, 128 * n, n) for n in range(4)]
        found += [(64 + 64 * t, 64, fc1_ref, 512 * n + 128 * t, n) for n in range(4) for t in range(4)]
        found += [(320, 256, fc2_ref, 128 * n, n) for n in range(4)]
        return [
            pltpu.make_async_copy(
                staged_ref.at[n % 2, :, n // 2, pl.ds(start, size), :],
                target.at[:, :, pl.ds(lane, 128)],
                sem.at[at],
            )
            for at, (start, size, target, lane, n) in enumerate(found)
            if first <= at < last
        ]

    def arrive(first, last):
        @pl.when(starting)
        def _():
            for copy in moves(first, last):
                copy.wait()

    @pl.when(starting)
    def _():
        for copy in moves():
            copy.start()

    for n in range(8):
        short = slice(64 * n, 64 * n + 64)
        proj_down[:, short] = tiles[0][0, n, 0, :, 0:64]
        proj_up[:, short] = tiles[0][0, n, 0, :, 64:128]
        fc1_down[:, short] = tiles[1][0, n, 0, :, 0:64]
        fc2_up[:, short] = tiles[1][0, n, 0, :, 64:128]
        for half in range(2):
            long = slice(256 * n + 128 * half, 256 * n + 128 * half + 128)
            fc1_up[:, long] = tiles[2 + half][0, n, 0]
            fc2_down[:, long] = tiles[4 + half][0, n, 0]

    def join(parts):
        return jnp.concatenate(parts, axis=0) if per_clip > 1 else parts[0]

    dy = join([dy_ref[e] for e in range(per_clip)])
    attn = join([attn_ref[e] for e in range(per_clip)])
    reduced_proj = dot(proj_down[...], attn, NT).astype(BF)
    arrive(0, 4)
    proj_w = proj_ref[...].reshape(feats, feats)
    middle = (
        join([x_ref[e].astype(F32) for e in range(per_clip)])
        + dot(attn, proj_w, NN)
        + proj_bias_ref[...]
        + dot(reduced_proj, proj_up[...], TN)
    )
    normed, inverse = norm_stats(middle)
    low = (normed * gain_ref[...]).astype(BF)
    reduced_fc1 = dot(fc1_down[...], low, NT).astype(BF)
    grad_reduced_fc2 = dot(fc2_up[...], dy, NT).astype(BF)
    per_chunk = chunk // fc2_ref.shape[1]
    steps = hidden // chunk

    def pre_of(j):
        at = slice(j * chunk, (j + 1) * chunk)
        pres[j % 2] = (
            dot(low, fc1_ref[:, :, at].reshape(feats, chunk), NN)
            + fc1_bias_ref[:, at]
            + dot(reduced_fc1, fc1_up[:, at], TN)
        )

    arrive(4, 20)
    pre_of(0)
    arrive(20, 24)
    for j in range(steps):
        at = slice(j * chunk, (j + 1) * chunk)
        if j + 1 < steps:
            pre_of(j + 1)
        fc2_w = fc2_ref[j * per_chunk : (j + 1) * per_chunk].reshape(chunk, feats)
        dact = dot(dy, fc2_w, NT) + dot(grad_reduced_fc2, fc2_down[:, at], TN)
        pre = pres[j % 2]
        bell = jnp.exp2((pre * pre) * (-0.5 * LOG2E))
        t = 1.0 / (1.0 + jnp.abs(pre) * (0.3275911 * 0.7071067811865476))
        poly = (
            (((0.5 * 1.061405429) * t - 0.5 * 1.453152027) * t + 0.5 * 1.421413741) * t
            - 0.5 * 0.284496736
        ) * t + 0.5 * 0.254829592
        tail = poly * t * bell
        below = jnp.where(pre >= 0.0, 1.0 - tail, tail)
        acts[:, at] = (pre * below).astype(BF)
        dpres[:, at] = (dact * (below + pre * bell * 0.3989422804014327)).astype(BF)
    act = acts[...]
    dpre = dpres[...]
    fc1_up_at = 3 * feats
    fc2_down_at = fc1_up_at + hidden
    fc2_up_at = fc2_down_at + hidden
    fc2_w = fc2_ref[...].reshape(hidden, feats)
    grad_reduced_fc1 = dot(fc1_up[...], dpre, NT).astype(BF)
    dlow = dot(dpre, fc1_ref[...].reshape(feats, hidden), NT) + dot(grad_reduced_fc1, fc1_down[...], TN)
    dx1 = dy.astype(F32) + norm_back(dlow, gain_ref[...], normed, inverse)
    branch = dx1.astype(BF)
    reduced_fc2 = dot(fc2_down[...], act, NT).astype(BF)
    total = (
        middle + fc2_bias_ref[...] + dot(act, fc2_w, NN) + dot(reduced_fc2, fc2_up[...], TN)
    ).astype(BF)
    grad_reduced_proj = dot(proj_up[...], branch, NT).astype(BF)
    dattn = (
        dot(branch, proj_w, NT) + dot(grad_reduced_proj, proj_down[...], TN)
    ).astype(BF)
    for e in range(per_clip):
        rows = slice(e * count, (e + 1) * count)
        act_ref[e] = total[rows]
        dx1_ref[e] = dx1[rows]
        dattn_ref[e] = dattn[rows]
    grad_ref[0, :, :feats] = dot(grad_reduced_proj, attn, NN)
    grad_ref[0, :, feats : 2 * feats] = dot(reduced_proj, branch, NN)
    grad_ref[0, :, 2 * feats : fc1_up_at] = dot(grad_reduced_fc1, low, NN)
    grad_ref[0, :, fc1_up_at:fc2_down_at] = dot(reduced_fc1, dpre, NN)
    grad_ref[0, :, fc2_down_at:fc2_up_at] = dot(grad_reduced_fc2, act, NN)
    grad_ref[0, :, fc2_up_at:] = dot(reduced_fc2, dy, NN)


PIECES = (
    (0, 0, 64),
    (0, 512, 192),
    (1, 0, 64),
    (1, 512, 64),
    (1, 1024, 64),
    (1, 5632, 64),
    (1, 1536, 256),
    (1, 3584, 256),
)


def gradient_rows(sources, part, j):
    halves = []
    for n in range(2):
        cells = []
        for array, start, width in PIECES:
            at = slice(start + j * width, start + (j + 1) * width)
            cells.append(sources[array][n, pl.ds(pl.multiple_of(part * 8, 8), 8), at])
        halves.append(jnp.concatenate(cells, axis=1))
    return jnp.concatenate(halves, axis=0)


def share_gradients(place, sources, ids_ref, refs, send, between):
    own, other, from_core, half, from_x, shares, from_clips, adapters, from_win, out = refs
    c, w, x, k = place.c, place.w, place.x, place.k
    clip_size = own.shape[0]
    for j in range(clip_size):
        other[j] = gradient_rows(sources, 1 - k, j).astype(BF)
    core_copy = send.copy(other, from_core, place.sibling)
    between[0]()
    for j in range(clip_size):
        own[j] = gradient_rows(sources, k, j)
    core_copy.wait_recv()
    own[...] += from_core[...].astype(F32)
    half[...] = own[:, :, pl.ds(pl.multiple_of((1 - x) * 512, 512), 512)].astype(BF)
    x_copy = send.copy(half, from_x, place.across)
    between[1]()
    x_copy.wait_recv()
    shares[...] = (
        own[:, :, pl.ds(pl.multiple_of(x * 512, 512), 512)] + from_x[...].astype(F32)
    ).astype(BF)
    from_clips[c] = shares[c]
    clip_copies = []
    for d in range(1, clip_size):
        to = (c + d) % clip_size
        clip_copies.append(send.copy(shares.at[to], from_clips.at[c], (to, w)))
    for copy in clip_copies:
        copy.wait_recv()
    for a in range(8):
        total = None
        for n in range(2 * clip_size):
            value = from_clips[n // 2].astype(F32)[8 * (n % 2) : 8 * (n % 2) + 8]
            value = jnp.where(ids_ref[n : n + 1, :] == float(a), value, 0.0)
            total = value if total is None else total + value
        adapters[a // 2, 8 * (a % 2) : 8 * (a % 2) + 8, :] = total
    from_win[w] = adapters[w]
    win_copies = []
    for d in range(1, 4):
        to = (w + d) % 4
        win_copies.append(send.copy(adapters.at[to], from_win.at[w], (c, to)))
    between[2]()
    for copy in win_copies:
        copy.wait_recv()
    for x2 in range(2):
        for k2 in range(2):
            for a in range(2):
                out[a, 8 * k2 : 8 * k2 + 8, 512 * x2 : 512 * x2 + 512] = from_win[
                    2 * x2 + k2, 8 * a : 8 * a + 8, :
                ]
    for copy in [core_copy, x_copy, *clip_copies, *win_copies]:
        copy.wait_send()


def attend_back_kernel(
    x_ref,
    gain_ref,
    weight_ref,
    down_ref,
    up_ref,
    probs_ref,
    attn_ref,
    qkv_ref,
    reduced_ref,
    dattn_ref,
    dx1_ref,
    *refs,
    scale,
    per_group,
    width,
    per_clip,
    remote_size,
):
    if remote_size:
        act_ref, grad_dense_ref, ids_ref, act_out_ref, dx_out_ref, sums_ref, *refs = refs
    else:
        dx_ref, grad_ref, *refs = refs
    values, keys_t, inner, dqkv, dquery_t, *refs = refs
    group = pl.program_id(1)
    groups = pl.num_programs(1)
    item = pl.program_id(0)
    step = item * groups + group
    if remote_size:
        items = act_ref.shape[0]
        place = Place(remote_size)
        act_rows = Rows(place, act_ref, *refs[:5])
        dx_own = refs[5]
        dx_rows = Rows(place, *refs[5:11])
        grad_ref = refs[11]
        share_refs, sems = refs[12:21], refs[21:]

        @pl.when(step == 0)
        def _():
            enter(
                [(place.c, (place.w + d) % 4) for d in range(1, 4)]
                + [((place.c + d) % remote_size, place.w) for d in range(1, remote_size)]
            )
            for i in range(items):
                act_rows.begin(i)

        for i in range(items):

            @pl.when(step == i + 1)
            def _():
                act_rows.mix(i)

            if i < items - 1:

                @pl.when(step == (i + 1) * 4 + 1)
                def _():
                    dx_rows.mix(i)

        @pl.when(step == 4 * items - 3)
        def _():
            for i in range(0, items, 2):
                act_rows.end(act_out_ref, i)
            act_rows.drain()

    feats = x_ref.shape[-1]
    rows = x_ref.shape[1]

    @pl.when(group == 0)
    def _():
        keys_t[...] = qkv_ref[0, :, feats : 2 * feats].T
        lane = lane_ids((rows, 128))
        ones = jnp.where(lane % width < 2, 1.0, 0.0).astype(BF)
        source = lax.broadcasted_iota(jnp.int32, (128, 128), 0)
        target = lane_ids((128, 128))
        pick = jnp.where(
            (source // width == target // width) & (target % width < 2), 1.0, 0.0
        ).astype(BF)
        pick = jnp.concatenate([pick, pick], axis=0)
        for g in range(feats // 128):
            at = slice(128 * g, 128 * g + 128)
            values[:, 256 * g : 256 * g + 128] = qkv_ref[0, :, 2 * feats + 128 * g : 2 * feats + 128 * g + 128]
            values[:, 256 * g + 128 : 256 * g + 256] = ones
            product = dattn_ref[0, :, at].astype(F32) * attn_ref[0, :, at].astype(F32)
            high = product.astype(BF)
            rest = (product - high.astype(F32)).astype(BF)
            sums = dot(jnp.concatenate([high, rest], axis=1), pick, NN)
            coarse = sums.astype(BF)
            fine = (sums - coarse.astype(F32)).astype(BF)
            inner[:, at] = -jnp.where(lane % width == 0, coarse, fine)

    blocks = pl.ds(pl.multiple_of(group * 128, 128), 128)
    values_now = values[:, pl.ds(pl.multiple_of(group * 256, 256), 256)]
    dattn_now = dattn_ref[0, :, blocks]
    inner_now = inner[:, blocks]
    query_now = qkv_ref[0, :, blocks]
    head_of_lane = lane_ids((rows, 128)) // width
    zero = jnp.zeros((rows, 128), BF)
    dvalue = None
    dkey = None
    for h in range(per_group):
        mine = head_of_lane == h
        dattn_own = jnp.where(mine, dattn_now, zero)
        query_own = jnp.where(mine, query_now, zero)
        right = jnp.concatenate([dattn_own, jnp.where(mine, inner_now, zero)], axis=1)
        probs = probs_ref[0, h]
        dscore = probs * dot(values_now, right, NT).astype(BF)
        partial = dot(probs, dattn_own, NN)
        dvalue = partial if dvalue is None else dvalue + partial
        partial = dot(dscore, query_own, NN)
        dkey = partial if dkey is None else dkey + partial
        at = pl.ds(pl.multiple_of((group * per_group + h) * width, width), width)
        dquery_t[at, :] = (dot(keys_t[at, :], dscore, NN) * scale).astype(BF)
    dqkv[:, pl.ds(pl.multiple_of(2 * feats + group * 128, 128), 128)] = dvalue.astype(BF)
    dqkv[:, pl.ds(pl.multiple_of(feats + group * 128, 128), 128)] = (dkey * LN2).astype(BF)

    @pl.when(group == groups - 1)
    def _():
        first = pl.program_id(0) % per_clip == 0
        dqkv[:, :feats] = dquery_t[...].T
        dall = dqkv[...]
        normed, inverse = norm_stats(x_ref[0].astype(F32))
        low = (normed * gain_ref[...]).astype(BF)
        grad_reduced = dot(up_ref[0], dall, NT).astype(BF)
        slot = item // per_clip if remote_size else 0
        add_rows(grad_ref, slot, slice(feats, 4 * feats), dot(reduced_ref[0], dall, NN), first)
        add_rows(grad_ref, slot, slice(0, feats), dot(grad_reduced, low, NN), first)
        dlow = (dot(dall, weight_ref[...], NT) + dot(grad_reduced, down_ref[0], TN)).astype(BF)
        dx = (dx1_ref[0] + norm_back(dlow.astype(F32), gain_ref[...], normed, inverse)).astype(BF)
        if not remote_size:
            dx_ref[0] = dx
            return
        dx_own[item] = dx
        for i in range(items):

            @pl.when(item == i)
            def _():
                dx_rows.begin(i)

    if remote_size:

        @pl.when(step == 4 * items - 1)
        def _():
            share_gradients(
                place,
                (grad_ref, grad_dense_ref),
                ids_ref,
                (*share_refs, sums_ref),
                Sender(*sems),
                (
                    lambda: dx_rows.mix(items - 1),
                    lambda: None,
                    lambda: [dx_rows.end(dx_out_ref, i) for i in range(0, items, 2)],
                ),
            )
            dx_rows.drain()


def whole(shape):
    return pl.BlockSpec(shape, lambda *at: (0,) * len(shape), pipeline_mode=pl.Buffered(1))


def compute(first, dy, adapter_ids, vectors, later, per_clip, remote_size):
    if remote_size:
        heads = first[1].shape[0]
        x_shape, rank = dy.shape, 16
    else:
        x, qkv_w, qkv_down, qkv_up, table = first
        heads, rank = table.shape[0], qkv_down.shape[1]
    items, rows, feats = dy.shape
    width = feats // heads
    per_group = 128 // width
    groups = heads // per_group
    scale = width**-0.5
    hidden = 4 * feats
    clips = items // per_clip

    def item(shape):
        return pl.BlockSpec((1, *shape), lambda i, *rest: (i,) + (0,) * len(shape))

    item_ids = adapter_ids
    any_space = pl.BlockSpec(memory_space=pl.ANY)

    def of_clip(shape):
        return pl.BlockSpec((1, *shape), lambda i, *rest: (i // per_clip, 0, 0))

    sems = pltpu.SemaphoreType.DMA
    if remote_size:
        shape = jax.ShapeDtypeStruct
        adapters = 8
        padded = 56 * heads
        ids = jnp.pad(adapter_ids.astype(F32)[None], ((0, 0), (0, 126)))
        args = (*first, ids, *[v.reshape(1, -1) for v in vectors], dy, *later)
        arg_specs = [whole(a.shape) for a in args]
        sent_out = [
            shape(dy.shape, BF),
            shape((2, remote_size, 2, 768, 128), BF),
            shape(dy.shape, BF),
            shape((feats, 3 * feats), BF),
            *[shape((1, n), F32) for n in (feats, feats, feats, hidden, feats)],
            shape((2 * remote_size, 512), F32),
        ]
        sent_specs = [whole(a.shape) for a in sent_out]
        sent_specs[1] = any_space
        row_scratch = [
            pltpu.VMEM(dy.shape, BF),
            pltpu.VMEM(dy.shape, BF),
            pltpu.VMEM((items, TOP, feats), BF),
            sems((2 * items,)),
            sems((2 * items,)),
        ]
        sent_scratch = [
            pltpu.VMEM((1, 3 * feats), F32),
            pltpu.VMEM((adapters, rank, feats), BF),
            pltpu.VMEM((adapters, rank, 3 * feats), BF),
            pltpu.VMEM((64, 512), BF),
            pltpu.VMEM((8, 128), F32),
            pltpu.VMEM((768, 128), BF),
            pltpu.VMEM((2, remote_size, 2, 64, 512), BF),
            pltpu.VMEM((remote_size, 8, 128), F32),
            pltpu.VMEM((15 * heads, 176), BF),
            pltpu.VMEM((15, padded, 128), F32),
            pltpu.VMEM((padded, 15 * 128), BF),
            pltpu.VMEM((8 * 128, rows), BF),
            *row_scratch,
            *row_scratch,
            *[sems((Gather.COPIES,)) for _ in range(4)],
            sems((remote_size,)),
            sems((remote_size,)),
            sems,
        ]
    else:
        gain1, qkv_bias, proj_bias, gain2, fc1_bias, fc2_bias = vectors
        clip_ids = jnp.broadcast_to(adapter_ids.astype(F32)[:, None], (clips, 128))
        args = (x, gain1, qkv_w, qkv_bias, clip_ids, qkv_down, qkv_up, table)
        arg_specs = [item((rows, feats)), *[whole(a.shape) for a in args[1:7]], any_space]
        sent_out, sent_specs, sent_scratch = [], [], []

    probs, attn, qkv, reduced, down_own, up_own, *arrived = pl.pallas_call(
        functools.partial(
            attend_kernel,
            scale=scale,
            per_group=per_group,
            width=width,
            per_clip=per_clip,
            remote_size=remote_size,
        ),
        grid=(items, groups),
        in_specs=arg_specs,
        out_specs=[
            pl.BlockSpec((1, per_group, rows, rows), lambda i, g: (i, g, 0, 0)),
            item((rows, feats)),
            item((rows, 3 * feats)),
            item((rank, rows)),
            of_clip((rank, feats)),
            of_clip((rank, 3 * feats)),
            *sent_specs,
        ],
        scratch_shapes=[
            pltpu.VMEM((rows, 2 * feats), BF),
            pltpu.VMEM((rows, feats), BF),
            pltpu.VMEM((feats, rows), BF),
            pltpu.VMEM((feats, rows), BF),
            pltpu.VMEM((2, rows, rows), F32),
            pltpu.VMEM((heads, rows, rows), F32),
            sems((groups,)),
            pltpu.VMEM((rows, 128), BF),
            *sent_scratch,
        ],
        out_shape=[
            jax.ShapeDtypeStruct((items, heads, rows, rows), BF),
            jax.ShapeDtypeStruct((items, rows, feats), BF),
            jax.ShapeDtypeStruct((items, rows, 3 * feats), BF),
            jax.ShapeDtypeStruct((items, rank, rows), BF),
            jax.ShapeDtypeStruct((clips, rank, feats), BF),
            jax.ShapeDtypeStruct((clips, rank, 3 * feats), BF),
            *sent_out,
        ],
        compiler_params=pltpu.CompilerParams(
            vmem_limit_bytes=VMEM_LIMIT,
            dimension_semantics=("arbitrary", "arbitrary"),
            **({"collective_id": 2, "has_side_effects": True} if remote_size else {}),
        ),
        cost_estimate=pl.CostEstimate(flops=4 * 10**10, bytes_accessed=10**7, transcendentals=0),
        name="attend",
    )(*args)
    if remote_size:
        dy, staged, x, qkv_w, gain1, proj_bias, gain2, fc1_bias, fc2_bias, all_ids = arrived
    else:
        (staged,) = later

    span = 4 * feats + 2 * hidden
    def tile(n):
        def index(c, ids):
            return ids[c] // 2 % 2, 0, ids[c] // 4, 36 + 2 * n + ids[c] % 2, 0

        return pl.BlockSpec((1, 8, 1, rank, 128), index)

    def clip(array_shape):
        return pl.BlockSpec((per_clip, *array_shape[1:]), lambda c, ids: (c, 0, 0))

    chunk = 512
    act, dx1, dattn, grad_dense = pl.pallas_call(
        functools.partial(dense_kernel, per_clip=per_clip, chunk=chunk),
        grid_spec=pltpu.PrefetchScalarGridSpec(
            num_scalar_prefetch=1,
            grid=(clips,),
            in_specs=[
                clip(x.shape),
                clip(x.shape),
                whole(gain2.shape),
                whole(proj_bias.shape),
                whole(fc1_bias.shape),
                whole(fc2_bias.shape),
                clip(x.shape),
                any_space,
                *[tile(n) for n in range(6)],
            ],
            out_specs=[
                clip(x.shape),
                clip(x.shape),
                clip(x.shape),
                pl.BlockSpec((1, rank, span), lambda c, ids: (c, 0, 0)),
            ],
            scratch_shapes=[
                pltpu.VMEM((8, feats // 8, feats), BF),
                pltpu.VMEM((8, feats // 8, hidden), BF),
                pltpu.VMEM((8, hidden // 8, feats), BF),
                *[pltpu.VMEM((rank, n), BF) for n in (feats, feats, feats, hidden, hidden, feats)],
                pltpu.VMEM((2, per_clip * rows, chunk), F32),
                pltpu.VMEM((per_clip * rows, hidden), BF),
                pltpu.VMEM((per_clip * rows, hidden), BF),
                pltpu.SemaphoreType.DMA((24,)),
            ],
        ),
        out_shape=[
            jax.ShapeDtypeStruct((items, rows, feats), BF),
            jax.ShapeDtypeStruct((items, rows, feats), F32),
            jax.ShapeDtypeStruct((items, rows, feats), BF),
            jax.ShapeDtypeStruct((clips, rank, span), F32),
        ],
        compiler_params=pltpu.CompilerParams(
            vmem_limit_bytes=VMEM_LIMIT, dimension_semantics=("arbitrary",)
        ),
        cost_estimate=pl.CostEstimate(flops=5 * 10**10, bytes_accessed=10**7, transcendentals=0),
        name="dense",
    )(
        item_ids, x, attn, gain2, proj_bias, fc1_bias, fc2_bias, dy, staged, *([staged] * 6)
    )

    if remote_size:
        assert (clips, per_clip) == (2, 2)
        count = remote_size
        back_in = (act, grad_dense, all_ids)
        back_out = [whole(x.shape), whole(x.shape), whole((2, rank, 1024))]
        back_shape = [
            jax.ShapeDtypeStruct(x.shape, BF),
            jax.ShapeDtypeStruct(x.shape, BF),
            jax.ShapeDtypeStruct((2, rank, 1024), F32),
        ]
        back_scratch = [
            *row_scratch,
            pltpu.VMEM(x.shape, BF),
            *row_scratch,
            pltpu.VMEM((clips, rank, 4 * feats), F32),
            pltpu.VMEM((count, 16, 1024), F32),
            pltpu.VMEM((count, 16, 1024), BF),
            pltpu.VMEM((count, 16, 1024), BF),
            pltpu.VMEM((count, 16, 512), BF),
            pltpu.VMEM((count, 16, 512), BF),
            pltpu.VMEM((count, 16, 512), BF),
            pltpu.VMEM((count, 16, 512), BF),
            pltpu.VMEM((4, 16, 512), F32),
            pltpu.VMEM((4, 16, 512), F32),
            sems((16,)),
            sems((16,)),
        ]
    else:
        back_in, back_scratch = (), []
        back_out = [
            item((rows, feats)),
            pl.BlockSpec((1, rank, 4 * feats), lambda i, g: (i // per_clip, 0, 0)),
        ]
        back_shape = [
            jax.ShapeDtypeStruct((items, rows, feats), BF),
            jax.ShapeDtypeStruct((clips, rank, 4 * feats), F32),
        ]
    results = pl.pallas_call(
        functools.partial(
            attend_back_kernel,
            scale=scale,
            per_group=per_group,
            width=width,
            per_clip=per_clip,
            remote_size=remote_size,
        ),
        grid=(items, groups),
        in_specs=[
            item((rows, feats)),
            whole(gain1.shape),
            whole(qkv_w.shape),
            of_clip((rank, feats)),
            of_clip((rank, 3 * feats)),
            pl.BlockSpec((1, per_group, rows, rows), lambda i, g: (i, g, 0, 0)),
            item((rows, feats)),
            item((rows, 3 * feats)),
            item((rank, rows)),
            item((rows, feats)),
            item((rows, feats)),
            *[whole(a.shape) for a in back_in],
        ],
        out_specs=back_out,
        scratch_shapes=[
            pltpu.VMEM((rows, 2 * feats), BF),
            pltpu.VMEM((feats, rows), BF),
            pltpu.VMEM((rows, feats), BF),
            pltpu.VMEM((rows, 3 * feats), BF),
            pltpu.VMEM((feats, rows), BF),
            *back_scratch,
        ],
        out_shape=back_shape,
        compiler_params=pltpu.CompilerParams(
            vmem_limit_bytes=VMEM_LIMIT, dimension_semantics=("arbitrary", "arbitrary"),
            **({"collective_id": 1, "has_side_effects": True} if remote_size else {}),
        ),
        cost_estimate=pl.CostEstimate(flops=5 * 10**10, bytes_accessed=10**7, transcendentals=0),
        name="attend_back",
    )(x, gain1, qkv_w, down_own, up_own, probs, attn, qkv, reduced, dattn, dx1, *back_in)
    if remote_size:
        return results
    return (act, *results, grad_dense)


def exchange(x, win_size):
    local = x.shape[1]
    bits = local.bit_length() - 1
    at = jnp.arange(TOK)
    taken = (at // 49 < 4, at // 7 % 7 < 3, at % 7 < 3)
    for bit, rows in zip((2, 1, 0), taken):
        if bit < bits:
            split = x.reshape(x.shape[0], local >> (bit + 1), 2, 1 << bit, TOK, -1)
            other = jnp.flip(split, axis=2).reshape(x.shape)
        else:
            other = lax.ppermute(x, "win", [(i, i ^ 1 << bit - bits) for i in range(win_size)])
        x = jnp.where(rows[None, None, :, None], other, x)
    return x


def bias_by_pair(table):
    heads = table.shape[0]
    side = jnp.arange(49)
    high, wide = (side // 7 + 4) % 7, (side % 7 + 4) % 7
    offset = (high[None, :] - high[:, None] + 6) * 13 + wide[None, :] - wide[:, None] + 6
    pick = (jnp.arange(169)[:, None, None] == offset[None]).astype(BF)
    found = jnp.einsum(
        "mad,dkq->mkaq", table.reshape(heads, 15, 169), pick, preferred_element_type=F32
    )
    found = (found * LOG2E).reshape(heads, 49, 15 * 49)
    blocks = []
    for key_block in range(8):
        t = (key_block + 4) % 8
        blocks.append(
            jnp.concatenate(
                (found[..., (11 - t) * 49 : (15 - t) * 49], found[..., (7 - t) * 49 : (11 - t) * 49]),
                axis=-1,
            )
        )
    return jnp.stack(blocks, axis=1).reshape(heads, TOK, TOK)


def gather(array, spec):
    for axis, name in enumerate(spec):
        if name is not None:
            array = lax.all_gather(array, name, axis=axis, tiled=True)
    return array


def stage_whole(proj_w, fc1_w, fc2_w, maps):
    proj_down, proj_up, fc1_down, fc1_up, fc2_down, fc2_up = maps
    count = proj_down.shape[0]

    def short(a):
        return a.reshape(4, count // 4 * 16, 8, 64).transpose(2, 0, 1, 3)

    def long(a):
        return a.reshape(4, count // 4 * 16, 8, 2, 128).transpose(2, 0, 3, 1, 4).reshape(8, 4, -1, 128)

    return jnp.concatenate(
        (
            proj_w.reshape(8, 64, 4, 128).transpose(0, 2, 1, 3),
            fc1_w.reshape(8, 64, 4, 4, 128).transpose(0, 2, 3, 1, 4).reshape(8, 4, 256, 128),
            fc2_w.reshape(8, 256, 4, 128).transpose(0, 2, 1, 3),
            jnp.concatenate((short(proj_down), short(proj_up)), axis=-1),
            jnp.concatenate((short(fc1_down), short(fc2_up)), axis=-1),
            long(fc1_up),
            long(fc2_down),
        ),
        axis=2,
    )


def by_core(staged):
    return staged.reshape(8, 2, 2, *staged.shape[2:]).transpose(2, 0, 1, 3, 4)


def per_device(
    tokens, cotangent, adapter_ids, ln1_gain, qkv_weight, qkv_bias, proj_weight, proj_bias, ln2_gain,
    fc1_weight, fc1_bias, fc2_weight, fc2_bias, bias_table, qkv_down, qkv_up, proj_down, proj_up,
    fc1_down, fc1_up, fc2_down, fc2_up, *, clip_size, win_size,
):
    clips, local, rows, feats = tokens.shape
    items = clips * local
    heads = bias_table.shape[0]
    vecs = (ln1_gain, qkv_bias, proj_bias, ln2_gain, fc1_bias, fc2_bias)
    flat = (items, rows, feats)
    downs = [a.transpose(0, 2, 1) for a in (qkv_down, proj_down, fc1_down, fc2_down)]
    own_kernels = (clip_size, win_size, clips, local) == (8, 4, 2, 2)
    if own_kernels:
        first = (tokens.reshape(flat), bias_table, qkv_weight, downs[0], qkv_up)
        dy = cotangent.reshape(flat)
        vectors = vecs
        later = (proj_weight, fc1_weight, fc2_weight, downs[1], proj_up, downs[2], fc1_up, downs[3], fc2_up)
    else:
        grid2, by_down, by_up = ("clip", "win"), ("win", None, "clip"), ("win", None, "clip")
        maps = (downs[1], proj_up, downs[2], fc1_up, downs[3], fc2_up)
        staged = stage_whole(
            *[gather(a, grid2) for a in (proj_weight, fc1_weight, fc2_weight)],
            [gather(a, by_up) for a in maps],
        )
        later = (by_core(staged),)
        vectors = [gather(v, ("clip",)).reshape(1, -1).astype(F32) for v in vecs]
        first = (
            exchange(tokens, win_size).reshape(flat),
            gather(qkv_weight, grid2),
            gather(downs[0], by_down),
            gather(qkv_up, by_up),
            bias_by_pair(bias_table),
        )
        dy = exchange(cotangent, win_size).reshape(flat)
    results = compute(
        first, dy, adapter_ids, vectors, later, local, clip_size if own_kernels else 0
    )
    if own_kernels:
        act_out, dx_out, sums = results
        qd, qu, pd, pu, f1d, f2u, f1u, f2d = [
            sums[..., first:last]
            for first, last in zip(
                (0, 64, 256, 320, 384, 448, 512, 768), (64, 256, 320, 384, 448, 512, 768, 1024)
            )
        ]
        turned = [a.transpose(0, 2, 1) for a in (qd, pd, f1d, f2d)]
        return (
            act_out.reshape(tokens.shape), dx_out.reshape(tokens.shape),
            turned[0], qu, turned[1], pu, turned[2], f1u, turned[3], f2u,
        )
    act, dx, grad_qkv, grad_dense = results
    activations = exchange(act.reshape(tokens.shape), win_size)
    input_grad = exchange(dx.reshape(tokens.shape), win_size)
    adapter_count = win_size * qkv_down.shape[0]
    hot = (adapter_ids[:, None] == jnp.arange(adapter_count)[None]).astype(F32)
    hidden = fc1_weight.shape[1] * win_size
    spans = (feats, 3 * feats, feats, feats, feats, hidden, hidden, feats)
    grads = jnp.concatenate((grad_qkv, grad_dense), axis=-1)
    rank = grads.shape[1]
    parts, at = [], 0
    for span in spans:
        parts.append(
            grads[..., at : at + span].reshape(clips, rank, clip_size, span // clip_size)
        )
        at += span
    mine = jnp.concatenate(parts, axis=-1)
    grown = jnp.sum(hot[:, :, None, None, None] * mine[:, None], axis=0)
    grown = grown.transpose(2, 0, 1, 3).astype(BF)
    total = lax.psum_scatter(grown, "clip", scatter_dimension=0, tiled=True)[0]
    total = lax.psum_scatter(total, "win", scatter_dimension=0, tiled=True).astype(F32)
    outs, at = [], 0
    for n, span in enumerate(spans):
        width = span // clip_size
        part = total[..., at : at + width]
        at += width
        outs.append(part.transpose(0, 2, 1) if n % 2 == 0 else part)
    return (activations, input_grad, *outs)


def solution(mesh):
    split = P("clip", "win", None, None)
    grid2 = P("clip", "win")
    down = P("win", "clip", None)
    up = P("win", None, "clip")
    one = P("clip")
    return jax.shard_map(
        functools.partial(
            per_device, clip_size=mesh.shape["clip"], win_size=mesh.shape["win"]
        ),
        mesh=mesh,
        in_specs=(
            split, split, one, one, grid2, one, grid2, one, one, grid2, one, grid2, one, P(),
            down, up, down, up, down, up, down, up,
        ),
        out_specs=(split, split, down, up, down, up, down, up, down, up),
        check_vma=False,
    )
```

```python
import functools
import jax
import jax.numpy as jnp
from jax import lax
from jax.experimental import pallas as pl
from jax.experimental.pallas import tpu as pltpu
from jax.sharding import PartitionSpec as P

BF = jnp.bfloat16
F32 = jnp.float32
NN = (((1,), (0,)), ((), ()))
NT = (((1,), (1,)), ((), ()))
TN = (((0,), (0,)), ((), ()))
LOG2E = 1.4426950408889634
LN2 = 0.6931471805599453
FAR = 1e9
VMEM_LIMIT = 60 * 2**20
TOK = 392
TOP = 208


def dot(left, right, dims):
    return lax.dot_general(left, right, dims, preferred_element_type=F32)


def lane_ids(shape):
    return lax.broadcasted_iota(jnp.int32, shape, len(shape) - 1)


def norm_stats(values):
    average = jnp.mean(values, axis=-1, keepdims=True)
    centred = values - average
    variance = jnp.mean(centred * centred, axis=-1, keepdims=True)
    inverse = lax.rsqrt(variance + 1e-05)
    return centred * inverse, inverse


def norm_back(gradient, gain, normed, inverse):
    scaled = gradient * gain
    centre = jnp.mean(scaled, axis=-1, keepdims=True)
    slope = jnp.mean(scaled * normed, axis=-1, keepdims=True)
    return inverse * (scaled - centre - normed * slope)


def add_rows(ref, n, at, value, first):
    @pl.when(first)
    def _():
        ref[n, :, at] = value

    @pl.when(jnp.logical_not(first))
    def _():
        ref[n, :, at] += value


MESH = pl.DeviceIdType.MESH


def enter(peers):
    barrier = pltpu.get_barrier_semaphore()
    for peer in peers:
        pl.semaphore_signal(barrier, inc=1, device_id=peer, device_id_type=MESH)
    pl.semaphore_wait(barrier, len(peers))


def remote(src, dst, send_sem, recv_sem, peer):
    return pltpu.make_async_remote_copy(
        src_ref=src,
        dst_ref=dst,
        send_sem=send_sem,
        recv_sem=recv_sem,
        device_id=peer,
        device_id_type=MESH,
    )


class Sender:
    def __init__(self, send_sem, recv_sem):
        self.send_sem, self.recv_sem, self.count = send_sem, recv_sem, 0

    def copy(self, src, dst, peer):
        n = self.count
        self.count += 1
        made = remote(src, dst, self.send_sem.at[n], self.recv_sem.at[n], peer)
        made.start()
        return made


def row_masks(rows):
    row = lax.broadcasted_iota(jnp.int32, (rows, 128), 0)
    return row < TOK // 2, row % 49 < 21, row % 7 < 3


def choose(mask, first, second):
    return jnp.concatenate(
        [
            jnp.where(mask, first[:, at : at + 128], second[:, at : at + 128])
            for at in range(0, first.shape[1], 128)
        ],
        axis=1,
    )


class Rows:
    def __init__(self, place, own, beside, mixed, tops, send_sem, recv_sem):
        self.place, self.own, self.beside, self.mixed, self.tops = place, own, beside, mixed, tops
        self.send_sem, self.recv_sem = send_sem, recv_sem
        self.items, self.rows, self.feats = own.shape

    def copy(self, kind, i):
        n = kind * self.items + i
        sems = self.send_sem.at[n], self.recv_sem.at[n]
        if kind == 0:
            return remote(self.own.at[i], self.beside.at[i], *sems, self.place.sibling)
        top = self.mixed.at[i, pl.ds(0, TOP)]
        return remote(top, self.tops.at[i], *sems, self.place.across)

    def begin(self, i):
        self.copy(0, i).start()

    def mix(self, i):
        self.copy(0, i).wait_recv()
        self.mixed[i] = choose(row_masks(self.rows)[1], self.beside[i], self.own[i])
        self.copy(1, i).start()

    def end(self, out, i):
        early, _, low_w = row_masks(self.rows)
        both = []
        for e in range(2):
            self.copy(1, i + e).wait_recv()
            top = choose(early[:TOP], self.tops[i + e], self.mixed[i + e, :TOP])
            both.append(jnp.concatenate([top, self.mixed[i + e, TOP:]], axis=0))
        for e in range(2):
            out[i + e] = choose(low_w, both[1 - e], both[e])

    def drain(self):
        for i in range(self.items):
            self.copy(0, i).wait_send()
            self.copy(1, i).wait_send()


class Place:
    def __init__(self, clip_size):
        self.c, self.w = lax.axis_index("clip"), lax.axis_index("win")
        self.z, self.y = self.c // 2, self.c % 2
        self.x, self.k = self.w // 2, self.w % 2
        self.zs = clip_size // 2
        self.sibling = (self.c, self.x * 2 + 1 - self.k)
        self.across = (self.c, (1 - self.x) * 2 + self.k)

    def clip_at(self, z_step, other_y):
        return (self.z + z_step + self.zs) % self.zs * 2 + (1 - self.y if other_y else self.y)

    def along_z(self, step):
        return (self.clip_at(step, False), self.w)

    def along_y(self):
        return (self.clip_at(0, True), self.w)


class Gather:
    COPIES = 29

    def __init__(self, place, unit, units, send_sem, recv_sem):
        self.place, self.unit, self.units = place, unit, units
        self.send_sem, self.recv_sem = send_sem, recv_sem
        self.hops = range(place.zs - 1)

    def make(self, kind, t=0):
        p, units = self.place, self.units
        kinds = ("up", "down", "y_up", "y_down", "s_up", "s_down", "sy_up", "sy_down")
        single = ("across", "own", "theirs", "y", "s_y")
        n = single.index(kind) if kind in single else 5 + 8 * t + kinds.index(kind)
        sems = self.send_sem.at[n], self.recv_sem.at[n]
        mine = units.at[p.k, p.c, p.x]
        if kind == "across":
            return remote(self.unit, mine, *sems, p.across)
        if kind == "own":
            return remote(self.unit, mine, *sems, p.sibling)
        if kind == "theirs":
            part = units.at[p.k, p.c, 1 - p.x]
        elif kind == "y":
            part = units.at[p.k, p.c]
        elif kind == "s_y":
            part = units.at[p.k, p.z * 2 + 1 - p.y]
        else:
            sign = -1 if kind.endswith("up") else 1
            far = p.z + sign * (t if kind in ("up", "down") else t + 1)
            part = units.at[p.k, far * 2 + (1 - p.y if kind.startswith("sy") else p.y)]
        if kind in ("up", "down"):
            peer = (p.c - 2 * sign, p.w)
        else:
            peer = p.along_y() if kind.startswith("y") else p.sibling
        return remote(part, part, *sems, peer)

    def when(self, kind, t, sending, act):
        p, last = self.place, self.place.zs - 1
        if kind.endswith("up"):
            holds = (p.z >= t) & (p.z < last) if sending and kind == "up" else p.z >= t + 1
        elif kind.endswith("down"):
            holds = (p.z <= last - t) & (p.z > 0) if sending and kind == "down" else p.z <= last - 1 - t
        else:
            act()
            return
        pl.when(holds)(act)

    def start(self, kind, t=0):
        self.when(kind, t, True, lambda: self.make(kind, t).start())

    def wait_recv(self, kind, t=0):
        self.when(kind, t, False, lambda: self.make(kind, t).wait_recv())

    def wait_send(self, kind, t=0):
        self.when(kind, t, True, lambda: self.make(kind, t).wait_send())

    def begin(self):
        self.start("across")
        self.start("own")

    def second(self):
        self.wait_recv("across")
        for kind in ("up", "down", "y", "theirs"):
            self.start(kind)

    def from_z(self, t):
        for way in ("up", "down"):
            self.wait_recv(way, t)
            if t + 1 in self.hops:
                self.start(way, t + 1)
            self.start("y_" + way, t)
            self.start("s_" + way, t)

    def from_y(self, t):
        if t < 0:
            self.wait_recv("y")
            self.start("s_y")
        else:
            for way in ("up", "down"):
                self.wait_recv("y_" + way, t)
                self.start("sy_" + way, t)

    def finish(self):
        for kind in ("own", "theirs", "s_y"):
            self.wait_recv(kind)
        for t in self.hops:
            for kind in ("s_up", "s_down", "sy_up", "sy_down"):
                self.wait_recv(kind, t)
        for kind in ("across", "own", "theirs", "y", "s_y"):
            self.wait_send(kind)
        for t in self.hops:
            for kind in ("up", "down", "y_up", "y_down", "s_up", "s_down", "sy_up", "sy_down"):
                self.wait_send(kind, t)


def pack_first(unit, vec, qkv_ref, qd_ref, qu_ref, ids_ref, vec_refs):
    unit[:, 0:384] = qkv_ref[...]
    for a in range(2):
        unit[16 * a : 16 * a + 16, 384:448] = qd_ref[a]
        unit[16 * a : 16 * a + 16, 448:512] = qu_ref[a, :, 0:64]
        unit[32 + 16 * a : 48 + 16 * a, 384:512] = qu_ref[a, :, 64:192]
    g1_ref, qb_ref, pb_ref, g2_ref, f1b_ref, f2b_ref = vec_refs
    vec[0:1, 0:64] = g1_ref[...].astype(F32)
    vec[0:1, 64:128] = qb_ref[:, 0:64].astype(F32)
    vec[1:2, :] = qb_ref[:, 64:192].astype(F32)
    vec[2:3, 0:64] = pb_ref[...].astype(F32)
    vec[2:3, 64:128] = g2_ref[...].astype(F32)
    vec[3:4, :] = f1b_ref[:, 0:128].astype(F32)
    vec[4:5, :] = f1b_ref[:, 128:256].astype(F32)
    vec[5:6, 0:64] = f2b_ref[...].astype(F32)
    vec[5:6, 64:128] = ids_ref[:, 0:64]
    vec[6:8, :] = jnp.zeros((2, 128), F32)


def unpack_vectors(vecs, outs):
    gain1, qkv_bias, proj_bias, gain2, fc1_bias, fc2_bias, ids = outs
    for c in range(vecs.shape[0]):
        v = vecs[c]
        short = slice(64 * c, 64 * c + 64)
        gain1[:, short] = v[0:1, 0:64]
        qkv_bias[:, 192 * c : 192 * c + 64] = v[0:1, 64:128]
        qkv_bias[:, 192 * c + 64 : 192 * c + 192] = v[1:2, :]
        proj_bias[:, short] = v[2:3, 0:64]
        gain2[:, short] = v[2:3, 64:128]
        fc1_bias[:, 256 * c : 256 * c + 128] = v[3:4, :]
        fc1_bias[:, 256 * c + 128 : 256 * c + 256] = v[4:5, :]
        fc2_bias[:, short] = v[5:6, 0:64]
        for n in range(2):
            ids[2 * c + n : 2 * c + n + 1, :] = jnp.broadcast_to(
                v[5:6, 64 + n : 65 + n], (1, ids.shape[1])
            )


def unpack_first(units, weight, down, up):
    for c in range(units.shape[1]):
        for n in range(4):
            unit = units.at[n % 2, c, n // 2]
            weight[64 * c : 64 * c + 64, 384 * n : 384 * n + 384] = unit[:, 0:384]
            for a in range(2):
                low = unit[16 * a : 16 * a + 16, 384:512]
                high = unit[32 + 16 * a : 48 + 16 * a, 384:512]
                down[2 * n + a, :, 64 * c : 64 * c + 64] = low[:, 0:64]
                up[2 * n + a, :, 192 * c : 192 * c + 64] = low[:, 64:128]
                up[2 * n + a, :, 192 * c + 64 : 192 * c + 192] = high


def pack_second(unit, refs):
    proj_ref, fc1_ref, fc2_ref, pd_ref, pu_ref, f1d_ref, f1u_ref, f2d_ref, f2u_ref = refs
    unit[0:64] = proj_ref[...]
    for t in range(4):
        unit[64 + 64 * t : 128 + 64 * t] = fc1_ref[:, 128 * t : 128 * t + 128]
    unit[320:576] = fc2_ref[...]
    for a in range(2):
        at = 576 + 16 * a
        unit[at : at + 16, 0:64] = pd_ref[a]
        unit[at : at + 16, 64:128] = pu_ref[a]
        unit[at + 32 : at + 48, 0:64] = f1d_ref[a]
        unit[at + 32 : at + 48, 64:128] = f2u_ref[a]
        for half in range(2):
            lanes = slice(128 * half, 128 * half + 128)
            unit[at + 64 + 32 * half : at + 80 + 32 * half] = f1u_ref[a, :, lanes]
            unit[at + 128 + 32 * half : at + 144 + 32 * half] = f2d_ref[a, :, lanes]


class Bias:
    def __init__(self, source, table, pairs, found, wide, select):
        self.source, self.table, self.pairs, self.found = source, table, pairs, found
        self.wide, self.select = wide, select
        self.heads = source.shape[0]

    def prepare(self):
        heads, pairs = self.heads, self.pairs
        pairs[...] = jnp.zeros(pairs.shape, BF)
        for a in range(15):
            pairs[a * heads : (a + 1) * heads, 0:169] = self.source[:, 169 * a : 169 * a + 169]

    def first(self, start, end):
        heads, pairs, found = self.heads, self.pairs, self.found
        lane = lane_ids((pairs.shape[1], 128))
        row = lax.broadcasted_iota(jnp.int32, (pairs.shape[1], 128), 0)
        query_at = (lane // 7 + 4) % 7 * 13 + (lane % 7 + 4) % 7
        wanted = jnp.where(lane < 49, row - query_at - 84, 10000)

        def one_key(key, carry):
            key_at = (key // 7 + 4) % 7 * 13 + (key % 7 + 4) % 7
            pick = jnp.where(wanted + key_at == 0, 1.0, 0.0).astype(BF)
            value = dot(pairs[...], pick, NN)
            for a in range(15):
                found[a, pl.ds(key, heads, stride=56), :] = value[a * heads : (a + 1) * heads]
            return carry

        lax.fori_loop(start, end, one_key, 0, unroll=2)

    def middle(self):
        for a in range(15):
            self.wide[:, 128 * a : 128 * a + 128] = self.found[a].astype(BF)
        row = lax.broadcasted_iota(jnp.int32, (128, TOK), 0)
        gap = lane_ids((128, TOK)) - row
        for t in range(8):
            self.select[128 * t : 128 * t + 128, :] = jnp.where(
                (gap == (t + 4) % 8 * 49) & (row < 49), 1.0, 0.0
            ).astype(BF)

    def last(self, blocks):
        for block in blocks:
            t = (block + 4) % 8
            value = dot(self.wide[:, (7 - t) * 128 : (15 - t) * 128], self.select[...], NN) * LOG2E
            for m in range(self.heads):
                self.table[m, 49 * block : 49 * block + 49, :] = value[56 * m : 56 * m + 49]


def attend_kernel(*refs, scale, per_group, width, per_clip, remote_size):
    if remote_size:
        tok_ref, source_ref, *refs = refs
        first_refs, vec_refs, refs = refs[:4], refs[4:10], refs[10:]
        dy_ref, second_refs, refs = refs[0], refs[1:10], refs[10:]
    else:
        x_ref, gain_ref, weight_ref, bias_ref, ids_ref, down_ref, up_ref, table_ref, *refs = refs
    probs_ref, out_ref, qkv_ref, reduced_ref, down_own, up_own, *refs = refs
    if remote_size:
        dy_out_ref, units_ref, x_ref, weight_ref, gain_ref, *vec_outs, ids_ref = refs[:10]
        refs = refs[10:]
    keys, queries, values_t, out_t, scores, table, table_sem, query_mask, *refs = refs
    group = pl.program_id(1)
    groups = pl.num_programs(1)
    item = pl.program_id(0)
    step = item * groups + group
    feats = x_ref.shape[-1]
    rows = x_ref.shape[1]

    if remote_size:
        bias_ref, down_ref, up_ref, unit1, vec, unit2, units1, vecs, *refs = refs
        bias = Bias(source_ref, table, *refs[:4])
        place = Place(remote_size)
        x_rows = Rows(place, tok_ref, *refs[4:9])
        dy_rows = Rows(place, dy_ref, *refs[9:14])
        gather1 = Gather(place, unit1, units1, *refs[14:16])
        gather2 = Gather(place, unit2, units_ref, *refs[16:18])
        vec_send, vec_recv, own_sem = refs[18:]
        items = dy_ref.shape[0]

        def vec_copy(d):
            to = ((place.c + d) % remote_size, place.w)
            return remote(vec, vecs.at[place.c], vec_send.at[d], vec_recv.at[d], to)

        @pl.when(step == 0)
        def _():
            pack_first(unit1, vec, *first_refs, vec_refs)
            pack_second(unit2, second_refs)
            mine = place.k, place.c, place.x
            units1[mine] = unit1[...]
            vecs[place.c] = vec[...]
            own = pltpu.make_async_copy(unit2, units_ref.at[mine], own_sem)
            own.start()
            enter(
                [place.sibling, place.across]
                + [((place.c + d) % remote_size, place.w) for d in range(1, remote_size)]
            )
            gather1.begin()
            for i in range(items):
                x_rows.begin(i)
            for d in range(1, remote_size):
                vec_copy(d).start()
            bias.prepare()
            gather1.second()
            pl.loop(0, items)(x_rows.mix)
            bias.first(0, 16)
            gather1.from_z(0)
            bias.first(16, 32)
            gather1.from_y(-1)
            gather1.from_z(1)
            bias.first(32, 50)
            gather1.from_y(0)
            gather1.from_z(2)
            bias.middle()
            gather1.from_y(1)
            bias.last(range(0, 4))
            gather1.from_y(2)
            own.wait()
            gather2.begin()
            bias.last(range(4, 8))
            for d in range(1, remote_size):
                vec_copy(d).wait_recv()
            unpack_vectors(vecs, (gain_ref, bias_ref, *vec_outs, ids_ref))
            gather1.finish()
            unpack_first(units1, weight_ref, down_ref, up_ref)
            x_rows.end(x_ref, 0)
            gather2.second()
            for d in range(1, remote_size):
                vec_copy(d).wait_send()

        @pl.when(step == 1)
        def _():
            for i in range(items):
                dy_rows.begin(i)

        @pl.when(step == 3)
        def _():
            pl.loop(0, items)(dy_rows.mix)

        for n in range(2, items, 2):

            @pl.when(step == 4 * n)
            def _():
                x_rows.end(x_ref, n)

        for t, at in enumerate((4, 8, 11)):

            @pl.when(step == at)
            def _():
                gather2.from_z(t)

        for t, at in ((-1, 5), (0, 9), (1, 12), (2, 15)):

            @pl.when(step == at)
            def _():
                gather2.from_y(t)

        @pl.when(step == 4 * items - 1)
        def _():
            for i in range(0, items, 2):
                dy_rows.end(dy_out_ref, i)
            gather2.finish()
            x_rows.drain()
            dy_rows.drain()

    else:

        def table_copy(g):
            at = pl.ds(g * per_group, per_group)
            return pltpu.make_async_copy(table_ref.at[at], table.at[at], table_sem.at[g])

        @pl.when(step == 0)
        def _():
            for g in range(table.shape[0] // per_group):
                table_copy(g).start()

    @pl.when((group == 0) & (item % per_clip == 0))
    def _():
        clip = item // per_clip
        if remote_size:
            clip = clip + place.c * 2
        ids = ids_ref[...]
        row = lax.broadcasted_iota(jnp.int32, ids.shape, 0)
        mine = jnp.sum(jnp.where(row == clip, ids, 0.0), axis=0, keepdims=True)[:, 0:1]
        for ref, target in ((down_ref, down_own), (up_ref, up_own)):
            total = jnp.zeros(ref.shape[1:], F32)
            for a in range(ref.shape[0]):
                total = total + jnp.where(
                    mine == float(a), ref[a].astype(F32), 0.0
                )
            target[0] = total.astype(BF)

    @pl.when(group == 0)
    def _():
        number = lax.axis_index("win") * per_clip + item % per_clip
        early, low_h, low_w = row_masks(rows)
        label = (
            jnp.where(early, number // 4 % 2 * 4, 0)
            + jnp.where(low_h, number // 2 % 2 * 2, 0)
            + jnp.where(low_w, number % 2, 0)
        )
        lane = lane_ids((rows, 128))
        same = label == lane
        key_mask = jnp.where(same, 1.0, 0.0).astype(BF)
        query_mask[...] = jnp.where(same | (lane >= 8), 0.0, -FAR).astype(BF)
        normed, _ = norm_stats(x_ref[item if remote_size else 0].astype(F32))
        low = (normed * gain_ref[...]).astype(BF)
        reduced = dot(down_own[0], low, NT).astype(BF)
        reduced_ref[0] = reduced

        def columns(part):
            at = pl.ds(part * feats, feats)
            return (
                dot(low, weight_ref[:, at], NN)
                + bias_ref[:, at]
                + dot(reduced, up_own[0, :, at], TN)
            )

        query = (columns(0) * (scale * LOG2E)).astype(BF)
        queries[...] = query
        qkv_ref[0, :, :feats] = query
        key = columns(1).astype(BF)
        qkv_ref[0, :, feats : 2 * feats] = key
        for g in range(feats // 128):
            keys[:, 256 * g : 256 * g + 128] = key[:, 128 * g : 128 * g + 128]
            keys[:, 256 * g + 128 : 256 * g + 256] = key_mask
        value = columns(2).astype(BF)
        qkv_ref[0, :, 2 * feats :] = value
        values_t[...] = value.T

    if not remote_size:

        @pl.when(item == 0)
        def _():
            table_copy(group).wait()

    keys_now = keys[:, pl.ds(pl.multiple_of(group * 256, 256), 256)]
    query_now = queries[:, pl.ds(pl.multiple_of(group * 128, 128), 128)]
    head_of_lane = lane_ids(query_now.shape) // width

    def raw(h):
        own = jnp.where(head_of_lane == h, query_now, jnp.zeros_like(query_now))
        own = jnp.concatenate([own, query_mask[...]], axis=1)
        return dot(keys_now, own, NT) + table[group * per_group + h]

    def finish(h):
        score = scores[h % 2]
        largest = jnp.max(score, axis=0, keepdims=True)
        probs = jnp.exp2(score - largest)
        total = jnp.sum(probs, axis=0, keepdims=True)
        probs = (probs * (1.0 / total)).astype(BF)
        probs_ref[0, h] = probs
        at = pl.ds(pl.multiple_of((group * per_group + h) * width, width), width)
        out_t[at, :] = dot(values_t[at, :], probs, NN).astype(BF)

    scores[0] = raw(0)
    for h in range(per_group):
        if h + 1 < per_group:
            scores[(h + 1) % 2] = raw(h + 1)
        finish(h)

    @pl.when(group == groups - 1)
    def _():
        out_ref[0] = out_t[...].T


def dense_kernel(
    ids_ref,
    x_ref,
    attn_ref,
    gain_ref,
    proj_bias_ref,
    fc1_bias_ref,
    fc2_bias_ref,
    dy_ref,
    staged_ref,
    *refs,
    per_clip,
    chunk,
):
    tiles, refs = refs[:6], refs[6:]
    act_ref, dx1_ref, dattn_ref, grad_ref, *refs = refs
    proj_ref, fc1_ref, fc2_ref, proj_down, proj_up, fc1_down, fc1_up, fc2_down, fc2_up, *refs = refs
    pres, acts, dpres, sem = refs
    starting = pl.program_id(0) == 0
    count = x_ref.shape[1]
    feats = x_ref.shape[-1]
    hidden = fc1_ref.shape[-1]

    def moves(first=0, last=24):
        found = [(0, 64, proj_ref, 128 * n, n) for n in range(4)]
        found += [(64 + 64 * t, 64, fc1_ref, 512 * n + 128 * t, n) for n in range(4) for t in range(4)]
        found += [(320, 256, fc2_ref, 128 * n, n) for n in range(4)]
        return [
            pltpu.make_async_copy(
                staged_ref.at[n % 2, :, n // 2, pl.ds(start, size), :],
                target.at[:, :, pl.ds(lane, 128)],
                sem.at[at],
            )
            for at, (start, size, target, lane, n) in enumerate(found)
            if first <= at < last
        ]

    def arrive(first, last):
        @pl.when(starting)
        def _():
            for copy in moves(first, last):
                copy.wait()

    @pl.when(starting)
    def _():
        for copy in moves():
            copy.start()

    for n in range(8):
        short = slice(64 * n, 64 * n + 64)
        proj_down[:, short] = tiles[0][0, n, 0, :, 0:64]
        proj_up[:, short] = tiles[0][0, n, 0, :, 64:128]
        fc1_down[:, short] = tiles[1][0, n, 0, :, 0:64]
        fc2_up[:, short] = tiles[1][0, n, 0, :, 64:128]
        for half in range(2):
            long = slice(256 * n + 128 * half, 256 * n + 128 * half + 128)
            fc1_up[:, long] = tiles[2 + half][0, n, 0]
            fc2_down[:, long] = tiles[4 + half][0, n, 0]

    def join(parts):
        return jnp.concatenate(parts, axis=0) if per_clip > 1 else parts[0]

    dy = join([dy_ref[e] for e in range(per_clip)])
    attn = join([attn_ref[e] for e in range(per_clip)])
    reduced_proj = dot(proj_down[...], attn, NT).astype(BF)
    arrive(0, 4)
    proj_w = proj_ref[...].reshape(feats, feats)
    middle = (
        join([x_ref[e].astype(F32) for e in range(per_clip)])
        + dot(attn, proj_w, NN)
        + proj_bias_ref[...]
        + dot(reduced_proj, proj_up[...], TN)
    )
    normed, inverse = norm_stats(middle)
    low = (normed * gain_ref[...]).astype(BF)
    reduced_fc1 = dot(fc1_down[...], low, NT).astype(BF)
    grad_reduced_fc2 = dot(fc2_up[...], dy, NT).astype(BF)
    per_chunk = chunk // fc2_ref.shape[1]
    steps = hidden // chunk

    def pre_of(j):
        at = slice(j * chunk, (j + 1) * chunk)
        pres[j % 2] = (
            dot(low, fc1_ref[:, :, at].reshape(feats, chunk), NN)
            + fc1_bias_ref[:, at]
            + dot(reduced_fc1, fc1_up[:, at], TN)
        )

    arrive(4, 20)
    pre_of(0)
    arrive(20, 24)
    for j in range(steps):
        at = slice(j * chunk, (j + 1) * chunk)
        if j + 1 < steps:
            pre_of(j + 1)
        fc2_w = fc2_ref[j * per_chunk : (j + 1) * per_chunk].reshape(chunk, feats)
        dact = dot(dy, fc2_w, NT) + dot(grad_reduced_fc2, fc2_down[:, at], TN)
        pre = pres[j % 2]
        bell = jnp.exp2((pre * pre) * (-0.5 * LOG2E))
        t = 1.0 / (1.0 + jnp.abs(pre) * (0.3275911 * 0.7071067811865476))
        poly = (
            (((0.5 * 1.061405429) * t - 0.5 * 1.453152027) * t + 0.5 * 1.421413741) * t
            - 0.5 * 0.284496736
        ) * t + 0.5 * 0.254829592
        tail = poly * t * bell
        below = jnp.where(pre >= 0.0, 1.0 - tail, tail)
        acts[:, at] = (pre * below).astype(BF)
        dpres[:, at] = (dact * (below + pre * bell * 0.3989422804014327)).astype(BF)
    act = acts[...]
    dpre = dpres[...]
    fc1_up_at = 3 * feats
    fc2_down_at = fc1_up_at + hidden
    fc2_up_at = fc2_down_at + hidden
    fc2_w = fc2_ref[...].reshape(hidden, feats)
    grad_reduced_fc1 = dot(fc1_up[...], dpre, NT).astype(BF)
    dlow = dot(dpre, fc1_ref[...].reshape(feats, hidden), NT) + dot(grad_reduced_fc1, fc1_down[...], TN)
    dx1 = dy.astype(F32) + norm_back(dlow, gain_ref[...], normed, inverse)
    branch = dx1.astype(BF)
    reduced_fc2 = dot(fc2_down[...], act, NT).astype(BF)
    total = (
        middle + fc2_bias_ref[...] + dot(act, fc2_w, NN) + dot(reduced_fc2, fc2_up[...], TN)
    ).astype(BF)
    grad_reduced_proj = dot(proj_up[...], branch, NT).astype(BF)
    dattn = (
        dot(branch, proj_w, NT) + dot(grad_reduced_proj, proj_down[...], TN)
    ).astype(BF)
    for e in range(per_clip):
        rows = slice(e * count, (e + 1) * count)
        act_ref[e] = total[rows]
        dx1_ref[e] = dx1[rows]
        dattn_ref[e] = dattn[rows]
    grad_ref[0, :, :feats] = dot(grad_reduced_proj, attn, NN)
    grad_ref[0, :, feats : 2 * feats] = dot(reduced_proj, branch, NN)
    grad_ref[0, :, 2 * feats : fc1_up_at] = dot(grad_reduced_fc1, low, NN)
    grad_ref[0, :, fc1_up_at:fc2_down_at] = dot(reduced_fc1, dpre, NN)
    grad_ref[0, :, fc2_down_at:fc2_up_at] = dot(grad_reduced_fc2, act, NN)
    grad_ref[0, :, fc2_up_at:] = dot(reduced_fc2, dy, NN)


PIECES = (
    (0, 0, 64),
    (0, 512, 192),
    (1, 0, 64),
    (1, 512, 64),
    (1, 1024, 64),
    (1, 5632, 64),
    (1, 1536, 256),
    (1, 3584, 256),
)


def gradient_rows(sources, part, j):
    halves = []
    for n in range(2):
        cells = []
        for array, start, width in PIECES:
            at = slice(start + j * width, start + (j + 1) * width)
            cells.append(sources[array][n, pl.ds(pl.multiple_of(part * 8, 8), 8), at])
        halves.append(jnp.concatenate(cells, axis=1))
    return jnp.concatenate(halves, axis=0)


def share_gradients(place, sources, ids_ref, refs, send, between):
    own, other, from_core, half, from_x, shares, from_clips, adapters, from_win, out = refs
    c, w, x, k = place.c, place.w, place.x, place.k
    clip_size = own.shape[0]
    for j in range(clip_size):
        other[j] = gradient_rows(sources, 1 - k, j).astype(BF)
    core_copy = send.copy(other, from_core, place.sibling)
    between[0]()
    for j in range(clip_size):
        own[j] = gradient_rows(sources, k, j)
    core_copy.wait_recv()
    own[...] += from_core[...].astype(F32)
    half[...] = own[:, :, pl.ds(pl.multiple_of((1 - x) * 512, 512), 512)].astype(BF)
    x_copy = send.copy(half, from_x, place.across)
    between[1]()
    x_copy.wait_recv()
    shares[...] = (
        own[:, :, pl.ds(pl.multiple_of(x * 512, 512), 512)] + from_x[...].astype(F32)
    ).astype(BF)
    from_clips[c] = shares[c]
    clip_copies = []
    for d in range(1, clip_size):
        to = (c + d) % clip_size
        clip_copies.append(send.copy(shares.at[to], from_clips.at[c], (to, w)))
    for copy in clip_copies:
        copy.wait_recv()
    for a in range(8):
        total = None
        for n in range(2 * clip_size):
            value = from_clips[n // 2].astype(F32)[8 * (n % 2) : 8 * (n % 2) + 8]
            value = jnp.where(ids_ref[n : n + 1, :] == float(a), value, 0.0)
            total = value if total is None else total + value
        adapters[a // 2, 8 * (a % 2) : 8 * (a % 2) + 8, :] = total
    from_win[w] = adapters[w]
    win_copies = []
    for d in range(1, 4):
        to = (w + d) % 4
        win_copies.append(send.copy(adapters.at[to], from_win.at[w], (c, to)))
    between[2]()
    for copy in win_copies:
        copy.wait_recv()
    for x2 in range(2):
        for k2 in range(2):
            for a in range(2):
                out[a, 8 * k2 : 8 * k2 + 8, 512 * x2 : 512 * x2 + 512] = from_win[
                    2 * x2 + k2, 8 * a : 8 * a + 8, :
                ]
    for copy in [core_copy, x_copy, *clip_copies, *win_copies]:
        copy.wait_send()


def attend_back_kernel(
    x_ref,
    gain_ref,
    weight_ref,
    down_ref,
    up_ref,
    probs_ref,
    attn_ref,
    qkv_ref,
    reduced_ref,
    dattn_ref,
    dx1_ref,
    *refs,
    scale,
    per_group,
    width,
    per_clip,
    remote_size,
):
    if remote_size:
        act_ref, grad_dense_ref, ids_ref, act_out_ref, dx_out_ref, sums_ref, *refs = refs
    else:
        dx_ref, grad_ref, *refs = refs
    values, keys_t, inner, dqkv, dquery_t, *refs = refs
    group = pl.program_id(1)
    groups = pl.num_programs(1)
    item = pl.program_id(0)
    step = item * groups + group
    if remote_size:
        items = act_ref.shape[0]
        place = Place(remote_size)
        act_rows = Rows(place, act_ref, *refs[:5])
        dx_own = refs[5]
        dx_rows = Rows(place, *refs[5:11])
        grad_ref = refs[11]
        share_refs, sems = refs[12:21], refs[21:]

        @pl.when(step == 0)
        def _():
            enter(
                [(place.c, (place.w + d) % 4) for d in range(1, 4)]
                + [((place.c + d) % remote_size, place.w) for d in range(1, remote_size)]
            )
            for i in range(items):
                act_rows.begin(i)

        for i in range(items):

            @pl.when(step == i + 1)
            def _():
                act_rows.mix(i)

            if i < items - 1:

                @pl.when(step == (i + 1) * 4 + 1)
                def _():
                    dx_rows.mix(i)

        @pl.when(step == 4 * items - 3)
        def _():
            for i in range(0, items, 2):
                act_rows.end(act_out_ref, i)
            act_rows.drain()

    feats = x_ref.shape[-1]
    rows = x_ref.shape[1]

    @pl.when(group == 0)
    def _():
        keys_t[...] = qkv_ref[0, :, feats : 2 * feats].T
        lane = lane_ids((rows, 128))
        ones = jnp.where(lane % width < 2, 1.0, 0.0).astype(BF)
        source = lax.broadcasted_iota(jnp.int32, (128, 128), 0)
        target = lane_ids((128, 128))
        pick = jnp.where(
            (source // width == target // width) & (target % width < 2), 1.0, 0.0
        ).astype(BF)
        pick = jnp.concatenate([pick, pick], axis=0)
        for g in range(feats // 128):
            at = slice(128 * g, 128 * g + 128)
            values[:, 256 * g : 256 * g + 128] = qkv_ref[0, :, 2 * feats + 128 * g : 2 * feats + 128 * g + 128]
            values[:, 256 * g + 128 : 256 * g + 256] = ones
            product = dattn_ref[0, :, at].astype(F32) * attn_ref[0, :, at].astype(F32)
            high = product.astype(BF)
            rest = (product - high.astype(F32)).astype(BF)
            sums = dot(jnp.concatenate([high, rest], axis=1), pick, NN)
            coarse = sums.astype(BF)
            fine = (sums - coarse.astype(F32)).astype(BF)
            inner[:, at] = -jnp.where(lane % width == 0, coarse, fine)

    blocks = pl.ds(pl.multiple_of(group * 128, 128), 128)
    values_now = values[:, pl.ds(pl.multiple_of(group * 256, 256), 256)]
    dattn_now = dattn_ref[0, :, blocks]
    inner_now = inner[:, blocks]
    query_now = qkv_ref[0, :, blocks]
    head_of_lane = lane_ids((rows, 128)) // width
    zero = jnp.zeros((rows, 128), BF)
    dvalue = None
    dkey = None
    for h in range(per_group):
        mine = head_of_lane == h
        dattn_own = jnp.where(mine, dattn_now, zero)
        query_own = jnp.where(mine, query_now, zero)
        right = jnp.concatenate([dattn_own, jnp.where(mine, inner_now, zero)], axis=1)
        probs = probs_ref[0, h]
        dscore = probs * dot(values_now, right, NT).astype(BF)
        partial = dot(probs, dattn_own, NN)
        dvalue = partial if dvalue is None else dvalue + partial
        partial = dot(dscore, query_own, NN)
        dkey = partial if dkey is None else dkey + partial
        at = pl.ds(pl.multiple_of((group * per_group + h) * width, width), width)
        dquery_t[at, :] = (dot(keys_t[at, :], dscore, NN) * scale).astype(BF)
    dqkv[:, pl.ds(pl.multiple_of(2 * feats + group * 128, 128), 128)] = dvalue.astype(BF)
    dqkv[:, pl.ds(pl.multiple_of(feats + group * 128, 128), 128)] = (dkey * LN2).astype(BF)

    @pl.when(group == groups - 1)
    def _():
        first = pl.program_id(0) % per_clip == 0
        dqkv[:, :feats] = dquery_t[...].T
        dall = dqkv[...]
        normed, inverse = norm_stats(x_ref[0].astype(F32))
        low = (normed * gain_ref[...]).astype(BF)
        grad_reduced = dot(up_ref[0], dall, NT).astype(BF)
        slot = item // per_clip if remote_size else 0
        add_rows(grad_ref, slot, slice(feats, 4 * feats), dot(reduced_ref[0], dall, NN), first)
        add_rows(grad_ref, slot, slice(0, feats), dot(grad_reduced, low, NN), first)
        dlow = (dot(dall, weight_ref[...], NT) + dot(grad_reduced, down_ref[0], TN)).astype(BF)
        dx = (dx1_ref[0] + norm_back(dlow.astype(F32), gain_ref[...], normed, inverse)).astype(BF)
        if not remote_size:
            dx_ref[0] = dx
            return
        dx_own[item] = dx
        for i in range(items):

            @pl.when(item == i)
            def _():
                dx_rows.begin(i)

    if remote_size:

        @pl.when(step == 4 * items - 1)
        def _():
            share_gradients(
                place,
                (grad_ref, grad_dense_ref),
                ids_ref,
                (*share_refs, sums_ref),
                Sender(*sems),
                (
                    lambda: dx_rows.mix(items - 1),
                    lambda: None,
                    lambda: [dx_rows.end(dx_out_ref, i) for i in range(0, items, 2)],
                ),
            )
            dx_rows.drain()


def whole(shape):
    return pl.BlockSpec(shape, lambda *at: (0,) * len(shape), pipeline_mode=pl.Buffered(1))


def compute(first, dy, adapter_ids, vectors, later, per_clip, remote_size):
    if remote_size:
        heads = first[1].shape[0]
        x_shape, rank = dy.shape, 16
    else:
        x, qkv_w, qkv_down, qkv_up, table = first
        heads, rank = table.shape[0], qkv_down.shape[1]
    items, rows, feats = dy.shape
    width = feats // heads
    per_group = 128 // width
    groups = heads // per_group
    scale = width**-0.5
    hidden = 4 * feats
    clips = items // per_clip

    def item(shape):
        return pl.BlockSpec((1, *shape), lambda i, *rest: (i,) + (0,) * len(shape))

    item_ids = adapter_ids
    any_space = pl.BlockSpec(memory_space=pl.ANY)

    def of_clip(shape):
        return pl.BlockSpec((1, *shape), lambda i, *rest: (i // per_clip, 0, 0))

    sems = pltpu.SemaphoreType.DMA
    if remote_size:
        shape = jax.ShapeDtypeStruct
        adapters = 8
        padded = 56 * heads
        ids = jnp.pad(adapter_ids.astype(F32)[None], ((0, 0), (0, 126)))
        args = (*first, ids, *[v.reshape(1, -1) for v in vectors], dy, *later)
        arg_specs = [whole(a.shape) for a in args]
        sent_out = [
            shape(dy.shape, BF),
            shape((2, remote_size, 2, 768, 128), BF),
            shape(dy.shape, BF),
            shape((feats, 3 * feats), BF),
            *[shape((1, n), F32) for n in (feats, feats, feats, hidden, feats)],
            shape((2 * remote_size, 512), F32),
        ]
        sent_specs = [whole(a.shape) for a in sent_out]
        sent_specs[1] = any_space
        row_scratch = [
            pltpu.VMEM(dy.shape, BF),
            pltpu.VMEM(dy.shape, BF),
            pltpu.VMEM((items, TOP, feats), BF),
            sems((2 * items,)),
            sems((2 * items,)),
        ]
        sent_scratch = [
            pltpu.VMEM((1, 3 * feats), F32),
            pltpu.VMEM((adapters, rank, feats), BF),
            pltpu.VMEM((adapters, rank, 3 * feats), BF),
            pltpu.VMEM((64, 512), BF),
            pltpu.VMEM((8, 128), F32),
            pltpu.VMEM((768, 128), BF),
            pltpu.VMEM((2, remote_size, 2, 64, 512), BF),
            pltpu.VMEM((remote_size, 8, 128), F32),
            pltpu.VMEM((15 * heads, 176), BF),
            pltpu.VMEM((15, padded, 128), F32),
            pltpu.VMEM((padded, 15 * 128), BF),
            pltpu.VMEM((8 * 128, rows), BF),
            *row_scratch,
            *row_scratch,
            *[sems((Gather.COPIES,)) for _ in range(4)],
            sems((remote_size,)),
            sems((remote_size,)),
            sems,
        ]
    else:
        gain1, qkv_bias, proj_bias, gain2, fc1_bias, fc2_bias = vectors
        clip_ids = jnp.broadcast_to(adapter_ids.astype(F32)[:, None], (clips, 128))
        args = (x, gain1, qkv_w, qkv_bias, clip_ids, qkv_down, qkv_up, table)
        arg_specs = [item((rows, feats)), *[whole(a.shape) for a in args[1:7]], any_space]
        sent_out, sent_specs, sent_scratch = [], [], []

    probs, attn, qkv, reduced, down_own, up_own, *arrived = pl.pallas_call(
        functools.partial(
            attend_kernel,
            scale=scale,
            per_group=per_group,
            width=width,
            per_clip=per_clip,
            remote_size=remote_size,
        ),
        grid=(items, groups),
        in_specs=arg_specs,
        out_specs=[
            pl.BlockSpec((1, per_group, rows, rows), lambda i, g: (i, g, 0, 0)),
            item((rows, feats)),
            item((rows, 3 * feats)),
            item((rank, rows)),
            of_clip((rank, feats)),
            of_clip((rank, 3 * feats)),
            *sent_specs,
        ],
        scratch_shapes=[
            pltpu.VMEM((rows, 2 * feats), BF),
            pltpu.VMEM((rows, feats), BF),
            pltpu.VMEM((feats, rows), BF),
            pltpu.VMEM((feats, rows), BF),
            pltpu.VMEM((2, rows, rows), F32),
            pltpu.VMEM((heads, rows, rows), F32),
            sems((groups,)),
            pltpu.VMEM((rows, 128), BF),
            *sent_scratch,
        ],
        out_shape=[
            jax.ShapeDtypeStruct((items, heads, rows, rows), BF),
            jax.ShapeDtypeStruct((items, rows, feats), BF),
            jax.ShapeDtypeStruct((items, rows, 3 * feats), BF),
            jax.ShapeDtypeStruct((items, rank, rows), BF),
            jax.ShapeDtypeStruct((clips, rank, feats), BF),
            jax.ShapeDtypeStruct((clips, rank, 3 * feats), BF),
            *sent_out,
        ],
        compiler_params=pltpu.CompilerParams(
            vmem_limit_bytes=VMEM_LIMIT,
            dimension_semantics=("arbitrary", "arbitrary"),
            **({"collective_id": 2, "has_side_effects": True} if remote_size else {}),
        ),
        cost_estimate=pl.CostEstimate(flops=4 * 10**10, bytes_accessed=10**7, transcendentals=0),
        name="attend",
    )(*args)
    if remote_size:
        dy, staged, x, qkv_w, gain1, proj_bias, gain2, fc1_bias, fc2_bias, all_ids = arrived
    else:
        (staged,) = later

    span = 4 * feats + 2 * hidden
    def tile(n):
        def index(c, ids):
            return ids[c] // 2 % 2, 0, ids[c] // 4, 36 + 2 * n + ids[c] % 2, 0

        return pl.BlockSpec((1, 8, 1, rank, 128), index)

    def clip(array_shape):
        return pl.BlockSpec((per_clip, *array_shape[1:]), lambda c, ids: (c, 0, 0))

    chunk = 512
    act, dx1, dattn, grad_dense = pl.pallas_call(
        functools.partial(dense_kernel, per_clip=per_clip, chunk=chunk),
        grid_spec=pltpu.PrefetchScalarGridSpec(
            num_scalar_prefetch=1,
            grid=(clips,),
            in_specs=[
                clip(x.shape),
                clip(x.shape),
                whole(gain2.shape),
                whole(proj_bias.shape),
                whole(fc1_bias.shape),
                whole(fc2_bias.shape),
                clip(x.shape),
                any_space,
                *[tile(n) for n in range(6)],
            ],
            out_specs=[
                clip(x.shape),
                clip(x.shape),
                clip(x.shape),
                pl.BlockSpec((1, rank, span), lambda c, ids: (c, 0, 0)),
            ],
            scratch_shapes=[
                pltpu.VMEM((8, feats // 8, feats), BF),
                pltpu.VMEM((8, feats // 8, hidden), BF),
                pltpu.VMEM((8, hidden // 8, feats), BF),
                *[pltpu.VMEM((rank, n), BF) for n in (feats, feats, feats, hidden, hidden, feats)],
                pltpu.VMEM((2, per_clip * rows, chunk), F32),
                pltpu.VMEM((per_clip * rows, hidden), BF),
                pltpu.VMEM((per_clip * rows, hidden), BF),
                pltpu.SemaphoreType.DMA((24,)),
            ],
        ),
        out_shape=[
            jax.ShapeDtypeStruct((items, rows, feats), BF),
            jax.ShapeDtypeStruct((items, rows, feats), F32),
            jax.ShapeDtypeStruct((items, rows, feats), BF),
            jax.ShapeDtypeStruct((clips, rank, span), F32),
        ],
        compiler_params=pltpu.CompilerParams(
            vmem_limit_bytes=VMEM_LIMIT, dimension_semantics=("arbitrary",)
        ),
        cost_estimate=pl.CostEstimate(flops=5 * 10**10, bytes_accessed=10**7, transcendentals=0),
        name="dense",
    )(
        item_ids, x, attn, gain2, proj_bias, fc1_bias, fc2_bias, dy, staged, *([staged] * 6)
    )

    if remote_size:
        assert (clips, per_clip) == (2, 2)
        count = remote_size
        back_in = (act, grad_dense, all_ids)
        back_out = [whole(x.shape), whole(x.shape), whole((2, rank, 1024))]
        back_shape = [
            jax.ShapeDtypeStruct(x.shape, BF),
            jax.ShapeDtypeStruct(x.shape, BF),
            jax.ShapeDtypeStruct((2, rank, 1024), F32),
        ]
        back_scratch = [
            *row_scratch,
            pltpu.VMEM(x.shape, BF),
            *row_scratch,
            pltpu.VMEM((clips, rank, 4 * feats), F32),
            pltpu.VMEM((count, 16, 1024), F32),
            pltpu.VMEM((count, 16, 1024), BF),
            pltpu.VMEM((count, 16, 1024), BF),
            pltpu.VMEM((count, 16, 512), BF),
            pltpu.VMEM((count, 16, 512), BF),
            pltpu.VMEM((count, 16, 512), BF),
            pltpu.VMEM((count, 16, 512), BF),
            pltpu.VMEM((4, 16, 512), F32),
            pltpu.VMEM((4, 16, 512), F32),
            sems((16,)),
            sems((16,)),
        ]
    else:
        back_in, back_scratch = (), []
        back_out = [
            item((rows, feats)),
            pl.BlockSpec((1, rank, 4 * feats), lambda i, g: (i // per_clip, 0, 0)),
        ]
        back_shape = [
            jax.ShapeDtypeStruct((items, rows, feats), BF),
            jax.ShapeDtypeStruct((clips, rank, 4 * feats), F32),
        ]
    results = pl.pallas_call(
        functools.partial(
            attend_back_kernel,
            scale=scale,
            per_group=per_group,
            width=width,
            per_clip=per_clip,
            remote_size=remote_size,
        ),
        grid=(items, groups),
        in_specs=[
            item((rows, feats)),
            whole(gain1.shape),
            whole(qkv_w.shape),
            of_clip((rank, feats)),
            of_clip((rank, 3 * feats)),
            pl.BlockSpec((1, per_group, rows, rows), lambda i, g: (i, g, 0, 0)),
            item((rows, feats)),
            item((rows, 3 * feats)),
            item((rank, rows)),
            item((rows, feats)),
            item((rows, feats)),
            *[whole(a.shape) for a in back_in],
        ],
        out_specs=back_out,
        scratch_shapes=[
            pltpu.VMEM((rows, 2 * feats), BF),
            pltpu.VMEM((feats, rows), BF),
            pltpu.VMEM((rows, feats), BF),
            pltpu.VMEM((rows, 3 * feats), BF),
            pltpu.VMEM((feats, rows), BF),
            *back_scratch,
        ],
        out_shape=back_shape,
        compiler_params=pltpu.CompilerParams(
            vmem_limit_bytes=VMEM_LIMIT, dimension_semantics=("arbitrary", "arbitrary"),
            **({"collective_id": 1, "has_side_effects": True} if remote_size else {}),
        ),
        cost_estimate=pl.CostEstimate(flops=5 * 10**10, bytes_accessed=10**7, transcendentals=0),
        name="attend_back",
    )(x, gain1, qkv_w, down_own, up_own, probs, attn, qkv, reduced, dattn, dx1, *back_in)
    if remote_size:
        return results
    return (act, *results, grad_dense)


def exchange(x, win_size):
    local = x.shape[1]
    bits = local.bit_length() - 1
    at = jnp.arange(TOK)
    taken = (at // 49 < 4, at // 7 % 7 < 3, at % 7 < 3)
    for bit, rows in zip((2, 1, 0), taken):
        if bit < bits:
            split = x.reshape(x.shape[0], local >> (bit + 1), 2, 1 << bit, TOK, -1)
            other = jnp.flip(split, axis=2).reshape(x.shape)
        else:
            other = lax.ppermute(x, "win", [(i, i ^ 1 << bit - bits) for i in range(win_size)])
        x = jnp.where(rows[None, None, :, None], other, x)
    return x


def bias_by_pair(table):
    heads = table.shape[0]
    side = jnp.arange(49)
    high, wide = (side // 7 + 4) % 7, (side % 7 + 4) % 7
    offset = (high[None, :] - high[:, None] + 6) * 13 + wide[None, :] - wide[:, None] + 6
    pick = (jnp.arange(169)[:, None, None] == offset[None]).astype(BF)
    found = jnp.einsum(
        "mad,dkq->mkaq", table.reshape(heads, 15, 169), pick, preferred_element_type=F32
    )
    found = (found * LOG2E).reshape(heads, 49, 15 * 49)
    blocks = []
    for key_block in range(8):
        t = (key_block + 4) % 8
        blocks.append(
            jnp.concatenate(
                (found[..., (11 - t) * 49 : (15 - t) * 49], found[..., (7 - t) * 49 : (11 - t) * 49]),
                axis=-1,
            )
        )
    return jnp.stack(blocks, axis=1).reshape(heads, TOK, TOK)


def gather(array, spec):
    for axis, name in enumerate(spec):
        if name is not None:
            array = lax.all_gather(array, name, axis=axis, tiled=True)
    return array


def stage_whole(proj_w, fc1_w, fc2_w, maps):
    proj_down, proj_up, fc1_down, fc1_up, fc2_down, fc2_up = maps
    count = proj_down.shape[0]

    def short(a):
        return a.reshape(4, count // 4 * 16, 8, 64).transpose(2, 0, 1, 3)

    def long(a):
        return a.reshape(4, count // 4 * 16, 8, 2, 128).transpose(2, 0, 3, 1, 4).reshape(8, 4, -1, 128)

    return jnp.concatenate(
        (
            proj_w.reshape(8, 64, 4, 128).transpose(0, 2, 1, 3),
            fc1_w.reshape(8, 64, 4, 4, 128).transpose(0, 2, 3, 1, 4).reshape(8, 4, 256, 128),
            fc2_w.reshape(8, 256, 4, 128).transpose(0, 2, 1, 3),
            jnp.concatenate((short(proj_down), short(proj_up)), axis=-1),
            jnp.concatenate((short(fc1_down), short(fc2_up)), axis=-1),
            long(fc1_up),
            long(fc2_down),
        ),
        axis=2,
    )


def by_core(staged):
    return staged.reshape(8, 2, 2, *staged.shape[2:]).transpose(2, 0, 1, 3, 4)


def per_device(
    tokens, cotangent, adapter_ids, ln1_gain, qkv_weight, qkv_bias, proj_weight, proj_bias, ln2_gain,
    fc1_weight, fc1_bias, fc2_weight, fc2_bias, bias_table, qkv_down, qkv_up, proj_down, proj_up,
    fc1_down, fc1_up, fc2_down, fc2_up, *, clip_size, win_size,
):
    clips, local, rows, feats = tokens.shape
    items = clips * local
    heads = bias_table.shape[0]
    vecs = (ln1_gain, qkv_bias, proj_bias, ln2_gain, fc1_bias, fc2_bias)
    flat = (items, rows, feats)
    downs = [a.transpose(0, 2, 1) for a in (qkv_down, proj_down, fc1_down, fc2_down)]
    own_kernels = (clip_size, win_size, clips, local) == (8, 4, 2, 2)
    if own_kernels:
        first = (tokens.reshape(flat), bias_table, qkv_weight, downs[0], qkv_up)
        dy = cotangent.reshape(flat)
        vectors = vecs
        later = (proj_weight, fc1_weight, fc2_weight, downs[1], proj_up, downs[2], fc1_up, downs[3], fc2_up)
    else:
        grid2, by_down, by_up = ("clip", "win"), ("win", None, "clip"), ("win", None, "clip")
        maps = (downs[1], proj_up, downs[2], fc1_up, downs[3], fc2_up)
        staged = stage_whole(
            *[gather(a, grid2) for a in (proj_weight, fc1_weight, fc2_weight)],
            [gather(a, by_up) for a in maps],
        )
        later = (by_core(staged),)
        vectors = [gather(v, ("clip",)).reshape(1, -1).astype(F32) for v in vecs]
        first = (
            exchange(tokens, win_size).reshape(flat),
            gather(qkv_weight, grid2),
            gather(downs[0], by_down),
            gather(qkv_up, by_up),
            bias_by_pair(bias_table),
        )
        dy = exchange(cotangent, win_size).reshape(flat)
    results = compute(
        first, dy, adapter_ids, vectors, later, local, clip_size if own_kernels else 0
    )
    if own_kernels:
        act_out, dx_out, sums = results
        qd, qu, pd, pu, f1d, f2u, f1u, f2d = [
            sums[..., first:last]
            for first, last in zip(
                (0, 64, 256, 320, 384, 448, 512, 768), (64, 256, 320, 384, 448, 512, 768, 1024)
            )
        ]
        turned = [a.transpose(0, 2, 1) for a in (qd, pd, f1d, f2d)]
        return (
            act_out.reshape(tokens.shape), dx_out.reshape(tokens.shape),
            turned[0], qu, turned[1], pu, turned[2], f1u, turned[3], f2u,
        )
    act, dx, grad_qkv, grad_dense = results
    activations = exchange(act.reshape(tokens.shape), win_size)
    input_grad = exchange(dx.reshape(tokens.shape), win_size)
    adapter_count = win_size * qkv_down.shape[0]
    hot = (adapter_ids[:, None] == jnp.arange(adapter_count)[None]).astype(F32)
    hidden = fc1_weight.shape[1] * win_size
    spans = (feats, 3 * feats, feats, feats, feats, hidden, hidden, feats)
    grads = jnp.concatenate((grad_qkv, grad_dense), axis=-1)
    rank = grads.shape[1]
    parts, at = [], 0
    for span in spans:
        parts.append(
            grads[..., at : at + span].reshape(clips, rank, clip_size, span // clip_size)
        )
        at += span
    mine = jnp.concatenate(parts, axis=-1)
    grown = jnp.sum(hot[:, :, None, None, None] * mine[:, None], axis=0)
    grown = grown.transpose(2, 0, 1, 3).astype(BF)
    total = lax.psum_scatter(grown, "clip", scatter_dimension=0, tiled=True)[0]
    total = lax.psum_scatter(total, "win", scatter_dimension=0, tiled=True).astype(F32)
    outs, at = [], 0
    for n, span in enumerate(spans):
        width = span // clip_size
        part = total[..., at : at + width]
        at += width
        outs.append(part.transpose(0, 2, 1) if n % 2 == 0 else part)
    return (activations, input_grad, *outs)


def solution(mesh):
    split = P("clip", "win", None, None)
    grid2 = P("clip", "win")
    down = P("win", "clip", None)
    up = P("win", None, "clip")
    one = P("clip")
    return jax.shard_map(
        functools.partial(
            per_device, clip_size=mesh.shape["clip"], win_size=mesh.shape["win"]
        ),
        mesh=mesh,
        in_specs=(
            split, split, one, one, grid2, one, grid2, one, one, grid2, one, grid2, one, P(),
            down, up, down, up, down, up, down, up,
        ),
        out_specs=(split, split, down, up, down, up, down, up, down, up),
        check_vma=False,
    )
```

```python
import functools
import jax
import jax.numpy as jnp
from jax import lax
from jax.experimental import pallas as pl
from jax.experimental.pallas import tpu as pltpu
from jax.sharding import PartitionSpec as P

BF = jnp.bfloat16
F32 = jnp.float32
NN = (((1,), (0,)), ((), ()))
NT = (((1,), (1,)), ((), ()))
TN = (((0,), (0,)), ((), ()))
LOG2E = 1.4426950408889634
LN2 = 0.6931471805599453
FAR = 1e9
VMEM_LIMIT = 60 * 2**20
TOK = 392
TOP = 208


def dot(left, right, dims):
    return lax.dot_general(left, right, dims, preferred_element_type=F32)


def lane_ids(shape):
    return lax.broadcasted_iota(jnp.int32, shape, len(shape) - 1)


def norm_stats(values):
    average = jnp.mean(values, axis=-1, keepdims=True)
    centred = values - average
    variance = jnp.mean(centred * centred, axis=-1, keepdims=True)
    inverse = lax.rsqrt(variance + 1e-05)
    return centred * inverse, inverse


def norm_back(gradient, gain, normed, inverse):
    scaled = gradient * gain
    centre = jnp.mean(scaled, axis=-1, keepdims=True)
    slope = jnp.mean(scaled * normed, axis=-1, keepdims=True)
    return inverse * (scaled - centre - normed * slope)


def add_rows(ref, n, at, value, first):
    @pl.when(first)
    def _():
        ref[n, :, at] = value

    @pl.when(jnp.logical_not(first))
    def _():
        ref[n, :, at] += value


MESH = pl.DeviceIdType.MESH


def enter(peers):
    barrier = pltpu.get_barrier_semaphore()
    for peer in peers:
        pl.semaphore_signal(barrier, inc=1, device_id=peer, device_id_type=MESH)
    pl.semaphore_wait(barrier, len(peers))


def remote(src, dst, send_sem, recv_sem, peer):
    return pltpu.make_async_remote_copy(
        src_ref=src,
        dst_ref=dst,
        send_sem=send_sem,
        recv_sem=recv_sem,
        device_id=peer,
        device_id_type=MESH,
    )


class Sender:
    def __init__(self, send_sem, recv_sem):
        self.send_sem, self.recv_sem, self.count = send_sem, recv_sem, 0

    def copy(self, src, dst, peer):
        n = self.count
        self.count += 1
        made = remote(src, dst, self.send_sem.at[n], self.recv_sem.at[n], peer)
        made.start()
        return made


def row_masks(rows):
    row = lax.broadcasted_iota(jnp.int32, (rows, 128), 0)
    return row < TOK // 2, row % 49 < 21, row % 7 < 3


def choose(mask, first, second):
    return jnp.concatenate(
        [
            jnp.where(mask, first[:, at : at + 128], second[:, at : at + 128])
            for at in range(0, first.shape[1], 128)
        ],
        axis=1,
    )


class Rows:
    def __init__(self, place, own, beside, mixed, tops, send_sem, recv_sem):
        self.place, self.own, self.beside, self.mixed, self.tops = place, own, beside, mixed, tops
        self.send_sem, self.recv_sem = send_sem, recv_sem
        self.items, self.rows, self.feats = own.shape

    def copy(self, kind, i):
        n = kind * self.items + i
        sems = self.send_sem.at[n], self.recv_sem.at[n]
        if kind == 0:
            return remote(self.own.at[i], self.beside.at[i], *sems, self.place.sibling)
        top = self.mixed.at[i, pl.ds(0, TOP)]
        return remote(top, self.tops.at[i], *sems, self.place.across)

    def begin(self, i):
        self.copy(0, i).start()

    def mix(self, i):
        self.copy(0, i).wait_recv()
        self.mixed[i] = choose(row_masks(self.rows)[1], self.beside[i], self.own[i])
        self.copy(1, i).start()

    def end(self, out, i):
        early, _, low_w = row_masks(self.rows)
        both = []
        for e in range(2):
            self.copy(1, i + e).wait_recv()
            top = choose(early[:TOP], self.tops[i + e], self.mixed[i + e, :TOP])
            both.append(jnp.concatenate([top, self.mixed[i + e, TOP:]], axis=0))
        for e in range(2):
            out[i + e] = choose(low_w, both[1 - e], both[e])

    def drain(self):
        for i in range(self.items):
            self.copy(0, i).wait_send()
            self.copy(1, i).wait_send()


class Place:
    def __init__(self, clip_size):
        self.c, self.w = lax.axis_index("clip"), lax.axis_index("win")
        self.z, self.y = self.c // 2, self.c % 2
        self.x, self.k = self.w // 2, self.w % 2
        self.zs = clip_size // 2
        self.sibling = (self.c, self.x * 2 + 1 - self.k)
        self.across = (self.c, (1 - self.x) * 2 + self.k)

    def clip_at(self, z_step, other_y):
        return (self.z + z_step + self.zs) % self.zs * 2 + (1 - self.y if other_y else self.y)

    def along_z(self, step):
        return (self.clip_at(step, False), self.w)

    def along_y(self):
        return (self.clip_at(0, True), self.w)


class Gather:
    COPIES = 29

    def __init__(self, place, unit, units, send_sem, recv_sem):
        self.place, self.unit, self.units = place, unit, units
        self.send_sem, self.recv_sem = send_sem, recv_sem
        self.hops = range(place.zs - 1)

    def make(self, kind, t=0):
        p, units = self.place, self.units
        kinds = ("up", "down", "y_up", "y_down", "s_up", "s_down", "sy_up", "sy_down")
        single = ("across", "own", "theirs", "y", "s_y")
        n = single.index(kind) if kind in single else 5 + 8 * t + kinds.index(kind)
        sems = self.send_sem.at[n], self.recv_sem.at[n]
        mine = units.at[p.k, p.c, p.x]
        if kind == "across":
            return remote(self.unit, mine, *sems, p.across)
        if kind == "own":
            return remote(self.unit, mine, *sems, p.sibling)
        if kind == "theirs":
            part = units.at[p.k, p.c, 1 - p.x]
        elif kind == "y":
            part = units.at[p.k, p.c]
        elif kind == "s_y":
            part = units.at[p.k, p.z * 2 + 1 - p.y]
        else:
            sign = -1 if kind.endswith("up") else 1
            far = p.z + sign * (t if kind in ("up", "down") else t + 1)
            part = units.at[p.k, far * 2 + (1 - p.y if kind.startswith("sy") else p.y)]
        if kind in ("up", "down"):
            peer = (p.c - 2 * sign, p.w)
        else:
            peer = p.along_y() if kind.startswith("y") else p.sibling
        return remote(part, part, *sems, peer)

    def when(self, kind, t, sending, act):
        p, last = self.place, self.place.zs - 1
        if kind.endswith("up"):
            holds = (p.z >= t) & (p.z < last) if sending and kind == "up" else p.z >= t + 1
        elif kind.endswith("down"):
            holds = (p.z <= last - t) & (p.z > 0) if sending and kind == "down" else p.z <= last - 1 - t
        else:
            act()
            return
        pl.when(holds)(act)

    def start(self, kind, t=0):
        self.when(kind, t, True, lambda: self.make(kind, t).start())

    def wait_recv(self, kind, t=0):
        self.when(kind, t, False, lambda: self.make(kind, t).wait_recv())

    def wait_send(self, kind, t=0):
        self.when(kind, t, True, lambda: self.make(kind, t).wait_send())

    def begin(self):
        self.start("across")
        self.start("own")

    def second(self):
        self.wait_recv("across")
        for kind in ("up", "down", "y", "theirs"):
            self.start(kind)

    def from_z(self, t):
        for way in ("up", "down"):
            self.wait_recv(way, t)
            if t + 1 in self.hops:
                self.start(way, t + 1)
            self.start("y_" + way, t)
            self.start("s_" + way, t)

    def from_y(self, t):
        if t < 0:
            self.wait_recv("y")
            self.start("s_y")
        else:
            for way in ("up", "down"):
                self.wait_recv("y_" + way, t)
                self.start("sy_" + way, t)

    def finish(self):
        for kind in ("own", "theirs", "s_y"):
            self.wait_recv(kind)
        for t in self.hops:
            for kind in ("s_up", "s_down", "sy_up", "sy_down"):
                self.wait_recv(kind, t)
        for kind in ("across", "own", "theirs", "y", "s_y"):
            self.wait_send(kind)
        for t in self.hops:
            for kind in ("up", "down", "y_up", "y_down", "s_up", "s_down", "sy_up", "sy_down"):
                self.wait_send(kind, t)


def pack_first(unit, vec, qkv_ref, qd_ref, qu_ref, ids_ref, vec_refs):
    unit[:, 0:384] = qkv_ref[...]
    for a in range(2):
        unit[16 * a : 16 * a + 16, 384:448] = qd_ref[a]
        unit[16 * a : 16 * a + 16, 448:512] = qu_ref[a, :, 0:64]
        unit[32 + 16 * a : 48 + 16 * a, 384:512] = qu_ref[a, :, 64:192]
    g1_ref, qb_ref, pb_ref, g2_ref, f1b_ref, f2b_ref = vec_refs
    vec[0:1, 0:64] = g1_ref[...].astype(F32)
    vec[0:1, 64:128] = qb_ref[:, 0:64].astype(F32)
    vec[1:2, :] = qb_ref[:, 64:192].astype(F32)
    vec[2:3, 0:64] = pb_ref[...].astype(F32)
    vec[2:3, 64:128] = g2_ref[...].astype(F32)
    vec[3:4, :] = f1b_ref[:, 0:128].astype(F32)
    vec[4:5, :] = f1b_ref[:, 128:256].astype(F32)
    vec[5:6, 0:64] = f2b_ref[...].astype(F32)
    vec[5:6, 64:128] = jnp.zeros((1, 64), F32)
    vec[5:6, 64:66] = ids_ref[...].astype(F32)
    vec[6:8, :] = jnp.zeros((2, 128), F32)


def unpack_vectors(vecs, outs):
    gain1, qkv_bias, proj_bias, gain2, fc1_bias, fc2_bias, ids = outs
    for c in range(vecs.shape[0]):
        v = vecs[c]
        short = slice(64 * c, 64 * c + 64)
        gain1[:, short] = v[0:1, 0:64]
        qkv_bias[:, 192 * c : 192 * c + 64] = v[0:1, 64:128]
        qkv_bias[:, 192 * c + 64 : 192 * c + 192] = v[1:2, :]
        proj_bias[:, short] = v[2:3, 0:64]
        gain2[:, short] = v[2:3, 64:128]
        fc1_bias[:, 256 * c : 256 * c + 128] = v[3:4, :]
        fc1_bias[:, 256 * c + 128 : 256 * c + 256] = v[4:5, :]
        fc2_bias[:, short] = v[5:6, 0:64]
        for n in range(2):
            ids[2 * c + n : 2 * c + n + 1, :] = jnp.broadcast_to(
                v[5:6, 64 + n : 65 + n], (1, ids.shape[1])
            )


def unpack_first(units, weight, down, up):
    for c in range(units.shape[1]):
        for n in range(4):
            unit = units.at[n % 2, c, n // 2]
            weight[64 * c : 64 * c + 64, 384 * n : 384 * n + 384] = unit[:, 0:384]
            for a in range(2):
                low = unit[16 * a : 16 * a + 16, 384:512]
                high = unit[32 + 16 * a : 48 + 16 * a, 384:512]
                down[2 * n + a, :, 64 * c : 64 * c + 64] = low[:, 0:64]
                up[2 * n + a, :, 192 * c : 192 * c + 64] = low[:, 64:128]
                up[2 * n + a, :, 192 * c + 64 : 192 * c + 192] = high


def pack_second(unit, refs):
    proj_ref, fc1_ref, fc2_ref, pd_ref, pu_ref, f1d_ref, f1u_ref, f2d_ref, f2u_ref = refs
    unit[0:64] = proj_ref[...]
    for t in range(4):
        unit[64 + 64 * t : 128 + 64 * t] = fc1_ref[:, 128 * t : 128 * t + 128]
    unit[320:576] = fc2_ref[...]
    for a in range(2):
        at = 576 + 16 * a
        unit[at : at + 16, 0:64] = pd_ref[a]
        unit[at : at + 16, 64:128] = pu_ref[a]
        unit[at + 32 : at + 48, 0:64] = f1d_ref[a]
        unit[at + 32 : at + 48, 64:128] = f2u_ref[a]
        for half in range(2):
            lanes = slice(128 * half, 128 * half + 128)
            unit[at + 64 + 32 * half : at + 80 + 32 * half] = f1u_ref[a, :, lanes]
            unit[at + 128 + 32 * half : at + 144 + 32 * half] = f2d_ref[a, :, lanes]


class Bias:
    def __init__(self, source, table, pairs, found, wide, select):
        self.source, self.table, self.pairs, self.found = source, table, pairs, found
        self.wide, self.select = wide, select
        self.heads = source.shape[0]

    def prepare(self):
        heads, pairs = self.heads, self.pairs
        pairs[...] = jnp.zeros(pairs.shape, BF)
        for a in range(15):
            pairs[a * heads : (a + 1) * heads, 0:169] = self.source[:, 169 * a : 169 * a + 169]

    def first(self, start, end):
        heads, pairs, found = self.heads, self.pairs, self.found
        lane = lane_ids((pairs.shape[1], 128))
        row = lax.broadcasted_iota(jnp.int32, (pairs.shape[1], 128), 0)
        query_at = (lane // 7 + 4) % 7 * 13 + (lane % 7 + 4) % 7
        wanted = jnp.where(lane < 49, row - query_at - 84, 10000)

        def one_key(key, carry):
            key_at = (key // 7 + 4) % 7 * 13 + (key % 7 + 4) % 7
            pick = jnp.where(wanted + key_at == 0, 1.0, 0.0).astype(BF)
            value = dot(pairs[...], pick, NN)
            for a in range(15):
                found[a, pl.ds(key, heads, stride=56), :] = value[a * heads : (a + 1) * heads]
            return carry

        lax.fori_loop(start, end, one_key, 0, unroll=2)

    def middle(self):
        for a in range(15):
            self.wide[:, 128 * a : 128 * a + 128] = self.found[a].astype(BF)
        row = lax.broadcasted_iota(jnp.int32, (128, TOK), 0)
        gap = lane_ids((128, TOK)) - row
        for t in range(8):
            self.select[128 * t : 128 * t + 128, :] = jnp.where(
                (gap == (t + 4) % 8 * 49) & (row < 49), 1.0, 0.0
            ).astype(BF)

    def last(self, blocks):
        for block in blocks:
            t = (block + 4) % 8
            value = dot(self.wide[:, (7 - t) * 128 : (15 - t) * 128], self.select[...], NN) * LOG2E
            for m in range(self.heads):
                self.table[m, 49 * block : 49 * block + 49, :] = value[56 * m : 56 * m + 49]


def attend_kernel(*refs, scale, per_group, width, per_clip, remote_size):
    if remote_size:
        tok_ref, source_ref, *refs = refs
        first_refs, vec_refs, refs = refs[:4], refs[4:10], refs[10:]
        dy_ref, second_refs, refs = refs[0], refs[1:10], refs[10:]
    else:
        x_ref, gain_ref, weight_ref, bias_ref, ids_ref, down_ref, up_ref, table_ref, *refs = refs
    probs_ref, out_ref, qkv_ref, reduced_ref, down_own, up_own, *refs = refs
    if remote_size:
        dy_out_ref, units_ref, x_ref, weight_ref, gain_ref, *vec_outs, ids_ref = refs[:10]
        refs = refs[10:]
    keys, queries, values_t, out_t, scores, table, table_sem, query_mask, *refs = refs
    group = pl.program_id(1)
    groups = pl.num_programs(1)
    item = pl.program_id(0)
    step = item * groups + group
    feats = x_ref.shape[-1]
    rows = x_ref.shape[1]

    if remote_size:
        bias_ref, down_ref, up_ref, unit1, vec, unit2, units1, vecs, *refs = refs
        bias = Bias(source_ref, table, *refs[:4])
        place = Place(remote_size)
        x_rows = Rows(place, tok_ref, *refs[4:9])
        dy_rows = Rows(place, dy_ref, *refs[9:14])
        gather1 = Gather(place, unit1, units1, *refs[14:16])
        gather2 = Gather(place, unit2, units_ref, *refs[16:18])
        vec_send, vec_recv, own_sem = refs[18:]
        items = dy_ref.shape[0]

        def vec_copy(d):
            to = ((place.c + d) % remote_size, place.w)
            return remote(vec, vecs.at[place.c], vec_send.at[d], vec_recv.at[d], to)

        @pl.when(step == 0)
        def _():
            pack_first(unit1, vec, *first_refs, vec_refs)
            pack_second(unit2, second_refs)
            mine = place.k, place.c, place.x
            units1[mine] = unit1[...]
            vecs[place.c] = vec[...]
            own = pltpu.make_async_copy(unit2, units_ref.at[mine], own_sem)
            own.start()
            enter(
                [place.sibling, place.across]
                + [((place.c + d) % remote_size, place.w) for d in range(1, remote_size)]
            )
            gather1.begin()
            for i in range(items):
                x_rows.begin(i)
            for d in range(1, remote_size):
                vec_copy(d).start()
            bias.prepare()
            gather1.second()
            pl.loop(0, items)(x_rows.mix)
            bias.first(0, 16)
            gather1.from_z(0)
            bias.first(16, 32)
            gather1.from_y(-1)
            gather1.from_z(1)
            bias.first(32, 50)
            gather1.from_y(0)
            gather1.from_z(2)
            bias.middle()
            gather1.from_y(1)
            bias.last(range(0, 4))
            gather1.from_y(2)
            own.wait()
            gather2.begin()
            bias.last(range(4, 8))
            for d in range(1, remote_size):
                vec_copy(d).wait_recv()
            unpack_vectors(vecs, (gain_ref, bias_ref, *vec_outs, ids_ref))
            gather1.finish()
            unpack_first(units1, weight_ref, down_ref, up_ref)
            x_rows.end(x_ref, 0)
            gather2.second()
            for d in range(1, remote_size):
                vec_copy(d).wait_send()

        @pl.when(step == 1)
        def _():
            for i in range(items):
                dy_rows.begin(i)

        @pl.when(step == 3)
        def _():
            pl.loop(0, items)(dy_rows.mix)

        for n in range(2, items, 2):

            @pl.when(step == 4 * n)
            def _():
                x_rows.end(x_ref, n)

        for t, at in enumerate((4, 8, 12)):

            @pl.when(step == at)
            def _():
                gather2.from_z(t)

        for t, at in ((-1, 5), (0, 9), (1, 13), (2, 15)):

            @pl.when(step == at)
            def _():
                gather2.from_y(t)

        @pl.when(step == 4 * items - 1)
        def _():
            for i in range(0, items, 2):
                dy_rows.end(dy_out_ref, i)
            gather2.finish()
            x_rows.drain()
            dy_rows.drain()

    else:

        def table_copy(g):
            at = pl.ds(g * per_group, per_group)
            return pltpu.make_async_copy(table_ref.at[at], table.at[at], table_sem.at[g])

        @pl.when(step == 0)
        def _():
            for g in range(table.shape[0] // per_group):
                table_copy(g).start()

    @pl.when((group == 0) & (item % per_clip == 0))
    def _():
        clip = item // per_clip
        if remote_size:
            clip = clip + place.c * 2
        ids = ids_ref[...]
        row = lax.broadcasted_iota(jnp.int32, ids.shape, 0)
        mine = jnp.sum(jnp.where(row == clip, ids, 0.0), axis=0, keepdims=True)[:, 0:1]
        for ref, target in ((down_ref, down_own), (up_ref, up_own)):
            total = jnp.zeros(ref.shape[1:], F32)
            for a in range(ref.shape[0]):
                total = total + jnp.where(
                    mine == float(a), ref[a].astype(F32), 0.0
                )
            target[0] = total.astype(BF)

    @pl.when(group == 0)
    def _():
        number = lax.axis_index("win") * per_clip + item % per_clip
        early, low_h, low_w = row_masks(rows)
        label = (
            jnp.where(early, number // 4 % 2 * 4, 0)
            + jnp.where(low_h, number // 2 % 2 * 2, 0)
            + jnp.where(low_w, number % 2, 0)
        )
        lane = lane_ids((rows, 128))
        same = label == lane
        key_mask = jnp.where(same, 1.0, 0.0).astype(BF)
        query_mask[...] = jnp.where(same | (lane >= 8), 0.0, -FAR).astype(BF)
        normed, _ = norm_stats(x_ref[item if remote_size else 0].astype(F32))
        low = (normed * gain_ref[...]).astype(BF)
        reduced = dot(down_own[0], low, NT).astype(BF)
        reduced_ref[0] = reduced

        def columns(part):
            at = pl.ds(part * feats, feats)
            return (
                dot(low, weight_ref[:, at], NN)
                + bias_ref[:, at]
                + dot(reduced, up_own[0, :, at], TN)
            )

        query = (columns(0) * (scale * LOG2E)).astype(BF)
        queries[...] = query
        qkv_ref[0, :, :feats] = query
        key = columns(1).astype(BF)
        qkv_ref[0, :, feats : 2 * feats] = key
        for g in range(feats // 128):
            keys[:, 256 * g : 256 * g + 128] = key[:, 128 * g : 128 * g + 128]
            keys[:, 256 * g + 128 : 256 * g + 256] = key_mask
        value = columns(2).astype(BF)
        qkv_ref[0, :, 2 * feats :] = value
        values_t[...] = value.T

    if not remote_size:

        @pl.when(item == 0)
        def _():
            table_copy(group).wait()

    keys_now = keys[:, pl.ds(pl.multiple_of(group * 256, 256), 256)]
    query_now = queries[:, pl.ds(pl.multiple_of(group * 128, 128), 128)]
    head_of_lane = lane_ids(query_now.shape) // width

    def raw(h):
        own = jnp.where(head_of_lane == h, query_now, jnp.zeros_like(query_now))
        own = jnp.concatenate([own, query_mask[...]], axis=1)
        return dot(keys_now, own, NT) + table[group * per_group + h]

    def finish(h):
        score = scores[h % 2]
        largest = jnp.max(score, axis=0, keepdims=True)
        probs = jnp.exp2(score - largest)
        total = jnp.sum(probs, axis=0, keepdims=True)
        probs = (probs * (1.0 / total)).astype(BF)
        probs_ref[0, h] = probs
        at = pl.ds(pl.multiple_of((group * per_group + h) * width, width), width)
        out_t[at, :] = dot(values_t[at, :], probs, NN).astype(BF)

    scores[0] = raw(0)
    for h in range(per_group):
        if h + 1 < per_group:
            scores[(h + 1) % 2] = raw(h + 1)
        finish(h)

    @pl.when(group == groups - 1)
    def _():
        out_ref[0] = out_t[...].T


def dense_kernel(
    ids_ref,
    x_ref,
    attn_ref,
    gain_ref,
    proj_bias_ref,
    fc1_bias_ref,
    fc2_bias_ref,
    dy_ref,
    staged_ref,
    *refs,
    per_clip,
    chunk,
):
    tiles, refs = refs[:6], refs[6:]
    act_ref, dx1_ref, dattn_ref, grad_ref, *refs = refs
    proj_ref, fc1_ref, fc2_ref, proj_down, proj_up, fc1_down, fc1_up, fc2_down, fc2_up, *refs = refs
    pres, acts, dpres, sem = refs
    starting = pl.program_id(0) == 0
    count = x_ref.shape[1]
    feats = x_ref.shape[-1]
    hidden = fc1_ref.shape[-1]

    def moves(first=0, last=24):
        found = [(0, 64, proj_ref, 128 * n, n) for n in range(4)]
        found += [(64 + 64 * t, 64, fc1_ref, 512 * n + 128 * t, n) for n in range(4) for t in range(4)]
        found += [(320, 256, fc2_ref, 128 * n, n) for n in range(4)]
        return [
            pltpu.make_async_copy(
                staged_ref.at[n % 2, :, n // 2, pl.ds(start, size), :],
                target.at[:, :, pl.ds(lane, 128)],
                sem.at[at],
            )
            for at, (start, size, target, lane, n) in enumerate(found)
            if first <= at < last
        ]

    def arrive(first, last):
        @pl.when(starting)
        def _():
            for copy in moves(first, last):
                copy.wait()

    @pl.when(starting)
    def _():
        for copy in moves():
            copy.start()

    for n in range(8):
        short = slice(64 * n, 64 * n + 64)
        proj_down[:, short] = tiles[0][0, n, 0, :, 0:64]
        proj_up[:, short] = tiles[0][0, n, 0, :, 64:128]
        fc1_down[:, short] = tiles[1][0, n, 0, :, 0:64]
        fc2_up[:, short] = tiles[1][0, n, 0, :, 64:128]
        for half in range(2):
            long = slice(256 * n + 128 * half, 256 * n + 128 * half + 128)
            fc1_up[:, long] = tiles[2 + half][0, n, 0]
            fc2_down[:, long] = tiles[4 + half][0, n, 0]

    def join(parts):
        return jnp.concatenate(parts, axis=0) if per_clip > 1 else parts[0]

    dy = join([dy_ref[e] for e in range(per_clip)])
    attn = join([attn_ref[e] for e in range(per_clip)])
    reduced_proj = dot(proj_down[...], attn, NT).astype(BF)
    arrive(0, 4)
    proj_w = proj_ref[...].reshape(feats, feats)
    middle = (
        join([x_ref[e].astype(F32) for e in range(per_clip)])
        + dot(attn, proj_w, NN)
        + proj_bias_ref[...]
        + dot(reduced_proj, proj_up[...], TN)
    )
    normed, inverse = norm_stats(middle)
    low = (normed * gain_ref[...]).astype(BF)
    reduced_fc1 = dot(fc1_down[...], low, NT).astype(BF)
    grad_reduced_fc2 = dot(fc2_up[...], dy, NT).astype(BF)
    per_chunk = chunk // fc2_ref.shape[1]
    steps = hidden // chunk

    def pre_of(j):
        at = slice(j * chunk, (j + 1) * chunk)
        pres[j % 2] = (
            dot(low, fc1_ref[:, :, at].reshape(feats, chunk), NN)
            + fc1_bias_ref[:, at]
            + dot(reduced_fc1, fc1_up[:, at], TN)
        )

    arrive(4, 20)
    pre_of(0)
    arrive(20, 24)
    for j in range(steps):
        at = slice(j * chunk, (j + 1) * chunk)
        if j + 1 < steps:
            pre_of(j + 1)
        fc2_w = fc2_ref[j * per_chunk : (j + 1) * per_chunk].reshape(chunk, feats)
        dact = dot(dy, fc2_w, NT) + dot(grad_reduced_fc2, fc2_down[:, at], TN)
        pre = pres[j % 2]
        bell = jnp.exp2((pre * pre) * (-0.5 * LOG2E))
        t = 1.0 / (1.0 + jnp.abs(pre) * (0.3275911 * 0.7071067811865476))
        poly = (
            (((0.5 * 1.061405429) * t - 0.5 * 1.453152027) * t + 0.5 * 1.421413741) * t
            - 0.5 * 0.284496736
        ) * t + 0.5 * 0.254829592
        tail = poly * t * bell
        below = jnp.where(pre >= 0.0, 1.0 - tail, tail)
        acts[:, at] = (pre * below).astype(BF)
        dpres[:, at] = (dact * (below + pre * bell * 0.3989422804014327)).astype(BF)
    act = acts[...]
    dpre = dpres[...]
    fc1_up_at = 3 * feats
    fc2_down_at = fc1_up_at + hidden
    fc2_up_at = fc2_down_at + hidden
    fc2_w = fc2_ref[...].reshape(hidden, feats)
    grad_reduced_fc1 = dot(fc1_up[...], dpre, NT).astype(BF)
    dlow = dot(dpre, fc1_ref[...].reshape(feats, hidden), NT) + dot(grad_reduced_fc1, fc1_down[...], TN)
    dx1 = dy.astype(F32) + norm_back(dlow, gain_ref[...], normed, inverse)
    branch = dx1.astype(BF)
    reduced_fc2 = dot(fc2_down[...], act, NT).astype(BF)
    total = (
        middle + fc2_bias_ref[...] + dot(act, fc2_w, NN) + dot(reduced_fc2, fc2_up[...], TN)
    ).astype(BF)
    grad_reduced_proj = dot(proj_up[...], branch, NT).astype(BF)
    dattn = (
        dot(branch, proj_w, NT) + dot(grad_reduced_proj, proj_down[...], TN)
    ).astype(BF)
    for e in range(per_clip):
        rows = slice(e * count, (e + 1) * count)
        act_ref[e] = total[rows]
        dx1_ref[e] = dx1[rows]
        dattn_ref[e] = dattn[rows]
    grad_ref[0, :, :feats] = dot(grad_reduced_proj, attn, NN)
    grad_ref[0, :, feats : 2 * feats] = dot(reduced_proj, branch, NN)
    grad_ref[0, :, 2 * feats : fc1_up_at] = dot(grad_reduced_fc1, low, NN)
    grad_ref[0, :, fc1_up_at:fc2_down_at] = dot(reduced_fc1, dpre, NN)
    grad_ref[0, :, fc2_down_at:fc2_up_at] = dot(grad_reduced_fc2, act, NN)
    grad_ref[0, :, fc2_up_at:] = dot(reduced_fc2, dy, NN)


PIECES = (
    (0, 0, 64),
    (0, 512, 192),
    (1, 0, 64),
    (1, 512, 64),
    (1, 1024, 64),
    (1, 5632, 64),
    (1, 1536, 256),
    (1, 3584, 256),
)


def gradient_rows(sources, part, j, pieces):
    halves = []
    for n in range(2):
        cells = []
        for array, start, width in pieces:
            at = slice(start + j * width, start + (j + 1) * width)
            cells.append(sources[array][n, pl.ds(pl.multiple_of(part * 8, 8), 8), at])
        halves.append(jnp.concatenate(cells, axis=1))
    return jnp.concatenate(halves, axis=0)


def early_gradients(place, sources, own, other):
    for j in range(own.shape[0]):
        own[j, :, 256:] = gradient_rows(sources, place.k, j, PIECES[2:])
        other[j, :, 256:] = gradient_rows(sources, 1 - place.k, j, PIECES[2:]).astype(BF)


def share_gradients(place, sources, ids_ref, refs, send, between):
    own, other, from_core, half, from_x, shares, from_clips, adapters, from_win, out = refs
    c, w, x, k = place.c, place.w, place.x, place.k
    clip_size = own.shape[0]
    for j in range(clip_size):
        other[j, :, 0:256] = gradient_rows(sources, 1 - k, j, PIECES[:2]).astype(BF)
    core_copy = send.copy(other, from_core, place.sibling)
    between[0]()
    for j in range(clip_size):
        own[j, :, 0:256] = gradient_rows(sources, k, j, PIECES[:2])
    core_copy.wait_recv()
    own[...] += from_core[...].astype(F32)
    half[...] = own[:, :, pl.ds(pl.multiple_of((1 - x) * 512, 512), 512)].astype(BF)
    x_copy = send.copy(half, from_x, place.across)
    between[1]()
    x_copy.wait_recv()
    shares[...] = (
        own[:, :, pl.ds(pl.multiple_of(x * 512, 512), 512)] + from_x[...].astype(F32)
    ).astype(BF)
    from_clips[c] = shares[c]
    clip_copies = []
    for d in range(1, clip_size):
        to = (c + d) % clip_size
        clip_copies.append(send.copy(shares.at[to], from_clips.at[c], (to, w)))
    for copy in clip_copies:
        copy.wait_recv()
    for a in range(8):
        total = None
        for n in range(2 * clip_size):
            value = from_clips[n // 2].astype(F32)[8 * (n % 2) : 8 * (n % 2) + 8]
            value = jnp.where(ids_ref[n : n + 1, :] == float(a), value, 0.0)
            total = value if total is None else total + value
        adapters[a // 2, 8 * (a % 2) : 8 * (a % 2) + 8, :] = total
    from_win[w] = adapters[w]
    win_copies = []
    for d in range(1, 4):
        to = (w + d) % 4
        win_copies.append(send.copy(adapters.at[to], from_win.at[w], (c, to)))
    between[2]()
    for copy in win_copies:
        copy.wait_recv()
    for x2 in range(2):
        for k2 in range(2):
            for a in range(2):
                out[a, 8 * k2 : 8 * k2 + 8, 512 * x2 : 512 * x2 + 512] = from_win[
                    2 * x2 + k2, 8 * a : 8 * a + 8, :
                ]
    for copy in [core_copy, x_copy, *clip_copies, *win_copies]:
        copy.wait_send()


def attend_back_kernel(
    x_ref,
    gain_ref,
    weight_ref,
    down_ref,
    up_ref,
    probs_ref,
    attn_ref,
    qkv_ref,
    reduced_ref,
    dattn_ref,
    dx1_ref,
    *refs,
    scale,
    per_group,
    width,
    per_clip,
    remote_size,
):
    if remote_size:
        act_ref, grad_dense_ref, ids_ref, act_out_ref, dx_out_ref, sums_ref, *refs = refs
    else:
        dx_ref, grad_ref, *refs = refs
    values, keys_t, inner, dqkv, dquery_t, *refs = refs
    group = pl.program_id(1)
    groups = pl.num_programs(1)
    item = pl.program_id(0)
    step = item * groups + group
    if remote_size:
        items = act_ref.shape[0]
        place = Place(remote_size)
        act_rows = Rows(place, act_ref, *refs[:5])
        dx_own = refs[5]
        dx_rows = Rows(place, *refs[5:11])
        grad_ref = refs[11]
        share_refs, sems = refs[12:21], refs[21:]

        @pl.when(step == 0)
        def _():
            enter(
                [(place.c, (place.w + d) % 4) for d in range(1, 4)]
                + [((place.c + d) % remote_size, place.w) for d in range(1, remote_size)]
            )
            for i in range(items):
                act_rows.begin(i)

        for i in range(items):

            @pl.when(step == i + 1)
            def _():
                act_rows.mix(i)

            if i < items - 1:

                @pl.when(step == (i + 1) * 4 + 1)
                def _():
                    dx_rows.mix(i)

        @pl.when(step == 6)
        def _():
            early_gradients(place, (None, grad_dense_ref), share_refs[0], share_refs[1])

        @pl.when(step == 4 * items - 3)
        def _():
            for i in range(0, items, 2):
                act_rows.end(act_out_ref, i)
            act_rows.drain()

    feats = x_ref.shape[-1]
    rows = x_ref.shape[1]

    @pl.when(group == 0)
    def _():
        keys_t[...] = qkv_ref[0, :, feats : 2 * feats].T
        lane = lane_ids((rows, 128))
        ones = jnp.where(lane % width < 2, 1.0, 0.0).astype(BF)
        source = lax.broadcasted_iota(jnp.int32, (128, 128), 0)
        target = lane_ids((128, 128))
        pick = jnp.where(
            (source // width == target // width) & (target % width < 2), 1.0, 0.0
        ).astype(BF)
        pick = jnp.concatenate([pick, pick], axis=0)
        for g in range(feats // 128):
            at = slice(128 * g, 128 * g + 128)
            values[:, 256 * g : 256 * g + 128] = qkv_ref[0, :, 2 * feats + 128 * g : 2 * feats + 128 * g + 128]
            values[:, 256 * g + 128 : 256 * g + 256] = ones
            product = dattn_ref[0, :, at].astype(F32) * attn_ref[0, :, at].astype(F32)
            high = product.astype(BF)
            rest = (product - high.astype(F32)).astype(BF)
            sums = dot(jnp.concatenate([high, rest], axis=1), pick, NN)
            coarse = sums.astype(BF)
            fine = (sums - coarse.astype(F32)).astype(BF)
            inner[:, at] = -jnp.where(lane % width == 0, coarse, fine)

    blocks = pl.ds(pl.multiple_of(group * 128, 128), 128)
    values_now = values[:, pl.ds(pl.multiple_of(group * 256, 256), 256)]
    dattn_now = dattn_ref[0, :, blocks]
    inner_now = inner[:, blocks]
    query_now = qkv_ref[0, :, blocks]
    head_of_lane = lane_ids((rows, 128)) // width
    zero = jnp.zeros((rows, 128), BF)
    dvalue = None
    dkey = None
    for h in range(per_group):
        mine = head_of_lane == h
        dattn_own = jnp.where(mine, dattn_now, zero)
        query_own = jnp.where(mine, query_now, zero)
        right = jnp.concatenate([dattn_own, jnp.where(mine, inner_now, zero)], axis=1)
        probs = probs_ref[0, h]
        dscore = probs * dot(values_now, right, NT).astype(BF)
        partial = dot(probs, dattn_own, NN)
        dvalue = partial if dvalue is None else dvalue + partial
        partial = dot(dscore, query_own, NN)
        dkey = partial if dkey is None else dkey + partial
        at = pl.ds(pl.multiple_of((group * per_group + h) * width, width), width)
        dquery_t[at, :] = (dot(keys_t[at, :], dscore, NN) * scale).astype(BF)
    dqkv[:, pl.ds(pl.multiple_of(2 * feats + group * 128, 128), 128)] = dvalue.astype(BF)
    dqkv[:, pl.ds(pl.multiple_of(feats + group * 128, 128), 128)] = (dkey * LN2).astype(BF)

    @pl.when(group == groups - 1)
    def _():
        first = pl.program_id(0) % per_clip == 0
        dqkv[:, :feats] = dquery_t[...].T
        dall = dqkv[...]
        normed, inverse = norm_stats(x_ref[0].astype(F32))
        low = (normed * gain_ref[...]).astype(BF)
        grad_reduced = dot(up_ref[0], dall, NT).astype(BF)
        slot = item // per_clip if remote_size else 0
        add_rows(grad_ref, slot, slice(feats, 4 * feats), dot(reduced_ref[0], dall, NN), first)
        add_rows(grad_ref, slot, slice(0, feats), dot(grad_reduced, low, NN), first)
        dlow = (dot(dall, weight_ref[...], NT) + dot(grad_reduced, down_ref[0], TN)).astype(BF)
        dx = (dx1_ref[0] + norm_back(dlow.astype(F32), gain_ref[...], normed, inverse)).astype(BF)
        if not remote_size:
            dx_ref[0] = dx
            return
        dx_own[item] = dx
        for i in range(items):

            @pl.when(item == i)
            def _():
                dx_rows.begin(i)

    if remote_size:

        @pl.when(step == 4 * items - 1)
        def _():
            share_gradients(
                place,
                (grad_ref, grad_dense_ref),
                ids_ref,
                (*share_refs, sums_ref),
                Sender(*sems),
                (
                    lambda: None,
                    lambda: dx_rows.mix(items - 1),
                    lambda: [dx_rows.end(dx_out_ref, i) for i in range(0, items, 2)],
                ),
            )
            dx_rows.drain()


def whole(shape):
    return pl.BlockSpec(shape, lambda *at: (0,) * len(shape), pipeline_mode=pl.Buffered(1))


def compute(first, dy, adapter_ids, vectors, later, per_clip, remote_size):
    if remote_size:
        heads = first[1].shape[0]
        x_shape, rank = dy.shape, 16
    else:
        x, qkv_w, qkv_down, qkv_up, table = first
        heads, rank = table.shape[0], qkv_down.shape[1]
    items, rows, feats = dy.shape
    width = feats // heads
    per_group = 128 // width
    groups = heads // per_group
    scale = width**-0.5
    hidden = 4 * feats
    clips = items // per_clip

    def item(shape):
        return pl.BlockSpec((1, *shape), lambda i, *rest: (i,) + (0,) * len(shape))

    item_ids = adapter_ids
    any_space = pl.BlockSpec(memory_space=pl.ANY)

    def of_clip(shape):
        return pl.BlockSpec((1, *shape), lambda i, *rest: (i // per_clip, 0, 0))

    sems = pltpu.SemaphoreType.DMA
    if remote_size:
        shape = jax.ShapeDtypeStruct
        adapters = 8
        padded = 56 * heads
        ids = adapter_ids[None]
        args = (*first, ids, *[v.reshape(1, -1) for v in vectors], dy, *later)
        arg_specs = [whole(a.shape) for a in args]
        sent_out = [
            shape(dy.shape, BF),
            shape((2, remote_size, 2, 768, 128), BF),
            shape(dy.shape, BF),
            shape((feats, 3 * feats), BF),
            *[shape((1, n), F32) for n in (feats, feats, feats, hidden, feats)],
            shape((2 * remote_size, 512), F32),
        ]
        sent_specs = [whole(a.shape) for a in sent_out]
        sent_specs[1] = any_space
        row_scratch = [
            pltpu.VMEM(dy.shape, BF),
            pltpu.VMEM(dy.shape, BF),
            pltpu.VMEM((items, TOP, feats), BF),
            sems((2 * items,)),
            sems((2 * items,)),
        ]
        sent_scratch = [
            pltpu.VMEM((1, 3 * feats), F32),
            pltpu.VMEM((adapters, rank, feats), BF),
            pltpu.VMEM((adapters, rank, 3 * feats), BF),
            pltpu.VMEM((64, 512), BF),
            pltpu.VMEM((8, 128), F32),
            pltpu.VMEM((768, 128), BF),
            pltpu.VMEM((2, remote_size, 2, 64, 512), BF),
            pltpu.VMEM((remote_size, 8, 128), F32),
            pltpu.VMEM((15 * heads, 176), BF),
            pltpu.VMEM((15, padded, 128), F32),
            pltpu.VMEM((padded, 15 * 128), BF),
            pltpu.VMEM((8 * 128, rows), BF),
            *row_scratch,
            *row_scratch,
            *[sems((Gather.COPIES,)) for _ in range(4)],
            sems((remote_size,)),
            sems((remote_size,)),
            sems,
        ]
    else:
        gain1, qkv_bias, proj_bias, gain2, fc1_bias, fc2_bias = vectors
        clip_ids = jnp.broadcast_to(adapter_ids.astype(F32)[:, None], (clips, 128))
        args = (x, gain1, qkv_w, qkv_bias, clip_ids, qkv_down, qkv_up, table)
        arg_specs = [item((rows, feats)), *[whole(a.shape) for a in args[1:7]], any_space]
        sent_out, sent_specs, sent_scratch = [], [], []

    probs, attn, qkv, reduced, down_own, up_own, *arrived = pl.pallas_call(
        functools.partial(
            attend_kernel,
            scale=scale,
            per_group=per_group,
            width=width,
            per_clip=per_clip,
            remote_size=remote_size,
        ),
        grid=(items, groups),
        in_specs=arg_specs,
        out_specs=[
            pl.BlockSpec((1, per_group, rows, rows), lambda i, g: (i, g, 0, 0)),
            item((rows, feats)),
            item((rows, 3 * feats)),
            item((rank, rows)),
            of_clip((rank, feats)),
            of_clip((rank, 3 * feats)),
            *sent_specs,
        ],
        scratch_shapes=[
            pltpu.VMEM((rows, 2 * feats), BF),
            pltpu.VMEM((rows, feats), BF),
            pltpu.VMEM((feats, rows), BF),
            pltpu.VMEM((feats, rows), BF),
            pltpu.VMEM((2, rows, rows), F32),
            pltpu.VMEM((heads, rows, rows), F32),
            sems((groups,)),
            pltpu.VMEM((rows, 128), BF),
            *sent_scratch,
        ],
        out_shape=[
            jax.ShapeDtypeStruct((items, heads, rows, rows), BF),
            jax.ShapeDtypeStruct((items, rows, feats), BF),
            jax.ShapeDtypeStruct((items, rows, 3 * feats), BF),
            jax.ShapeDtypeStruct((items, rank, rows), BF),
            jax.ShapeDtypeStruct((clips, rank, feats), BF),
            jax.ShapeDtypeStruct((clips, rank, 3 * feats), BF),
            *sent_out,
        ],
        compiler_params=pltpu.CompilerParams(
            vmem_limit_bytes=VMEM_LIMIT,
            dimension_semantics=("arbitrary", "arbitrary"),
            **({"collective_id": 2, "has_side_effects": True} if remote_size else {}),
        ),
        cost_estimate=pl.CostEstimate(flops=4 * 10**10, bytes_accessed=10**7, transcendentals=0),
        name="attend",
    )(*args)
    if remote_size:
        dy, staged, x, qkv_w, gain1, proj_bias, gain2, fc1_bias, fc2_bias, all_ids = arrived
    else:
        (staged,) = later

    span = 4 * feats + 2 * hidden
    def tile(n):
        def index(c, ids):
            return ids[c] // 2 % 2, 0, ids[c] // 4, 36 + 2 * n + ids[c] % 2, 0

        return pl.BlockSpec((1, 8, 1, rank, 128), index)

    def clip(array_shape):
        return pl.BlockSpec((per_clip, *array_shape[1:]), lambda c, ids: (c, 0, 0))

    chunk = 512
    act, dx1, dattn, grad_dense = pl.pallas_call(
        functools.partial(dense_kernel, per_clip=per_clip, chunk=chunk),
        grid_spec=pltpu.PrefetchScalarGridSpec(
            num_scalar_prefetch=1,
            grid=(clips,),
            in_specs=[
                clip(x.shape),
                clip(x.shape),
                whole(gain2.shape),
                whole(proj_bias.shape),
                whole(fc1_bias.shape),
                whole(fc2_bias.shape),
                clip(x.shape),
                any_space,
                *[tile(n) for n in range(6)],
            ],
            out_specs=[
                clip(x.shape),
                clip(x.shape),
                clip(x.shape),
                pl.BlockSpec((1, rank, span), lambda c, ids: (c, 0, 0)),
            ],
            scratch_shapes=[
                pltpu.VMEM((8, feats // 8, feats), BF),
                pltpu.VMEM((8, feats // 8, hidden), BF),
                pltpu.VMEM((8, hidden // 8, feats), BF),
                *[pltpu.VMEM((rank, n), BF) for n in (feats, feats, feats, hidden, hidden, feats)],
                pltpu.VMEM((2, per_clip * rows, chunk), F32),
                pltpu.VMEM((per_clip * rows, hidden), BF),
                pltpu.VMEM((per_clip * rows, hidden), BF),
                pltpu.SemaphoreType.DMA((24,)),
            ],
        ),
        out_shape=[
            jax.ShapeDtypeStruct((items, rows, feats), BF),
            jax.ShapeDtypeStruct((items, rows, feats), F32),
            jax.ShapeDtypeStruct((items, rows, feats), BF),
            jax.ShapeDtypeStruct((clips, rank, span), F32),
        ],
        compiler_params=pltpu.CompilerParams(
            vmem_limit_bytes=VMEM_LIMIT, dimension_semantics=("arbitrary",)
        ),
        cost_estimate=pl.CostEstimate(flops=5 * 10**10, bytes_accessed=10**7, transcendentals=0),
        name="dense",
    )(
        item_ids, x, attn, gain2, proj_bias, fc1_bias, fc2_bias, dy, staged, *([staged] * 6)
    )

    if remote_size:
        assert (clips, per_clip) == (2, 2)
        count = remote_size
        back_in = (act, grad_dense, all_ids)
        back_out = [whole(x.shape), whole(x.shape), whole((2, rank, 1024))]
        back_shape = [
            jax.ShapeDtypeStruct(x.shape, BF),
            jax.ShapeDtypeStruct(x.shape, BF),
            jax.ShapeDtypeStruct((2, rank, 1024), F32),
        ]
        back_scratch = [
            *row_scratch,
            pltpu.VMEM(x.shape, BF),
            *row_scratch,
            pltpu.VMEM((clips, rank, 4 * feats), F32),
            pltpu.VMEM((count, 16, 1024), F32),
            pltpu.VMEM((count, 16, 1024), BF),
            pltpu.VMEM((count, 16, 1024), BF),
            pltpu.VMEM((count, 16, 512), BF),
            pltpu.VMEM((count, 16, 512), BF),
            pltpu.VMEM((count, 16, 512), BF),
            pltpu.VMEM((count, 16, 512), BF),
            pltpu.VMEM((4, 16, 512), F32),
            pltpu.VMEM((4, 16, 512), F32),
            sems((16,)),
            sems((16,)),
        ]
    else:
        back_in, back_scratch = (), []
        back_out = [
            item((rows, feats)),
            pl.BlockSpec((1, rank, 4 * feats), lambda i, g: (i // per_clip, 0, 0)),
        ]
        back_shape = [
            jax.ShapeDtypeStruct((items, rows, feats), BF),
            jax.ShapeDtypeStruct((clips, rank, 4 * feats), F32),
        ]
    results = pl.pallas_call(
        functools.partial(
            attend_back_kernel,
            scale=scale,
            per_group=per_group,
            width=width,
            per_clip=per_clip,
            remote_size=remote_size,
        ),
        grid=(items, groups),
        in_specs=[
            item((rows, feats)),
            whole(gain1.shape),
            whole(qkv_w.shape),
            of_clip((rank, feats)),
            of_clip((rank, 3 * feats)),
            pl.BlockSpec((1, per_group, rows, rows), lambda i, g: (i, g, 0, 0)),
            item((rows, feats)),
            item((rows, 3 * feats)),
            item((rank, rows)),
            item((rows, feats)),
            item((rows, feats)),
            *[whole(a.shape) for a in back_in],
        ],
        out_specs=back_out,
        scratch_shapes=[
            pltpu.VMEM((rows, 2 * feats), BF),
            pltpu.VMEM((feats, rows), BF),
            pltpu.VMEM((rows, feats), BF),
            pltpu.VMEM((rows, 3 * feats), BF),
            pltpu.VMEM((feats, rows), BF),
            *back_scratch,
        ],
        out_shape=back_shape,
        compiler_params=pltpu.CompilerParams(
            vmem_limit_bytes=VMEM_LIMIT, dimension_semantics=("arbitrary", "arbitrary"),
            **({"collective_id": 1, "has_side_effects": True} if remote_size else {}),
        ),
        cost_estimate=pl.CostEstimate(flops=5 * 10**10, bytes_accessed=10**7, transcendentals=0),
        name="attend_back",
    )(x, gain1, qkv_w, down_own, up_own, probs, attn, qkv, reduced, dattn, dx1, *back_in)
    if remote_size:
        return results
    return (act, *results, grad_dense)


def exchange(x, win_size):
    local = x.shape[1]
    bits = local.bit_length() - 1
    at = jnp.arange(TOK)
    taken = (at // 49 < 4, at // 7 % 7 < 3, at % 7 < 3)
    for bit, rows in zip((2, 1, 0), taken):
        if bit < bits:
            split = x.reshape(x.shape[0], local >> (bit + 1), 2, 1 << bit, TOK, -1)
            other = jnp.flip(split, axis=2).reshape(x.shape)
        else:
            other = lax.ppermute(x, "win", [(i, i ^ 1 << bit - bits) for i in range(win_size)])
        x = jnp.where(rows[None, None, :, None], other, x)
    return x


def bias_by_pair(table):
    heads = table.shape[0]
    side = jnp.arange(49)
    high, wide = (side // 7 + 4) % 7, (side % 7 + 4) % 7
    offset = (high[None, :] - high[:, None] + 6) * 13 + wide[None, :] - wide[:, None] + 6
    pick = (jnp.arange(169)[:, None, None] == offset[None]).astype(BF)
    found = jnp.einsum(
        "mad,dkq->mkaq", table.reshape(heads, 15, 169), pick, preferred_element_type=F32
    )
    found = (found * LOG2E).reshape(heads, 49, 15 * 49)
    blocks = []
    for key_block in range(8):
        t = (key_block + 4) % 8
        blocks.append(
            jnp.concatenate(
                (found[..., (11 - t) * 49 : (15 - t) * 49], found[..., (7 - t) * 49 : (11 - t) * 49]),
                axis=-1,
            )
        )
    return jnp.stack(blocks, axis=1).reshape(heads, TOK, TOK)


def gather(array, spec):
    for axis, name in enumerate(spec):
        if name is not None:
            array = lax.all_gather(array, name, axis=axis, tiled=True)
    return array


def stage_whole(proj_w, fc1_w, fc2_w, maps):
    proj_down, proj_up, fc1_down, fc1_up, fc2_down, fc2_up = maps
    count = proj_down.shape[0]

    def short(a):
        return a.reshape(4, count // 4 * 16, 8, 64).transpose(2, 0, 1, 3)

    def long(a):
        return a.reshape(4, count // 4 * 16, 8, 2, 128).transpose(2, 0, 3, 1, 4).reshape(8, 4, -1, 128)

    return jnp.concatenate(
        (
            proj_w.reshape(8, 64, 4, 128).transpose(0, 2, 1, 3),
            fc1_w.reshape(8, 64, 4, 4, 128).transpose(0, 2, 3, 1, 4).reshape(8, 4, 256, 128),
            fc2_w.reshape(8, 256, 4, 128).transpose(0, 2, 1, 3),
            jnp.concatenate((short(proj_down), short(proj_up)), axis=-1),
            jnp.concatenate((short(fc1_down), short(fc2_up)), axis=-1),
            long(fc1_up),
            long(fc2_down),
        ),
        axis=2,
    )


def by_core(staged):
    return staged.reshape(8, 2, 2, *staged.shape[2:]).transpose(2, 0, 1, 3, 4)


def per_device(
    tokens, cotangent, adapter_ids, ln1_gain, qkv_weight, qkv_bias, proj_weight, proj_bias, ln2_gain,
    fc1_weight, fc1_bias, fc2_weight, fc2_bias, bias_table, qkv_down, qkv_up, proj_down, proj_up,
    fc1_down, fc1_up, fc2_down, fc2_up, *, clip_size, win_size,
):
    clips, local, rows, feats = tokens.shape
    items = clips * local
    heads = bias_table.shape[0]
    vecs = (ln1_gain, qkv_bias, proj_bias, ln2_gain, fc1_bias, fc2_bias)
    flat = (items, rows, feats)
    downs = [a.transpose(0, 2, 1) for a in (qkv_down, proj_down, fc1_down, fc2_down)]
    own_kernels = (clip_size, win_size, clips, local) == (8, 4, 2, 2)
    if own_kernels:
        first = (tokens.reshape(flat), bias_table, qkv_weight, downs[0], qkv_up)
        dy = cotangent.reshape(flat)
        vectors = vecs
        later = (proj_weight, fc1_weight, fc2_weight, downs[1], proj_up, downs[2], fc1_up, downs[3], fc2_up)
    else:
        grid2, by_down, by_up = ("clip", "win"), ("win", None, "clip"), ("win", None, "clip")
        maps = (downs[1], proj_up, downs[2], fc1_up, downs[3], fc2_up)
        staged = stage_whole(
            *[gather(a, grid2) for a in (proj_weight, fc1_weight, fc2_weight)],
            [gather(a, by_up) for a in maps],
        )
        later = (by_core(staged),)
        vectors = [gather(v, ("clip",)).reshape(1, -1).astype(F32) for v in vecs]
        first = (
            exchange(tokens, win_size).reshape(flat),
            gather(qkv_weight, grid2),
            gather(downs[0], by_down),
            gather(qkv_up, by_up),
            bias_by_pair(bias_table),
        )
        dy = exchange(cotangent, win_size).reshape(flat)
    results = compute(
        first, dy, adapter_ids, vectors, later, local, clip_size if own_kernels else 0
    )
    if own_kernels:
        act_out, dx_out, sums = results
        qd, qu, pd, pu, f1d, f2u, f1u, f2d = [
            sums[..., first:last]
            for first, last in zip(
                (0, 64, 256, 320, 384, 448, 512, 768), (64, 256, 320, 384, 448, 512, 768, 1024)
            )
        ]
        turned = [a.transpose(0, 2, 1) for a in (qd, pd, f1d, f2d)]
        return (
            act_out.reshape(tokens.shape), dx_out.reshape(tokens.shape),
            turned[0], qu, turned[1], pu, turned[2], f1u, turned[3], f2u,
        )
    act, dx, grad_qkv, grad_dense = results
    activations = exchange(act.reshape(tokens.shape), win_size)
    input_grad = exchange(dx.reshape(tokens.shape), win_size)
    adapter_count = win_size * qkv_down.shape[0]
    hot = (adapter_ids[:, None] == jnp.arange(adapter_count)[None]).astype(F32)
    hidden = fc1_weight.shape[1] * win_size
    spans = (feats, 3 * feats, feats, feats, feats, hidden, hidden, feats)
    grads = jnp.concatenate((grad_qkv, grad_dense), axis=-1)
    rank = grads.shape[1]
    parts, at = [], 0
    for span in spans:
        parts.append(
            grads[..., at : at + span].reshape(clips, rank, clip_size, span // clip_size)
        )
        at += span
    mine = jnp.concatenate(parts, axis=-1)
    grown = jnp.sum(hot[:, :, None, None, None] * mine[:, None], axis=0)
    grown = grown.transpose(2, 0, 1, 3).astype(BF)
    total = lax.psum_scatter(grown, "clip", scatter_dimension=0, tiled=True)[0]
    total = lax.psum_scatter(total, "win", scatter_dimension=0, tiled=True).astype(F32)
    outs, at = [], 0
    for n, span in enumerate(spans):
        width = span // clip_size
        part = total[..., at : at + width]
        at += width
        outs.append(part.transpose(0, 2, 1) if n % 2 == 0 else part)
    return (activations, input_grad, *outs)


def solution(mesh):
    split = P("clip", "win", None, None)
    grid2 = P("clip", "win")
    down = P("win", "clip", None)
    up = P("win", None, "clip")
    one = P("clip")
    return jax.shard_map(
        functools.partial(
            per_device, clip_size=mesh.shape["clip"], win_size=mesh.shape["win"]
        ),
        mesh=mesh,
        in_specs=(
            split, split, one, one, grid2, one, grid2, one, one, grid2, one, grid2, one, P(),
            down, up, down, up, down, up, down, up,
        ),
        out_specs=(split, split, down, up, down, up, down, up, down, up),
        check_vma=False,
    )
```

```python
import functools
import jax
import jax.numpy as jnp
from jax import lax
from jax.experimental import pallas as pl
from jax.experimental.pallas import tpu as pltpu
from jax.sharding import PartitionSpec as P

BF = jnp.bfloat16
F32 = jnp.float32
NN = (((1,), (0,)), ((), ()))
NT = (((1,), (1,)), ((), ()))
TN = (((0,), (0,)), ((), ()))
LOG2E = 1.4426950408889634
LN2 = 0.6931471805599453
FAR = 1e9
VMEM_LIMIT = 60 * 2**20
TOK = 392
TOP = 208


def dot(left, right, dims):
    return lax.dot_general(left, right, dims, preferred_element_type=F32)


def lane_ids(shape):
    return lax.broadcasted_iota(jnp.int32, shape, len(shape) - 1)


def norm_stats(values):
    average = jnp.mean(values, axis=-1, keepdims=True)
    centred = values - average
    variance = jnp.mean(centred * centred, axis=-1, keepdims=True)
    inverse = lax.rsqrt(variance + 1e-05)
    return centred * inverse, inverse


def norm_back(gradient, gain, normed, inverse):
    scaled = gradient * gain
    centre = jnp.mean(scaled, axis=-1, keepdims=True)
    slope = jnp.mean(scaled * normed, axis=-1, keepdims=True)
    return inverse * (scaled - centre - normed * slope)


def add_rows(ref, n, at, value, first):
    @pl.when(first)
    def _():
        ref[n, :, at] = value

    @pl.when(jnp.logical_not(first))
    def _():
        ref[n, :, at] += value


MESH = pl.DeviceIdType.MESH


def enter(peers):
    barrier = pltpu.get_barrier_semaphore()
    for peer in peers:
        pl.semaphore_signal(barrier, inc=1, device_id=peer, device_id_type=MESH)
    pl.semaphore_wait(barrier, len(peers))


def remote(src, dst, send_sem, recv_sem, peer):
    return pltpu.make_async_remote_copy(
        src_ref=src,
        dst_ref=dst,
        send_sem=send_sem,
        recv_sem=recv_sem,
        device_id=peer,
        device_id_type=MESH,
    )


class Sender:
    def __init__(self, send_sem, recv_sem):
        self.send_sem, self.recv_sem, self.count = send_sem, recv_sem, 0

    def copy(self, src, dst, peer):
        n = self.count
        self.count += 1
        made = remote(src, dst, self.send_sem.at[n], self.recv_sem.at[n], peer)
        made.start()
        return made


def row_masks(rows):
    row = lax.broadcasted_iota(jnp.int32, (rows, 128), 0)
    return row < TOK // 2, row % 49 < 21, row % 7 < 3


def choose(mask, first, second):
    return jnp.concatenate(
        [
            jnp.where(mask, first[:, at : at + 128], second[:, at : at + 128])
            for at in range(0, first.shape[1], 128)
        ],
        axis=1,
    )


class Rows:
    def __init__(self, place, own, beside, mixed, tops, send_sem, recv_sem):
        self.place, self.own, self.beside, self.mixed, self.tops = place, own, beside, mixed, tops
        self.send_sem, self.recv_sem = send_sem, recv_sem
        self.items, self.rows, self.feats = own.shape

    def copy(self, kind, i):
        n = kind * self.items + i
        sems = self.send_sem.at[n], self.recv_sem.at[n]
        if kind == 0:
            return remote(self.own.at[i], self.beside.at[i], *sems, self.place.sibling)
        top = self.mixed.at[i, pl.ds(0, TOP)]
        return remote(top, self.tops.at[i], *sems, self.place.across)

    def begin(self, i):
        self.copy(0, i).start()

    def mix(self, i):
        self.copy(0, i).wait_recv()
        self.mixed[i] = choose(row_masks(self.rows)[1], self.beside[i], self.own[i])
        self.copy(1, i).start()

    def end(self, out, i):
        early, _, low_w = row_masks(self.rows)
        both = []
        for e in range(2):
            self.copy(1, i + e).wait_recv()
            top = choose(early[:TOP], self.tops[i + e], self.mixed[i + e, :TOP])
            both.append(jnp.concatenate([top, self.mixed[i + e, TOP:]], axis=0))
        for e in range(2):
            out[i + e] = choose(low_w, both[1 - e], both[e])

    def drain(self):
        for i in range(self.items):
            self.copy(0, i).wait_send()
            self.copy(1, i).wait_send()


class Place:
    def __init__(self, clip_size):
        self.c, self.w = lax.axis_index("clip"), lax.axis_index("win")
        self.z, self.y = self.c // 2, self.c % 2
        self.x, self.k = self.w // 2, self.w % 2
        self.zs = clip_size // 2
        self.sibling = (self.c, self.x * 2 + 1 - self.k)
        self.across = (self.c, (1 - self.x) * 2 + self.k)

    def clip_at(self, z_step, other_y):
        return (self.z + z_step + self.zs) % self.zs * 2 + (1 - self.y if other_y else self.y)

    def along_z(self, step):
        return (self.clip_at(step, False), self.w)

    def along_y(self):
        return (self.clip_at(0, True), self.w)


class Gather:
    COPIES = 29

    def __init__(self, place, unit, units, send_sem, recv_sem):
        self.place, self.unit, self.units = place, unit, units
        self.send_sem, self.recv_sem = send_sem, recv_sem
        self.hops = range(place.zs - 1)

    def make(self, kind, t=0):
        p, units = self.place, self.units
        kinds = ("up", "down", "y_up", "y_down", "s_up", "s_down", "sy_up", "sy_down")
        single = ("across", "own", "theirs", "y", "s_y")
        n = single.index(kind) if kind in single else 5 + 8 * t + kinds.index(kind)
        sems = self.send_sem.at[n], self.recv_sem.at[n]
        mine = units.at[p.k, p.c, p.x]
        if kind == "across":
            return remote(self.unit, mine, *sems, p.across)
        if kind == "own":
            return remote(self.unit, mine, *sems, p.sibling)
        if kind == "theirs":
            part = units.at[p.k, p.c, 1 - p.x]
        elif kind == "y":
            part = units.at[p.k, p.c]
        elif kind == "s_y":
            part = units.at[p.k, p.z * 2 + 1 - p.y]
        else:
            sign = -1 if kind.endswith("up") else 1
            far = p.z + sign * (t if kind in ("up", "down") else t + 1)
            part = units.at[p.k, far * 2 + (1 - p.y if kind.startswith("sy") else p.y)]
        if kind in ("up", "down"):
            peer = (p.c - 2 * sign, p.w)
        else:
            peer = p.along_y() if kind.startswith("y") else p.sibling
        return remote(part, part, *sems, peer)

    def when(self, kind, t, sending, act):
        p, last = self.place, self.place.zs - 1
        if kind.endswith("up"):
            holds = (p.z >= t) & (p.z < last) if sending and kind == "up" else p.z >= t + 1
        elif kind.endswith("down"):
            holds = (p.z <= last - t) & (p.z > 0) if sending and kind == "down" else p.z <= last - 1 - t
        else:
            act()
            return
        pl.when(holds)(act)

    def start(self, kind, t=0):
        self.when(kind, t, True, lambda: self.make(kind, t).start())

    def wait_recv(self, kind, t=0):
        self.when(kind, t, False, lambda: self.make(kind, t).wait_recv())

    def wait_send(self, kind, t=0):
        self.when(kind, t, True, lambda: self.make(kind, t).wait_send())

    def begin(self):
        self.start("across")
        self.start("own")

    def second(self):
        self.wait_recv("across")
        for kind in ("up", "down", "y", "theirs"):
            self.start(kind)

    def from_z(self, t):
        for way in ("up", "down"):
            self.wait_recv(way, t)
            if t + 1 in self.hops:
                self.start(way, t + 1)
            self.start("y_" + way, t)
            self.start("s_" + way, t)

    def from_y(self, t):
        if t < 0:
            self.wait_recv("y")
            self.start("s_y")
        else:
            for way in ("up", "down"):
                self.wait_recv("y_" + way, t)
                self.start("sy_" + way, t)

    def finish(self):
        for kind in ("own", "theirs", "s_y"):
            self.wait_recv(kind)
        for t in self.hops:
            for kind in ("s_up", "s_down", "sy_up", "sy_down"):
                self.wait_recv(kind, t)
        for kind in ("across", "own", "theirs", "y", "s_y"):
            self.wait_send(kind)
        for t in self.hops:
            for kind in ("up", "down", "y_up", "y_down", "s_up", "s_down", "sy_up", "sy_down"):
                self.wait_send(kind, t)


def pack_first(unit, vec, qkv_ref, qd_ref, qu_ref, ids_ref, vec_refs):
    unit[:, 0:384] = qkv_ref[...]
    for a in range(2):
        unit[16 * a : 16 * a + 16, 384:448] = qd_ref[a]
        unit[16 * a : 16 * a + 16, 448:512] = qu_ref[a, :, 0:64]
        unit[32 + 16 * a : 48 + 16 * a, 384:512] = qu_ref[a, :, 64:192]
    g1_ref, qb_ref, pb_ref, g2_ref, f1b_ref, f2b_ref = vec_refs
    vec[0:1, 0:64] = g1_ref[...].astype(F32)
    vec[0:1, 64:128] = qb_ref[:, 0:64].astype(F32)
    vec[1:2, :] = qb_ref[:, 64:192].astype(F32)
    vec[2:3, 0:64] = pb_ref[...].astype(F32)
    vec[2:3, 64:128] = g2_ref[...].astype(F32)
    vec[3:4, :] = f1b_ref[:, 0:128].astype(F32)
    vec[4:5, :] = f1b_ref[:, 128:256].astype(F32)
    vec[5:6, 0:64] = f2b_ref[...].astype(F32)
    vec[5:6, 64:128] = jnp.zeros((1, 64), F32)
    vec[5:6, 64:66] = ids_ref[...].astype(F32)
    vec[6:8, :] = jnp.zeros((2, 128), F32)


def unpack_vectors(vecs, outs):
    gain1, qkv_bias, proj_bias, gain2, fc1_bias, fc2_bias, ids = outs
    for c in range(vecs.shape[0]):
        v = vecs[c]
        short = slice(64 * c, 64 * c + 64)
        gain1[:, short] = v[0:1, 0:64]
        qkv_bias[:, 192 * c : 192 * c + 64] = v[0:1, 64:128]
        qkv_bias[:, 192 * c + 64 : 192 * c + 192] = v[1:2, :]
        proj_bias[:, short] = v[2:3, 0:64]
        gain2[:, short] = v[2:3, 64:128]
        fc1_bias[:, 256 * c : 256 * c + 128] = v[3:4, :]
        fc1_bias[:, 256 * c + 128 : 256 * c + 256] = v[4:5, :]
        fc2_bias[:, short] = v[5:6, 0:64]
        for n in range(2):
            ids[2 * c + n : 2 * c + n + 1, :] = jnp.broadcast_to(
                v[5:6, 64 + n : 65 + n], (1, ids.shape[1])
            )


def unpack_first(units, weight, down, up):
    for c in range(units.shape[1]):
        for n in range(4):
            unit = units.at[n % 2, c, n // 2]
            weight[64 * c : 64 * c + 64, 384 * n : 384 * n + 384] = unit[:, 0:384]
            for a in range(2):
                low = unit[16 * a : 16 * a + 16, 384:512]
                high = unit[32 + 16 * a : 48 + 16 * a, 384:512]
                down[2 * n + a, :, 64 * c : 64 * c + 64] = low[:, 0:64]
                up[2 * n + a, :, 192 * c : 192 * c + 64] = low[:, 64:128]
                up[2 * n + a, :, 192 * c + 64 : 192 * c + 192] = high


def pack_second(unit, refs):
    proj_ref, fc1_ref, fc2_ref, pd_ref, pu_ref, f1d_ref, f1u_ref, f2d_ref, f2u_ref = refs
    unit[0:64] = proj_ref[...]
    for t in range(4):
        unit[64 + 64 * t : 128 + 64 * t] = fc1_ref[:, 128 * t : 128 * t + 128]
    unit[320:576] = fc2_ref[...]
    for a in range(2):
        at = 576 + 16 * a
        unit[at : at + 16, 0:64] = pd_ref[a]
        unit[at : at + 16, 64:128] = pu_ref[a]
        unit[at + 32 : at + 48, 0:64] = f1d_ref[a]
        unit[at + 32 : at + 48, 64:128] = f2u_ref[a]
        for half in range(2):
            lanes = slice(128 * half, 128 * half + 128)
            unit[at + 64 + 32 * half : at + 80 + 32 * half] = f1u_ref[a, :, lanes]
            unit[at + 128 + 32 * half : at + 144 + 32 * half] = f2d_ref[a, :, lanes]


class Bias:
    def __init__(self, source, table, pairs, found, wide, select):
        self.source, self.table, self.pairs, self.found = source, table, pairs, found
        self.wide, self.select = wide, select
        self.heads = source.shape[0]

    def prepare(self):
        heads, pairs = self.heads, self.pairs
        pairs[...] = jnp.zeros(pairs.shape, BF)
        for a in range(15):
            pairs[a * heads : (a + 1) * heads, 0:169] = self.source[:, 169 * a : 169 * a + 169]

    def first(self, start, end):
        heads, pairs, found = self.heads, self.pairs, self.found
        lane = lane_ids((pairs.shape[1], 128))
        row = lax.broadcasted_iota(jnp.int32, (pairs.shape[1], 128), 0)
        query_at = (lane // 7 + 4) % 7 * 13 + (lane % 7 + 4) % 7
        wanted = jnp.where(lane < 49, row - query_at - 84, 10000)

        def one_key(key, carry):
            key_at = (key // 7 + 4) % 7 * 13 + (key % 7 + 4) % 7
            pick = jnp.where(wanted + key_at == 0, 1.0, 0.0).astype(BF)
            value = dot(pairs[...], pick, NN)
            for a in range(15):
                found[a, pl.ds(key, heads, stride=56), :] = value[a * heads : (a + 1) * heads]
            return carry

        lax.fori_loop(start, end, one_key, 0, unroll=2)

    def middle(self):
        for a in range(15):
            self.wide[:, 128 * a : 128 * a + 128] = self.found[a].astype(BF)
        row = lax.broadcasted_iota(jnp.int32, (128, TOK), 0)
        gap = lane_ids((128, TOK)) - row
        for t in range(8):
            self.select[128 * t : 128 * t + 128, :] = jnp.where(
                (gap == (t + 4) % 8 * 49) & (row < 49), 1.0, 0.0
            ).astype(BF)

    def last(self, blocks):
        for block in blocks:
            t = (block + 4) % 8
            value = dot(self.wide[:, (7 - t) * 128 : (15 - t) * 128], self.select[...], NN) * LOG2E
            for m in range(self.heads):
                self.table[m, 49 * block : 49 * block + 49, :] = value[56 * m : 56 * m + 49]


def attend_kernel(*refs, scale, per_group, width, per_clip, remote_size):
    if remote_size:
        tok_ref, source_ref, *refs = refs
        first_refs, vec_refs, refs = refs[:4], refs[4:10], refs[10:]
        dy_ref, second_refs, refs = refs[0], refs[1:10], refs[10:]
    else:
        x_ref, gain_ref, weight_ref, bias_ref, ids_ref, down_ref, up_ref, table_ref, *refs = refs
    probs_ref, out_ref, qkv_ref, reduced_ref, down_own, up_own, *refs = refs
    if remote_size:
        dy_out_ref, units_ref, x_ref, weight_ref, gain_ref, *vec_outs, ids_ref = refs[:10]
        refs = refs[10:]
    keys, queries, values_t, out_t, scores, table, table_sem, query_mask, *refs = refs
    group = pl.program_id(1)
    groups = pl.num_programs(1)
    item = pl.program_id(0)
    step = item * groups + group
    feats = x_ref.shape[-1]
    rows = x_ref.shape[1]

    if remote_size:
        bias_ref, down_ref, up_ref, unit1, vec, unit2, units1, vecs, *refs = refs
        bias = Bias(source_ref, table, *refs[:4])
        place = Place(remote_size)
        x_rows = Rows(place, tok_ref, *refs[4:9])
        dy_rows = Rows(place, dy_ref, *refs[9:14])
        gather1 = Gather(place, unit1, units1, *refs[14:16])
        gather2 = Gather(place, unit2, units_ref, *refs[16:18])
        vec_send, vec_recv, own_sem = refs[18:]
        items = dy_ref.shape[0]

        def vec_copy(d):
            to = ((place.c + d) % remote_size, place.w)
            return remote(vec, vecs.at[place.c], vec_send.at[d], vec_recv.at[d], to)

        @pl.when(step == 0)
        def _():
            pack_first(unit1, vec, *first_refs, vec_refs)
            pack_second(unit2, second_refs)
            mine = place.k, place.c, place.x
            units1[mine] = unit1[...]
            vecs[place.c] = vec[...]
            own = pltpu.make_async_copy(unit2, units_ref.at[mine], own_sem)
            own.start()
            enter(
                [place.sibling, place.across]
                + [((place.c + d) % remote_size, place.w) for d in range(1, remote_size)]
            )
            gather1.begin()
            for i in range(items):
                x_rows.begin(i)
            for d in range(1, remote_size):
                vec_copy(d).start()
            bias.prepare()
            gather1.second()
            pl.loop(0, items)(x_rows.mix)
            bias.first(0, 16)
            gather1.from_z(0)
            bias.first(16, 32)
            gather1.from_y(-1)
            gather1.from_z(1)
            bias.first(32, 50)
            gather1.from_y(0)
            gather1.from_z(2)
            bias.middle()
            gather1.from_y(1)
            bias.last(range(0, 4))
            gather1.from_y(2)
            own.wait()
            gather2.begin()
            bias.last(range(4, 8))
            for d in range(1, remote_size):
                vec_copy(d).wait_recv()
            unpack_vectors(vecs, (gain_ref, bias_ref, *vec_outs, ids_ref))
            gather1.finish()
            unpack_first(units1, weight_ref, down_ref, up_ref)
            x_rows.end(x_ref, 0)
            gather2.second()
            for d in range(1, remote_size):
                vec_copy(d).wait_send()

        @pl.when(step == 1)
        def _():
            for i in range(items):
                dy_rows.begin(i)

        @pl.when(step == 3)
        def _():
            pl.loop(0, items)(dy_rows.mix)

        for n in range(2, items, 2):

            @pl.when(step == 4 * n)
            def _():
                x_rows.end(x_ref, n)

        for t, at in enumerate((4, 8, 12)):

            @pl.when(step == at)
            def _():
                gather2.from_z(t)

        for t, at in ((-1, 5), (0, 9), (1, 13), (2, 15)):

            @pl.when(step == at)
            def _():
                gather2.from_y(t)

        @pl.when(step == 4 * items - 1)
        def _():
            for i in range(0, items, 2):
                dy_rows.end(dy_out_ref, i)
            gather2.finish()
            x_rows.drain()
            dy_rows.drain()

    else:

        def table_copy(g):
            at = pl.ds(g * per_group, per_group)
            return pltpu.make_async_copy(table_ref.at[at], table.at[at], table_sem.at[g])

        @pl.when(step == 0)
        def _():
            for g in range(table.shape[0] // per_group):
                table_copy(g).start()

    @pl.when((group == 0) & (item % per_clip == 0))
    def _():
        clip = item // per_clip
        if remote_size:
            clip = clip + place.c * 2
        ids = ids_ref[...]
        row = lax.broadcasted_iota(jnp.int32, ids.shape, 0)
        mine = jnp.sum(jnp.where(row == clip, ids, 0.0), axis=0, keepdims=True)[:, 0:1]
        for ref, target in ((down_ref, down_own), (up_ref, up_own)):
            total = jnp.zeros(ref.shape[1:], F32)
            for a in range(ref.shape[0]):
                total = total + jnp.where(
                    mine == float(a), ref[a].astype(F32), 0.0
                )
            target[0] = total.astype(BF)

    @pl.when(group == 0)
    def _():
        number = lax.axis_index("win") * per_clip + item % per_clip
        early, low_h, low_w = row_masks(rows)
        label = (
            jnp.where(early, number // 4 % 2 * 4, 0)
            + jnp.where(low_h, number // 2 % 2 * 2, 0)
            + jnp.where(low_w, number % 2, 0)
        )
        lane = lane_ids((rows, 128))
        same = label == lane
        key_mask = jnp.where(same, 1.0, 0.0).astype(BF)
        query_mask[...] = jnp.where(same | (lane >= 8), 0.0, -FAR).astype(BF)
        normed, _ = norm_stats(x_ref[item if remote_size else 0].astype(F32))
        low = (normed * gain_ref[...]).astype(BF)
        reduced = dot(down_own[0], low, NT).astype(BF)
        reduced_ref[0] = reduced

        def columns(part):
            at = pl.ds(part * feats, feats)
            return (
                dot(low, weight_ref[:, at], NN)
                + bias_ref[:, at]
                + dot(reduced, up_own[0, :, at], TN)
            )

        query = (columns(0) * (scale * LOG2E)).astype(BF)
        queries[...] = query
        qkv_ref[0, :, :feats] = query
        key = columns(1).astype(BF)
        qkv_ref[0, :, feats : 2 * feats] = key
        for g in range(feats // 128):
            keys[:, 256 * g : 256 * g + 128] = key[:, 128 * g : 128 * g + 128]
            keys[:, 256 * g + 128 : 256 * g + 256] = key_mask
        value = columns(2).astype(BF)
        qkv_ref[0, :, 2 * feats :] = value
        values_t[...] = value.T

    if not remote_size:

        @pl.when(item == 0)
        def _():
            table_copy(group).wait()

    keys_now = keys[:, pl.ds(pl.multiple_of(group * 256, 256), 256)]
    query_now = queries[:, pl.ds(pl.multiple_of(group * 128, 128), 128)]
    head_of_lane = lane_ids(query_now.shape) // width

    def raw(h):
        own = jnp.where(head_of_lane == h, query_now, jnp.zeros_like(query_now))
        own = jnp.concatenate([own, query_mask[...]], axis=1)
        return dot(keys_now, own, NT) + table[group * per_group + h]

    def finish(h):
        score = scores[h % 2]
        largest = jnp.max(score, axis=0, keepdims=True)
        probs = jnp.exp2(score - largest)
        total = jnp.sum(probs, axis=0, keepdims=True)
        probs = (probs * (1.0 / total)).astype(BF)
        probs_ref[0, h] = probs
        at = pl.ds(pl.multiple_of((group * per_group + h) * width, width), width)
        out_t[at, :] = dot(values_t[at, :], probs, NN).astype(BF)

    scores[0] = raw(0)
    for h in range(per_group):
        if h + 1 < per_group:
            scores[(h + 1) % 2] = raw(h + 1)
        finish(h)

    @pl.when(group == groups - 1)
    def _():
        out_ref[0] = out_t[...].T


def dense_kernel(
    ids_ref,
    x_ref,
    attn_ref,
    gain_ref,
    proj_bias_ref,
    fc1_bias_ref,
    fc2_bias_ref,
    dy_ref,
    staged_ref,
    *refs,
    per_clip,
    chunk,
):
    tiles, refs = refs[:6], refs[6:]
    act_ref, dx1_ref, dattn_ref, grad_ref, *refs = refs
    proj_ref, fc1_ref, fc2_ref, proj_down, proj_up, fc1_down, fc1_up, fc2_down, fc2_up, *refs = refs
    pres, acts, dpres, sem = refs
    starting = pl.program_id(0) == 0
    count = x_ref.shape[1]
    feats = x_ref.shape[-1]
    hidden = fc1_ref.shape[-1]

    def moves(first=0, last=24):
        found = [(0, 64, proj_ref, 128 * n, n) for n in range(4)]
        found += [(64 + 64 * t, 64, fc1_ref, 512 * n + 128 * t, n) for n in range(4) for t in range(4)]
        found += [(320, 256, fc2_ref, 128 * n, n) for n in range(4)]
        return [
            pltpu.make_async_copy(
                staged_ref.at[n % 2, :, n // 2, pl.ds(start, size), :],
                target.at[:, :, pl.ds(lane, 128)],
                sem.at[at],
            )
            for at, (start, size, target, lane, n) in enumerate(found)
            if first <= at < last
        ]

    def arrive(first, last):
        @pl.when(starting)
        def _():
            for copy in moves(first, last):
                copy.wait()

    @pl.when(starting)
    def _():
        for copy in moves():
            copy.start()

    for n in range(8):
        short = slice(64 * n, 64 * n + 64)
        proj_down[:, short] = tiles[0][0, n, 0, :, 0:64]
        proj_up[:, short] = tiles[0][0, n, 0, :, 64:128]
        fc1_down[:, short] = tiles[1][0, n, 0, :, 0:64]
        fc2_up[:, short] = tiles[1][0, n, 0, :, 64:128]
        for half in range(2):
            long = slice(256 * n + 128 * half, 256 * n + 128 * half + 128)
            fc1_up[:, long] = tiles[2 + half][0, n, 0]
            fc2_down[:, long] = tiles[4 + half][0, n, 0]

    def join(parts):
        return jnp.concatenate(parts, axis=0) if per_clip > 1 else parts[0]

    dy = join([dy_ref[e] for e in range(per_clip)])
    attn = join([attn_ref[e] for e in range(per_clip)])
    reduced_proj = dot(proj_down[...], attn, NT).astype(BF)
    arrive(0, 4)
    proj_w = proj_ref[...].reshape(feats, feats)
    middle = (
        join([x_ref[e].astype(F32) for e in range(per_clip)])
        + dot(attn, proj_w, NN)
        + proj_bias_ref[...]
        + dot(reduced_proj, proj_up[...], TN)
    )
    normed, inverse = norm_stats(middle)
    low = (normed * gain_ref[...]).astype(BF)
    reduced_fc1 = dot(fc1_down[...], low, NT).astype(BF)
    grad_reduced_fc2 = dot(fc2_up[...], dy, NT).astype(BF)
    per_chunk = chunk // fc2_ref.shape[1]
    steps = hidden // chunk

    def pre_of(j):
        at = slice(j * chunk, (j + 1) * chunk)
        pres[j % 2] = (
            dot(low, fc1_ref[:, :, at].reshape(feats, chunk), NN)
            + fc1_bias_ref[:, at]
            + dot(reduced_fc1, fc1_up[:, at], TN)
        )

    arrive(4, 20)
    pre_of(0)
    arrive(20, 24)
    for j in range(steps):
        at = slice(j * chunk, (j + 1) * chunk)
        if j + 1 < steps:
            pre_of(j + 1)
        fc2_w = fc2_ref[j * per_chunk : (j + 1) * per_chunk].reshape(chunk, feats)
        dact = dot(dy, fc2_w, NT) + dot(grad_reduced_fc2, fc2_down[:, at], TN)
        pre = pres[j % 2]
        bell = jnp.exp2((pre * pre) * (-0.5 * LOG2E))
        t = 1.0 / (1.0 + jnp.abs(pre) * (0.3275911 * 0.7071067811865476))
        poly = (
            (((0.5 * 1.061405429) * t - 0.5 * 1.453152027) * t + 0.5 * 1.421413741) * t
            - 0.5 * 0.284496736
        ) * t + 0.5 * 0.254829592
        tail = poly * t * bell
        below = jnp.where(pre >= 0.0, 1.0 - tail, tail)
        acts[:, at] = (pre * below).astype(BF)
        dpres[:, at] = (dact * (below + pre * bell * 0.3989422804014327)).astype(BF)
    act = acts[...]
    dpre = dpres[...]
    fc1_up_at = 3 * feats
    fc2_down_at = fc1_up_at + hidden
    fc2_up_at = fc2_down_at + hidden
    fc2_w = fc2_ref[...].reshape(hidden, feats)
    grad_reduced_fc1 = dot(fc1_up[...], dpre, NT).astype(BF)
    dlow = dot(dpre, fc1_ref[...].reshape(feats, hidden), NT) + dot(grad_reduced_fc1, fc1_down[...], TN)
    dx1 = dy.astype(F32) + norm_back(dlow, gain_ref[...], normed, inverse)
    branch = dx1.astype(BF)
    reduced_fc2 = dot(fc2_down[...], act, NT).astype(BF)
    total = (
        middle + fc2_bias_ref[...] + dot(act, fc2_w, NN) + dot(reduced_fc2, fc2_up[...], TN)
    ).astype(BF)
    grad_reduced_proj = dot(proj_up[...], branch, NT).astype(BF)
    dattn = (
        dot(branch, proj_w, NT) + dot(grad_reduced_proj, proj_down[...], TN)
    ).astype(BF)
    for e in range(per_clip):
        rows = slice(e * count, (e + 1) * count)
        act_ref[e] = total[rows]
        dx1_ref[e] = dx1[rows]
        dattn_ref[e] = dattn[rows]
    grad_ref[0, :, :feats] = dot(grad_reduced_proj, attn, NN)
    grad_ref[0, :, feats : 2 * feats] = dot(reduced_proj, branch, NN)
    grad_ref[0, :, 2 * feats : fc1_up_at] = dot(grad_reduced_fc1, low, NN)
    grad_ref[0, :, fc1_up_at:fc2_down_at] = dot(reduced_fc1, dpre, NN)
    grad_ref[0, :, fc2_down_at:fc2_up_at] = dot(grad_reduced_fc2, act, NN)
    grad_ref[0, :, fc2_up_at:] = dot(reduced_fc2, dy, NN)


PIECES = (
    (0, 0, 64),
    (0, 512, 192),
    (1, 0, 64),
    (1, 512, 64),
    (1, 1024, 64),
    (1, 5632, 64),
    (1, 1536, 256),
    (1, 3584, 256),
)


def gradient_rows(sources, part, j, pieces):
    halves = []
    for n in range(2):
        cells = []
        for array, start, width in pieces:
            at = slice(start + j * width, start + (j + 1) * width)
            cells.append(sources[array][n, pl.ds(pl.multiple_of(part * 8, 8), 8), at])
        halves.append(jnp.concatenate(cells, axis=1))
    return jnp.concatenate(halves, axis=0)


def early_gradients(place, sources, own, other):
    for j in range(own.shape[0]):
        own[j, :, 256:] = gradient_rows(sources, place.k, j, PIECES[2:])
        other[j, :, 256:] = gradient_rows(sources, 1 - place.k, j, PIECES[2:]).astype(BF)


def share_gradients(place, sources, ids_ref, refs, send, between):
    own, other, from_core, half, from_x, shares, from_clips, adapters, from_win, out = refs
    c, w, x, k = place.c, place.w, place.x, place.k
    clip_size = own.shape[0]
    for j in range(clip_size):
        other[j, :, 0:256] = gradient_rows(sources, 1 - k, j, PIECES[:2]).astype(BF)
    core_copy = send.copy(other, from_core, place.sibling)
    between[0]()
    for j in range(clip_size):
        own[j, :, 0:256] = gradient_rows(sources, k, j, PIECES[:2])
    core_copy.wait_recv()
    own[...] += from_core[...].astype(F32)
    half[...] = own[:, :, pl.ds(pl.multiple_of((1 - x) * 512, 512), 512)].astype(BF)
    x_copy = send.copy(half, from_x, place.across)
    between[1]()
    x_copy.wait_recv()
    shares[...] = (
        own[:, :, pl.ds(pl.multiple_of(x * 512, 512), 512)] + from_x[...].astype(F32)
    ).astype(BF)
    from_clips[c] = shares[c]
    clip_copies = []
    for d in range(1, clip_size):
        to = (c + d) % clip_size
        clip_copies.append(send.copy(shares.at[to], from_clips.at[c], (to, w)))
    for copy in clip_copies:
        copy.wait_recv()
    for a in range(8):
        total = None
        for n in range(2 * clip_size):
            value = from_clips[n // 2].astype(F32)[8 * (n % 2) : 8 * (n % 2) + 8]
            value = jnp.where(ids_ref[n : n + 1, :] == float(a), value, 0.0)
            total = value if total is None else total + value
        adapters[a // 2, 8 * (a % 2) : 8 * (a % 2) + 8, :] = total
    from_win[w] = adapters[w]
    win_copies = []
    for d in range(1, 4):
        to = (w + d) % 4
        win_copies.append(send.copy(adapters.at[to], from_win.at[w], (c, to)))
    between[2]()
    for copy in win_copies:
        copy.wait_recv()
    for x2 in range(2):
        for k2 in range(2):
            for a in range(2):
                out[a, 8 * k2 : 8 * k2 + 8, 512 * x2 : 512 * x2 + 512] = from_win[
                    2 * x2 + k2, 8 * a : 8 * a + 8, :
                ]
    for copy in [core_copy, x_copy, *clip_copies, *win_copies]:
        copy.wait_send()


def attend_back_kernel(
    x_ref,
    gain_ref,
    weight_ref,
    down_ref,
    up_ref,
    probs_ref,
    attn_ref,
    qkv_ref,
    reduced_ref,
    dattn_ref,
    dx1_ref,
    *refs,
    scale,
    per_group,
    width,
    per_clip,
    remote_size,
):
    if remote_size:
        act_ref, grad_dense_ref, ids_ref, act_out_ref, dx_out_ref, sums_ref, *refs = refs
    else:
        dx_ref, grad_ref, *refs = refs
    values, keys_t, inner, dqkv, dquery_t, *refs = refs
    group = pl.program_id(1)
    groups = pl.num_programs(1)
    item = pl.program_id(0)
    step = item * groups + group
    if remote_size:
        items = act_ref.shape[0]
        place = Place(remote_size)
        act_rows = Rows(place, act_ref, *refs[:5])
        dx_own = refs[5]
        dx_rows = Rows(place, *refs[5:11])
        grad_ref = refs[11]
        share_refs, sems = refs[12:21], refs[21:]

        @pl.when(step == 0)
        def _():
            enter(
                [(place.c, (place.w + d) % 4) for d in range(1, 4)]
                + [((place.c + d) % remote_size, place.w) for d in range(1, remote_size)]
            )
            for i in range(items):
                act_rows.begin(i)

        for i in range(items):

            @pl.when(step == i + 1)
            def _():
                act_rows.mix(i)

            if i < items - 1:

                @pl.when(step == (i + 1) * 4 + 1)
                def _():
                    dx_rows.mix(i)

        @pl.when(step == 6)
        def _():
            early_gradients(place, (None, grad_dense_ref), share_refs[0], share_refs[1])

        @pl.when(step == 4 * items - 3)
        def _():
            for i in range(0, items, 2):
                act_rows.end(act_out_ref, i)
            act_rows.drain()

    feats = x_ref.shape[-1]
    rows = x_ref.shape[1]

    @pl.when(group == 0)
    def _():
        keys_t[...] = qkv_ref[0, :, feats : 2 * feats].T
        lane = lane_ids((rows, 128))
        ones = jnp.where(lane % width < 2, 1.0, 0.0).astype(BF)
        source = lax.broadcasted_iota(jnp.int32, (128, 128), 0)
        target = lane_ids((128, 128))
        pick = jnp.where(
            (source // width == target // width) & (target % width < 2), 1.0, 0.0
        ).astype(BF)
        pick = jnp.concatenate([pick, pick], axis=0)
        for g in range(feats // 128):
            at = slice(128 * g, 128 * g + 128)
            values[:, 256 * g : 256 * g + 128] = qkv_ref[0, :, 2 * feats + 128 * g : 2 * feats + 128 * g + 128]
            values[:, 256 * g + 128 : 256 * g + 256] = ones
            product = dattn_ref[0, :, at].astype(F32) * attn_ref[0, :, at].astype(F32)
            high = product.astype(BF)
            rest = (product - high.astype(F32)).astype(BF)
            sums = dot(jnp.concatenate([high, rest], axis=1), pick, NN)
            coarse = sums.astype(BF)
            fine = (sums - coarse.astype(F32)).astype(BF)
            inner[:, at] = -jnp.where(lane % width == 0, coarse, fine)

    blocks = pl.ds(pl.multiple_of(group * 128, 128), 128)
    values_now = values[:, pl.ds(pl.multiple_of(group * 256, 256), 256)]
    dattn_now = dattn_ref[0, :, blocks]
    inner_now = inner[:, blocks]
    query_now = qkv_ref[0, :, blocks]
    head_of_lane = lane_ids((rows, 128)) // width
    zero = jnp.zeros((rows, 128), BF)
    dvalue = None
    dkey = None

    def dprobs_of(h):
        mine = head_of_lane == h
        dattn_own = jnp.where(mine, dattn_now, zero)
        right = jnp.concatenate([dattn_own, jnp.where(mine, inner_now, zero)], axis=1)
        return dattn_own, dot(values_now, right, NT).astype(BF)

    ready = dprobs_of(0)
    for h in range(per_group):
        dattn_own, dprobs = ready
        if h + 1 < per_group:
            ready = dprobs_of(h + 1)
        query_own = jnp.where(head_of_lane == h, query_now, zero)
        probs = probs_ref[0, h]
        dscore = probs * dprobs
        partial = dot(probs, dattn_own, NN)
        dvalue = partial if dvalue is None else dvalue + partial
        partial = dot(dscore, query_own, NN)
        dkey = partial if dkey is None else dkey + partial
        at = pl.ds(pl.multiple_of((group * per_group + h) * width, width), width)
        dquery_t[at, :] = (dot(keys_t[at, :], dscore, NN) * scale).astype(BF)
    dqkv[:, pl.ds(pl.multiple_of(2 * feats + group * 128, 128), 128)] = dvalue.astype(BF)
    dqkv[:, pl.ds(pl.multiple_of(feats + group * 128, 128), 128)] = (dkey * LN2).astype(BF)

    @pl.when(group == groups - 1)
    def _():
        first = pl.program_id(0) % per_clip == 0
        dqkv[:, :feats] = dquery_t[...].T
        dall = dqkv[...]
        normed, inverse = norm_stats(x_ref[0].astype(F32))
        low = (normed * gain_ref[...]).astype(BF)
        grad_reduced = dot(up_ref[0], dall, NT).astype(BF)
        slot = item // per_clip if remote_size else 0
        add_rows(grad_ref, slot, slice(feats, 4 * feats), dot(reduced_ref[0], dall, NN), first)
        add_rows(grad_ref, slot, slice(0, feats), dot(grad_reduced, low, NN), first)
        dlow = (dot(dall, weight_ref[...], NT) + dot(grad_reduced, down_ref[0], TN)).astype(BF)
        dx = (dx1_ref[0] + norm_back(dlow.astype(F32), gain_ref[...], normed, inverse)).astype(BF)
        if not remote_size:
            dx_ref[0] = dx
            return
        dx_own[item] = dx
        for i in range(items):

            @pl.when(item == i)
            def _():
                dx_rows.begin(i)

    if remote_size:

        @pl.when(step == 4 * items - 1)
        def _():
            share_gradients(
                place,
                (grad_ref, grad_dense_ref),
                ids_ref,
                (*share_refs, sums_ref),
                Sender(*sems),
                (
                    lambda: None,
                    lambda: dx_rows.mix(items - 1),
                    lambda: [dx_rows.end(dx_out_ref, i) for i in range(0, items, 2)],
                ),
            )
            dx_rows.drain()


def whole(shape):
    return pl.BlockSpec(shape, lambda *at: (0,) * len(shape), pipeline_mode=pl.Buffered(1))


def compute(first, dy, adapter_ids, vectors, later, per_clip, remote_size):
    if remote_size:
        heads = first[1].shape[0]
        x_shape, rank = dy.shape, 16
    else:
        x, qkv_w, qkv_down, qkv_up, table = first
        heads, rank = table.shape[0], qkv_down.shape[1]
    items, rows, feats = dy.shape
    width = feats // heads
    per_group = 128 // width
    groups = heads // per_group
    scale = width**-0.5
    hidden = 4 * feats
    clips = items // per_clip

    def item(shape):
        return pl.BlockSpec((1, *shape), lambda i, *rest: (i,) + (0,) * len(shape))

    item_ids = adapter_ids
    any_space = pl.BlockSpec(memory_space=pl.ANY)

    def of_clip(shape):
        return pl.BlockSpec((1, *shape), lambda i, *rest: (i // per_clip, 0, 0))

    sems = pltpu.SemaphoreType.DMA
    if remote_size:
        shape = jax.ShapeDtypeStruct
        adapters = 8
        padded = 56 * heads
        ids = adapter_ids[None]
        args = (*first, ids, *[v.reshape(1, -1) for v in vectors], dy, *later)
        arg_specs = [whole(a.shape) for a in args]
        sent_out = [
            shape(dy.shape, BF),
            shape((2, remote_size, 2, 768, 128), BF),
            shape(dy.shape, BF),
            shape((feats, 3 * feats), BF),
            *[shape((1, n), F32) for n in (feats, feats, feats, hidden, feats)],
            shape((2 * remote_size, 512), F32),
        ]
        sent_specs = [whole(a.shape) for a in sent_out]
        sent_specs[1] = any_space
        row_scratch = [
            pltpu.VMEM(dy.shape, BF),
            pltpu.VMEM(dy.shape, BF),
            pltpu.VMEM((items, TOP, feats), BF),
            sems((2 * items,)),
            sems((2 * items,)),
        ]
        sent_scratch = [
            pltpu.VMEM((1, 3 * feats), F32),
            pltpu.VMEM((adapters, rank, feats), BF),
            pltpu.VMEM((adapters, rank, 3 * feats), BF),
            pltpu.VMEM((64, 512), BF),
            pltpu.VMEM((8, 128), F32),
            pltpu.VMEM((768, 128), BF),
            pltpu.VMEM((2, remote_size, 2, 64, 512), BF),
            pltpu.VMEM((remote_size, 8, 128), F32),
            pltpu.VMEM((15 * heads, 176), BF),
            pltpu.VMEM((15, padded, 128), F32),
            pltpu.VMEM((padded, 15 * 128), BF),
            pltpu.VMEM((8 * 128, rows), BF),
            *row_scratch,
            *row_scratch,
            *[sems((Gather.COPIES,)) for _ in range(4)],
            sems((remote_size,)),
            sems((remote_size,)),
            sems,
        ]
    else:
        gain1, qkv_bias, proj_bias, gain2, fc1_bias, fc2_bias = vectors
        clip_ids = jnp.broadcast_to(adapter_ids.astype(F32)[:, None], (clips, 128))
        args = (x, gain1, qkv_w, qkv_bias, clip_ids, qkv_down, qkv_up, table)
        arg_specs = [item((rows, feats)), *[whole(a.shape) for a in args[1:7]], any_space]
        sent_out, sent_specs, sent_scratch = [], [], []

    probs, attn, qkv, reduced, down_own, up_own, *arrived = pl.pallas_call(
        functools.partial(
            attend_kernel,
            scale=scale,
            per_group=per_group,
            width=width,
            per_clip=per_clip,
            remote_size=remote_size,
        ),
        grid=(items, groups),
        in_specs=arg_specs,
        out_specs=[
            pl.BlockSpec((1, per_group, rows, rows), lambda i, g: (i, g, 0, 0)),
            item((rows, feats)),
            item((rows, 3 * feats)),
            item((rank, rows)),
            of_clip((rank, feats)),
            of_clip((rank, 3 * feats)),
            *sent_specs,
        ],
        scratch_shapes=[
            pltpu.VMEM((rows, 2 * feats), BF),
            pltpu.VMEM((rows, feats), BF),
            pltpu.VMEM((feats, rows), BF),
            pltpu.VMEM((feats, rows), BF),
            pltpu.VMEM((2, rows, rows), F32),
            pltpu.VMEM((heads, rows, rows), F32),
            sems((groups,)),
            pltpu.VMEM((rows, 128), BF),
            *sent_scratch,
        ],
        out_shape=[
            jax.ShapeDtypeStruct((items, heads, rows, rows), BF),
            jax.ShapeDtypeStruct((items, rows, feats), BF),
            jax.ShapeDtypeStruct((items, rows, 3 * feats), BF),
            jax.ShapeDtypeStruct((items, rank, rows), BF),
            jax.ShapeDtypeStruct((clips, rank, feats), BF),
            jax.ShapeDtypeStruct((clips, rank, 3 * feats), BF),
            *sent_out,
        ],
        compiler_params=pltpu.CompilerParams(
            vmem_limit_bytes=VMEM_LIMIT,
            dimension_semantics=("arbitrary", "arbitrary"),
            **({"collective_id": 2, "has_side_effects": True} if remote_size else {}),
        ),
        cost_estimate=pl.CostEstimate(flops=4 * 10**10, bytes_accessed=10**7, transcendentals=0),
        name="attend",
    )(*args)
    if remote_size:
        dy, staged, x, qkv_w, gain1, proj_bias, gain2, fc1_bias, fc2_bias, all_ids = arrived
    else:
        (staged,) = later

    span = 4 * feats + 2 * hidden
    def tile(n):
        def index(c, ids):
            return ids[c] // 2 % 2, 0, ids[c] // 4, 36 + 2 * n + ids[c] % 2, 0

        return pl.BlockSpec((1, 8, 1, rank, 128), index)

    def clip(array_shape):
        return pl.BlockSpec((per_clip, *array_shape[1:]), lambda c, ids: (c, 0, 0))

    chunk = 512
    act, dx1, dattn, grad_dense = pl.pallas_call(
        functools.partial(dense_kernel, per_clip=per_clip, chunk=chunk),
        grid_spec=pltpu.PrefetchScalarGridSpec(
            num_scalar_prefetch=1,
            grid=(clips,),
            in_specs=[
                clip(x.shape),
                clip(x.shape),
                whole(gain2.shape),
                whole(proj_bias.shape),
                whole(fc1_bias.shape),
                whole(fc2_bias.shape),
                clip(x.shape),
                any_space,
                *[tile(n) for n in range(6)],
            ],
            out_specs=[
                clip(x.shape),
                clip(x.shape),
                clip(x.shape),
                pl.BlockSpec((1, rank, span), lambda c, ids: (c, 0, 0)),
            ],
            scratch_shapes=[
                pltpu.VMEM((8, feats // 8, feats), BF),
                pltpu.VMEM((8, feats // 8, hidden), BF),
                pltpu.VMEM((8, hidden // 8, feats), BF),
                *[pltpu.VMEM((rank, n), BF) for n in (feats, feats, feats, hidden, hidden, feats)],
                pltpu.VMEM((2, per_clip * rows, chunk), F32),
                pltpu.VMEM((per_clip * rows, hidden), BF),
                pltpu.VMEM((per_clip * rows, hidden), BF),
                pltpu.SemaphoreType.DMA((24,)),
            ],
        ),
        out_shape=[
            jax.ShapeDtypeStruct((items, rows, feats), BF),
            jax.ShapeDtypeStruct((items, rows, feats), F32),
            jax.ShapeDtypeStruct((items, rows, feats), BF),
            jax.ShapeDtypeStruct((clips, rank, span), F32),
        ],
        compiler_params=pltpu.CompilerParams(
            vmem_limit_bytes=VMEM_LIMIT, dimension_semantics=("arbitrary",)
        ),
        cost_estimate=pl.CostEstimate(flops=5 * 10**10, bytes_accessed=10**7, transcendentals=0),
        name="dense",
    )(
        item_ids, x, attn, gain2, proj_bias, fc1_bias, fc2_bias, dy, staged, *([staged] * 6)
    )

    if remote_size:
        assert (clips, per_clip) == (2, 2)
        count = remote_size
        back_in = (act, grad_dense, all_ids)
        back_out = [whole(x.shape), whole(x.shape), whole((2, rank, 1024))]
        back_shape = [
            jax.ShapeDtypeStruct(x.shape, BF),
            jax.ShapeDtypeStruct(x.shape, BF),
            jax.ShapeDtypeStruct((2, rank, 1024), F32),
        ]
        back_scratch = [
            *row_scratch,
            pltpu.VMEM(x.shape, BF),
            *row_scratch,
            pltpu.VMEM((clips, rank, 4 * feats), F32),
            pltpu.VMEM((count, 16, 1024), F32),
            pltpu.VMEM((count, 16, 1024), BF),
            pltpu.VMEM((count, 16, 1024), BF),
            pltpu.VMEM((count, 16, 512), BF),
            pltpu.VMEM((count, 16, 512), BF),
            pltpu.VMEM((count, 16, 512), BF),
            pltpu.VMEM((count, 16, 512), BF),
            pltpu.VMEM((4, 16, 512), F32),
            pltpu.VMEM((4, 16, 512), F32),
            sems((16,)),
            sems((16,)),
        ]
    else:
        back_in, back_scratch = (), []
        back_out = [
            item((rows, feats)),
            pl.BlockSpec((1, rank, 4 * feats), lambda i, g: (i // per_clip, 0, 0)),
        ]
        back_shape = [
            jax.ShapeDtypeStruct((items, rows, feats), BF),
            jax.ShapeDtypeStruct((clips, rank, 4 * feats), F32),
        ]
    results = pl.pallas_call(
        functools.partial(
            attend_back_kernel,
            scale=scale,
            per_group=per_group,
            width=width,
            per_clip=per_clip,
            remote_size=remote_size,
        ),
        grid=(items, groups),
        in_specs=[
            item((rows, feats)),
            whole(gain1.shape),
            whole(qkv_w.shape),
            of_clip((rank, feats)),
            of_clip((rank, 3 * feats)),
            pl.BlockSpec((1, per_group, rows, rows), lambda i, g: (i, g, 0, 0)),
            item((rows, feats)),
            item((rows, 3 * feats)),
            item((rank, rows)),
            item((rows, feats)),
            item((rows, feats)),
            *[whole(a.shape) for a in back_in],
        ],
        out_specs=back_out,
        scratch_shapes=[
            pltpu.VMEM((rows, 2 * feats), BF),
            pltpu.VMEM((feats, rows), BF),
            pltpu.VMEM((rows, feats), BF),
            pltpu.VMEM((rows, 3 * feats), BF),
            pltpu.VMEM((feats, rows), BF),
            *back_scratch,
        ],
        out_shape=back_shape,
        compiler_params=pltpu.CompilerParams(
            vmem_limit_bytes=VMEM_LIMIT, dimension_semantics=("arbitrary", "arbitrary"),
            **({"collective_id": 1, "has_side_effects": True} if remote_size else {}),
        ),
        cost_estimate=pl.CostEstimate(flops=5 * 10**10, bytes_accessed=10**7, transcendentals=0),
        name="attend_back",
    )(x, gain1, qkv_w, down_own, up_own, probs, attn, qkv, reduced, dattn, dx1, *back_in)
    if remote_size:
        return results
    return (act, *results, grad_dense)


def exchange(x, win_size):
    local = x.shape[1]
    bits = local.bit_length() - 1
    at = jnp.arange(TOK)
    taken = (at // 49 < 4, at // 7 % 7 < 3, at % 7 < 3)
    for bit, rows in zip((2, 1, 0), taken):
        if bit < bits:
            split = x.reshape(x.shape[0], local >> (bit + 1), 2, 1 << bit, TOK, -1)
            other = jnp.flip(split, axis=2).reshape(x.shape)
        else:
            other = lax.ppermute(x, "win", [(i, i ^ 1 << bit - bits) for i in range(win_size)])
        x = jnp.where(rows[None, None, :, None], other, x)
    return x


def bias_by_pair(table):
    heads = table.shape[0]
    side = jnp.arange(49)
    high, wide = (side // 7 + 4) % 7, (side % 7 + 4) % 7
    offset = (high[None, :] - high[:, None] + 6) * 13 + wide[None, :] - wide[:, None] + 6
    pick = (jnp.arange(169)[:, None, None] == offset[None]).astype(BF)
    found = jnp.einsum(
        "mad,dkq->mkaq", table.reshape(heads, 15, 169), pick, preferred_element_type=F32
    )
    found = (found * LOG2E).reshape(heads, 49, 15 * 49)
    blocks = []
    for key_block in range(8):
        t = (key_block + 4) % 8
        blocks.append(
            jnp.concatenate(
                (found[..., (11 - t) * 49 : (15 - t) * 49], found[..., (7 - t) * 49 : (11 - t) * 49]),
                axis=-1,
            )
        )
    return jnp.stack(blocks, axis=1).reshape(heads, TOK, TOK)


def gather(array, spec):
    for axis, name in enumerate(spec):
        if name is not None:
            array = lax.all_gather(array, name, axis=axis, tiled=True)
    return array


def stage_whole(proj_w, fc1_w, fc2_w, maps):
    proj_down, proj_up, fc1_down, fc1_up, fc2_down, fc2_up = maps
    count = proj_down.shape[0]

    def short(a):
        return a.reshape(4, count // 4 * 16, 8, 64).transpose(2, 0, 1, 3)

    def long(a):
        return a.reshape(4, count // 4 * 16, 8, 2, 128).transpose(2, 0, 3, 1, 4).reshape(8, 4, -1, 128)

    return jnp.concatenate(
        (
            proj_w.reshape(8, 64, 4, 128).transpose(0, 2, 1, 3),
            fc1_w.reshape(8, 64, 4, 4, 128).transpose(0, 2, 3, 1, 4).reshape(8, 4, 256, 128),
            fc2_w.reshape(8, 256, 4, 128).transpose(0, 2, 1, 3),
            jnp.concatenate((short(proj_down), short(proj_up)), axis=-1),
            jnp.concatenate((short(fc1_down), short(fc2_up)), axis=-1),
            long(fc1_up),
            long(fc2_down),
        ),
        axis=2,
    )


def by_core(staged):
    return staged.reshape(8, 2, 2, *staged.shape[2:]).transpose(2, 0, 1, 3, 4)


def per_device(
    tokens, cotangent, adapter_ids, ln1_gain, qkv_weight, qkv_bias, proj_weight, proj_bias, ln2_gain,
    fc1_weight, fc1_bias, fc2_weight, fc2_bias, bias_table, qkv_down, qkv_up, proj_down, proj_up,
    fc1_down, fc1_up, fc2_down, fc2_up, *, clip_size, win_size,
):
    clips, local, rows, feats = tokens.shape
    items = clips * local
    heads = bias_table.shape[0]
    vecs = (ln1_gain, qkv_bias, proj_bias, ln2_gain, fc1_bias, fc2_bias)
    flat = (items, rows, feats)
    downs = [a.transpose(0, 2, 1) for a in (qkv_down, proj_down, fc1_down, fc2_down)]
    own_kernels = (clip_size, win_size, clips, local) == (8, 4, 2, 2)
    if own_kernels:
        first = (tokens.reshape(flat), bias_table, qkv_weight, downs[0], qkv_up)
        dy = cotangent.reshape(flat)
        vectors = vecs
        later = (proj_weight, fc1_weight, fc2_weight, downs[1], proj_up, downs[2], fc1_up, downs[3], fc2_up)
    else:
        grid2, by_down, by_up = ("clip", "win"), ("win", None, "clip"), ("win", None, "clip")
        maps = (downs[1], proj_up, downs[2], fc1_up, downs[3], fc2_up)
        staged = stage_whole(
            *[gather(a, grid2) for a in (proj_weight, fc1_weight, fc2_weight)],
            [gather(a, by_up) for a in maps],
        )
        later = (by_core(staged),)
        vectors = [gather(v, ("clip",)).reshape(1, -1).astype(F32) for v in vecs]
        first = (
            exchange(tokens, win_size).reshape(flat),
            gather(qkv_weight, grid2),
            gather(downs[0], by_down),
            gather(qkv_up, by_up),
            bias_by_pair(bias_table),
        )
        dy = exchange(cotangent, win_size).reshape(flat)
    results = compute(
        first, dy, adapter_ids, vectors, later, local, clip_size if own_kernels else 0
    )
    if own_kernels:
        act_out, dx_out, sums = results
        qd, qu, pd, pu, f1d, f2u, f1u, f2d = [
            sums[..., first:last]
            for first, last in zip(
                (0, 64, 256, 320, 384, 448, 512, 768), (64, 256, 320, 384, 448, 512, 768, 1024)
            )
        ]
        turned = [a.transpose(0, 2, 1) for a in (qd, pd, f1d, f2d)]
        return (
            act_out.reshape(tokens.shape), dx_out.reshape(tokens.shape),
            turned[0], qu, turned[1], pu, turned[2], f1u, turned[3], f2u,
        )
    act, dx, grad_qkv, grad_dense = results
    activations = exchange(act.reshape(tokens.shape), win_size)
    input_grad = exchange(dx.reshape(tokens.shape), win_size)
    adapter_count = win_size * qkv_down.shape[0]
    hot = (adapter_ids[:, None] == jnp.arange(adapter_count)[None]).astype(F32)
    hidden = fc1_weight.shape[1] * win_size
    spans = (feats, 3 * feats, feats, feats, feats, hidden, hidden, feats)
    grads = jnp.concatenate((grad_qkv, grad_dense), axis=-1)
    rank = grads.shape[1]
    parts, at = [], 0
    for span in spans:
        parts.append(
            grads[..., at : at + span].reshape(clips, rank, clip_size, span // clip_size)
        )
        at += span
    mine = jnp.concatenate(parts, axis=-1)
    grown = jnp.sum(hot[:, :, None, None, None] * mine[:, None], axis=0)
    grown = grown.transpose(2, 0, 1, 3).astype(BF)
    total = lax.psum_scatter(grown, "clip", scatter_dimension=0, tiled=True)[0]
    total = lax.psum_scatter(total, "win", scatter_dimension=0, tiled=True).astype(F32)
    outs, at = [], 0
    for n, span in enumerate(spans):
        width = span // clip_size
        part = total[..., at : at + width]
        at += width
        outs.append(part.transpose(0, 2, 1) if n % 2 == 0 else part)
    return (activations, input_grad, *outs)


def solution(mesh):
    split = P("clip", "win", None, None)
    grid2 = P("clip", "win")
    down = P("win", "clip", None)
    up = P("win", None, "clip")
    one = P("clip")
    return jax.shard_map(
        functools.partial(
            per_device, clip_size=mesh.shape["clip"], win_size=mesh.shape["win"]
        ),
        mesh=mesh,
        in_specs=(
            split, split, one, one, grid2, one, grid2, one, one, grid2, one, grid2, one, P(),
            down, up, down, up, down, up, down, up,
        ),
        out_specs=(split, split, down, up, down, up, down, up, down, up),
        check_vma=False,
    )
```
